32 devices in a mesh: row: 8 (over y, x, core), col: 4 (over z).
Axes of the slice: x: 2, y: 2, z: 4, core: 2. Of those that a mesh axis runs over, the one named last changes fastest.
Arguments:
- features: bfloat16 [16384, 256], P('col', 'row'), may hold values from -6 to 6
- weight: bfloat16 [256, 256], replicated, may hold values from -0.375 to 0.375
- adj_values: bfloat16 [8, 4, 96, 128, 128], P('row', 'col'), may hold values from -0.125 to 0.125
- block_rows: int32 [8, 4, 96], P('row', 'col'), may hold values from 0 to 15, as said below
- block_cols: int32 [8, 4, 96], P('row', 'col'), may hold values from 0 to 31
- block_counts: int32 [8, 4], P('row', 'col'), may hold values from 1 to 96, as said below
- cotangent: bfloat16 [16384, 256], P(('row', 'col')), may hold values from -6 to 6
Outputs:
- output: bfloat16 [16384, 256], P(('row', 'col'))
- grad_weight: float32 [256, 256], replicated
- grad_features: bfloat16 [16384, 256], P('col', 'row')
The draws below stay inside these ranges and needn't reach their ends.
Inputs may be any that keep to these rules, and one draw needn't show every extreme that they name: Within one tile the pairs (block_rows, block_cols) over all 96 slots are distinct. `block_counts`: some tile holds exactly 96 live blocks and some other tile exactly one in every draw.
All inputs are finite; a program needn't handle non-finite values.
Results may differ from the reference program's by a relative error of at most 0.029.
Values may be sent and summed in bfloat16 or wider, within the bound.
No kernel may reach another device: no remote copies, remote signals or barrier semaphores. Data moves between devices by JAX's collectives and lax.ppermute only.
A program may use at most 64 MiB of HBM per device.

```python
import math
import jax
import jax.numpy as jnp
from jax import lax

F = 256
BLK = 128
RB = 16
CB = 32
MAXB = 96
NODES = 16384
N_ROW = 8
N_COL = 4


def tile_slots(key):
    base_key = jax.random.fold_in(key, 7)
    tile_keys = jax.random.split(base_key, N_ROW * N_COL)
    orders = jax.vmap(lambda tile_key: jax.random.permutation(tile_key, RB * CB))(tile_keys)
    return orders[:, :MAXB].reshape(N_ROW, N_COL, MAXB).astype(jnp.int32)


def draw_block_rows(key, part):
    return (tile_slots(key) // CB).astype(jnp.int32)


def draw_block_cols(key, part):
    return (tile_slots(key) % CB).astype(jnp.int32)


def draw_block_counts(key, part):
    first_key, second_key, third_key, fourth_key = jax.random.split(jax.random.fold_in(key, 11), 4)
    levels = jax.random.randint(first_key, (N_ROW, 1), MAXB // 4, MAXB + 1, dtype=jnp.int32)
    jitter = jax.random.randint(second_key, (N_ROW, N_COL), 0, MAXB // 8 + 1, dtype=jnp.int32)
    counts = jnp.maximum(levels - jitter, 1)
    total_tiles = N_ROW * N_COL
    chosen = jax.random.randint(third_key, (), 0, total_tiles, dtype=jnp.int32)
    step_away = jax.random.randint(fourth_key, (), 1, total_tiles, dtype=jnp.int32)
    lonely = (chosen + step_away) % total_tiles
    places = jnp.arange(total_tiles, dtype=jnp.int32).reshape(N_ROW, N_COL)
    counts = jnp.where(places == lonely, 1, counts)
    return jnp.where(places == chosen, MAXB, counts).astype(jnp.int32)


def block_scale(own_key, shape, pieces, least, largest):
    level = 1.0
    for dim, shards_of in pieces:
        steps = jax.random.uniform(jax.random.fold_in(jax.random.fold_in(own_key, 6), dim), (shards_of,), jnp.float32, least / len(pieces), largest / len(pieces))
        level = level * jnp.repeat(jnp.exp(steps), shape[dim] // shards_of).reshape((-1,) + (1,) * (len(shape) - 1 - dim))
    return level


def scatter_about(stream_key, shape, scale, bound, cuts=(), held_as=jnp.bfloat16):
    entries = scale * jax.random.normal(stream_key, shape, jnp.float32)
    if cuts:
        entries = entries * block_scale(stream_key, shape, cuts, -0.22, 0.18)
    return jnp.clip(entries, -bound, bound).astype(held_as)


def setup_inputs(seed: int = 0) -> dict:
    key_of = jax.random.split(jax.random.key(seed), 8)
    return {
        "features": scatter_about(key_of[0], (NODES, F), 1.0, 6.0, ((0, 4), (1, 8))),
        "weight": scatter_about(key_of[1], (F, F), F ** -0.5, 0.375),
        "adj_values": scatter_about(key_of[2], (N_ROW, N_COL, MAXB, BLK, BLK), (5 * MAXB * N_COL * BLK // (8 * RB)) ** -0.5, 0.125, ((0, 8), (1, 4))),
        "block_rows": draw_block_rows(jax.random.fold_in(key_of[7], 71), 0),
        "block_cols": draw_block_cols(jax.random.fold_in(key_of[7], 71), 0),
        "block_counts": draw_block_counts(jax.random.fold_in(key_of[7], 71), 0),
        "cotangent": scatter_about(key_of[6], (NODES, F), 1.0, 6.0, ((0, 32),)),
    }


def reference(features, weight, adj_values, block_rows, block_cols, block_counts, cotangent):
    is_live = (jnp.arange(MAXB, dtype=jnp.int32)[None, None, :] < block_counts[:, :, None]).astype(jnp.float32)
    panels = features.reshape(N_COL, CB, BLK, F)

    def forward_group(row_group):

        def tile(col_group):
            tile_vals = adj_values[row_group, col_group].astype(jnp.float32) * is_live[row_group, col_group][:, None, None]
            picked = panels[col_group][block_cols[row_group, col_group]].astype(jnp.float32)
            product = jnp.einsum('bij,bjf->bif', tile_vals, picked, precision=lax.Precision.HIGHEST)
            return jnp.zeros((RB, BLK, F), jnp.float32).at[block_rows[row_group, col_group]].add(product)
        return lax.optimization_barrier(jnp.sum(lax.map(tile, jnp.arange(N_COL, dtype=jnp.int32)), axis=0))
    aggregated = lax.map(forward_group, jnp.arange(N_ROW, dtype=jnp.int32)).reshape(NODES, F).astype(jnp.bfloat16)
    preact = jnp.dot(aggregated, weight, preferred_element_type=jnp.float32)
    output = jax.nn.silu(preact).astype(jnp.bfloat16)
    sigmoid_pre = jax.nn.sigmoid(preact)
    slopes = sigmoid_pre * (1.0 + preact * (1.0 - sigmoid_pre))
    deltas = (cotangent.astype(jnp.float32) * slopes).astype(jnp.bfloat16)
    grad_weight = jnp.dot(aggregated.T, deltas, preferred_element_type=jnp.float32) * (1.0 / math.sqrt(NODES))
    backward = jnp.dot(deltas, weight.T, preferred_element_type=jnp.float32).astype(jnp.bfloat16)
    back_slabs = backward.reshape(N_ROW, RB, BLK, F)

    def backward_group(col_group):

        def tile(row_group):
            tile_vals = adj_values[row_group, col_group].astype(jnp.float32) * is_live[row_group, col_group][:, None, None]
            picked = back_slabs[row_group][block_rows[row_group, col_group]].astype(jnp.float32)
            product = jnp.einsum('bij,bif->bjf', tile_vals, picked, precision=lax.Precision.HIGHEST)
            summed = jnp.zeros((CB, BLK, F), jnp.float32).at[block_cols[row_group, col_group]].add(product)
            rounded = lax.optimization_barrier(summed.astype(jnp.bfloat16))
            return rounded.astype(jnp.float32)
        return lax.optimization_barrier(jnp.sum(lax.map(tile, jnp.arange(N_ROW, dtype=jnp.int32)), axis=0))
    grad_features = lax.map(backward_group, jnp.arange(N_COL, dtype=jnp.int32)).reshape(NODES, F).astype(jnp.bfloat16)
    return (output, grad_weight, grad_features)
```

```python
import functools
import math

import jax
import jax.numpy as jnp
from jax import lax
from jax.experimental import pallas as pl
from jax.experimental.pallas import tpu as pltpu
from jax.sharding import PartitionSpec as P

VMEM = pl.BlockSpec(memory_space=pltpu.VMEM)
SMEM = pl.BlockSpec(memory_space=pltpu.SMEM)
LIMIT = 40 * 1024 * 1024
NT = (((1,), (1,)), ((), ()))
NN = (((1,), (0,)), ((), ()))


def params():
    return pltpu.CompilerParams(vmem_limit_bytes=LIMIT)


def product_loop(count, source_ids, target_ids, adj, source, total, dims):
    slots = adj.shape[0]
    turn = math.gcd(slots, 8)
    total[...] = jnp.zeros_like(total)

    def step(index, carry):
        first = index * turn
        products = []
        for k in range(turn):
            operand = source[source_ids[first + k]]
            products.append(
                lax.dot_general(operand, adj[first + k], dims, preferred_element_type=jnp.float32)
            )
        for k in range(turn):
            target = target_ids[first + k]
            live = first + k < count
            total[target] += jnp.where(live, products[k], 0.0)
        return carry

    lax.fori_loop(0, (count + turn - 1) // turn, step, 0)


def forward_kernel(n_parts, place, count, rows, cols, adj, *refs):
    parts = refs[:n_parts]
    source, total = refs[-2:]
    outs = refs[n_parts:-2]
    size = adj.shape[1]
    row = 0
    for part in parts:
        depth = part.shape[0]
        for c in range(source.shape[0]):
            source[c, row : row + depth, :] = part[:, c * size : (c + 1) * size]
        row += depth
    product_loop(count[0], cols, rows, adj, source, total, NT)
    blocks = total.shape[0] // len(outs)
    for k, out in enumerate(outs):
        first = (place[0] ^ k) * blocks
        for i in range(blocks):
            out[:, i * size : (i + 1) * size] = total[first + i].astype(out.dtype)


def forward(place, count, rows, cols, adj, parts, row_blocks, n_out):
    size = adj.shape[1]
    depth = sum(part.shape[0] for part in parts)
    col_blocks = parts[0].shape[1] // size
    wide = row_blocks * size // n_out
    return pl.pallas_call(
        functools.partial(forward_kernel, len(parts)),
        out_shape=[jax.ShapeDtypeStruct((depth, wide), jnp.bfloat16)] * n_out,
        in_specs=[SMEM] * 4 + [VMEM] * (1 + len(parts)),
        out_specs=[VMEM] * n_out,
        scratch_shapes=[
            pltpu.VMEM((col_blocks, depth, size), jnp.bfloat16),
            pltpu.VMEM((row_blocks, depth, size), jnp.float32),
        ],
        compiler_params=params(),
        name="forward_products",
    )(place, count, rows, cols, adj, *parts)


def backward_kernel(n_parts, place, count, rows, cols, adj, *refs):
    parts = refs[:n_parts]
    source, total = refs[-2:]
    outs = refs[n_parts:-2]
    size = adj.shape[1]
    blocks = source.shape[0] // n_parts
    for k, part in enumerate(parts):
        first = (place[0] ^ k) * blocks
        for i in range(blocks):
            source[first + i] = part[:, i * size : (i + 1) * size]
    product_loop(count[0], rows, cols, adj, source, total, NN)
    row = 0
    for out in outs:
        depth = out.shape[0]
        for c in range(total.shape[0]):
            out[:, c * size : (c + 1) * size] = total[c, row : row + depth, :].astype(out.dtype)
        row += depth


def backward(place, count, rows, cols, adj, parts, col_blocks, n_out):
    size = adj.shape[1]
    depth = parts[0].shape[0]
    row_blocks = sum(part.shape[1] for part in parts) // size
    return pl.pallas_call(
        functools.partial(backward_kernel, len(parts)),
        out_shape=[jax.ShapeDtypeStruct((depth // n_out, col_blocks * size), jnp.bfloat16)] * n_out,
        in_specs=[SMEM] * 4 + [VMEM] * (1 + len(parts)),
        out_specs=[VMEM] * n_out,
        scratch_shapes=[
            pltpu.VMEM((row_blocks, depth, size), jnp.bfloat16),
            pltpu.VMEM((col_blocks, depth, size), jnp.float32),
        ],
        compiler_params=params(),
        name="backward_products",
    )(place, count, rows, cols, adj, *parts)


def middle_kernel(sizes, n_sum, n_row, row, weight, cotangent, *refs):
    terms = refs[: n_sum * len(sizes)]
    outs = refs[n_sum * len(sizes) : -1]
    output, deltas, aggregated = outs[:3]
    backs = outs[3:]
    ordered = refs[-1]
    depth = weight.shape[0] // n_row
    for j in range(n_row):
        first = pl.multiple_of((row[0] ^ j) * depth, depth)
        ordered[j * depth : (j + 1) * depth, :] = weight[pl.ds(first, depth), :]
    first = 0
    for p, size in enumerate(sizes):
        summed = terms[p * n_sum][...].astype(jnp.float32)
        for k in range(1, n_sum):
            summed += terms[p * n_sum + k][...].astype(jnp.float32)
        aggregated[first : first + size, :] = summed.astype(jnp.bfloat16)
        first += size
    nodes_first = aggregated[...].T
    preact = jnp.dot(nodes_first, ordered[...], preferred_element_type=jnp.float32)
    gate = jax.nn.sigmoid(preact)
    output[...] = (preact * gate).astype(jnp.bfloat16)
    slopes = gate * (1.0 + preact * (1.0 - gate))
    delta = (cotangent[...].astype(jnp.float32) * slopes).astype(jnp.bfloat16)
    deltas[...] = delta
    first = 0
    for back, size in zip(backs, sizes):
        back[...] = lax.dot_general(
            ordered[first : first + size, :], delta, NT, preferred_element_type=jnp.float32
        ).astype(jnp.bfloat16)
        first += size


def middle(n_row, row, weight, cotangent, pieces):
    sizes = [piece[0].shape[0] for piece in pieces]
    nodes = cotangent.shape[0]
    features = weight.shape[0]
    shape = jax.ShapeDtypeStruct
    outs = [
        shape((nodes, features), jnp.bfloat16),
        shape((nodes, features), jnp.bfloat16),
        shape((features, nodes), jnp.bfloat16),
    ] + [shape((size, nodes), jnp.bfloat16) for size in sizes]
    flat = [term for piece in pieces for term in piece]
    results = pl.pallas_call(
        functools.partial(middle_kernel, sizes, len(pieces[0]), n_row),
        out_shape=outs,
        in_specs=[SMEM] + [VMEM] * (2 + len(flat)),
        out_specs=[VMEM] * len(outs),
        scratch_shapes=[pltpu.VMEM(weight.shape, jnp.bfloat16)],
        compiler_params=params(),
        name="layer",
    )(row, weight, cotangent, *flat)
    return results[0], results[1], results[2], results[3:]


def gradient_kernel(scale, aggregated, deltas, even, odd):
    product = jnp.dot(aggregated[...], deltas[...], preferred_element_type=jnp.float32) * scale
    depth = even.shape[1]
    for j in range(even.shape[0]):
        even[j] = product[2 * j * depth : (2 * j + 1) * depth, :]
        odd[j] = product[(2 * j + 1) * depth : (2 * j + 2) * depth, :]


def gradient(n_row, scale, aggregated, deltas):
    features = aggregated.shape[0]
    half = jax.ShapeDtypeStruct((n_row // 2, features // n_row, deltas.shape[1]), jnp.float32)
    return pl.pallas_call(
        functools.partial(gradient_kernel, scale),
        out_shape=[half, half],
        in_specs=[VMEM] * 2,
        out_specs=[VMEM] * 2,
        compiler_params=params(),
        name="weight_gradient",
    )(aggregated, deltas)


def place_kernel(row, even, odd, out):
    depth = even.shape[1]
    for j in range(even.shape[0]):
        for side, ref in enumerate((even, odd)):
            first = pl.multiple_of((row[0] ^ (2 * j + side)) * depth, depth)
            out[pl.ds(first, depth), :] = ref[j]


def place_rows(row, even, odd):
    pairs, depth, wide = even.shape
    return pl.pallas_call(
        place_kernel,
        out_shape=jax.ShapeDtypeStruct((2 * pairs * depth, wide), jnp.float32),
        in_specs=[SMEM, VMEM, VMEM],
        out_specs=VMEM,
        compiler_params=params(),
        name="place_rows",
    )(row, even, odd)


def swap(value, axis, k):
    size = lax.axis_size(axis)
    return lax.ppermute(value, axis, [(i, i ^ k) for i in range(size)])


def wide_sum(values):
    total = values[0].astype(jnp.float32)
    for value in values[1:]:
        total = total + value.astype(jnp.float32)
    return total


def partners(n_row):
    near = [k for k in range(2, n_row, 2) if k & (k - 1) == 0]
    far = [k for k in range(2, n_row, 2) if k & (k - 1) != 0]
    groups = [[0], near, far]
    return [group for group in groups if group]


def whole_reduce(n_row, n_col, even, odd):
    even = even + swap(odd, "row", 1)
    mine = even[0]
    for j in range(1, n_row // 2):
        mine = mine + swap(even[j], "row", 2 * j)
    total = mine
    for k in range(1, n_col):
        total = total + swap(mine, "col", k)
    gathered = [total] + [swap(total, "row", 2 * j) for j in range(1, n_row // 2)]
    even = jnp.stack(gathered)
    return even, swap(even, "row", 1)


def shards_exchanged(features, weight, adj_values, block_rows, block_cols, block_counts, cotangent):
    n_row = lax.axis_size("row")
    n_col = lax.axis_size("col")
    adj = adj_values[0, 0]
    rows = block_rows[0, 0]
    cols = block_cols[0, 0]
    count = block_counts.reshape(1)
    size = adj.shape[1]
    nodes = cotangent.shape[0] * n_row * n_col
    row_blocks = cotangent.shape[0] * n_col // size
    col_blocks = features.shape[0] // size
    row = lax.axis_index("row").reshape(1)
    col = lax.axis_index("col").reshape(1)
    groups = partners(n_row)
    own = features.T

    arrived = {0: own}
    for k in range(2, n_row, 2):
        arrived[k] = swap(own, "row", k)
    sums = []
    for group in groups:
        parts = []
        for k in group:
            parts += [arrived[k], swap(arrived[k], "row", 1)]
        terms = forward(col, count, rows, cols, adj, parts, row_blocks, n_col)
        sums.append([terms[0]] + [swap(terms[k], "col", k) for k in range(1, n_col)])

    output, deltas, aggregated, backs = middle(n_row, row, weight, cotangent, sums)

    collected = []
    for group, back in reversed(list(zip(groups, backs))):
        parts = [back] + [swap(back, "col", k) for k in range(1, n_col)]
        terms = backward(col, count, rows, cols, adj, parts, col_blocks, 2 * len(group))
        for j, k in enumerate(group):
            other = swap(terms[2 * j + 1], "row", 1)
            if k == 0:
                collected += [terms[2 * j], other]
            else:
                pair = wide_sum([terms[2 * j], other]).astype(jnp.bfloat16)
                collected.append(swap(pair, "row", k))
    grad_features = wide_sum(collected).astype(jnp.bfloat16).T

    even, odd = gradient(n_row, 1.0 / math.sqrt(nodes), aggregated, deltas)
    even, odd = whole_reduce(n_row, n_col, even, odd)
    grad_weight = place_rows(row, even, odd)
    return output, grad_weight, grad_features


def shards_gathered(features, weight, adj_values, block_rows, block_cols, block_counts, cotangent):
    n_row = lax.axis_size("row")
    n_col = lax.axis_size("col")
    adj = adj_values[0, 0]
    rows = block_rows[0, 0]
    cols = block_cols[0, 0]
    count = block_counts.reshape(1)
    size = adj.shape[1]
    nodes = cotangent.shape[0] * n_row * n_col
    row_blocks = cotangent.shape[0] * n_col // size
    col_blocks = features.shape[0] // size
    zero = jnp.zeros((1,), jnp.int32)
    panels = lax.all_gather(features.T, "row", axis=0, tiled=True)
    (terms,) = forward(zero, count, rows, cols, adj, [panels], row_blocks, 1)
    part = lax.psum_scatter(terms, "col", scatter_dimension=1, tiled=True)
    output, deltas, aggregated, (back,) = middle(1, zero, weight, cotangent, [[part]])
    slab = lax.all_gather(back, "col", axis=1, tiled=True)
    (column_terms,) = backward(zero, count, rows, cols, adj, [slab], col_blocks, 1)
    grad_features = lax.psum_scatter(column_terms, "row", scatter_dimension=0, tiled=True).T
    even, odd = gradient(2, 1.0 / math.sqrt(nodes), aggregated, deltas)
    grad_weight = lax.psum(jnp.concatenate([even[0], odd[0]]), ("row", "col"))
    return output, grad_weight, grad_features


def solution(mesh):
    n_row = mesh.shape["row"]
    n_col = mesh.shape["col"]
    exchanged = n_row == 8 and n_col == 4
    return jax.shard_map(
        shards_exchanged if exchanged else shards_gathered,
        mesh=mesh,
        in_specs=(
            P("col", "row"),
            P(),
            P("row", "col", None, None, None),
            P("row", "col", None),
            P("row", "col", None),
            P("row", "col"),
            P(("row", "col"), None),
        ),
        out_specs=(P(("row", "col"), None), P(), P("col", "row")),
        check_vma=False,
    )
```

```python
import functools
import math

import jax
import jax.numpy as jnp
from jax import lax
from jax.experimental import pallas as pl
from jax.experimental.pallas import tpu as pltpu
from jax.sharding import PartitionSpec as P

VMEM = pl.BlockSpec(memory_space=pltpu.VMEM)
SMEM = pl.BlockSpec(memory_space=pltpu.SMEM)
LIMIT = 16 * 1024 * 1024
NT = (((1,), (1,)), ((), ()))
NN = (((1,), (0,)), ((), ()))


def params():
    return pltpu.CompilerParams(vmem_limit_bytes=LIMIT)


def product_loop(count, source_ids, target_ids, adj, source, total, dims):
    slots = adj.shape[0]
    turn = math.gcd(slots, 8)
    total[...] = jnp.zeros_like(total)

    def step(index, carry):
        first = index * turn
        products = []
        for k in range(turn):
            operand = source[source_ids[first + k]]
            products.append(
                lax.dot_general(operand, adj[first + k], dims, preferred_element_type=jnp.float32)
            )
        for k in range(turn):
            target = target_ids[first + k]
            live = first + k < count
            total[target] += jnp.where(live, products[k], 0.0)
        return carry

    lax.fori_loop(0, (count + turn - 1) // turn, step, 0)


def forward_kernel(n_parts, layout, place, count, rows, cols, adj, *refs):
    parts = refs[:n_parts]
    source, total = refs[-2:]
    outs = refs[n_parts:-2]
    size = adj.shape[1]
    row = 0
    for part in parts:
        depth = part.shape[0]
        for c in range(source.shape[0]):
            source[c, row : row + depth, :] = part[:, c * size : (c + 1) * size]
        row += depth
    product_loop(count[0], cols, rows, adj, source, total, NT)
    depth = total.shape[1]
    blocks = total.shape[0] * size // outs[0].shape[1]
    for out, chunks in zip(outs, layout):
        for n, k in enumerate(chunks):
            first = (place[0] ^ k) * blocks
            for i in range(blocks):
                out[n * depth : (n + 1) * depth, i * size : (i + 1) * size] = total[first + i].astype(
                    out.dtype
                )


def forward(place, count, rows, cols, adj, parts, row_blocks, layout):
    size = adj.shape[1]
    depth = sum(part.shape[0] for part in parts)
    col_blocks = parts[0].shape[1] // size
    wide = row_blocks * size // sum(len(chunks) for chunks in layout)
    return pl.pallas_call(
        functools.partial(forward_kernel, len(parts), layout),
        out_shape=[
            jax.ShapeDtypeStruct((len(chunks) * depth, wide), jnp.bfloat16) for chunks in layout
        ],
        in_specs=[SMEM] * 4 + [VMEM] * (1 + len(parts)),
        out_specs=[VMEM] * len(layout),
        scratch_shapes=[
            pltpu.VMEM((col_blocks, depth, size), jnp.bfloat16),
            pltpu.VMEM((row_blocks, depth, size), jnp.float32),
        ],
        compiler_params=params(),
        name="forward_products",
    )(place, count, rows, cols, adj, *parts)


def backward_kernel(n_parts, layout, place, count, rows, cols, adj, *refs):
    parts = refs[:n_parts]
    source, total = refs[-2:]
    outs = refs[n_parts:-2]
    size = adj.shape[1]
    depth = source.shape[1]
    blocks = parts[0].shape[1] // size
    for part, chunks in zip(parts, layout):
        for n, k in enumerate(chunks):
            first = (place[0] ^ k) * blocks
            for i in range(blocks):
                source[first + i] = part[n * depth : (n + 1) * depth, i * size : (i + 1) * size]
    product_loop(count[0], rows, cols, adj, source, total, NN)
    row = 0
    for out in outs:
        depth = out.shape[0]
        for c in range(total.shape[0]):
            out[:, c * size : (c + 1) * size] = total[c, row : row + depth, :].astype(out.dtype)
        row += depth


def backward(place, count, rows, cols, adj, parts, layout, col_blocks, n_out):
    size = adj.shape[1]
    depth = parts[0].shape[0] // len(layout[0])
    row_blocks = sum(len(chunks) for chunks in layout) * parts[0].shape[1] // size
    return pl.pallas_call(
        functools.partial(backward_kernel, len(parts), layout),
        out_shape=[jax.ShapeDtypeStruct((depth // n_out, col_blocks * size), jnp.bfloat16)] * n_out,
        in_specs=[SMEM] * 4 + [VMEM] * (1 + len(parts)),
        out_specs=[VMEM] * n_out,
        scratch_shapes=[
            pltpu.VMEM((row_blocks, depth, size), jnp.bfloat16),
            pltpu.VMEM((col_blocks, depth, size), jnp.float32),
        ],
        compiler_params=params(),
        name="backward_products",
    )(place, count, rows, cols, adj, *parts)


def middle_kernel(sizes, n_sum, n_row, row, weight, cotangent, *refs):
    terms = refs[: n_sum * len(sizes)]
    outs = refs[n_sum * len(sizes) : -1]
    output, deltas, aggregated = outs[:3]
    backs = outs[3:]
    ordered = refs[-1]
    depth = weight.shape[0] // n_row
    for j in range(n_row):
        first = pl.multiple_of((row[0] ^ j) * depth, depth)
        ordered[j * depth : (j + 1) * depth, :] = weight[pl.ds(first, depth), :]
    first = 0
    for p, size in enumerate(sizes):
        summed = terms[p * n_sum][:size, :].astype(jnp.float32)
        for k in range(1, n_sum):
            summed += terms[p * n_sum + k][:size, :].astype(jnp.float32)
        aggregated[first : first + size, :] = summed.astype(jnp.bfloat16)
        first += size
    nodes_first = aggregated[...].T
    preact = jnp.dot(nodes_first, ordered[...], preferred_element_type=jnp.float32)
    gate = jax.nn.sigmoid(preact)
    output[...] = (preact * gate).astype(jnp.bfloat16)
    slopes = gate * (1.0 + preact * (1.0 - gate))
    delta = (cotangent[...].astype(jnp.float32) * slopes).astype(jnp.bfloat16)
    deltas[...] = delta
    first = 0
    for back, size in zip(backs, sizes):
        back[...] = lax.dot_general(
            ordered[first : first + size, :], delta, NT, preferred_element_type=jnp.float32
        ).astype(jnp.bfloat16)
        first += size


def middle(n_row, row, weight, cotangent, pieces):
    sizes = [piece[0].shape[0] for piece in pieces]
    nodes = cotangent.shape[0]
    features = weight.shape[0]
    shape = jax.ShapeDtypeStruct
    outs = [
        shape((nodes, features), jnp.bfloat16),
        shape((nodes, features), jnp.bfloat16),
        shape((features, nodes), jnp.bfloat16),
    ] + [shape((size, nodes), jnp.bfloat16) for size in sizes]
    flat = [term for piece in pieces for term in piece]
    results = pl.pallas_call(
        functools.partial(middle_kernel, sizes, len(pieces[0]), n_row),
        out_shape=outs,
        in_specs=[SMEM] + [VMEM] * (2 + len(flat)),
        out_specs=[VMEM] * len(outs),
        scratch_shapes=[pltpu.VMEM(weight.shape, jnp.bfloat16)],
        compiler_params=params(),
        name="layer",
    )(row, weight, cotangent, *flat)
    return results[0], results[1], results[2], results[3:]


def gradient_kernel(scale, aggregated, deltas, even, odd):
    product = jnp.dot(aggregated[...], deltas[...], preferred_element_type=jnp.float32) * scale
    depth = even.shape[1]
    for j in range(even.shape[0]):
        even[j] = product[2 * j * depth : (2 * j + 1) * depth, :]
        odd[j] = product[(2 * j + 1) * depth : (2 * j + 2) * depth, :]


def gradient(n_row, scale, aggregated, deltas):
    features = aggregated.shape[0]
    half = jax.ShapeDtypeStruct((n_row // 2, features // n_row, deltas.shape[1]), jnp.float32)
    return pl.pallas_call(
        functools.partial(gradient_kernel, scale),
        out_shape=[half, half],
        in_specs=[VMEM] * 2,
        out_specs=[VMEM] * 2,
        compiler_params=params(),
        name="weight_gradient",
    )(aggregated, deltas)


def place_kernel(order, row, *refs):
    out = refs[-1]
    for ref, chunks in zip(refs[:-1], order):
        depth = ref.shape[1]
        for n, k in enumerate(chunks):
            first = pl.multiple_of((row[0] ^ k) * depth, depth)
            out[pl.ds(first, depth), :] = ref[n]


def place_rows(row, order, parts):
    _, depth, wide = parts[0].shape
    chunks = sum(part.shape[0] for part in parts)
    return pl.pallas_call(
        functools.partial(place_kernel, order),
        out_shape=jax.ShapeDtypeStruct((chunks * depth, wide), jnp.float32),
        in_specs=[SMEM] + [VMEM] * len(parts),
        out_specs=VMEM,
        compiler_params=params(),
        name="place_rows",
    )(row, *parts)


def swap(value, axis, k):
    size = lax.axis_size(axis)
    return lax.ppermute(value, axis, [(i, i ^ k) for i in range(size)])


def wide_sum(values):
    total = values[0].astype(jnp.float32)
    for value in values[1:]:
        total = total + value.astype(jnp.float32)
    return total


def after(value, *earlier):
    return lax.optimization_barrier((value, *earlier))[0]


def whole_reduce(row, even, odd):
    even = even + swap(odd, "row", 1)
    pair = even[0::2] + swap(even[1::2], "row", 2)
    mine = pair[:1] + swap(pair[1:], "row", 4)
    mine = mine + swap(mine, "col", 1)
    mine = mine + swap(mine, "col", 2)
    pair = jnp.concatenate([mine, swap(mine, "row", 4)])
    other = swap(pair, "row", 2)
    even = jnp.concatenate([pair, other])
    return place_rows(row, [(0, 4, 2, 6), (1, 5, 3, 7)], [even, swap(even, "row", 1)])


def shards_exchanged(features, weight, adj_values, block_rows, block_cols, block_counts, cotangent):
    n_row = lax.axis_size("row")
    n_col = lax.axis_size("col")
    adj = adj_values[0, 0]
    rows = block_rows[0, 0]
    cols = block_cols[0, 0]
    count = block_counts.reshape(1)
    size = adj.shape[1]
    nodes = cotangent.shape[0] * n_row * n_col
    row_blocks = cotangent.shape[0] * n_col // size
    col_blocks = features.shape[0] // size
    row = lax.axis_index("row").reshape(1)
    col = lax.axis_index("col").reshape(1)
    own = features.T

    near = [swap(own, "row", 2), swap(own, "row", 4)]
    sibling = swap(own, "row", 1)
    layout = [(0,), (2,), (1, 3)]
    sums = []

    def product(parts):
        return forward(col, count, rows, cols, adj, parts, row_blocks, layout)

    def fold(kept, beyond, received):
        depth = beyond.shape[0]
        passed = wide_sum([beyond, received[depth:]]).astype(jnp.bfloat16)
        return [kept, received, swap(passed, "col", 2)]

    kept0, beyond0, send0 = product([own, sibling])
    received0 = swap(send0, "col", 1)
    far = swap(after(own, send0), "row", 6)
    near = [after(part, send0) for part in near]
    parts = []
    for part in near:
        parts += [part, swap(part, "row", 1)]
    sums.append(fold(kept0, beyond0, received0))
    kept1, beyond1, send1 = product(parts)
    received1 = swap(send1, "col", 1)
    far = after(far, send1)
    kept2, beyond2, send2 = product([far, swap(far, "row", 1)])
    received2 = swap(send2, "col", 1)
    sums.append(fold(kept1, beyond1, received1))
    sums.append(fold(kept2, beyond2, received2))

    output, deltas, aggregated, backs = middle(n_row, row, weight, cotangent, sums)

    firsts = [swap(back, "col", 2) for back in backs]
    layout = [(0,), (2,), (1, 3)]
    collected = []
    for p, keys in ((1, (2, 4)), (2, (6,)), (0, (0,))):
        pair = jnp.concatenate([backs[p], firsts[p]])
        parts = [backs[p], firsts[p], swap(pair, "col", 1)]
        terms = backward(col, count, rows, cols, adj, parts, layout, col_blocks, 2 * len(keys))
        for j, k in enumerate(keys):
            other = swap(terms[2 * j + 1], "row", 1)
            if k == 0:
                collected += [terms[2 * j], other]
            else:
                joined = wide_sum([terms[2 * j], other]).astype(jnp.bfloat16)
                collected.append(swap(joined, "row", k))
    grad_features = wide_sum(collected).astype(jnp.bfloat16).T

    even, odd = gradient(n_row, 1.0 / math.sqrt(nodes), aggregated, deltas)
    grad_weight = whole_reduce(row, even, odd)
    return output, grad_weight, grad_features


def shards_gathered(features, weight, adj_values, block_rows, block_cols, block_counts, cotangent):
    n_row = lax.axis_size("row")
    n_col = lax.axis_size("col")
    adj = adj_values[0, 0]
    rows = block_rows[0, 0]
    cols = block_cols[0, 0]
    count = block_counts.reshape(1)
    size = adj.shape[1]
    nodes = cotangent.shape[0] * n_row * n_col
    row_blocks = cotangent.shape[0] * n_col // size
    col_blocks = features.shape[0] // size
    zero = jnp.zeros((1,), jnp.int32)
    panels = lax.all_gather(features.T, "row", axis=0, tiled=True)
    (terms,) = forward(zero, count, rows, cols, adj, [panels], row_blocks, [(0,)])
    part = lax.psum_scatter(terms, "col", scatter_dimension=1, tiled=True)
    output, deltas, aggregated, (back,) = middle(1, zero, weight, cotangent, [[part]])
    slab = lax.all_gather(back, "col", axis=1, tiled=True)
    (column_terms,) = backward(zero, count, rows, cols, adj, [slab], [(0,)], col_blocks, 1)
    grad_features = lax.psum_scatter(column_terms, "row", scatter_dimension=0, tiled=True).T
    even, odd = gradient(2, 1.0 / math.sqrt(nodes), aggregated, deltas)
    grad_weight = lax.psum(jnp.concatenate([even[0], odd[0]]), ("row", "col"))
    return output, grad_weight, grad_features


def solution(mesh):
    n_row = mesh.shape["row"]
    n_col = mesh.shape["col"]
    exchanged = n_row == 8 and n_col == 4
    return jax.shard_map(
        shards_exchanged if exchanged else shards_gathered,
        mesh=mesh,
        in_specs=(
            P("col", "row"),
            P(),
            P("row", "col", None, None, None),
            P("row", "col", None),
            P("row", "col", None),
            P("row", "col"),
            P(("row", "col"), None),
        ),
        out_specs=(P(("row", "col"), None), P(), P("col", "row")),
        check_vma=False,
    )
```

```python
import functools
import math

import jax
import jax.numpy as jnp
from jax import lax
from jax.experimental import pallas as pl
from jax.experimental.pallas import tpu as pltpu
from jax.sharding import PartitionSpec as P

VMEM = pl.BlockSpec(memory_space=pltpu.VMEM)
SMEM = pl.BlockSpec(memory_space=pltpu.SMEM)
HBM = pl.BlockSpec(memory_space=pltpu.HBM)
MIB = 1024 * 1024
NT = (((1,), (1,)), ((), ()))
NN = (((1,), (0,)), ((), ()))


COST = pl.CostEstimate(flops=10**9, bytes_accessed=1, transcendentals=0)


def params(mib):
    return pltpu.CompilerParams(vmem_limit_bytes=mib * MIB)


def fuse(name, function, *values):
    shapes = jax.eval_shape(function, *values)

    def kernel(*refs):
        results = function(*[ref[...] for ref in refs[: len(values)]])
        for ref, result in zip(refs[len(values) :], results):
            ref[...] = result

    return pl.pallas_call(
        kernel,
        out_shape=shapes,
        in_specs=[VMEM] * len(values),
        out_specs=[VMEM] * len(shapes),
        compiler_params=params(4),
        cost_estimate=COST,
        name=name,
    )(*values)


def turn_of(slots):
    return math.gcd(slots, 8)


def product_loop(count, source_ids, target_ids, adj, source, total, dims, ready=None):
    turn = turn_of(adj.shape[0])
    total[...] = jnp.zeros_like(total)

    def step(index, carry):
        first = index * turn
        if ready is not None:
            ready(index)
        products = []
        for k in range(turn):
            operand = source[source_ids[first + k]]
            products.append(
                lax.dot_general(operand, adj[first + k], dims, preferred_element_type=jnp.float32)
            )
        for k in range(turn):
            target = target_ids[first + k]
            live = first + k < count
            total[target] += jnp.where(live, products[k], 0.0)
        return carry

    lax.fori_loop(0, (count + turn - 1) // turn, step, 0)


def forward_kernel(n_parts, layout, fetch, place, count, rows, cols, adj, *refs):
    parts = refs[:n_parts]
    source, total = refs[n_parts + len(layout) + fetch :][:2]
    outs = refs[n_parts : n_parts + len(layout)]
    size = adj.shape[1]
    ready = None
    if fetch:
        stored, adj, sem = adj, refs[n_parts + len(layout)], refs[-1]
        turn = turn_of(adj.shape[0])
        turns = (count[0] + turn - 1) // turn

        def copy(index):
            blocks = pl.ds(index * turn, turn)
            return pltpu.make_async_copy(stored.at[blocks], adj.at[blocks], sem.at[index])

        def begin(index, carry):
            copy(index).start()
            return carry

        lax.fori_loop(0, turns, begin, 0)

        def ready(index):
            copy(index).wait()

    row = 0
    for part in parts:
        depth = part.shape[0]
        for c in range(source.shape[0]):
            source[c, row : row + depth, :] = part[:, c * size : (c + 1) * size]
        row += depth
    product_loop(count[0], cols, rows, adj, source, total, NT, ready)
    depth = total.shape[1]
    blocks = outs[0].shape[1] // size
    for out, chunks in zip(outs, layout):
        for n, k in enumerate(chunks):
            first = (place[0] ^ k) * blocks
            for i in range(blocks):
                out[n * depth : (n + 1) * depth, i * size : (i + 1) * size] = total[first + i].astype(
                    out.dtype
                )


def forward(place, count, rows, cols, adj, parts, row_blocks, layout, fetch=False):
    size = adj.shape[1]
    depth = sum(part.shape[0] for part in parts)
    col_blocks = parts[0].shape[1] // size
    wide = row_blocks * size // sum(len(chunks) for chunks in layout)
    outs = [jax.ShapeDtypeStruct((len(chunks) * depth, wide), jnp.bfloat16) for chunks in layout]
    scratch = [
        pltpu.VMEM((col_blocks, depth, size), jnp.bfloat16),
        pltpu.VMEM((row_blocks, depth, size), jnp.float32),
    ]
    if fetch:
        outs.append(jax.ShapeDtypeStruct(adj.shape, adj.dtype))
        scratch.append(pltpu.SemaphoreType.DMA((adj.shape[0] // turn_of(adj.shape[0]),)))
    return pl.pallas_call(
        functools.partial(forward_kernel, len(parts), layout, fetch),
        out_shape=outs,
        in_specs=[SMEM] * 4 + [HBM if fetch else VMEM] + [VMEM] * len(parts),
        out_specs=[VMEM] * len(outs),
        scratch_shapes=scratch,
        compiler_params=params(14),
        cost_estimate=COST,
        name="forward_products",
    )(place, count, rows, cols, adj, *parts)


def backward_kernel(n_parts, layout, place, count, rows, cols, adj, *refs):
    parts = refs[:n_parts]
    source, total = refs[-2:]
    outs = refs[n_parts:-2]
    size = adj.shape[1]
    depth = source.shape[1]
    blocks = parts[0].shape[1] // size
    for part, chunks in zip(parts, layout):
        for n, k in enumerate(chunks):
            first = (place[0] ^ k) * blocks
            for i in range(blocks):
                source[first + i] = part[n * depth : (n + 1) * depth, i * size : (i + 1) * size]
    product_loop(count[0], rows, cols, adj, source, total, NN)
    row = 0
    for out in outs:
        depth = out.shape[0]
        for c in range(total.shape[0]):
            out[:, c * size : (c + 1) * size] = total[c, row : row + depth, :].astype(out.dtype)
        row += depth


def backward(place, count, rows, cols, adj, parts, layout, col_blocks, n_out):
    size = adj.shape[1]
    depth = parts[0].shape[0] // len(layout[0])
    row_blocks = sum(len(chunks) for chunks in layout) * parts[0].shape[1] // size
    return pl.pallas_call(
        functools.partial(backward_kernel, len(parts), layout),
        out_shape=[jax.ShapeDtypeStruct((depth // n_out, col_blocks * size), jnp.bfloat16)] * n_out,
        in_specs=[SMEM] * 4 + [VMEM] * (1 + len(parts)),
        out_specs=[VMEM] * n_out,
        scratch_shapes=[
            pltpu.VMEM((row_blocks, depth, size), jnp.bfloat16),
            pltpu.VMEM((col_blocks, depth, size), jnp.float32),
        ],
        compiler_params=params(14),
        cost_estimate=COST,
        name="backward_products",
    )(place, count, rows, cols, adj, *parts)


def middle_kernel(sizes, n_sum, n_row, row, weight, cotangent, *refs):
    terms = refs[: n_sum * len(sizes)]
    outs = refs[n_sum * len(sizes) : -1]
    output, deltas, aggregated = outs[:3]
    backs = outs[3:]
    ordered = refs[-1]
    depth = weight.shape[0] // n_row
    for j in range(n_row):
        first = pl.multiple_of((row[0] ^ j) * depth, depth)
        ordered[j * depth : (j + 1) * depth, :] = weight[pl.ds(first, depth), :]
    first = 0
    for p, size in enumerate(sizes):
        summed = terms[p * n_sum][:size, :].astype(jnp.float32)
        for k in range(1, n_sum):
            summed += terms[p * n_sum + k][:size, :].astype(jnp.float32)
        aggregated[first : first + size, :] = summed.astype(jnp.bfloat16)
        first += size
    nodes_first = aggregated[...].T
    preact = jnp.dot(nodes_first, ordered[...], preferred_element_type=jnp.float32)
    gate = jax.nn.sigmoid(preact)
    output[...] = (preact * gate).astype(jnp.bfloat16)
    slopes = gate * (1.0 + preact * (1.0 - gate))
    delta = (cotangent[...].astype(jnp.float32) * slopes).astype(jnp.bfloat16)
    deltas[...] = delta
    first = 0
    for back, size in zip(backs, sizes):
        back[...] = lax.dot_general(
            ordered[first : first + size, :], delta, NT, preferred_element_type=jnp.float32
        ).astype(jnp.bfloat16)
        first += size


def middle(n_row, row, weight, cotangent, pieces):
    sizes = [piece[0].shape[0] for piece in pieces]
    nodes = cotangent.shape[0]
    features = weight.shape[0]
    shape = jax.ShapeDtypeStruct
    outs = [
        shape((nodes, features), jnp.bfloat16),
        shape((nodes, features), jnp.bfloat16),
        shape((features, nodes), jnp.bfloat16),
    ] + [shape((size, nodes), jnp.bfloat16) for size in sizes]
    flat = [term for piece in pieces for term in piece]
    results = pl.pallas_call(
        functools.partial(middle_kernel, sizes, len(pieces[0]), n_row),
        out_shape=outs,
        in_specs=[SMEM] + [VMEM] * (2 + len(flat)),
        out_specs=[VMEM] * len(outs),
        scratch_shapes=[pltpu.VMEM(weight.shape, jnp.bfloat16)],
        compiler_params=params(10),
        cost_estimate=COST,
        name="layer",
    )(row, weight, cotangent, *flat)
    return results[0], results[1], results[2], results[3:]


def gradient_kernel(scale, order, aggregated, deltas, *outs):
    product = jnp.dot(aggregated[...], deltas[...], preferred_element_type=jnp.float32) * scale
    for out, chunks in zip(outs, order):
        depth = out.shape[1]
        for n, k in enumerate(chunks):
            out[n] = product[k * depth : (k + 1) * depth, :]


def gradient(scale, order, aggregated, deltas):
    depth = aggregated.shape[0] // sum(len(chunks) for chunks in order)
    outs = [jax.ShapeDtypeStruct((len(chunks), depth, deltas.shape[1]), jnp.float32) for chunks in order]
    return pl.pallas_call(
        functools.partial(gradient_kernel, scale, order),
        out_shape=outs,
        in_specs=[VMEM] * 2,
        out_specs=[VMEM] * len(outs),
        compiler_params=params(6),
        cost_estimate=COST,
        name="weight_gradient",
    )(aggregated, deltas)


def place_kernel(order, row, *refs):
    out = refs[-1]
    for ref, chunks in zip(refs[:-1], order):
        depth = ref.shape[1]
        for n, k in enumerate(chunks):
            first = pl.multiple_of((row[0] ^ k) * depth, depth)
            out[pl.ds(first, depth), :] = ref[n]


def place_rows(row, order, parts):
    _, depth, wide = parts[0].shape
    chunks = sum(part.shape[0] for part in parts)
    return pl.pallas_call(
        functools.partial(place_kernel, order),
        out_shape=jax.ShapeDtypeStruct((chunks * depth, wide), jnp.float32),
        in_specs=[SMEM] + [VMEM] * len(parts),
        out_specs=VMEM,
        compiler_params=params(4),
        cost_estimate=COST,
        name="place_rows",
    )(row, *parts)


def swap(value, axis, k):
    size = lax.axis_size(axis)
    return lax.ppermute(value, axis, [(i, i ^ k) for i in range(size)])


def wide_sum(*values):
    total = values[0].astype(jnp.float32)
    for value in values[1:]:
        total = total + value.astype(jnp.float32)
    return (total.astype(values[0].dtype),)


def after(value, *earlier):
    return lax.optimization_barrier((value, *earlier))[0]


def split_sum(kept, received):
    half = kept.shape[0] // 2
    total = kept + received
    return total[:half], total[half:]


def join(*values):
    return (jnp.concatenate(values),)


def whole_reduce(row, even, odd):
    pair, sent = fuse("gradient_sum", split_sum, even, swap(odd, "row", 1))
    mine, sent = fuse("gradient_sum", split_sum, pair, swap(sent, "row", 2))
    (mine,) = fuse("gradient_sum", wide_sum, mine, swap(sent, "row", 4))
    (mine,) = fuse("gradient_sum", wide_sum, mine, swap(mine, "col", 1))
    (mine,) = fuse("gradient_sum", wide_sum, mine, swap(mine, "col", 2))
    (pair,) = fuse("gradient_join", join, mine, swap(mine, "row", 4))
    (even,) = fuse("gradient_join", join, pair, swap(pair, "row", 2))
    return place_rows(row, [(0, 4, 2, 6), (1, 5, 3, 7)], [even, swap(even, "row", 1)])


def shards_exchanged(features, weight, adj_values, block_rows, block_cols, block_counts, cotangent):
    n_row = lax.axis_size("row")
    n_col = lax.axis_size("col")
    adj = adj_values[0, 0]
    rows = block_rows[0, 0]
    cols = block_cols[0, 0]
    count = block_counts.reshape(1)
    size = adj.shape[1]
    nodes = cotangent.shape[0] * n_row * n_col
    row_blocks = cotangent.shape[0] * n_col // size
    col_blocks = features.shape[0] // size
    row = lax.axis_index("row").reshape(1)
    col = lax.axis_index("col").reshape(1)
    own = features.T

    near = [swap(own, "row", 2), swap(own, "row", 4)]
    sibling = swap(own, "row", 1)
    far = swap(own, "row", 6)
    layout = [(0,), (2,), (1, 3)]

    def pass_on(beyond, received):
        return wide_sum(beyond, received[beyond.shape[0] :])

    def fold(kept, beyond, received):
        (passed,) = fuse("pass_on", pass_on, beyond, received)
        return [kept, received, swap(passed, "col", 2)]

    kept0, beyond0, send0, tile = forward(
        col, count, rows, cols, adj, [own, sibling], row_blocks, layout, True
    )

    def product(parts):
        return forward(col, count, rows, cols, tile, parts, row_blocks, layout)

    received0 = swap(send0, "col", 1)
    parts = []
    for part in near:
        part = after(part, send0)
        parts += [part, swap(part, "row", 1)]
    kept1, beyond1, send1 = product(parts)
    received1 = swap(send1, "col", 1)
    sum0 = fold(kept0, beyond0, after(received0, send1))
    far = after(far, send1)
    kept2, beyond2, send2 = product([after(far, sum0[2]), swap(far, "row", 1)])
    received2 = swap(send2, "col", 1)
    sum1 = fold(kept1, beyond1, after(received1, send2))
    sum2 = fold(kept2, beyond2, after(received2, sum1[1]))

    output, deltas, aggregated, backs = middle(n_row, row, weight, cotangent, [sum0, sum1, sum2])

    firsts = [swap(back, "col", 2) for back in backs]
    pairs = []
    for p in (2, 1, 0):
        first = after(firsts[p], *pairs)
        pairs += fuse("join", join, backs[p], first)
    others = [swap(pair, "col", 1) for pair in pairs]

    def columns(p, other, n_out):
        parts = [backs[p], firsts[p], other]
        return backward(col, count, rows, cols, tile, parts, layout, col_blocks, n_out)

    mine, sent = columns(2, after(others[0], pairs[1]), 2)
    from_sibling = swap(sent, "row", 1)
    (joined,) = fuse("pair_sum", wide_sum, mine, after(from_sibling, pairs[2]))
    collected = [swap(joined, "row", 6)]
    terms = columns(1, after(others[1], joined), 4)
    from_sibling = [swap(terms[1], "row", 1), swap(terms[3], "row", 1)]
    joined = []
    for j, k in ((0, 2), (1, 4)):
        joined += fuse("pair_sum", wide_sum, terms[2 * j], from_sibling[j])
        collected.append(swap(joined[j], "row", k))
    mine, sent = columns(0, after(others[2], collected[0], *joined), 2)
    collected += [mine, swap(sent, "row", 1)]
    (grad_features,) = fuse("feature_sum", wide_sum, *collected)

    order = [(0, 4, 2, 6), (1, 5, 3, 7)]
    even, odd = gradient(1.0 / math.sqrt(nodes), order, aggregated, deltas)
    grad_weight = whole_reduce(row, even, odd)
    return output, grad_weight, grad_features.T


def shards_gathered(features, weight, adj_values, block_rows, block_cols, block_counts, cotangent):
    n_row = lax.axis_size("row")
    n_col = lax.axis_size("col")
    adj = adj_values[0, 0]
    rows = block_rows[0, 0]
    cols = block_cols[0, 0]
    count = block_counts.reshape(1)
    size = adj.shape[1]
    nodes = cotangent.shape[0] * n_row * n_col
    row_blocks = cotangent.shape[0] * n_col // size
    col_blocks = features.shape[0] // size
    zero = jnp.zeros((1,), jnp.int32)
    panels = lax.all_gather(features.T, "row", axis=0, tiled=True)
    (terms,) = forward(zero, count, rows, cols, adj, [panels], row_blocks, [(0,)])
    part = lax.psum_scatter(terms, "col", scatter_dimension=1, tiled=True)
    output, deltas, aggregated, (back,) = middle(1, zero, weight, cotangent, [[part]])
    slab = lax.all_gather(back, "col", axis=1, tiled=True)
    (column_terms,) = backward(zero, count, rows, cols, adj, [slab], [(0,)], col_blocks, 1)
    grad_features = lax.psum_scatter(column_terms, "row", scatter_dimension=0, tiled=True).T
    (part,) = gradient(1.0 / math.sqrt(nodes), [(0,)], aggregated, deltas)
    grad_weight = lax.psum(part[0], ("row", "col"))
    return output, grad_weight, grad_features


def solution(mesh):
    n_row = mesh.shape["row"]
    n_col = mesh.shape["col"]
    exchanged = n_row == 8 and n_col == 4
    return jax.shard_map(
        shards_exchanged if exchanged else shards_gathered,
        mesh=mesh,
        in_specs=(
            P("col", "row"),
            P(),
            P("row", "col", None, None, None),
            P("row", "col", None),
            P("row", "col", None),
            P("row", "col"),
            P(("row", "col"), None),
        ),
        out_specs=(P(("row", "col"), None), P(), P("col", "row")),
        check_vma=False,
    )
```

```python
import functools
import math

import jax
import jax.numpy as jnp
from jax import lax
from jax.experimental import pallas as pl
from jax.experimental.pallas import tpu as pltpu
from jax.sharding import PartitionSpec as P

VMEM = pl.BlockSpec(memory_space=pltpu.VMEM)
SMEM = pl.BlockSpec(memory_space=pltpu.SMEM)
HBM = pl.BlockSpec(memory_space=pltpu.HBM)
MIB = 1024 * 1024
NT = (((1,), (1,)), ((), ()))
NN = (((1,), (0,)), ((), ()))


COSTS = {"layer": 1, "feature_sum": 1}


def cost(name):
    return pl.CostEstimate(flops=int(COSTS.get(name, 1e9)), bytes_accessed=1, transcendentals=0)


def params(mib):
    return pltpu.CompilerParams(vmem_limit_bytes=mib * MIB)


def fuse(name, function, *values):
    shapes = jax.eval_shape(function, *values)

    def kernel(*refs):
        results = function(*[ref[...] for ref in refs[: len(values)]])
        for ref, result in zip(refs[len(values) :], results):
            ref[...] = result

    return pl.pallas_call(
        kernel,
        out_shape=shapes,
        in_specs=[VMEM] * len(values),
        out_specs=[VMEM] * len(shapes),
        compiler_params=params(4),
        cost_estimate=cost(name),
        name=name,
    )(*values)


def turn_of(slots):
    return math.gcd(slots, 8)


def product_loop(count, source_ids, target_ids, adj, source, total, dims, ready=None):
    turn = turn_of(adj.shape[0])
    total[...] = jnp.zeros_like(total)

    def step(index, carry):
        first = index * turn
        if ready is not None:
            ready(index)
        products = []
        for k in range(turn):
            operand = source[source_ids[first + k]]
            products.append(
                lax.dot_general(operand, adj[first + k], dims, preferred_element_type=jnp.float32)
            )
        for k in range(turn):
            target = target_ids[first + k]
            live = first + k < count
            total[target] += jnp.where(live, products[k], 0.0)
        return carry

    lax.fori_loop(0, (count + turn - 1) // turn, step, 0)


def forward_kernel(n_parts, layout, fetch, place, count, rows, cols, adj, *refs):
    parts = refs[:n_parts]
    source, total = refs[n_parts + len(layout) + 3 * fetch :][:2]
    outs = refs[n_parts : n_parts + len(layout)]
    size = adj.shape[1]
    ready = None
    if fetch:
        stored, stored_ids = adj, (rows, cols)
        adj, *kept_ids = refs[n_parts + len(layout) :][:3]
        rows, cols, sem, ids_sem = refs[-4:]
        ids = [
            pltpu.make_async_copy(source_ids, target_ids, ids_sem.at[n])
            for n, (source_ids, target_ids) in enumerate(zip(stored_ids * 2, (rows, cols, *kept_ids)))
        ]
        for copy_ids in ids:
            copy_ids.start()
        turn = turn_of(adj.shape[0])
        turns = (count[0, 0] + turn - 1) // turn

        def copy(index):
            blocks = pl.ds(index * turn, turn)
            return pltpu.make_async_copy(stored.at[blocks], adj.at[blocks], sem.at[index])

        def begin(index, carry):
            copy(index).start()
            return carry

        lax.fori_loop(0, turns, begin, 0)

        def ready(index):
            copy(index).wait()

    row = 0
    for part in parts:
        depth = part.shape[0]
        for c in range(source.shape[0]):
            source[c, row : row + depth, :] = part[:, c * size : (c + 1) * size]
        row += depth
    if fetch:
        for copy_ids in ids:
            copy_ids.wait()
    product_loop(count[0, 0], cols, rows, adj, source, total, NT, ready)
    depth = total.shape[1]
    blocks = outs[0].shape[1] // size
    for out, chunks in zip(outs, layout):
        for n, k in enumerate(chunks):
            first = (place[0] ^ k) * blocks
            for i in range(blocks):
                out[n * depth : (n + 1) * depth, i * size : (i + 1) * size] = total[first + i].astype(
                    out.dtype
                )


def forward(place, count, rows, cols, adj, parts, row_blocks, layout, fetch=False):
    size = adj.shape[1]
    depth = sum(part.shape[0] for part in parts)
    col_blocks = parts[0].shape[1] // size
    wide = row_blocks * size // sum(len(chunks) for chunks in layout)
    outs = [jax.ShapeDtypeStruct((len(chunks) * depth, wide), jnp.bfloat16) for chunks in layout]
    scratch = [
        pltpu.VMEM((col_blocks, depth, size), jnp.bfloat16),
        pltpu.VMEM((row_blocks, depth, size), jnp.float32),
    ]
    if fetch:
        outs += [jax.ShapeDtypeStruct(array.shape, array.dtype) for array in (adj, rows, cols)]
        scratch += [pltpu.SMEM(rows.shape, rows.dtype), pltpu.SMEM(cols.shape, cols.dtype)]
        scratch.append(pltpu.SemaphoreType.DMA((adj.shape[0] // turn_of(adj.shape[0]),)))
        scratch.append(pltpu.SemaphoreType.DMA((4,)))
    return pl.pallas_call(
        functools.partial(forward_kernel, len(parts), layout, fetch),
        out_shape=outs,
        in_specs=[SMEM] * 2 + ([HBM] * 3 if fetch else [SMEM, SMEM, VMEM]) + [VMEM] * len(parts),
        out_specs=[VMEM] * len(outs),
        scratch_shapes=scratch,
        compiler_params=params(14),
        cost_estimate=cost("forward_products"),
        name="forward_products",
    )(place, count, rows, cols, adj, *parts)


def backward_kernel(n_parts, layout, place, count, rows, cols, adj, *refs):
    parts = refs[:n_parts]
    source, total = refs[-2:]
    outs = refs[n_parts:-2]
    size = adj.shape[1]
    depth = source.shape[1]
    blocks = parts[0].shape[1] // size
    for part, chunks in zip(parts, layout):
        for n, k in enumerate(chunks):
            first = (place[0] ^ k) * blocks
            for i in range(blocks):
                source[first + i] = part[n * depth : (n + 1) * depth, i * size : (i + 1) * size]
    product_loop(count[0, 0], rows, cols, adj, source, total, NN)
    row = 0
    for out in outs:
        depth = out.shape[0]
        for c in range(total.shape[0]):
            out[:, c * size : (c + 1) * size] = total[c, row : row + depth, :].astype(out.dtype)
        row += depth


def backward(place, count, rows, cols, adj, parts, layout, col_blocks, n_out):
    size = adj.shape[1]
    depth = parts[0].shape[0] // len(layout[0])
    row_blocks = sum(len(chunks) for chunks in layout) * parts[0].shape[1] // size
    return pl.pallas_call(
        functools.partial(backward_kernel, len(parts), layout),
        out_shape=[jax.ShapeDtypeStruct((depth // n_out, col_blocks * size), jnp.bfloat16)] * n_out,
        in_specs=[SMEM] * 4 + [VMEM] * (1 + len(parts)),
        out_specs=[VMEM] * n_out,
        scratch_shapes=[
            pltpu.VMEM((row_blocks, depth, size), jnp.bfloat16),
            pltpu.VMEM((col_blocks, depth, size), jnp.float32),
        ],
        compiler_params=params(14),
        cost_estimate=cost("backward_products"),
        name="backward_products",
    )(place, count, rows, cols, adj, *parts)


def middle_kernel(sizes, out_sizes, n_sum, n_row, row, weight, cotangent, *refs):
    terms = refs[: n_sum * len(sizes)]
    outs = refs[n_sum * len(sizes) : -1]
    output, deltas, aggregated = outs[:3]
    backs = outs[3:]
    ordered = refs[-1]
    depth = weight.shape[0] // n_row
    for j in range(n_row):
        first = pl.multiple_of((row[0] ^ j) * depth, depth)
        ordered[j * depth : (j + 1) * depth, :] = weight[pl.ds(first, depth), :]
    first = 0
    for p, size in enumerate(sizes):
        summed = terms[p * n_sum][:size, :].astype(jnp.float32)
        for k in range(1, n_sum):
            summed += terms[p * n_sum + k][:size, :].astype(jnp.float32)
        aggregated[first : first + size, :] = summed.astype(jnp.bfloat16)
        first += size
    nodes_first = aggregated[...].T
    preact = jnp.dot(nodes_first, ordered[...], preferred_element_type=jnp.float32)
    gate = jax.nn.sigmoid(preact)
    output[...] = (preact * gate).astype(jnp.bfloat16)
    slopes = gate * (1.0 + preact * (1.0 - gate))
    delta = (cotangent[...].astype(jnp.float32) * slopes).astype(jnp.bfloat16)
    deltas[...] = delta
    first = 0
    for back, size in zip(backs, out_sizes):
        back[...] = lax.dot_general(
            ordered[first : first + size, :], delta, NT, preferred_element_type=jnp.float32
        ).astype(jnp.bfloat16)
        first += size


def middle(n_row, row, weight, cotangent, pieces, out_chunks):
    sizes = [piece[0].shape[0] for piece in pieces]
    out_sizes = [chunks * weight.shape[0] // n_row for chunks in out_chunks]
    nodes = cotangent.shape[0]
    features = weight.shape[0]
    shape = jax.ShapeDtypeStruct
    outs = [
        shape((nodes, features), jnp.bfloat16),
        shape((nodes, features), jnp.bfloat16),
        shape((features, nodes), jnp.bfloat16),
    ] + [shape((size, nodes), jnp.bfloat16) for size in out_sizes]
    flat = [term for piece in pieces for term in piece]
    results = pl.pallas_call(
        functools.partial(middle_kernel, sizes, out_sizes, len(pieces[0]), n_row),
        out_shape=outs,
        in_specs=[SMEM] + [VMEM] * (2 + len(flat)),
        out_specs=[VMEM] * len(outs),
        scratch_shapes=[pltpu.VMEM(weight.shape, jnp.bfloat16)],
        compiler_params=params(10),
        cost_estimate=cost("layer"),
        name="layer",
    )(row, weight, cotangent, *flat)
    return results[0], results[1], results[2], results[3:]


def gradient_kernel(scale, order, aggregated, deltas, *outs):
    product = jnp.dot(aggregated[...], deltas[...], preferred_element_type=jnp.float32) * scale
    for out, chunks in zip(outs, order):
        depth = out.shape[1]
        for n, k in enumerate(chunks):
            out[n] = product[k * depth : (k + 1) * depth, :]


def gradient(scale, order, aggregated, deltas):
    depth = aggregated.shape[0] // sum(len(chunks) for chunks in order)
    outs = [jax.ShapeDtypeStruct((len(chunks), depth, deltas.shape[1]), jnp.float32) for chunks in order]
    return pl.pallas_call(
        functools.partial(gradient_kernel, scale, order),
        out_shape=outs,
        in_specs=[VMEM] * 2,
        out_specs=[VMEM] * len(outs),
        compiler_params=params(6),
        cost_estimate=cost("weight_gradient"),
        name="weight_gradient",
    )(aggregated, deltas)


def place_kernel(order, row, *refs):
    out = refs[-1]
    for ref, chunks in zip(refs[:-1], order):
        depth = ref.shape[1]
        for n, k in enumerate(chunks):
            first = pl.multiple_of((row[0] ^ k) * depth, depth)
            out[pl.ds(first, depth), :] = ref[n]


def place_rows(row, order, parts):
    _, depth, wide = parts[0].shape
    chunks = sum(part.shape[0] for part in parts)
    return pl.pallas_call(
        functools.partial(place_kernel, order),
        out_shape=jax.ShapeDtypeStruct((chunks * depth, wide), jnp.float32),
        in_specs=[SMEM] + [VMEM] * len(parts),
        out_specs=VMEM,
        compiler_params=params(4),
        cost_estimate=cost("place_rows"),
        name="place_rows",
    )(row, *parts)


def swap(value, axis, k):
    size = lax.axis_size(axis)
    return lax.ppermute(value, axis, [(i, i ^ k) for i in range(size)])


def wide_sum(*values):
    total = values[0].astype(jnp.float32)
    for value in values[1:]:
        total = total + value.astype(jnp.float32)
    return (total.astype(values[0].dtype),)


def after(value, *earlier):
    return lax.optimization_barrier((value, *earlier))[0]


def join(*values):
    return (jnp.concatenate(values),)


def pair_sum(mine, received):
    total = mine + received
    return tuple(total[n : n + 1] for n in range(total.shape[0]))


def shards_exchanged(features, weight, adj_values, block_rows, block_cols, block_counts, cotangent):
    n_row = lax.axis_size("row")
    n_col = lax.axis_size("col")
    adj = adj_values[0, 0]
    rows = block_rows[0, 0]
    cols = block_cols[0, 0]
    count = block_counts
    size = adj.shape[1]
    nodes = cotangent.shape[0] * n_row * n_col
    row_blocks = cotangent.shape[0] * n_col // size
    col_blocks = features.shape[0] // size
    row = lax.axis_index("row").reshape(1)
    col = lax.axis_index("col").reshape(1)
    own = after(features.T, row, col)

    sibling = swap(own, "row", 1)
    others = [swap(own, "row", k) for k in range(2, n_row, 2)]
    layout = [(k,) for k in range(n_col)]

    def scatter(terms):
        return [terms[0]] + [swap(terms[k], "col", k) for k in range(1, n_col)]

    constrain = pltpu.with_memory_space_constraint
    tile, rows, cols = (constrain(array, pltpu.HBM) for array in (adj, rows, cols))
    *terms, tile, rows, cols = forward(
        col, count, rows, cols, tile, [own, sibling], row_blocks, layout, True
    )
    sums = [scatter(terms)]
    others = [after(part, *terms) for part in others]
    parts = []
    for part in others:
        parts += [part, swap(part, "row", 1)]
    parts[-1] = after(parts[-1], *sums[0])
    sums.append(scatter(forward(col, count, rows, cols, tile, parts, row_blocks, layout)))

    sizes = [2, 4, 2]
    output, deltas, aggregated, backs = middle(n_row, row, weight, cotangent, sums, sizes)
    gathered = [[back] + [swap(back, "col", k) for k in range(1, n_col)] for back in backs]

    def columns(piece, earlier):
        parts = list(gathered[piece])
        parts[-1] = after(parts[-1], *earlier)
        n_out = sizes[piece]
        return backward(col, count, rows, cols, tile, parts, layout, col_blocks, n_out)

    evens = tuple(range(0, n_row, 2))
    order = [evens, tuple(range(1, n_row, 2))]
    even, odd = gradient(1.0 / math.sqrt(nodes), order, aggregated, deltas)
    chunk, *sent = fuse("gradient_sum", pair_sum, even, swap(odd, "row", 1))
    from_rows = [swap(part, "row", k) for part, k in zip(sent, evens[1:])]

    terms = columns(2, sent)
    other = swap(terms[1], "row", 1)
    (joined,) = fuse("pair_sum", wide_sum, terms[0], other)
    collected = [swap(joined, "row", 6)]

    (chunk,) = fuse("gradient_sum", wide_sum, chunk, *from_rows)
    from_cols = [swap(chunk, "col", k) for k in range(1, n_col)]

    terms = columns(1, [joined, chunk])
    received = [swap(term, "row", 1) for term in terms[1::2]]
    joined = []
    for term, other, k in zip(terms[::2], received, (2, 4)):
        joined += fuse("pair_sum", wide_sum, term, other)
        collected.append(swap(joined[-1], "row", k))

    (chunk,) = fuse("gradient_sum", wide_sum, chunk, *from_cols)
    (even,) = fuse("gradient_join", join, chunk, *[swap(chunk, "row", k) for k in evens[1:]])

    mine, sent = columns(0, [collected[0], *joined, chunk])
    collected += [mine, swap(sent, "row", 1)]
    (grad_features,) = fuse("feature_sum", wide_sum, *collected)
    grad_weight = place_rows(row, order, [even, swap(even, "row", 1)])
    return output, grad_weight, grad_features.T


def shards_gathered(features, weight, adj_values, block_rows, block_cols, block_counts, cotangent):
    n_row = lax.axis_size("row")
    n_col = lax.axis_size("col")
    adj = adj_values[0, 0]
    rows = block_rows[0, 0]
    cols = block_cols[0, 0]
    count = block_counts
    size = adj.shape[1]
    nodes = cotangent.shape[0] * n_row * n_col
    row_blocks = cotangent.shape[0] * n_col // size
    col_blocks = features.shape[0] // size
    zero = jnp.zeros((1,), jnp.int32)
    panels = lax.all_gather(features.T, "row", axis=0, tiled=True)
    (terms,) = forward(zero, count, rows, cols, adj, [panels], row_blocks, [(0,)])
    part = lax.psum_scatter(terms, "col", scatter_dimension=1, tiled=True)
    output, deltas, aggregated, (back,) = middle(1, zero, weight, cotangent, [[part]], [1])
    slab = lax.all_gather(back, "col", axis=1, tiled=True)
    (column_terms,) = backward(zero, count, rows, cols, adj, [slab], [(0,)], col_blocks, 1)
    grad_features = lax.psum_scatter(column_terms, "row", scatter_dimension=0, tiled=True).T
    (part,) = gradient(1.0 / math.sqrt(nodes), [(0,)], aggregated, deltas)
    grad_weight = lax.psum(part[0], ("row", "col"))
    return output, grad_weight, grad_features


def solution(mesh):
    n_row = mesh.shape["row"]
    n_col = mesh.shape["col"]
    exchanged = n_row == 8 and n_col == 4
    return jax.shard_map(
        shards_exchanged if exchanged else shards_gathered,
        mesh=mesh,
        in_specs=(
            P("col", "row"),
            P(),
            P("row", "col", None, None, None),
            P("row", "col", None),
            P("row", "col", None),
            P("row", "col"),
            P(("row", "col"), None),
        ),
        out_specs=(P(("row", "col"), None), P(), P("col", "row")),
        check_vma=False,
    )
```

```python
import functools
import math

import jax
import jax.numpy as jnp
from jax import lax
from jax.experimental import pallas as pl
from jax.experimental.pallas import tpu as pltpu
from jax.sharding import PartitionSpec as P

VMEM = pl.BlockSpec(memory_space=pltpu.VMEM)
SMEM = pl.BlockSpec(memory_space=pltpu.SMEM)
HBM = pl.BlockSpec(memory_space=pltpu.HBM)
MIB = 1024 * 1024
NT = (((1,), (1,)), ((), ()))
NN = (((1,), (0,)), ((), ()))


COSTS = {"fetch": 1e9, "forward_products": 1e9, "backward_products": 1e9}


def cost(name):
    return pl.CostEstimate(flops=int(COSTS.get(name, 1)), bytes_accessed=1, transcendentals=0)


def params(mib):
    return pltpu.CompilerParams(vmem_limit_bytes=mib * MIB)


def fuse(name, function, *values):
    shapes = jax.eval_shape(function, *values)

    def kernel(*refs):
        results = function(*[ref[...] for ref in refs[: len(values)]])
        for ref, result in zip(refs[len(values) :], results):
            ref[...] = result

    return pl.pallas_call(
        kernel,
        out_shape=shapes,
        in_specs=[VMEM] * len(values),
        out_specs=[VMEM] * len(shapes),
        compiler_params=params(4),
        cost_estimate=cost(name),
        name=name,
    )(*values)


def turn_of(slots):
    return math.gcd(slots, 8)


def product_loop(count, source_ids, target_ids, adj, source, total, dims):
    turn = turn_of(adj.shape[0])
    total[...] = jnp.zeros_like(total)

    def step(index, carry):
        first = index * turn
        products = []
        for k in range(turn):
            operand = source[source_ids[first + k]]
            products.append(
                lax.dot_general(operand, adj[first + k], dims, preferred_element_type=jnp.float32)
            )
        for k in range(turn):
            target = target_ids[first + k]
            live = first + k < count
            total[target] += jnp.where(live, products[k], 0.0)
        return carry

    lax.fori_loop(0, (count + turn - 1) // turn, step, 0)


def fetch_kernel(count, rows, cols, tile, *refs):
    outs, (sem, ids_sem) = refs[:3], refs[3:]
    ids = [
        pltpu.make_async_copy(source, target, ids_sem.at[n])
        for n, (source, target) in enumerate(zip((rows, cols), outs))
    ]
    for copy in ids:
        copy.start()
    turn = turn_of(tile.shape[0])

    def copy_turn(index):
        blocks = pl.ds(index * turn, turn)
        return pltpu.make_async_copy(tile.at[blocks], outs[2].at[blocks], sem.at[index])

    def begin(index, carry):
        copy_turn(index).start()
        return carry

    def finish(index, carry):
        copy_turn(index).wait()
        return carry

    turns = (count[0, 0] + turn - 1) // turn
    lax.fori_loop(0, turns, begin, 0)
    lax.fori_loop(0, turns, finish, 0)
    for copy in ids:
        copy.wait()


def fetch(count, *arrays):
    blocks = arrays[2].shape[0]
    return pl.pallas_call(
        fetch_kernel,
        out_shape=[jax.ShapeDtypeStruct(array.shape, array.dtype) for array in arrays],
        in_specs=[SMEM] + [HBM] * len(arrays),
        out_specs=[VMEM] * len(arrays),
        scratch_shapes=[
            pltpu.SemaphoreType.DMA((blocks // turn_of(blocks),)),
            pltpu.SemaphoreType.DMA((2,)),
        ],
        compiler_params=params(4),
        cost_estimate=cost("fetch"),
        name="fetch",
    )(count, *[pltpu.with_memory_space_constraint(array, pltpu.HBM) for array in arrays])


def forward_kernel(n_parts, layout, place, count, rows, cols, adj, *refs):
    parts = refs[:n_parts]
    outs = refs[n_parts:-2]
    source, total = refs[-2:]
    size = adj.shape[1]
    row = 0
    for part in parts:
        depth = part.shape[0]
        for c in range(source.shape[0]):
            source[c, row : row + depth, :] = part[:, c * size : (c + 1) * size]
        row += depth
    product_loop(count[0, 0], cols, rows, adj, source, total, NT)
    depth = total.shape[1]
    blocks = outs[0].shape[1] // size
    for out, chunks in zip(outs, layout):
        for n, k in enumerate(chunks):
            first = (place[0] ^ k) * blocks
            for i in range(blocks):
                out[n * depth : (n + 1) * depth, i * size : (i + 1) * size] = total[first + i].astype(
                    out.dtype
                )


def forward(place, count, rows, cols, adj, parts, row_blocks, layout):
    size = adj.shape[1]
    depth = sum(part.shape[0] for part in parts)
    col_blocks = parts[0].shape[1] // size
    wide = row_blocks * size // sum(len(chunks) for chunks in layout)
    outs = [jax.ShapeDtypeStruct((len(chunks) * depth, wide), jnp.bfloat16) for chunks in layout]
    return pl.pallas_call(
        functools.partial(forward_kernel, len(parts), layout),
        out_shape=outs,
        in_specs=[SMEM] * 4 + [VMEM] * (1 + len(parts)),
        out_specs=[VMEM] * len(outs),
        scratch_shapes=[
            pltpu.VMEM((col_blocks, depth, size), jnp.bfloat16),
            pltpu.VMEM((row_blocks, depth, size), jnp.float32),
        ],
        compiler_params=params(14),
        cost_estimate=cost("forward_products"),
        name="forward_products",
    )(place, count, rows, cols, adj, *parts)


def backward_kernel(n_parts, chunks, place, count, rows, cols, adj, *refs):
    parts = refs[:n_parts]
    outs = refs[n_parts:-2]
    source, total = refs[-2:]
    size = adj.shape[1]
    depth = source.shape[1] // len(chunks)
    blocks = parts[0].shape[1] // size
    for k, part in enumerate(parts):
        first = (place[0] ^ k) * blocks
        for i in range(blocks):
            for n, chunk in enumerate(chunks):
                source[first + i, n * depth : (n + 1) * depth, :] = part[
                    chunk * depth : (chunk + 1) * depth, i * size : (i + 1) * size
                ]
    product_loop(count[0, 0], rows, cols, adj, source, total, NN)
    row = 0
    for out in outs:
        depth = out.shape[0]
        for c in range(total.shape[0]):
            out[:, c * size : (c + 1) * size] = total[c, row : row + depth, :].astype(out.dtype)
        row += depth


def backward(place, count, rows, cols, adj, parts, depth, out_chunks, col_blocks):
    size = adj.shape[1]
    chunks = [chunk for group in out_chunks for chunk in group]
    row_blocks = len(parts) * parts[0].shape[1] // size
    return pl.pallas_call(
        functools.partial(backward_kernel, len(parts), chunks),
        out_shape=[
            jax.ShapeDtypeStruct((len(group) * depth, col_blocks * size), jnp.bfloat16)
            for group in out_chunks
        ],
        in_specs=[SMEM] * 4 + [VMEM] * (1 + len(parts)),
        out_specs=[VMEM] * len(out_chunks),
        scratch_shapes=[
            pltpu.VMEM((row_blocks, len(chunks) * depth, size), jnp.bfloat16),
            pltpu.VMEM((col_blocks, len(chunks) * depth, size), jnp.float32),
        ],
        compiler_params=params(14),
        cost_estimate=cost("backward_products"),
        name="backward_products",
    )(place, count, rows, cols, adj, *parts)


def middle_kernel(sizes, n_sum, n_row, row, weight, cotangent, *refs):
    terms = refs[: n_sum * len(sizes)]
    outs = refs[n_sum * len(sizes) : -1]
    output, deltas, aggregated, back = outs
    ordered = refs[-1]
    depth = weight.shape[0] // n_row
    for j in range(n_row):
        first = pl.multiple_of((row[0] ^ j) * depth, depth)
        ordered[j * depth : (j + 1) * depth, :] = weight[pl.ds(first, depth), :]
    first = 0
    for p, size in enumerate(sizes):
        summed = terms[p * n_sum][:size, :].astype(jnp.float32)
        for k in range(1, n_sum):
            summed += terms[p * n_sum + k][:size, :].astype(jnp.float32)
        aggregated[first : first + size, :] = summed.astype(jnp.bfloat16)
        first += size
    nodes_first = aggregated[...].T
    preact = jnp.dot(nodes_first, ordered[...], preferred_element_type=jnp.float32)
    gate = jax.nn.sigmoid(preact)
    output[...] = (preact * gate).astype(jnp.bfloat16)
    slopes = gate * (1.0 + preact * (1.0 - gate))
    delta = (cotangent[...].astype(jnp.float32) * slopes).astype(jnp.bfloat16)
    deltas[...] = delta
    back[...] = lax.dot_general(ordered[...], delta, NT, preferred_element_type=jnp.float32).astype(
        jnp.bfloat16
    )


def middle(n_row, row, weight, cotangent, pieces):
    sizes = [piece[0].shape[0] for piece in pieces]
    nodes = cotangent.shape[0]
    features = weight.shape[0]
    shape = jax.ShapeDtypeStruct
    outs = [
        shape((nodes, features), jnp.bfloat16),
        shape((nodes, features), jnp.bfloat16),
        shape((features, nodes), jnp.bfloat16),
        shape((features, nodes), jnp.bfloat16),
    ]
    flat = [term for piece in pieces for term in piece]
    return pl.pallas_call(
        functools.partial(middle_kernel, sizes, len(pieces[0]), n_row),
        out_shape=outs,
        in_specs=[SMEM] + [VMEM] * (2 + len(flat)),
        out_specs=[VMEM] * len(outs),
        scratch_shapes=[pltpu.VMEM(weight.shape, jnp.bfloat16)],
        compiler_params=params(10),
        cost_estimate=cost("layer"),
        name="layer",
    )(row, weight, cotangent, *flat)


def gradient_kernel(scale, order, aggregated, deltas, *outs):
    product = jnp.dot(aggregated[...], deltas[...], preferred_element_type=jnp.float32) * scale
    for out, chunks in zip(outs, order):
        depth = out.shape[1]
        for n, k in enumerate(chunks):
            out[n] = product[k * depth : (k + 1) * depth, :]


def gradient(scale, order, aggregated, deltas):
    depth = aggregated.shape[0] // sum(len(chunks) for chunks in order)
    outs = [jax.ShapeDtypeStruct((len(chunks), depth, deltas.shape[1]), jnp.float32) for chunks in order]
    return pl.pallas_call(
        functools.partial(gradient_kernel, scale, order),
        out_shape=outs,
        in_specs=[VMEM] * 2,
        out_specs=[VMEM] * len(outs),
        compiler_params=params(6),
        cost_estimate=cost("weight_gradient"),
        name="weight_gradient",
    )(aggregated, deltas)


def place_kernel(order, row, *refs):
    out = refs[-1]
    for ref, chunks in zip(refs[:-1], order):
        depth = ref.shape[1]
        for n, k in enumerate(chunks):
            first = pl.multiple_of((row[0] ^ k) * depth, depth)
            out[pl.ds(first, depth), :] = ref[n]


def place_rows(row, order, parts):
    _, depth, wide = parts[0].shape
    chunks = sum(part.shape[0] for part in parts)
    return pl.pallas_call(
        functools.partial(place_kernel, order),
        out_shape=jax.ShapeDtypeStruct((chunks * depth, wide), jnp.float32),
        in_specs=[SMEM] + [VMEM] * len(parts),
        out_specs=VMEM,
        compiler_params=params(4),
        cost_estimate=cost("place_rows"),
        name="place_rows",
    )(row, *parts)


def swap(value, axis, k):
    size = lax.axis_size(axis)
    return lax.ppermute(value, axis, [(i, i ^ k) for i in range(size)])


def wide_sum(*values):
    total = values[0].astype(jnp.float32)
    for value in values[1:]:
        total = total + value.astype(jnp.float32)
    return (total.astype(values[0].dtype),)


def after(value, *earlier):
    return lax.optimization_barrier((value, *earlier))[0]


def join(*values):
    return (jnp.stack(values),)


def pair_sum(mine, received):
    return tuple(part.astype(mine.dtype) for part in mine + received)


def pair_sum_rows(depth, mine, received):
    total = mine.astype(jnp.float32) + received.astype(jnp.float32)
    return tuple(
        total[first : first + depth].astype(mine.dtype) for first in range(0, total.shape[0], depth)
    )


def shards_exchanged(features, weight, adj_values, block_rows, block_cols, block_counts, cotangent):
    n_row = lax.axis_size("row")
    n_col = lax.axis_size("col")
    adj = adj_values[0, 0]
    rows = block_rows[0, 0]
    cols = block_cols[0, 0]
    count = block_counts
    size = adj.shape[1]
    nodes = cotangent.shape[0] * n_row * n_col
    row_blocks = cotangent.shape[0] * n_col // size
    col_blocks = features.shape[0] // size
    row = lax.axis_index("row").reshape(1)
    col = lax.axis_index("col").reshape(1)
    own = after(features.T, row, col)

    sibling = swap(own, "row", 1)
    others = [swap(own, "row", k) for k in range(2, n_row, 2)]
    layout = [(k,) for k in range(n_col)]
    rows, cols, tile = fetch(count, rows, cols, adj)
    parts = [own, sibling]
    for part in others:
        part = after(part, tile)
        parts += [part, swap(part, "row", 1)]
    terms = forward(col, count, rows, cols, tile, parts, row_blocks, layout)
    sums = [terms[0]] + [swap(terms[k], "col", k) for k in range(1, n_col)]
    output, deltas, aggregated, back = middle(n_row, row, weight, cotangent, [sums])
    gathered = [back] + [swap(back, "col", k) for k in range(1, n_col)]

    evens = tuple(range(0, n_row, 2))
    order = [evens, tuple(range(1, n_row, 2))]
    even, odd = gradient(1.0 / math.sqrt(nodes), order, aggregated, deltas)
    chunk, *sent = fuse("gradient_sum", pair_sum, even, swap(odd, "row", 1))
    from_rows = [swap(part, "row", k) for part, k in zip(sent, evens[1:])]
    (chunk,) = fuse("gradient_sum", wide_sum, chunk, *from_rows)

    depth = features.shape[1]

    def columns(pair, *earlier):
        parts = [gathered[0], after(gathered[1], *earlier), *gathered[2:]]
        groups = [pair, tuple(k + 1 for k in pair)]
        mine, sent = backward(col, count, rows, cols, tile, parts, depth, groups, col_blocks)
        return fuse("pair_sum", functools.partial(pair_sum_rows, depth), mine, swap(sent, "row", 1))

    from_cols = [swap(chunk, "col", k) for k in range(1, n_col)]
    near, far = columns((2, 6), chunk)
    collected = [swap(near, "row", 2), swap(far, "row", 6)]
    (chunk,) = fuse("gradient_sum", wide_sum, chunk, *from_cols)
    mine, near = columns((0, 4), far, chunk)
    collected += [swap(near, "row", 4), mine]

    (even,) = fuse("gradient_join", join, chunk, *[swap(chunk, "row", k) for k in evens[1:]])
    grad_weight = place_rows(row, order, [even, swap(even, "row", 1)])
    (grad_features,) = fuse("feature_sum", wide_sum, *collected)
    return output, grad_weight, grad_features.T


def shards_gathered(features, weight, adj_values, block_rows, block_cols, block_counts, cotangent):
    n_row = lax.axis_size("row")
    n_col = lax.axis_size("col")
    adj = adj_values[0, 0]
    rows = block_rows[0, 0]
    cols = block_cols[0, 0]
    count = block_counts
    size = adj.shape[1]
    nodes = cotangent.shape[0] * n_row * n_col
    row_blocks = cotangent.shape[0] * n_col // size
    col_blocks = features.shape[0] // size
    zero = jnp.zeros((1,), jnp.int32)
    panels = lax.all_gather(features.T, "row", axis=0, tiled=True)
    (terms,) = forward(zero, count, rows, cols, adj, [panels], row_blocks, [(0,)])
    part = lax.psum_scatter(terms, "col", scatter_dimension=1, tiled=True)
    output, deltas, aggregated, back = middle(1, zero, weight, cotangent, [[part]])
    slab = lax.all_gather(back, "col", axis=1, tiled=True)
    (column_terms,) = backward(
        zero, count, rows, cols, adj, [slab], slab.shape[0], [(0,)], col_blocks
    )
    grad_features = lax.psum_scatter(column_terms, "row", scatter_dimension=0, tiled=True).T
    (part,) = gradient(1.0 / math.sqrt(nodes), [(0,)], aggregated, deltas)
    grad_weight = lax.psum(part[0], ("row", "col"))
    return output, grad_weight, grad_features


def solution(mesh):
    n_row = mesh.shape["row"]
    n_col = mesh.shape["col"]
    exchanged = n_row == 8 and n_col == 4
    return jax.shard_map(
        shards_exchanged if exchanged else shards_gathered,
        mesh=mesh,
        in_specs=(
            P("col", "row"),
            P(),
            P("row", "col", None, None, None),
            P("row", "col", None),
            P("row", "col", None),
            P("row", "col"),
            P(("row", "col"), None),
        ),
        out_specs=(P(("row", "col"), None), P(), P("col", "row")),
        check_vma=False,
    )
```

```python
import functools
import math

import jax
import jax.numpy as jnp
from jax import lax
from jax.experimental import pallas as pl
from jax.experimental.pallas import tpu as pltpu
from jax.sharding import PartitionSpec as P

VMEM = pl.BlockSpec(memory_space=pltpu.VMEM)
SMEM = pl.BlockSpec(memory_space=pltpu.SMEM)
HBM = pl.BlockSpec(memory_space=pltpu.HBM)
MIB = 1024 * 1024
NT = (((1,), (1,)), ((), ()))
NN = (((1,), (0,)), ((), ()))


COSTS = {"fetch": 1e9, "forward_products": 1e9, "backward_products": 1e9}


def cost(name):
    return pl.CostEstimate(flops=int(COSTS.get(name, 1)), bytes_accessed=1, transcendentals=0)


def params(mib):
    return pltpu.CompilerParams(vmem_limit_bytes=mib * MIB)


def fuse(name, function, *values):
    shapes = jax.eval_shape(function, *values)

    def kernel(*refs):
        results = function(*[ref[...] for ref in refs[: len(values)]])
        for ref, result in zip(refs[len(values) :], results):
            ref[...] = result

    return pl.pallas_call(
        kernel,
        out_shape=shapes,
        in_specs=[VMEM] * len(values),
        out_specs=[VMEM] * len(shapes),
        compiler_params=params(4),
        cost_estimate=cost(name),
        name=name,
    )(*values)


def turn_of(slots):
    return math.gcd(slots, 8)


def product_loop(count, source_ids, target_ids, adj, source, total, dims):
    turn = turn_of(adj.shape[0])
    total[...] = jnp.zeros_like(total)

    def step(index, carry):
        first = index * turn
        products = []
        for k in range(turn):
            operand = source[source_ids[first + k]]
            products.append(
                lax.dot_general(operand, adj[first + k], dims, preferred_element_type=jnp.float32)
            )
        for k in range(turn):
            target = target_ids[first + k]
            live = first + k < count
            total[target] += jnp.where(live, products[k], 0.0)
        return carry

    lax.fori_loop(0, (count + turn - 1) // turn, step, 0)


def fetch_kernel(count, rows, cols, tile, *refs):
    outs, (sem, ids_sem) = refs[:3], refs[3:]
    ids = [
        pltpu.make_async_copy(source, target, ids_sem.at[n])
        for n, (source, target) in enumerate(zip((rows, cols), outs))
    ]
    for copy in ids:
        copy.start()
    turn = turn_of(tile.shape[0])

    def copy_turn(index):
        blocks = pl.ds(index * turn, turn)
        return pltpu.make_async_copy(tile.at[blocks], outs[2].at[blocks], sem.at[index])

    def begin(index, carry):
        copy_turn(index).start()
        return carry

    def finish(index, carry):
        copy_turn(index).wait()
        return carry

    turns = (count[0, 0] + turn - 1) // turn
    lax.fori_loop(0, turns, begin, 0)
    lax.fori_loop(0, turns, finish, 0)
    for copy in ids:
        copy.wait()


def fetch(count, *arrays):
    blocks = arrays[2].shape[0]
    return pl.pallas_call(
        fetch_kernel,
        out_shape=[jax.ShapeDtypeStruct(array.shape, array.dtype) for array in arrays],
        in_specs=[SMEM] + [HBM] * len(arrays),
        out_specs=[VMEM] * len(arrays),
        scratch_shapes=[
            pltpu.SemaphoreType.DMA((blocks // turn_of(blocks),)),
            pltpu.SemaphoreType.DMA((2,)),
        ],
        compiler_params=params(4),
        cost_estimate=cost("fetch"),
        name="fetch",
    )(count, *[pltpu.with_memory_space_constraint(array, pltpu.HBM) for array in arrays])


def forward_kernel(n_parts, count, rows, cols, adj, *refs):
    parts = refs[:n_parts]
    outs = refs[n_parts:-2]
    source, total = refs[-2:]
    size = adj.shape[1]
    row = 0
    for part in parts:
        depth = part.shape[0]
        for c in range(source.shape[0]):
            source[c, row : row + depth, :] = part[:, c * size : (c + 1) * size]
        row += depth
    product_loop(count[0, 0], cols, rows, adj, source, total, NT)
    (out,) = outs
    blocks = out.shape[2] // size
    for n in range(out.shape[0]):
        for i in range(blocks):
            out[n, :, i * size : (i + 1) * size] = total[n * blocks + i].astype(out.dtype)


def forward(count, rows, cols, adj, parts, row_blocks, n_chunks):
    size = adj.shape[1]
    depth = sum(part.shape[0] for part in parts)
    col_blocks = parts[0].shape[1] // size
    return pl.pallas_call(
        functools.partial(forward_kernel, len(parts)),
        out_shape=jax.ShapeDtypeStruct((n_chunks, depth, row_blocks * size // n_chunks), jnp.bfloat16),
        in_specs=[SMEM] * 3 + [VMEM] * (1 + len(parts)),
        out_specs=VMEM,
        scratch_shapes=[
            pltpu.VMEM((col_blocks, depth, size), jnp.bfloat16),
            pltpu.VMEM((row_blocks, depth, size), jnp.float32),
        ],
        compiler_params=params(14),
        cost_estimate=cost("forward_products"),
        name="forward_products",
    )(count, rows, cols, adj, *parts)


def backward_kernel(chunks, count, rows, cols, adj, slab, *refs):
    outs = refs[:-2]
    source, total = refs[-2:]
    size = adj.shape[1]
    depth = source.shape[1] // len(chunks)
    blocks = slab.shape[2] // size
    for k in range(slab.shape[0]):
        for i in range(blocks):
            for n, chunk in enumerate(chunks):
                source[k * blocks + i, n * depth : (n + 1) * depth, :] = slab[
                    k, chunk * depth : (chunk + 1) * depth, i * size : (i + 1) * size
                ]
    product_loop(count[0, 0], rows, cols, adj, source, total, NN)
    row = 0
    for out in outs:
        depth = out.shape[0]
        for c in range(total.shape[0]):
            out[:, c * size : (c + 1) * size] = total[c, row : row + depth, :].astype(out.dtype)
        row += depth


def backward(count, rows, cols, adj, slab, depth, out_chunks, col_blocks):
    size = adj.shape[1]
    chunks = [chunk for group in out_chunks for chunk in group]
    row_blocks = slab.shape[0] * slab.shape[2] // size
    return pl.pallas_call(
        functools.partial(backward_kernel, chunks),
        out_shape=[
            jax.ShapeDtypeStruct((len(group) * depth, col_blocks * size), jnp.bfloat16)
            for group in out_chunks
        ],
        in_specs=[SMEM] * 3 + [VMEM] * 2,
        out_specs=[VMEM] * len(out_chunks),
        scratch_shapes=[
            pltpu.VMEM((row_blocks, len(chunks) * depth, size), jnp.bfloat16),
            pltpu.VMEM((col_blocks, len(chunks) * depth, size), jnp.float32),
        ],
        compiler_params=params(14),
        cost_estimate=cost("backward_products"),
        name="backward_products",
    )(count, rows, cols, adj, slab)


def middle_kernel(n_row, row, weight, cotangent, terms, output, deltas, aggregated, back, ordered):
    depth = weight.shape[0] // n_row
    for j in range(n_row):
        first = pl.multiple_of((row[0] ^ j) * depth, depth)
        ordered[j * depth : (j + 1) * depth, :] = weight[pl.ds(first, depth), :]
    summed = terms[0].astype(jnp.float32)
    for k in range(1, terms.shape[0]):
        summed += terms[k].astype(jnp.float32)
    aggregated[...] = summed.astype(jnp.bfloat16)
    nodes_first = aggregated[...].T
    preact = jnp.dot(nodes_first, ordered[...], preferred_element_type=jnp.float32)
    gate = jax.nn.sigmoid(preact)
    output[...] = (preact * gate).astype(jnp.bfloat16)
    slopes = gate * (1.0 + preact * (1.0 - gate))
    delta = (cotangent[...].astype(jnp.float32) * slopes).astype(jnp.bfloat16)
    deltas[...] = delta
    product = lax.dot_general(ordered[...], delta, NT, preferred_element_type=jnp.float32)
    for k in range(back.shape[0]):
        back[k] = product.astype(jnp.bfloat16)


def middle(n_row, row, weight, cotangent, terms, copies):
    nodes = cotangent.shape[0]
    features = weight.shape[0]
    shape = jax.ShapeDtypeStruct
    return pl.pallas_call(
        functools.partial(middle_kernel, n_row),
        out_shape=[
            shape((nodes, features), jnp.bfloat16),
            shape((nodes, features), jnp.bfloat16),
            shape((features, nodes), jnp.bfloat16),
            shape((copies, features, nodes), jnp.bfloat16),
        ],
        in_specs=[SMEM] + [VMEM] * 3,
        out_specs=[VMEM] * 4,
        scratch_shapes=[pltpu.VMEM(weight.shape, jnp.bfloat16)],
        compiler_params=params(10),
        cost_estimate=cost("layer"),
        name="layer",
    )(row, weight, cotangent, terms)


def gradient_kernel(scale, row, aggregated, deltas, out):
    product = jnp.dot(aggregated[...], deltas[...], preferred_element_type=jnp.float32) * scale
    depth = out.shape[1]
    for j in range(out.shape[0]):
        out[row[0] ^ j] = product[j * depth : (j + 1) * depth, :]


def gradient(scale, n_row, row, aggregated, deltas):
    features = aggregated.shape[0]
    return pl.pallas_call(
        functools.partial(gradient_kernel, scale),
        out_shape=[jax.ShapeDtypeStruct((n_row, features // n_row, deltas.shape[1]), jnp.float32)],
        in_specs=[SMEM] + [VMEM] * 2,
        out_specs=[VMEM],
        compiler_params=params(6),
        cost_estimate=cost("weight_gradient"),
        name="weight_gradient",
    )(row, aggregated, deltas)


def swap(value, axis, k):
    size = lax.axis_size(axis)
    return lax.ppermute(value, axis, [(i, i ^ k) for i in range(size)])


def wide_sum(*values):
    total = values[0].astype(jnp.float32)
    for value in values[1:]:
        total = total + value.astype(jnp.float32)
    return (total.astype(values[0].dtype),)


def after(value, *earlier):
    return lax.optimization_barrier((value, *earlier))[0]


def exchange(value, axis, groups=None):
    return lax.all_to_all(value, axis, 0, 0, tiled=True, axis_index_groups=groups)


def sum_parts(copies, value):
    total = value[0]
    for k in range(1, value.shape[0]):
        total = total + value[k]
    return (jnp.broadcast_to(total[None], (copies, *total.shape)),)


def pair_sum(mine, received):
    return tuple(part.astype(mine.dtype) for part in mine + received)


def pair_sum_rows(depth, mine, received):
    total = mine.astype(jnp.float32) + received.astype(jnp.float32)
    return tuple(
        total[first : first + depth].astype(mine.dtype) for first in range(0, total.shape[0], depth)
    )


def shards_exchanged(features, weight, adj_values, block_rows, block_cols, block_counts, cotangent):
    n_row = lax.axis_size("row")
    n_col = lax.axis_size("col")
    adj = adj_values[0, 0]
    rows = block_rows[0, 0]
    cols = block_cols[0, 0]
    count = block_counts
    size = adj.shape[1]
    nodes = cotangent.shape[0] * n_row * n_col
    row_blocks = cotangent.shape[0] * n_col // size
    col_blocks = features.shape[0] // size
    row = lax.axis_index("row").reshape(1)
    own = after(features.T, row)

    sibling = swap(own, "row", 1)
    others = [swap(own, "row", k) for k in range(2, n_row, 2)]
    rows, cols, tile = fetch(count, rows, cols, adj)
    parts = [own, sibling]
    for part in others:
        part = after(part, tile)
        parts += [part, swap(part, "row", 1)]
    terms = forward(count, rows, cols, tile, parts, row_blocks, n_col)
    output, deltas, aggregated, back = middle(
        n_row, row, weight, cotangent, exchange(terms, "col"), n_col
    )
    slab = exchange(back, "col")

    (product,) = gradient(1.0 / math.sqrt(nodes), n_row, row, aggregated, deltas)
    (chunk,) = fuse("gradient_sum", functools.partial(sum_parts, n_col), exchange(product, "row"))
    (chunk,) = fuse("gradient_sum", functools.partial(sum_parts, n_row), exchange(chunk, "col"))
    grad_weight = exchange(chunk, "row").reshape(weight.shape)

    depth = features.shape[1]

    def columns(pair, *earlier):
        groups = [pair, tuple(k + 1 for k in pair)]
        mine, sent = backward(count, rows, cols, tile, after(slab, *earlier), depth, groups, col_blocks)
        return fuse("pair_sum", functools.partial(pair_sum_rows, depth), mine, swap(sent, "row", 1))

    near, far = columns((2, 6))
    collected = [swap(near, "row", 2), swap(far, "row", 6)]
    mine, near = columns((0, 4))
    collected += [swap(near, "row", 4), mine]
    (grad_features,) = fuse("feature_sum", wide_sum, *collected)
    return output, grad_weight, grad_features.T


def shards_gathered(features, weight, adj_values, block_rows, block_cols, block_counts, cotangent):
    n_row = lax.axis_size("row")
    n_col = lax.axis_size("col")
    adj = adj_values[0, 0]
    rows = block_rows[0, 0]
    cols = block_cols[0, 0]
    count = block_counts
    size = adj.shape[1]
    nodes = cotangent.shape[0] * n_row * n_col
    row_blocks = cotangent.shape[0] * n_col // size
    col_blocks = features.shape[0] // size
    zero = jnp.zeros((1,), jnp.int32)
    panels = lax.all_gather(features.T, "row", axis=0, tiled=True)
    terms = forward(count, rows, cols, adj, [panels], row_blocks, 1)
    part = lax.psum_scatter(terms, "col", scatter_dimension=2, tiled=True)
    output, deltas, aggregated, back = middle(1, zero, weight, cotangent, part, 1)
    slab = lax.all_gather(back, "col", axis=2, tiled=True)
    (column_terms,) = backward(count, rows, cols, adj, slab, slab.shape[1], [(0,)], col_blocks)
    grad_features = lax.psum_scatter(column_terms, "row", scatter_dimension=0, tiled=True).T
    (product,) = gradient(1.0 / math.sqrt(nodes), 1, zero, aggregated, deltas)
    grad_weight = lax.psum(product[0], ("row", "col"))
    return output, grad_weight, grad_features


def solution(mesh):
    n_row = mesh.shape["row"]
    n_col = mesh.shape["col"]
    exchanged = n_row == 8 and n_col == 4
    return jax.shard_map(
        shards_exchanged if exchanged else shards_gathered,
        mesh=mesh,
        in_specs=(
            P("col", "row"),
            P(),
            P("row", "col", None, None, None),
            P("row", "col", None),
            P("row", "col", None),
            P("row", "col"),
            P(("row", "col"), None),
        ),
        out_specs=(P(("row", "col"), None), P(), P("col", "row")),
        check_vma=False,
    )
```

```python
import functools
import math

import jax
import jax.numpy as jnp
from jax import lax
from jax.experimental import pallas as pl
from jax.experimental.pallas import tpu as pltpu
from jax.sharding import PartitionSpec as P

VMEM = pl.BlockSpec(memory_space=pltpu.VMEM)
SMEM = pl.BlockSpec(memory_space=pltpu.SMEM)
HBM = pl.BlockSpec(memory_space=pltpu.HBM)
MIB = 1024 * 1024
NT = (((1,), (1,)), ((), ()))
NN = (((1,), (0,)), ((), ()))


COSTS = {"fetch": 1e9, "forward_products": 1e9, "backward_products": 1e9}


def cost(name):
    return pl.CostEstimate(flops=int(COSTS.get(name, 1)), bytes_accessed=1, transcendentals=0)


def params(mib):
    return pltpu.CompilerParams(vmem_limit_bytes=mib * MIB)


def fuse(name, function, *values):
    shapes = jax.eval_shape(function, *values)

    def kernel(*refs):
        results = function(*[ref[...] for ref in refs[: len(values)]])
        for ref, result in zip(refs[len(values) :], results):
            ref[...] = result

    return pl.pallas_call(
        kernel,
        out_shape=shapes,
        in_specs=[VMEM] * len(values),
        out_specs=[VMEM] * len(shapes),
        compiler_params=params(4),
        cost_estimate=cost(name),
        name=name,
    )(*values)


def turn_of(slots):
    return math.gcd(slots, 8)


def product_loop(count, source_ids, target_ids, adj, source, total, dims):
    turn = turn_of(adj.shape[0])
    total[...] = jnp.zeros_like(total)

    def step(index, carry):
        first = index * turn
        products = []
        for k in range(turn):
            operand = source[source_ids[first + k]]
            products.append(
                lax.dot_general(operand, adj[first + k], dims, preferred_element_type=jnp.float32)
            )
        for k in range(turn):
            target = target_ids[first + k]
            live = first + k < count
            total[target] += jnp.where(live, products[k], 0.0)
        return carry

    lax.fori_loop(0, (count + turn - 1) // turn, step, 0)


def fetch_kernel(count, rows, cols, tile, *refs):
    outs, (sem, ids_sem) = refs[:3], refs[3:]
    ids = [
        pltpu.make_async_copy(source, target, ids_sem.at[n])
        for n, (source, target) in enumerate(zip((rows, cols), outs))
    ]
    for copy in ids:
        copy.start()
    turn = turn_of(tile.shape[0])

    def copy_turn(index):
        blocks = pl.ds(index * turn, turn)
        return pltpu.make_async_copy(tile.at[blocks], outs[2].at[blocks], sem.at[index])

    def begin(index, carry):
        copy_turn(index).start()
        return carry

    def finish(index, carry):
        copy_turn(index).wait()
        return carry

    turns = (count[0, 0] + turn - 1) // turn
    lax.fori_loop(0, turns, begin, 0)
    lax.fori_loop(0, turns, finish, 0)
    for copy in ids:
        copy.wait()


def fetch(count, *arrays):
    blocks = arrays[2].shape[0]
    return pl.pallas_call(
        fetch_kernel,
        out_shape=[jax.ShapeDtypeStruct(array.shape, array.dtype) for array in arrays],
        in_specs=[SMEM] + [HBM] * len(arrays),
        out_specs=[VMEM] * len(arrays),
        scratch_shapes=[
            pltpu.SemaphoreType.DMA((blocks // turn_of(blocks),)),
            pltpu.SemaphoreType.DMA((2,)),
        ],
        compiler_params=params(4),
        cost_estimate=cost("fetch"),
        name="fetch",
    )(count, *[pltpu.with_memory_space_constraint(array, pltpu.HBM) for array in arrays])


def forward_kernel(n_parts, layout, place, count, rows, cols, adj, *refs):
    parts = refs[:n_parts]
    outs = refs[n_parts:-2]
    source, total = refs[-2:]
    size = adj.shape[1]
    row = 0
    for part in parts:
        depth = part.shape[0]
        for c in range(source.shape[0]):
            source[c, row : row + depth, :] = part[:, c * size : (c + 1) * size]
        row += depth
    product_loop(count[0, 0], cols, rows, adj, source, total, NT)
    depth = total.shape[1]
    blocks = outs[0].shape[1] // size
    for out, chunks in zip(outs, layout):
        for n, k in enumerate(chunks):
            first = (place[0] ^ k) * blocks
            for i in range(blocks):
                out[n * depth : (n + 1) * depth, i * size : (i + 1) * size] = total[first + i].astype(
                    out.dtype
                )


def forward(place, count, rows, cols, adj, parts, row_blocks, layout):
    size = adj.shape[1]
    depth = sum(part.shape[0] for part in parts)
    col_blocks = parts[0].shape[1] // size
    wide = row_blocks * size // sum(len(chunks) for chunks in layout)
    outs = [jax.ShapeDtypeStruct((len(chunks) * depth, wide), jnp.bfloat16) for chunks in layout]
    return pl.pallas_call(
        functools.partial(forward_kernel, len(parts), layout),
        out_shape=outs,
        in_specs=[SMEM] * 4 + [VMEM] * (1 + len(parts)),
        out_specs=[VMEM] * len(outs),
        scratch_shapes=[
            pltpu.VMEM((col_blocks, depth, size), jnp.bfloat16),
            pltpu.VMEM((row_blocks, depth, size), jnp.float32),
        ],
        compiler_params=params(14),
        cost_estimate=cost("forward_products"),
        name="forward_products",
    )(place, count, rows, cols, adj, *parts)


def backward_kernel(n_parts, place, count, rows, cols, adj, *refs):
    parts = refs[:n_parts]
    outs = refs[n_parts:-2]
    source, total = refs[-2:]
    size = adj.shape[1]
    depth = source.shape[1]
    blocks = parts[0].shape[1] // size
    for k, part in enumerate(parts):
        first = (place[0] ^ k) * blocks
        for i in range(blocks):
            source[first + i] = part[:depth, i * size : (i + 1) * size]
    product_loop(count[0, 0], rows, cols, adj, source, total, NN)
    row = 0
    for out in outs:
        depth = out.shape[0]
        for c in range(total.shape[0]):
            out[:, c * size : (c + 1) * size] = total[c, row : row + depth, :].astype(out.dtype)
        row += depth


def backward(place, count, rows, cols, adj, parts, out_depths, col_blocks):
    size = adj.shape[1]
    row_blocks = len(parts) * parts[0].shape[1] // size
    return pl.pallas_call(
        functools.partial(backward_kernel, len(parts)),
        out_shape=[jax.ShapeDtypeStruct((depth, col_blocks * size), jnp.bfloat16) for depth in out_depths],
        in_specs=[SMEM] * 4 + [VMEM] * (1 + len(parts)),
        out_specs=[VMEM] * len(out_depths),
        scratch_shapes=[
            pltpu.VMEM((row_blocks, sum(out_depths), size), jnp.bfloat16),
            pltpu.VMEM((col_blocks, sum(out_depths), size), jnp.float32),
        ],
        compiler_params=params(14),
        cost_estimate=cost("backward_products"),
        name="backward_products",
    )(place, count, rows, cols, adj, *parts)


def middle_kernel(sizes, order, n_sum, n_row, row, weight, cotangent, *refs):
    terms = refs[: n_sum * len(sizes)]
    outs = refs[n_sum * len(sizes) : -1]
    output, deltas, aggregated, *backs = outs
    ordered = refs[-1]
    depth = weight.shape[0] // n_row
    for j in range(n_row):
        first = pl.multiple_of((row[0] ^ j) * depth, depth)
        ordered[j * depth : (j + 1) * depth, :] = weight[pl.ds(first, depth), :]
    first = 0
    for p, size in enumerate(sizes):
        summed = terms[p * n_sum][:size, :].astype(jnp.float32)
        for k in range(1, n_sum):
            summed += terms[p * n_sum + k][:size, :].astype(jnp.float32)
        aggregated[first : first + size, :] = summed.astype(jnp.bfloat16)
        first += size
    nodes_first = aggregated[...].T
    preact = jnp.dot(nodes_first, ordered[...], preferred_element_type=jnp.float32)
    gate = jax.nn.sigmoid(preact)
    output[...] = (preact * gate).astype(jnp.bfloat16)
    slopes = gate * (1.0 + preact * (1.0 - gate))
    delta = (cotangent[...].astype(jnp.float32) * slopes).astype(jnp.bfloat16)
    deltas[...] = delta
    product = lax.dot_general(ordered[...], delta, NT, preferred_element_type=jnp.float32)
    for back, chunks in zip(backs, order):
        for n, k in enumerate(chunks):
            back[n * depth : (n + 1) * depth, :] = product[k * depth : (k + 1) * depth, :].astype(jnp.bfloat16)


def middle(n_row, row, weight, cotangent, pieces, order):
    sizes = [piece[0].shape[0] for piece in pieces]
    nodes = cotangent.shape[0]
    features = weight.shape[0]
    shape = jax.ShapeDtypeStruct
    outs = [
        shape((nodes, features), jnp.bfloat16),
        shape((nodes, features), jnp.bfloat16),
        shape((features, nodes), jnp.bfloat16),
    ] + [shape((len(chunks) * features // n_row, nodes), jnp.bfloat16) for chunks in order]
    flat = [term for piece in pieces for term in piece]
    return pl.pallas_call(
        functools.partial(middle_kernel, sizes, order, len(pieces[0]), n_row),
        out_shape=outs,
        in_specs=[SMEM] + [VMEM] * (2 + len(flat)),
        out_specs=[VMEM] * len(outs),
        scratch_shapes=[pltpu.VMEM(weight.shape, jnp.bfloat16)],
        compiler_params=params(10),
        cost_estimate=cost("layer"),
        name="layer",
    )(row, weight, cotangent, *flat)


def gradient_kernel(scale, order, aggregated, deltas, *outs):
    product = jnp.dot(aggregated[...], deltas[...], preferred_element_type=jnp.float32) * scale
    for out, chunks in zip(outs, order):
        depth = out.shape[1]
        for n, k in enumerate(chunks):
            out[n] = product[k * depth : (k + 1) * depth, :]


def gradient(scale, order, aggregated, deltas):
    depth = aggregated.shape[0] // sum(len(chunks) for chunks in order)
    outs = [jax.ShapeDtypeStruct((len(chunks), depth, deltas.shape[1]), jnp.float32) for chunks in order]
    return pl.pallas_call(
        functools.partial(gradient_kernel, scale, order),
        out_shape=outs,
        in_specs=[VMEM] * 2,
        out_specs=[VMEM] * len(outs),
        compiler_params=params(6),
        cost_estimate=cost("weight_gradient"),
        name="weight_gradient",
    )(aggregated, deltas)


def place_kernel(order, row, *refs):
    out = refs[-1]
    for ref, chunks in zip(refs[:-1], order):
        depth = ref.shape[1]
        for n, k in enumerate(chunks):
            first = pl.multiple_of((row[0] ^ k) * depth, depth)
            out[pl.ds(first, depth), :] = ref[n]


def place_rows(row, order, parts):
    _, depth, wide = parts[0].shape
    chunks = sum(part.shape[0] for part in parts)
    return pl.pallas_call(
        functools.partial(place_kernel, order),
        out_shape=jax.ShapeDtypeStruct((chunks * depth, wide), jnp.float32),
        in_specs=[SMEM] + [VMEM] * len(parts),
        out_specs=VMEM,
        compiler_params=params(4),
        cost_estimate=cost("place_rows"),
        name="place_rows",
    )(row, *parts)


def swap(value, axis, k):
    size = lax.axis_size(axis)
    return lax.ppermute(value, axis, [(i, i ^ k) for i in range(size)])


def wide_sum(*values):
    total = values[0].astype(jnp.float32)
    for value in values[1:]:
        total = total + value.astype(jnp.float32)
    return (total.astype(values[0].dtype),)


def after(value, *earlier):
    return lax.optimization_barrier((value, *earlier))[0]


def join(*values):
    return (jnp.stack(values),)


def with_chunk(rows, *parts):
    total = functools.reduce(jnp.add, parts)
    high = total.astype(jnp.bfloat16)
    low = (total - high.astype(jnp.float32)).astype(jnp.bfloat16)
    return (jnp.concatenate([rows, jnp.concatenate([high, low], axis=1)]),)


def chunk_sum(depth, *values):
    sums = []
    for value in values:
        halves = value[-depth:].astype(jnp.float32)
        wide = halves.shape[1] // 2
        sums.append(halves[:, :wide] + halves[:, wide:])
    while len(sums) > 1:
        sums = [sums[n] + sums[n + 1] for n in range(0, len(sums), 2)]
    return (sums[0],)


def pair_sum(mine, *received):
    return tuple(mine + jnp.concatenate(received))


def pair_sum_rows(depth, mine, *received):
    total = mine.astype(jnp.float32) + jnp.concatenate(received).astype(jnp.float32)
    return tuple(
        total[first : first + depth].astype(mine.dtype) for first in range(0, total.shape[0], depth)
    )


def shards_exchanged(features, weight, adj_values, block_rows, block_cols, block_counts, cotangent):
    n_row = lax.axis_size("row")
    n_col = lax.axis_size("col")
    adj = adj_values[0, 0]
    rows = block_rows[0, 0]
    cols = block_cols[0, 0]
    count = block_counts
    size = adj.shape[1]
    nodes = cotangent.shape[0] * n_row * n_col
    row_blocks = cotangent.shape[0] * n_col // size
    col_blocks = features.shape[0] // size
    row = lax.axis_index("row").reshape(1)
    col = lax.axis_index("col").reshape(1)
    own = after(features.T, row, col)

    depth = features.shape[1]
    layout = [(k,) for k in range(n_col)]

    def to_cols(value):
        return [value] + [swap(value, "col", k) for k in range(1, n_col)]

    near = [k for k in range(2, n_row, 2) if k & (k - 1) == 0]
    far = [k for k in range(2, n_row, 2) if k & (k - 1) != 0]
    sibling = swap(own, "row", 1)
    from_near = [swap(own, "row", k) for k in near]
    rows, cols, tile = fetch(count, rows, cols, adj)
    from_near = [after(part, tile) for part in from_near]
    from_far = [swap(after(own, *from_near), "row", k) for k in far]

    def forward_piece(parts, whole):
        parts = parts + [piece for part in whole for piece in (part, swap(part, "row", 1))]
        terms = forward(col, count, rows, cols, tile, parts, row_blocks, layout)
        return terms, [terms[0]] + [swap(terms[k], "col", k) for k in range(1, n_col)]

    terms, first = forward_piece([own, sibling], from_near)
    _, second = forward_piece([], [after(part, *terms) for part in from_far])
    sums = [first, second]
    pairs = [(2, 6), (0, 4)]
    order = [pair + tuple(k + 1 for k in pair) for pair in pairs]
    output, deltas, aggregated, *backs = middle(n_row, row, weight, cotangent, sums, order)
    first = to_cols(backs[0])

    evens = tuple(range(0, n_row, 2))
    places = [evens, tuple(range(1, n_row, 2))]
    even, *odd = gradient(1.0 / math.sqrt(nodes), [places[0], places[1][:2], places[1][2:]], aggregated, deltas)
    chunk, *sent = fuse("gradient_sum", pair_sum, even, *[swap(part, "row", 1) for part in odd])
    from_rows = [swap(part, "row", k) for part, k in zip(sent, evens[1:])]
    (back,) = fuse("with_chunk", with_chunk, backs[1], chunk, *from_rows)
    second = to_cols(back)

    def columns(parts, *earlier):
        parts = [after(parts[0], *earlier), *parts[1:]]
        out_depths = [2 * depth] + [depth // 2] * 4
        mine, *sent = backward(col, count, rows, cols, tile, parts, out_depths, col_blocks)
        received = [swap(part, "row", 1) for part in sent]
        return fuse("pair_sum", functools.partial(pair_sum_rows, depth), mine, *received)

    terms = columns(first, back)
    collected = [swap(term, "row", k) for term, k in zip(terms, pairs[0])]
    second[1] = after(second[1], *terms)
    (chunk,) = fuse("chunk_sum", functools.partial(chunk_sum, depth), *second)
    from_rows = [swap(chunk, "row", k) for k in evens[1:]]
    mine, term = columns(second, chunk, *terms)
    collected += [swap(term, "row", pairs[1][1]), mine]
    (even,) = fuse("gradient_join", join, chunk, *from_rows)
    grad_weight = place_rows(row, places, [even, swap(even, "row", 1)])
    (grad_features,) = fuse("feature_sum", wide_sum, *collected)
    return output, grad_weight, grad_features.T


def shards_gathered(features, weight, adj_values, block_rows, block_cols, block_counts, cotangent):
    n_row = lax.axis_size("row")
    n_col = lax.axis_size("col")
    adj = adj_values[0, 0]
    rows = block_rows[0, 0]
    cols = block_cols[0, 0]
    count = block_counts
    size = adj.shape[1]
    nodes = cotangent.shape[0] * n_row * n_col
    row_blocks = cotangent.shape[0] * n_col // size
    col_blocks = features.shape[0] // size
    zero = jnp.zeros((1,), jnp.int32)
    panels = lax.all_gather(features.T, "row", axis=0, tiled=True)
    (terms,) = forward(zero, count, rows, cols, adj, [panels], row_blocks, [(0,)])
    part = lax.psum_scatter(terms, "col", scatter_dimension=1, tiled=True)
    output, deltas, aggregated, back = middle(1, zero, weight, cotangent, [[part]], [(0,)])
    slab = lax.all_gather(back, "col", axis=1, tiled=True)
    (column_terms,) = backward(zero, count, rows, cols, adj, [slab], [slab.shape[0]], col_blocks)
    grad_features = lax.psum_scatter(column_terms, "row", scatter_dimension=0, tiled=True).T
    (part,) = gradient(1.0 / math.sqrt(nodes), [(0,)], aggregated, deltas)
    grad_weight = lax.psum(part[0], ("row", "col"))
    return output, grad_weight, grad_features


def solution(mesh):
    n_row = mesh.shape["row"]
    n_col = mesh.shape["col"]
    exchanged = n_row == 8 and n_col == 4
    return jax.shard_map(
        shards_exchanged if exchanged else shards_gathered,
        mesh=mesh,
        in_specs=(
            P("col", "row"),
            P(),
            P("row", "col", None, None, None),
            P("row", "col", None),
            P("row", "col", None),
            P("row", "col"),
            P(("row", "col"), None),
        ),
        out_specs=(P(("row", "col"), None), P(), P("col", "row")),
        check_vma=False,
    )
```

```python
import functools
import math

import jax
import jax.numpy as jnp
from jax import lax
from jax.experimental import pallas as pl
from jax.experimental.pallas import tpu as pltpu
from jax.sharding import PartitionSpec as P

VMEM = pl.BlockSpec(memory_space=pltpu.VMEM)
SMEM = pl.BlockSpec(memory_space=pltpu.SMEM)
HBM = pl.BlockSpec(memory_space=pltpu.HBM)
MIB = 1024 * 1024
NT = (((1,), (1,)), ((), ()))
NN = (((1,), (0,)), ((), ()))


COSTS = {"fetch": 1e9, "forward_products": 1e9, "backward_products": 1e9}


def cost(name):
    return pl.CostEstimate(flops=int(COSTS.get(name, 1)), bytes_accessed=1, transcendentals=0)


def params(mib):
    return pltpu.CompilerParams(vmem_limit_bytes=mib * MIB)


def fuse(name, function, *values):
    shapes = jax.eval_shape(function, *values)

    def kernel(*refs):
        results = function(*[ref[...] for ref in refs[: len(values)]])
        for ref, result in zip(refs[len(values) :], results):
            ref[...] = result

    return pl.pallas_call(
        kernel,
        out_shape=shapes,
        in_specs=[VMEM] * len(values),
        out_specs=[VMEM] * len(shapes),
        compiler_params=params(4),
        cost_estimate=cost(name),
        name=name,
    )(*values)


def turn_of(slots):
    return math.gcd(slots, 8)


def product_loop(count, source_ids, target_ids, adj, source, total, dims):
    turn = turn_of(adj.shape[0])
    total[...] = jnp.zeros_like(total)

    def step(index, carry):
        first = index * turn
        products = []
        for k in range(turn):
            operand = source[source_ids[first + k]]
            products.append(
                lax.dot_general(operand, adj[first + k], dims, preferred_element_type=jnp.float32)
            )
        for k in range(turn):
            target = target_ids[first + k]
            live = first + k < count
            total[target] += jnp.where(live, products[k], 0.0)
        return carry

    lax.fori_loop(0, (count + turn - 1) // turn, step, 0)


def fetch_kernel(count, rows, cols, tile, *refs):
    outs, (sem, ids_sem) = refs[:3], refs[3:]
    ids = [
        pltpu.make_async_copy(source, target, ids_sem.at[n])
        for n, (source, target) in enumerate(zip((rows, cols), outs))
    ]
    for copy in ids:
        copy.start()
    turn = turn_of(tile.shape[0])

    def copy_turn(index):
        blocks = pl.ds(index * turn, turn)
        return pltpu.make_async_copy(tile.at[blocks], outs[2].at[blocks], sem.at[index])

    def begin(index, carry):
        copy_turn(index).start()
        return carry

    def finish(index, carry):
        copy_turn(index).wait()
        return carry

    turns = (count[0, 0] + turn - 1) // turn
    lax.fori_loop(0, turns, begin, 0)
    lax.fori_loop(0, turns, finish, 0)
    for copy in ids:
        copy.wait()


def fetch(count, *arrays):
    blocks = arrays[2].shape[0]
    return pl.pallas_call(
        fetch_kernel,
        out_shape=[jax.ShapeDtypeStruct(array.shape, array.dtype) for array in arrays],
        in_specs=[SMEM] + [HBM] * len(arrays),
        out_specs=[VMEM] * len(arrays),
        scratch_shapes=[
            pltpu.SemaphoreType.DMA((blocks // turn_of(blocks),)),
            pltpu.SemaphoreType.DMA((2,)),
        ],
        compiler_params=params(4),
        cost_estimate=cost("fetch"),
        name="fetch",
    )(count, *[pltpu.with_memory_space_constraint(array, pltpu.HBM) for array in arrays])


def forward_kernel(n_parts, layout, place, count, rows, cols, adj, *refs):
    parts = refs[:n_parts]
    outs = refs[n_parts:-2]
    source, total = refs[-2:]
    size = adj.shape[1]
    row = 0
    for part in parts:
        depth = part.shape[0]
        for c in range(source.shape[0]):
            source[c, row : row + depth, :] = part[:, c * size : (c + 1) * size]
        row += depth
    product_loop(count[0, 0], cols, rows, adj, source, total, NT)
    depth = total.shape[1]
    blocks = outs[0].shape[1] // size
    for out, chunks in zip(outs, layout):
        for n, k in enumerate(chunks):
            first = (place[0] ^ k) * blocks
            for i in range(blocks):
                out[n * depth : (n + 1) * depth, i * size : (i + 1) * size] = total[first + i].astype(
                    out.dtype
                )


def forward(place, count, rows, cols, adj, parts, row_blocks, layout):
    size = adj.shape[1]
    depth = sum(part.shape[0] for part in parts)
    col_blocks = parts[0].shape[1] // size
    wide = row_blocks * size // sum(len(chunks) for chunks in layout)
    outs = [jax.ShapeDtypeStruct((len(chunks) * depth, wide), jnp.bfloat16) for chunks in layout]
    return pl.pallas_call(
        functools.partial(forward_kernel, len(parts), layout),
        out_shape=outs,
        in_specs=[SMEM] * 4 + [VMEM] * (1 + len(parts)),
        out_specs=[VMEM] * len(outs),
        scratch_shapes=[
            pltpu.VMEM((col_blocks, depth, size), jnp.bfloat16),
            pltpu.VMEM((row_blocks, depth, size), jnp.float32),
        ],
        compiler_params=params(14),
        cost_estimate=cost("forward_products"),
        name="forward_products",
    )(place, count, rows, cols, adj, *parts)


def backward_kernel(spots, place, count, rows, cols, adj, *refs):
    n_parts = 1 + max(part for part, _ in spots)
    parts = refs[:n_parts]
    outs = refs[n_parts:-2]
    source, total = refs[-2:]
    size = adj.shape[1]
    depth = source.shape[1]
    blocks = parts[0].shape[1] // size
    for k, (part, row) in enumerate(spots):
        first = (place[0] ^ k) * blocks
        for i in range(blocks):
            source[first + i] = parts[part][row : row + depth, i * size : (i + 1) * size]
    product_loop(count[0, 0], rows, cols, adj, source, total, NN)
    row = 0
    for out in outs:
        depth = out.shape[0]
        for c in range(total.shape[0]):
            out[:, c * size : (c + 1) * size] = total[c, row : row + depth, :].astype(out.dtype)
        row += depth


def backward(place, count, rows, cols, adj, parts, spots, out_depths, col_blocks):
    size = adj.shape[1]
    row_blocks = len(spots) * parts[0].shape[1] // size
    return pl.pallas_call(
        functools.partial(backward_kernel, spots),
        out_shape=[jax.ShapeDtypeStruct((depth, col_blocks * size), jnp.bfloat16) for depth in out_depths],
        in_specs=[SMEM] * 4 + [VMEM] * (1 + len(parts)),
        out_specs=[VMEM] * len(out_depths),
        scratch_shapes=[
            pltpu.VMEM((row_blocks, sum(out_depths), size), jnp.bfloat16),
            pltpu.VMEM((col_blocks, sum(out_depths), size), jnp.float32),
        ],
        compiler_params=params(14),
        cost_estimate=cost("backward_products"),
        name="backward_products",
    )(place, count, rows, cols, adj, *parts)


def middle_kernel(sizes, order, n_sum, n_row, row, weight, cotangent, *refs):
    terms = refs[: n_sum * len(sizes)]
    outs = refs[n_sum * len(sizes) : -1]
    output, deltas, aggregated, *backs = outs
    ordered = refs[-1]
    depth = weight.shape[0] // n_row
    for j in range(n_row):
        first = pl.multiple_of((row[0] ^ j) * depth, depth)
        ordered[j * depth : (j + 1) * depth, :] = weight[pl.ds(first, depth), :]
    first = 0
    for p, size in enumerate(sizes):
        summed = terms[p * n_sum][:size, :].astype(jnp.float32)
        for k in range(1, n_sum):
            summed += terms[p * n_sum + k][:size, :].astype(jnp.float32)
        aggregated[first : first + size, :] = summed.astype(jnp.bfloat16)
        first += size
    nodes_first = aggregated[...].T
    preact = jnp.dot(nodes_first, ordered[...], preferred_element_type=jnp.float32)
    gate = jax.nn.sigmoid(preact)
    output[...] = (preact * gate).astype(jnp.bfloat16)
    slopes = gate * (1.0 + preact * (1.0 - gate))
    delta = (cotangent[...].astype(jnp.float32) * slopes).astype(jnp.bfloat16)
    deltas[...] = delta
    product = lax.dot_general(ordered[...], delta, NT, preferred_element_type=jnp.float32)
    for back, chunks in zip(backs, order):
        for n, k in enumerate(chunks):
            back[n * depth : (n + 1) * depth, :] = product[k * depth : (k + 1) * depth, :].astype(jnp.bfloat16)


def middle(n_row, row, weight, cotangent, pieces, order):
    sizes = [piece[0].shape[0] for piece in pieces]
    nodes = cotangent.shape[0]
    features = weight.shape[0]
    shape = jax.ShapeDtypeStruct
    outs = [
        shape((nodes, features), jnp.bfloat16),
        shape((nodes, features), jnp.bfloat16),
        shape((features, nodes), jnp.bfloat16),
    ] + [shape((len(chunks) * features // n_row, nodes), jnp.bfloat16) for chunks in order]
    flat = [term for piece in pieces for term in piece]
    return pl.pallas_call(
        functools.partial(middle_kernel, sizes, order, len(pieces[0]), n_row),
        out_shape=outs,
        in_specs=[SMEM] + [VMEM] * (2 + len(flat)),
        out_specs=[VMEM] * len(outs),
        scratch_shapes=[pltpu.VMEM(weight.shape, jnp.bfloat16)],
        compiler_params=params(10),
        cost_estimate=cost("layer"),
        name="layer",
    )(row, weight, cotangent, *flat)


def gradient_kernel(scale, order, aggregated, deltas, *outs):
    product = jnp.dot(aggregated[...], deltas[...], preferred_element_type=jnp.float32) * scale
    for out, chunks in zip(outs, order):
        depth = out.shape[1]
        for n, k in enumerate(chunks):
            out[n] = product[k * depth : (k + 1) * depth, :]


def gradient(scale, order, aggregated, deltas):
    depth = aggregated.shape[0] // sum(len(chunks) for chunks in order)
    outs = [jax.ShapeDtypeStruct((len(chunks), depth, deltas.shape[1]), jnp.float32) for chunks in order]
    return pl.pallas_call(
        functools.partial(gradient_kernel, scale, order),
        out_shape=outs,
        in_specs=[VMEM] * 2,
        out_specs=[VMEM] * len(outs),
        compiler_params=params(6),
        cost_estimate=cost("weight_gradient"),
        name="weight_gradient",
    )(aggregated, deltas)


def place_kernel(order, row, *refs):
    out = refs[-1]
    for ref, chunks in zip(refs[:-1], order):
        depth = ref.shape[1]
        for n, k in enumerate(chunks):
            first = pl.multiple_of((row[0] ^ k) * depth, depth)
            out[pl.ds(first, depth), :] = ref[n]


def place_rows(row, order, parts):
    _, depth, wide = parts[0].shape
    chunks = sum(part.shape[0] for part in parts)
    return pl.pallas_call(
        functools.partial(place_kernel, order),
        out_shape=jax.ShapeDtypeStruct((chunks * depth, wide), jnp.float32),
        in_specs=[SMEM] + [VMEM] * len(parts),
        out_specs=VMEM,
        compiler_params=params(4),
        cost_estimate=cost("place_rows"),
        name="place_rows",
    )(row, *parts)


def swap(value, axis, k):
    size = lax.axis_size(axis)
    return lax.ppermute(value, axis, [(i, i ^ k) for i in range(size)])


def wide_sum(*values):
    total = values[0].astype(jnp.float32)
    for value in values[1:]:
        total = total + value.astype(jnp.float32)
    return (total.astype(values[0].dtype),)


def after(value, *earlier):
    return lax.optimization_barrier((value, *earlier))[0]


def join(*values):
    return (jnp.stack(values),)


def with_chunk(mine, other, *parts):
    total = functools.reduce(jnp.add, parts)
    high = total.astype(jnp.bfloat16)
    low = (total - high.astype(jnp.float32)).astype(jnp.bfloat16)
    return (jnp.concatenate([mine, other, jnp.concatenate([high, low], axis=1)]),)


def chunk_sum(depth, *values):
    total = None
    for value in values:
        halves = value[-depth:].astype(jnp.float32)
        wide = halves.shape[1] // 2
        chunk = halves[:, :wide] + halves[:, wide:]
        total = chunk if total is None else total + chunk
    return (total,)


def pair_sum(mine, *received):
    return tuple(mine + jnp.concatenate(received))


def pair_sum_rows(depth, mine, *received):
    total = mine.astype(jnp.float32) + jnp.concatenate(received).astype(jnp.float32)
    return tuple(
        total[first : first + depth].astype(mine.dtype) for first in range(0, total.shape[0], depth)
    )


def shards_exchanged(features, weight, adj_values, block_rows, block_cols, block_counts, cotangent):
    n_row = lax.axis_size("row")
    n_col = lax.axis_size("col")
    adj = adj_values[0, 0]
    rows = block_rows[0, 0]
    cols = block_cols[0, 0]
    count = block_counts
    size = adj.shape[1]
    nodes = cotangent.shape[0] * n_row * n_col
    row_blocks = cotangent.shape[0] * n_col // size
    col_blocks = features.shape[0] // size
    row = lax.axis_index("row").reshape(1)
    col = lax.axis_index("col").reshape(1)
    own = after(features.T, row, col)

    depth = features.shape[1]
    near = [k for k in range(2, n_row, 2) if k & (k - 1) == 0]
    far = [k for k in range(2, n_row, 2) if k & (k - 1) != 0]
    sibling = swap(own, "row", 1)
    from_near = [swap(own, "row", k) for k in near]
    rows, cols, tile = fetch(count, rows, cols, adj)
    from_near = [after(part, tile) for part in from_near]
    from_far = [swap(after(own, *from_near), "row", k) for k in far]

    def pass_on(beyond, received):
        return wide_sum(beyond, received[beyond.shape[0] :])

    def forward_piece(parts, whole):
        parts = parts + [piece for part in whole for piece in (part, swap(part, "row", 1))]
        kept, beyond, sent = forward(col, count, rows, cols, tile, parts, row_blocks, [(0,), (2,), (1, 3)])
        return kept, beyond, swap(sent, "col", 1)

    def fold(kept, beyond, received):
        (passed,) = fuse("pass_on", pass_on, beyond, received)
        return [kept, received, swap(passed, "col", 2)]

    piece = forward_piece([own, sibling], from_near)
    far_piece = forward_piece([], [after(part, *piece[:2]) for part in from_far])
    first = fold(*piece[:2], after(piece[2], *far_piece[:2]))
    second = fold(*far_piece[:2], after(far_piece[2], first[1]))

    evens = tuple(range(0, n_row, 2))
    odds = tuple(range(1, n_row, 2))
    output, deltas, aggregated, back = middle(
        n_row, row, weight, cotangent, [first, second], [evens + odds]
    )
    beyond = swap(back, "col", 2)

    even, *odd = gradient(1.0 / math.sqrt(nodes), [evens, odds[:2], odds[2:]], aggregated, deltas)
    chunk, *sent = fuse("gradient_sum", pair_sum, even, *[swap(part, "row", 1) for part in odd])
    from_rows = [swap(part, "row", k) for part, k in zip(sent, evens[1:])]
    (whole,) = fuse("with_chunk", with_chunk, back, beyond, chunk, *from_rows)
    received = swap(whole, "col", 1)
    (chunk,) = fuse("chunk_sum", functools.partial(chunk_sum, depth), whole, received)
    other = swap(chunk, "col", 2)

    features_all = back.shape[0]
    mine, *sent = backward(
        col,
        count,
        rows,
        cols,
        tile,
        [back, after(received, chunk), beyond],
        [(0, 0), (1, 0), (2, 0), (1, features_all)],
        [features_all // 2] + [features_all // 4] * 2,
        col_blocks,
    )
    from_sibling = [swap(part, "row", 1) for part in sent]
    (chunk,) = fuse("chunk_sum", wide_sum, chunk, after(other, mine))
    from_rows = [swap(chunk, "row", k) for k in evens[1:]]
    from_sibling[0] = after(from_sibling[0], *from_rows)
    terms = fuse("pair_sum", functools.partial(pair_sum_rows, depth), mine, *from_sibling)
    collected = [terms[0]] + [swap(term, "row", k) for term, k in zip(terms[1:], evens[1:])]
    (even,) = fuse("gradient_join", join, chunk, *from_rows)
    grad_weight = place_rows(row, [evens, odds], [even, swap(even, "row", 1)])
    (grad_features,) = fuse("feature_sum", wide_sum, *collected)
    return output, grad_weight, grad_features.T


def shards_gathered(features, weight, adj_values, block_rows, block_cols, block_counts, cotangent):
    n_row = lax.axis_size("row")
    n_col = lax.axis_size("col")
    adj = adj_values[0, 0]
    rows = block_rows[0, 0]
    cols = block_cols[0, 0]
    count = block_counts
    size = adj.shape[1]
    nodes = cotangent.shape[0] * n_row * n_col
    row_blocks = cotangent.shape[0] * n_col // size
    col_blocks = features.shape[0] // size
    zero = jnp.zeros((1,), jnp.int32)
    panels = lax.all_gather(features.T, "row", axis=0, tiled=True)
    (terms,) = forward(zero, count, rows, cols, adj, [panels], row_blocks, [(0,)])
    part = lax.psum_scatter(terms, "col", scatter_dimension=1, tiled=True)
    output, deltas, aggregated, back = middle(1, zero, weight, cotangent, [[part]], [(0,)])
    slab = lax.all_gather(back, "col", axis=1, tiled=True)
    (column_terms,) = backward(zero, count, rows, cols, adj, [slab], [(0, 0)], [slab.shape[0]], col_blocks)
    grad_features = lax.psum_scatter(column_terms, "row", scatter_dimension=0, tiled=True).T
    (part,) = gradient(1.0 / math.sqrt(nodes), [(0,)], aggregated, deltas)
    grad_weight = lax.psum(part[0], ("row", "col"))
    return output, grad_weight, grad_features


def solution(mesh):
    n_row = mesh.shape["row"]
    n_col = mesh.shape["col"]
    exchanged = n_row == 8 and n_col == 4
    return jax.shard_map(
        shards_exchanged if exchanged else shards_gathered,
        mesh=mesh,
        in_specs=(
            P("col", "row"),
            P(),
            P("row", "col", None, None, None),
            P("row", "col", None),
            P("row", "col", None),
            P("row", "col"),
            P(("row", "col"), None),
        ),
        out_specs=(P(("row", "col"), None), P(), P("col", "row")),
        check_vma=False,
    )
```

```python
import functools
import math

import jax
import jax.numpy as jnp
from jax import lax
from jax.experimental import pallas as pl
from jax.experimental.pallas import tpu as pltpu
from jax.sharding import PartitionSpec as P

VMEM = pl.BlockSpec(memory_space=pltpu.VMEM)
SMEM = pl.BlockSpec(memory_space=pltpu.SMEM)
HBM = pl.BlockSpec(memory_space=pltpu.HBM)
MIB = 1024 * 1024
NT = (((1,), (1,)), ((), ()))
NN = (((1,), (0,)), ((), ()))


COSTS = {"fetch": 1e9, "forward_products": 1e9, "backward_products": 1e9}


def cost(name):
    return pl.CostEstimate(flops=int(COSTS.get(name, 1)), bytes_accessed=1, transcendentals=0)


def params(mib):
    return pltpu.CompilerParams(vmem_limit_bytes=mib * MIB)


def fuse(name, function, *values):
    shapes = jax.eval_shape(function, *values)

    def kernel(*refs):
        results = function(*[ref[...] for ref in refs[: len(values)]])
        for ref, result in zip(refs[len(values) :], results):
            ref[...] = result

    return pl.pallas_call(
        kernel,
        out_shape=shapes,
        in_specs=[VMEM] * len(values),
        out_specs=[VMEM] * len(shapes),
        compiler_params=params(4),
        cost_estimate=cost(name),
        name=name,
    )(*values)


def turn_of(slots):
    return math.gcd(slots, 8)


def product_loop(count, source_ids, target_ids, adj, source, total, dims):
    turn = turn_of(adj.shape[0])
    spare = total.shape[0] - 1
    total[...] = jnp.zeros_like(total)

    def step(index, carry):
        first = index * turn
        for k in range(turn):
            slot = first + k
            product = lax.dot_general(
                source[source_ids[slot]], adj[slot], dims, preferred_element_type=jnp.float32
            )
            target = jnp.where(slot < count, target_ids[slot], spare)
            total[target] += product
        return carry

    lax.fori_loop(0, (count + turn - 1) // turn, step, 0)


def fetch_kernel(count, rows, cols, tile, *refs):
    outs, (sem, ids_sem) = refs[:3], refs[3:]
    ids = [
        pltpu.make_async_copy(source, target, ids_sem.at[n])
        for n, (source, target) in enumerate(zip((rows, cols), outs))
    ]
    for copy in ids:
        copy.start()
    turn = turn_of(tile.shape[0])

    def copy_turn(index):
        blocks = pl.ds(index * turn, turn)
        return pltpu.make_async_copy(tile.at[blocks], outs[2].at[blocks], sem.at[index])

    def begin(index, carry):
        copy_turn(index).start()
        return carry

    def finish(index, carry):
        copy_turn(index).wait()
        return carry

    turns = (count[0, 0] + turn - 1) // turn
    lax.fori_loop(0, turns, begin, 0)
    lax.fori_loop(0, turns, finish, 0)
    for copy in ids:
        copy.wait()


def fetch(count, *arrays):
    blocks = arrays[2].shape[0]
    return pl.pallas_call(
        fetch_kernel,
        out_shape=[jax.ShapeDtypeStruct(array.shape, array.dtype) for array in arrays],
        in_specs=[SMEM] + [HBM] * len(arrays),
        out_specs=[VMEM] * len(arrays),
        scratch_shapes=[
            pltpu.SemaphoreType.DMA((blocks // turn_of(blocks),)),
            pltpu.SemaphoreType.DMA((2,)),
        ],
        compiler_params=params(4),
        cost_estimate=cost("fetch"),
        name="fetch",
    )(count, *[pltpu.with_memory_space_constraint(array, pltpu.HBM) for array in arrays])


def forward_kernel(n_parts, depths, layout, place, count, rows, cols, adj, *refs):
    parts = refs[:n_parts]
    outs = refs[n_parts:-2]
    source, total = refs[-2:]
    size = adj.shape[1]
    row = 0
    for part in parts:
        depth = part.shape[0]
        for c in range(source.shape[0]):
            source[c, row : row + depth, :] = part[:, c * size : (c + 1) * size]
        row += depth
    product_loop(count[0, 0], cols, rows, adj, source, total, NT)
    blocks = outs[0].shape[1] // size
    outs = iter(outs)
    row = 0
    for depth in depths:
        for chunks in layout:
            out = next(outs)
            for n, k in enumerate(chunks):
                first = (place[0] ^ k) * blocks
                for i in range(blocks):
                    out[n * depth : (n + 1) * depth, i * size : (i + 1) * size] = total[
                        first + i, row : row + depth, :
                    ].astype(out.dtype)
        row += depth


def forward(place, count, rows, cols, adj, parts, row_blocks, depths, layout):
    size = adj.shape[1]
    col_blocks = parts[0].shape[1] // size
    wide = row_blocks * size // sum(len(chunks) for chunks in layout)
    outs = [
        jax.ShapeDtypeStruct((len(chunks) * depth, wide), jnp.bfloat16)
        for depth in depths
        for chunks in layout
    ]
    return pl.pallas_call(
        functools.partial(forward_kernel, len(parts), depths, layout),
        out_shape=outs,
        in_specs=[SMEM] * 4 + [VMEM] * (1 + len(parts)),
        out_specs=[VMEM] * len(outs),
        scratch_shapes=[
            pltpu.VMEM((col_blocks, sum(depths), size), jnp.bfloat16),
            pltpu.VMEM((row_blocks + 1, sum(depths), size), jnp.float32),
        ],
        compiler_params=params(14),
        cost_estimate=cost("forward_products"),
        name="forward_products",
    )(place, count, rows, cols, adj, *parts)


def backward_kernel(spots, depths, place, count, rows, cols, adj, *refs):
    n_parts = 1 + max(part for places in spots for part, _ in places)
    parts = refs[:n_parts]
    outs = refs[n_parts:-2]
    source, total = refs[-2:]
    size = adj.shape[1]
    blocks = parts[0].shape[1] // size
    for k, places in enumerate(spots):
        first = (place[0] ^ k) * blocks
        row = 0
        for (part, offset), depth in zip(places, depths):
            for i in range(blocks):
                source[first + i, row : row + depth, :] = parts[part][
                    offset : offset + depth, i * size : (i + 1) * size
                ]
            row += depth
    product_loop(count[0, 0], rows, cols, adj, source, total, NN)
    row = 0
    for out in outs:
        depth = out.shape[0]
        for c in range(total.shape[0] - 1):
            out[:, c * size : (c + 1) * size] = total[c, row : row + depth, :].astype(out.dtype)
        row += depth


def backward(place, count, rows, cols, adj, parts, spots, depths, out_depths, col_blocks):
    size = adj.shape[1]
    row_blocks = len(spots) * parts[0].shape[1] // size
    return pl.pallas_call(
        functools.partial(backward_kernel, spots, depths),
        out_shape=[jax.ShapeDtypeStruct((depth, col_blocks * size), jnp.bfloat16) for depth in out_depths],
        in_specs=[SMEM] * 4 + [VMEM] * (1 + len(parts)),
        out_specs=[VMEM] * len(out_depths),
        scratch_shapes=[
            pltpu.VMEM((row_blocks, sum(out_depths), size), jnp.bfloat16),
            pltpu.VMEM((col_blocks + 1, sum(out_depths), size), jnp.float32),
        ],
        compiler_params=params(14),
        cost_estimate=cost("backward_products"),
        name="backward_products",
    )(place, count, rows, cols, adj, *parts)


def middle_kernel(sizes, order, n_sum, n_row, row, weight, cotangent, *refs):
    terms = refs[: n_sum * len(sizes)]
    outs = refs[n_sum * len(sizes) : -1]
    output, deltas, aggregated, *backs = outs
    ordered = refs[-1]
    depth = weight.shape[0] // n_row
    for j in range(n_row):
        first = pl.multiple_of((row[0] ^ j) * depth, depth)
        ordered[j * depth : (j + 1) * depth, :] = weight[pl.ds(first, depth), :]
    first = 0
    for p, size in enumerate(sizes):
        summed = terms[p * n_sum][:size, :].astype(jnp.float32)
        for k in range(1, n_sum):
            summed += terms[p * n_sum + k][:size, :].astype(jnp.float32)
        aggregated[first : first + size, :] = summed.astype(jnp.bfloat16)
        first += size
    nodes_first = aggregated[...].T
    preact = jnp.dot(nodes_first, ordered[...], preferred_element_type=jnp.float32)
    gate = jax.nn.sigmoid(preact)
    output[...] = (preact * gate).astype(jnp.bfloat16)
    slopes = gate * (1.0 + preact * (1.0 - gate))
    delta = (cotangent[...].astype(jnp.float32) * slopes).astype(jnp.bfloat16)
    deltas[...] = delta
    product = lax.dot_general(ordered[...], delta, NT, preferred_element_type=jnp.float32)
    product = product.astype(jnp.bfloat16)
    rows = [product[k * depth : (k + 1) * depth, :] for k in order]
    product = jnp.concatenate(rows)
    first = 0
    for back in backs:
        back[...] = product[first : first + back.shape[0], :]
        first += back.shape[0]


def middle(n_row, row, weight, cotangent, pieces, order, depths):
    sizes = [piece[0].shape[0] for piece in pieces]
    nodes = cotangent.shape[0]
    features = weight.shape[0]
    shape = jax.ShapeDtypeStruct
    outs = [
        shape((nodes, features), jnp.bfloat16),
        shape((nodes, features), jnp.bfloat16),
        shape((features, nodes), jnp.bfloat16),
    ] + [shape((depth, nodes), jnp.bfloat16) for depth in depths]
    flat = [term for piece in pieces for term in piece]
    return pl.pallas_call(
        functools.partial(middle_kernel, sizes, order, len(pieces[0]), n_row),
        out_shape=outs,
        in_specs=[SMEM] + [VMEM] * (2 + len(flat)),
        out_specs=[VMEM] * len(outs),
        scratch_shapes=[pltpu.VMEM(weight.shape, jnp.bfloat16)],
        compiler_params=params(10),
        cost_estimate=cost("layer"),
        name="layer",
    )(row, weight, cotangent, *flat)


def gradient_kernel(scale, order, aggregated, deltas, *outs):
    product = jnp.dot(aggregated[...], deltas[...], preferred_element_type=jnp.float32) * scale
    for out, chunks in zip(outs, order):
        depth = out.shape[1]
        for n, k in enumerate(chunks):
            out[n] = product[k * depth : (k + 1) * depth, :]


def gradient(scale, order, aggregated, deltas):
    depth = aggregated.shape[0] // sum(len(chunks) for chunks in order)
    outs = [jax.ShapeDtypeStruct((len(chunks), depth, deltas.shape[1]), jnp.float32) for chunks in order]
    return pl.pallas_call(
        functools.partial(gradient_kernel, scale, order),
        out_shape=outs,
        in_specs=[VMEM] * 2,
        out_specs=[VMEM] * len(outs),
        compiler_params=params(6),
        cost_estimate=cost("weight_gradient"),
        name="weight_gradient",
    )(aggregated, deltas)


def place_kernel(order, row, *refs):
    out = refs[-1]
    for ref, chunks in zip(refs[:-1], order):
        depth = ref.shape[1]
        for n, k in enumerate(chunks):
            first = pl.multiple_of((row[0] ^ k) * depth, depth)
            out[pl.ds(first, depth), :] = ref[n]


def place_rows(row, order, parts):
    _, depth, wide = parts[0].shape
    chunks = sum(part.shape[0] for part in parts)
    return pl.pallas_call(
        functools.partial(place_kernel, order),
        out_shape=jax.ShapeDtypeStruct((chunks * depth, wide), jnp.float32),
        in_specs=[SMEM] + [VMEM] * len(parts),
        out_specs=VMEM,
        compiler_params=params(4),
        cost_estimate=cost("place_rows"),
        name="place_rows",
    )(row, *parts)


def swap(value, axis, k):
    size = lax.axis_size(axis)
    return lax.ppermute(value, axis, [(i, i ^ k) for i in range(size)])


def wide_sum(*values):
    total = values[0].astype(jnp.float32)
    for value in values[1:]:
        total = total + value.astype(jnp.float32)
    return (total.astype(values[0].dtype),)


def after(value, *earlier):
    return lax.optimization_barrier((value, *earlier))[0]


def stack(*values):
    return (jnp.concatenate(values),)


def join(*values):
    return (jnp.stack(values),)


def with_chunk(mine, other, *parts):
    total = functools.reduce(jnp.add, parts)
    high = total.astype(jnp.bfloat16)
    low = (total - high.astype(jnp.float32)).astype(jnp.bfloat16)
    return (jnp.concatenate([mine, other, jnp.concatenate([high, low], axis=1)]),)


def chunk_sum(depth, *values):
    total = None
    for value in values:
        halves = value[-depth:].astype(jnp.float32)
        wide = halves.shape[1] // 2
        chunk = halves[:, :wide] + halves[:, wide:]
        total = chunk if total is None else total + chunk
    return (total,)


def pair_sum(mine, *received):
    return tuple(mine + jnp.concatenate(received))


def pair_sum_rows(depth, mine, *received):
    total = mine.astype(jnp.float32) + jnp.concatenate(received).astype(jnp.float32)
    return tuple(
        total[first : first + depth].astype(mine.dtype) for first in range(0, total.shape[0], depth)
    )


def shards_exchanged(features, weight, adj_values, block_rows, block_cols, block_counts, cotangent):
    n_row = lax.axis_size("row")
    n_col = lax.axis_size("col")
    adj = adj_values[0, 0]
    rows = block_rows[0, 0]
    cols = block_cols[0, 0]
    count = block_counts
    size = adj.shape[1]
    nodes = cotangent.shape[0] * n_row * n_col
    row_blocks = cotangent.shape[0] * n_col // size
    col_blocks = features.shape[0] // size
    row = lax.axis_index("row").reshape(1)
    col = lax.axis_index("col").reshape(1)
    own = after(features.T, row, col)

    depth = features.shape[1]
    near = [k for k in range(2, n_row, 2) if k & (k - 1) == 0]
    far = [k for k in range(2, n_row, 2) if k & (k - 1) != 0]
    sibling = swap(own, "row", 1)
    from_near = [swap(own, "row", k) for k in near]
    rows, cols, tile = fetch(count, rows, cols, adj)
    from_near = [after(part, tile) for part in from_near]
    from_far = [swap(after(own, *from_near), "row", k) for k in far]

    def pass_on(beyond, received):
        return wide_sum(beyond, received[beyond.shape[0] :])

    def forward_pieces(parts, whole, depths):
        parts = parts + [piece for part in whole for piece in (part, swap(part, "row", 1))]
        outs = forward(col, count, rows, cols, tile, parts, row_blocks, depths, [(0,), (2,), (1, 3)])
        outs = [outs[n : n + 3] for n in range(0, len(outs), 3)]
        return [(kept, beyond, swap(sent, "col", 1)) for kept, beyond, sent in outs]

    def fold(piece, *earlier):
        kept, beyond, received = piece
        received = after(received, *earlier)
        (passed,) = fuse("pass_on", pass_on, beyond, received)
        return [kept, received, swap(passed, "col", 2)]

    n_near = 2 * depth * (1 + len(near))
    cut = n_near // 2 + 16
    pieces = forward_pieces([own, sibling], from_near, [cut, n_near - cut])
    from_far = [after(part, pieces[0][0]) for part in from_far]
    pieces += forward_pieces([], from_far, [2 * depth * len(far)])
    sums = []
    for piece in pieces:
        sums.append(fold(piece, *(sums[-1][1:2] if sums else ())))

    evens = tuple(range(0, n_row, 2))
    odds = tuple(range(1, n_row, 2))
    n_all = weight.shape[0]
    cut = n_all // 2 + 32
    cuts = [cut, n_all - cut]
    output, deltas, aggregated, *backs = middle(n_row, row, weight, cotangent, sums, evens + odds, cuts)
    beyond = [swap(back, "col", 2) for back in backs]

    even, *odd = gradient(1.0 / math.sqrt(nodes), [evens, odds[:2], odds[2:]], aggregated, deltas)
    chunk, *sent = fuse("gradient_sum", pair_sum, even, *[swap(part, "row", 1) for part in odd])
    from_rows = [swap(part, "row", k) for part, k in zip(sent, evens[1:])]
    (chunk,) = fuse("chunk_sum", wide_sum, chunk, *from_rows)
    chunks = [chunk, swap(chunk, "col", 2)]

    (large,) = fuse("stack", stack, backs[0], after(beyond[0], chunk))
    (small,) = fuse("with_chunk", with_chunk, backs[1], after(beyond[1], large), *chunks)
    large_received, small_received = swap(large, "col", 1), swap(small, "col", 1)
    (chunk,) = fuse("chunk_sum", functools.partial(chunk_sum, depth), small, small_received)

    mine, *sent = backward(
        col,
        count,
        rows,
        cols,
        tile,
        [*backs, *beyond, after(large_received, chunk), small_received],
        [[(0, 0), (1, 0)], [(4, 0), (5, 0)], [(2, 0), (3, 0)], [(4, cuts[0]), (5, cuts[1])]],
        cuts,
        [n_all // 2] + [n_all // 4] * 2,
        col_blocks,
    )
    from_sibling = [swap(part, "row", 1) for part in sent]
    from_rows = [swap(chunk, "row", k) for k in evens[1:]]
    from_sibling[0] = after(from_sibling[0], *from_rows)
    terms = fuse("pair_sum", functools.partial(pair_sum_rows, depth), mine, *from_sibling)
    collected = [terms[0]] + [swap(term, "row", k) for term, k in zip(terms[1:], evens[1:])]
    (even,) = fuse("gradient_join", join, chunk, *from_rows)
    grad_weight = place_rows(row, [evens, odds], [even, swap(even, "row", 1)])
    (grad_features,) = fuse("feature_sum", wide_sum, *collected)
    return output, grad_weight, grad_features.T


def shards_gathered(features, weight, adj_values, block_rows, block_cols, block_counts, cotangent):
    n_row = lax.axis_size("row")
    n_col = lax.axis_size("col")
    adj = adj_values[0, 0]
    rows = block_rows[0, 0]
    cols = block_cols[0, 0]
    count = block_counts
    size = adj.shape[1]
    nodes = cotangent.shape[0] * n_row * n_col
    row_blocks = cotangent.shape[0] * n_col // size
    col_blocks = features.shape[0] // size
    zero = jnp.zeros((1,), jnp.int32)
    panels = lax.all_gather(features.T, "row", axis=0, tiled=True)
    (terms,) = forward(zero, count, rows, cols, adj, [panels], row_blocks, [panels.shape[0]], [(0,)])
    part = lax.psum_scatter(terms, "col", scatter_dimension=1, tiled=True)
    output, deltas, aggregated, back = middle(1, zero, weight, cotangent, [[part]], (0,), [weight.shape[0]])
    slab = lax.all_gather(back, "col", axis=1, tiled=True)
    (column_terms,) = backward(zero, count, rows, cols, adj, [slab], [[(0, 0)]], [slab.shape[0]], [slab.shape[0]], col_blocks)
    grad_features = lax.psum_scatter(column_terms, "row", scatter_dimension=0, tiled=True).T
    (part,) = gradient(1.0 / math.sqrt(nodes), [(0,)], aggregated, deltas)
    grad_weight = lax.psum(part[0], ("row", "col"))
    return output, grad_weight, grad_features


def solution(mesh):
    n_row = mesh.shape["row"]
    n_col = mesh.shape["col"]
    exchanged = n_row == 8 and n_col == 4
    return jax.shard_map(
        shards_exchanged if exchanged else shards_gathered,
        mesh=mesh,
        in_specs=(
            P("col", "row"),
            P(),
            P("row", "col", None, None, None),
            P("row", "col", None),
            P("row", "col", None),
            P("row", "col"),
            P(("row", "col"), None),
        ),
        out_specs=(P(("row", "col"), None), P(), P("col", "row")),
        check_vma=False,
    )
```

```python
import functools
import math

import jax
import jax.numpy as jnp
from jax import lax
from jax.experimental import pallas as pl
from jax.experimental.pallas import tpu as pltpu
from jax.sharding import PartitionSpec as P

VMEM = pl.BlockSpec(memory_space=pltpu.VMEM)
SMEM = pl.BlockSpec(memory_space=pltpu.SMEM)
HBM = pl.BlockSpec(memory_space=pltpu.HBM)
MIB = 1024 * 1024
NT = (((1,), (1,)), ((), ()))
NN = (((1,), (0,)), ((), ()))


COST = pl.CostEstimate(flops=1, bytes_accessed=1, transcendentals=0)


def params(mib):
    return pltpu.CompilerParams(vmem_limit_bytes=mib * MIB)


def fuse(name, function, *values):
    shapes = jax.eval_shape(function, *values)

    def kernel(*refs):
        results = function(*[ref[...] for ref in refs[: len(values)]])
        for ref, result in zip(refs[len(values) :], results):
            ref[...] = result

    return pl.pallas_call(
        kernel,
        out_shape=shapes,
        in_specs=[VMEM] * len(values),
        out_specs=[VMEM] * len(shapes),
        compiler_params=params(4),
        cost_estimate=COST,
        name=name,
    )(*values)


def turn_of(slots):
    return math.gcd(slots, 8)


def product_loop(count, source_ids, target_ids, adj, source, total, dims):
    turn = turn_of(adj.shape[0])
    spare = total.shape[0] - 1
    total[...] = jnp.zeros_like(total)

    def step(index, carry):
        first = index * turn
        for k in range(turn):
            slot = first + k
            product = lax.dot_general(
                source[source_ids[slot]], adj[slot], dims, preferred_element_type=jnp.float32
            )
            target = jnp.where(slot < count, target_ids[slot], spare)
            total[target] += product
        return carry

    lax.fori_loop(0, (count + turn - 1) // turn, step, 0)


def fetch_kernel(count, rows, cols, features, tile, *refs):
    outs, (sem, small_sem) = refs[:5], refs[5:]
    half = features.shape[0] // 2
    sources = (rows, cols, features.at[pl.ds(0, half)], features.at[pl.ds(half, half)])
    small = [
        pltpu.make_async_copy(source, target, small_sem.at[n])
        for n, (source, target) in enumerate(zip(sources, outs))
    ]
    for copy in small:
        copy.start()
    turn = turn_of(tile.shape[0])

    def copy_turn(index):
        blocks = pl.ds(index * turn, turn)
        return pltpu.make_async_copy(tile.at[blocks], outs[4].at[blocks], sem.at[index])

    def begin(index, carry):
        copy_turn(index).start()
        return carry

    def wait(index, carry):
        copy_turn(index).wait()
        return carry

    turns = (count[0, 0] + turn - 1) // turn
    lax.fori_loop(0, turns, begin, 0)
    lax.fori_loop(0, turns, wait, 0)
    for copy in small:
        copy.wait()


def fetch(count, rows, cols, features, tile):
    arrays = (rows, cols, features, tile)
    half = jax.ShapeDtypeStruct((features.shape[0] // 2, features.shape[1]), features.dtype)
    outs = [jax.ShapeDtypeStruct(array.shape, array.dtype) for array in (rows, cols)] + [half] * 2
    return pl.pallas_call(
        fetch_kernel,
        out_shape=outs + [jax.ShapeDtypeStruct(tile.shape, tile.dtype)],
        in_specs=[SMEM] + [HBM] * 4,
        out_specs=[VMEM] * 5,
        scratch_shapes=[
            pltpu.SemaphoreType.DMA((tile.shape[0] // turn_of(tile.shape[0]),)),
            pltpu.SemaphoreType.DMA((4,)),
        ],
        compiler_params=params(4),
        cost_estimate=COST,
        name="fetch",
    )(count, *[pltpu.with_memory_space_constraint(array, pltpu.HBM) for array in arrays])


def forward_kernel(n_parts, depths, layout, place, count, rows, cols, adj, *refs):
    parts = refs[:n_parts]
    outs = refs[n_parts:-2]
    source, total = refs[-2:]
    size = adj.shape[1]
    row = 0
    for part in parts:
        depth = part.shape[0]
        for c in range(source.shape[0]):
            source[c, row : row + depth, :] = part[:, c * size : (c + 1) * size]
        row += depth
    product_loop(count[0, 0], cols, rows, adj, source, total, NT)
    blocks = outs[0].shape[1] // size
    outs = iter(outs)
    row = 0
    for depth in depths:
        for chunks in layout:
            out = next(outs)
            for n, k in enumerate(chunks):
                first = (place[0] ^ k) * blocks
                for i in range(blocks):
                    out[n * depth : (n + 1) * depth, i * size : (i + 1) * size] = total[
                        first + i, row : row + depth, :
                    ].astype(out.dtype)
        row += depth


def forward(place, count, rows, cols, adj, parts, row_blocks, depths, layout):
    size = adj.shape[1]
    col_blocks = parts[0].shape[1] // size
    wide = row_blocks * size // sum(len(chunks) for chunks in layout)
    outs = [
        jax.ShapeDtypeStruct((len(chunks) * depth, wide), jnp.bfloat16)
        for depth in depths
        for chunks in layout
    ]
    return pl.pallas_call(
        functools.partial(forward_kernel, len(parts), depths, layout),
        out_shape=outs,
        in_specs=[SMEM] * 4 + [VMEM] * (1 + len(parts)),
        out_specs=[VMEM] * len(outs),
        scratch_shapes=[
            pltpu.VMEM((col_blocks, sum(depths), size), jnp.bfloat16),
            pltpu.VMEM((row_blocks + 1, sum(depths), size), jnp.float32),
        ],
        compiler_params=params(14),
        cost_estimate=COST,
        name="forward_products",
    )(place, count, rows, cols, adj, *parts)


def backward_kernel(spots, depths, place, count, rows, cols, adj, *refs):
    n_parts = 1 + max(part for places in spots for part, _ in places)
    parts = refs[:n_parts]
    outs = refs[n_parts:-2]
    source, total = refs[-2:]
    size = adj.shape[1]
    blocks = parts[0].shape[1] // size
    for k, places in enumerate(spots):
        first = (place[0] ^ k) * blocks
        row = 0
        for (part, offset), depth in zip(places, depths):
            for i in range(blocks):
                source[first + i, row : row + depth, :] = parts[part][
                    offset : offset + depth, i * size : (i + 1) * size
                ]
            row += depth
    product_loop(count[0, 0], rows, cols, adj, source, total, NN)
    row = 0
    for out in outs:
        depth = out.shape[0]
        for c in range(total.shape[0] - 1):
            out[:, c * size : (c + 1) * size] = total[c, row : row + depth, :].astype(out.dtype)
        row += depth


def backward(place, count, rows, cols, adj, parts, spots, depths, out_depths, col_blocks):
    size = adj.shape[1]
    row_blocks = len(spots) * parts[0].shape[1] // size
    return pl.pallas_call(
        functools.partial(backward_kernel, spots, depths),
        out_shape=[jax.ShapeDtypeStruct((depth, col_blocks * size), jnp.bfloat16) for depth in out_depths],
        in_specs=[SMEM] * 4 + [VMEM] * (1 + len(parts)),
        out_specs=[VMEM] * len(out_depths),
        scratch_shapes=[
            pltpu.VMEM((row_blocks, sum(out_depths), size), jnp.bfloat16),
            pltpu.VMEM((col_blocks + 1, sum(out_depths), size), jnp.float32),
        ],
        compiler_params=params(14),
        cost_estimate=COST,
        name="backward_products",
    )(place, count, rows, cols, adj, *parts)


def middle_kernel(sizes, order, n_sum, n_row, row, weight, cotangent, *refs):
    terms = refs[: n_sum * len(sizes)]
    outs = refs[n_sum * len(sizes) : -1]
    output, deltas, aggregated, *backs = outs
    ordered = refs[-1]
    depth = weight.shape[0] // n_row
    for j in range(n_row):
        first = pl.multiple_of((row[0] ^ j) * depth, depth)
        ordered[j * depth : (j + 1) * depth, :] = weight[pl.ds(first, depth), :]
    first = 0
    for p, size in enumerate(sizes):
        summed = terms[p * n_sum][:size, :].astype(jnp.float32)
        for k in range(1, n_sum):
            summed += terms[p * n_sum + k][:size, :].astype(jnp.float32)
        aggregated[first : first + size, :] = summed.astype(jnp.bfloat16)
        first += size
    nodes_first = aggregated[...].T
    preact = jnp.dot(nodes_first, ordered[...], preferred_element_type=jnp.float32)
    gate = jax.nn.sigmoid(preact)
    output[...] = (preact * gate).astype(jnp.bfloat16)
    slopes = gate * (1.0 + preact * (1.0 - gate))
    delta = (cotangent[...].astype(jnp.float32) * slopes).astype(jnp.bfloat16)
    deltas[...] = delta
    product = lax.dot_general(ordered[...], delta, NT, preferred_element_type=jnp.float32)
    product = product.astype(jnp.bfloat16)
    rows = [product[k * depth : (k + 1) * depth, :] for k in order]
    product = jnp.concatenate(rows)
    first = 0
    for back in backs:
        back[...] = product[first : first + back.shape[0], :]
        first += back.shape[0]


def middle(n_row, row, weight, cotangent, pieces, order, depths):
    sizes = [piece[0].shape[0] for piece in pieces]
    nodes = cotangent.shape[0]
    features = weight.shape[0]
    shape = jax.ShapeDtypeStruct
    outs = [
        shape((nodes, features), jnp.bfloat16),
        shape((nodes, features), jnp.bfloat16),
        shape((features, nodes), jnp.bfloat16),
    ] + [shape((depth, nodes), jnp.bfloat16) for depth in depths]
    flat = [term for piece in pieces for term in piece]
    return pl.pallas_call(
        functools.partial(middle_kernel, sizes, order, len(pieces[0]), n_row),
        out_shape=outs,
        in_specs=[SMEM] + [VMEM] * (2 + len(flat)),
        out_specs=[VMEM] * len(outs),
        scratch_shapes=[pltpu.VMEM(weight.shape, jnp.bfloat16)],
        compiler_params=params(10),
        cost_estimate=COST,
        name="layer",
    )(row, weight, cotangent, *flat)


def gradient_kernel(scale, order, aggregated, deltas, *outs):
    product = jnp.dot(aggregated[...], deltas[...], preferred_element_type=jnp.float32) * scale
    for out, chunks in zip(outs, order):
        depth = out.shape[1]
        for n, k in enumerate(chunks):
            out[n] = product[k * depth : (k + 1) * depth, :]


def gradient(scale, order, aggregated, deltas):
    depth = aggregated.shape[0] // sum(len(chunks) for chunks in order)
    outs = [jax.ShapeDtypeStruct((len(chunks), depth, deltas.shape[1]), jnp.float32) for chunks in order]
    return pl.pallas_call(
        functools.partial(gradient_kernel, scale, order),
        out_shape=outs,
        in_specs=[VMEM] * 2,
        out_specs=[VMEM] * len(outs),
        compiler_params=params(6),
        cost_estimate=COST,
        name="weight_gradient",
    )(aggregated, deltas)


def swap(value, axis, k):
    size = lax.axis_size(axis)
    return lax.ppermute(value, axis, [(i, i ^ k) for i in range(size)])


def wide_sum(*values):
    total = values[0].astype(jnp.float32)
    for value in values[1:]:
        total = total + value.astype(jnp.float32)
    return (total.astype(values[0].dtype),)


def after(value, *earlier):
    return lax.optimization_barrier((value, *earlier))[0]


def stack(*values):
    return (jnp.concatenate(values),)


def with_chunk(mine, other, *parts):
    total = functools.reduce(jnp.add, parts)
    high = total.astype(jnp.bfloat16)
    low = (total - high.astype(jnp.float32)).astype(jnp.bfloat16)
    return (jnp.concatenate([mine, other, jnp.concatenate([high, low], axis=1)]),)


def chunk_sum(depth, *values):
    total = None
    for value in values:
        halves = value[-depth:].astype(jnp.float32)
        wide = halves.shape[1] // 2
        chunk = halves[:, :wide] + halves[:, wide:]
        total = chunk if total is None else total + chunk
    return (total,)


def pair_sum(mine, *received):
    return tuple(mine + jnp.concatenate(received))


def row_payloads(depth, chunk, sibling, mine, *received):
    total = (mine.astype(jnp.float32) + jnp.concatenate(received).astype(jnp.float32)).astype(mine.dtype)
    gradient_chunks = jnp.concatenate([chunk.astype(mine.dtype), sibling.astype(mine.dtype)], axis=1)
    parts = [total[first : first + depth] for first in range(0, total.shape[0], depth)]
    return parts[0], *[jnp.concatenate([part, gradient_chunks], axis=1) for part in parts[1:]]


def finish_kernel(row, chunk, sibling, mine, *refs):
    received = refs[:-2]
    grad_features, grad_weight = refs[-2:]
    depth, nodes = mine.shape
    total = mine[...].astype(jnp.float32)
    for part in received:
        total += part[:, :nodes].astype(jnp.float32)
    grad_features[...] = total.astype(mine.dtype)
    wide = grad_weight.shape[1]
    own = [ref[...].astype(mine.dtype) for ref in (chunk, sibling)]
    chunks = own + [part[:, nodes + n * wide : nodes + (n + 1) * wide] for part in received for n in range(2)]
    for k, value in enumerate(chunks):
        first = pl.multiple_of((row[0] ^ k) * depth, depth)
        grad_weight[pl.ds(first, depth), :] = value.astype(jnp.float32)


def finish(row, chunk, sibling, mine, received):
    n_chunks = 2 * (1 + len(received))
    return pl.pallas_call(
        finish_kernel,
        out_shape=[
            jax.ShapeDtypeStruct(mine.shape, mine.dtype),
            jax.ShapeDtypeStruct((n_chunks * chunk.shape[0], chunk.shape[1]), jnp.float32),
        ],
        in_specs=[SMEM] + [VMEM] * (3 + len(received)),
        out_specs=[VMEM] * 2,
        compiler_params=params(8),
        cost_estimate=COST,
        name="finish",
    )(row, chunk, sibling, mine, *received)


def shards_exchanged(features, weight, adj_values, block_rows, block_cols, block_counts, cotangent):
    n_row = lax.axis_size("row")
    n_col = lax.axis_size("col")
    adj = adj_values[0, 0]
    rows = block_rows[0, 0]
    cols = block_cols[0, 0]
    count = block_counts
    size = adj.shape[1]
    nodes = cotangent.shape[0] * n_row * n_col
    row_blocks = cotangent.shape[0] * n_col // size
    col_blocks = features.shape[0] // size
    row = lax.axis_index("row").reshape(1)
    col = lax.axis_index("col").reshape(1)
    own = after(features.T, row, col)

    depth = features.shape[1]
    near = [k for k in range(2, n_row, 2) if k & (k - 1) == 0]
    far = [k for k in range(2, n_row, 2) if k & (k - 1) != 0]
    sibling = swap(own, "row", 1)
    from_near = [swap(own, "row", k) for k in near]
    rows, cols, *halves, tile = fetch(count, rows, cols, own, adj)
    from_near = [after(part, tile) for part in from_near]
    from_far = [swap(half, "row", k) for k in far for half in halves]

    def pass_on(beyond, received):
        return wide_sum(beyond, received[beyond.shape[0] :])

    def forward_pieces(parts, depths):
        outs = forward(col, count, rows, cols, tile, parts, row_blocks, depths, [(0,), (2,), (1, 3)])
        outs = [outs[n : n + 3] for n in range(0, len(outs), 3)]
        return [(kept, beyond, swap(sent, "col", 1)) for kept, beyond, sent in outs]

    def fold(piece, *earlier):
        kept, beyond, received = piece
        received = after(received, *earlier)
        (passed,) = fuse("pass_on", pass_on, beyond, received)
        return [kept, received, swap(passed, "col", 2)]

    n_near = 2 * depth * (1 + len(near))
    cut = n_near // 2 + 16
    parts = [own, sibling] + [piece for part in from_near for piece in (part, swap(part, "row", 1))]
    pieces = forward_pieces(parts, [cut, n_near - cut])
    from_far = [after(part, pieces[0][0]) for part in from_far]
    parts = []
    for n in range(0, len(from_far), 2):
        halves = from_far[n : n + 2]
        parts += halves + [swap(half, "row", 1) for half in halves]
    pieces += forward_pieces(parts, [2 * depth * len(far)])
    sums = []
    for piece in pieces:
        sums.append(fold(piece, *(sums[-1][1:2] if sums else ())))

    evens = tuple(range(0, n_row, 2))
    odds = tuple(range(1, n_row, 2))
    n_all = weight.shape[0]
    cut = n_all // 2 + 16
    cuts = [cut, n_all - cut]
    output, deltas, aggregated, *backs = middle(n_row, row, weight, cotangent, sums, evens + odds, cuts)
    beyond = [swap(back, "col", 2) for back in backs]

    even, *odd = gradient(1.0 / math.sqrt(nodes), [evens, odds[:2], odds[2:]], aggregated, deltas)
    chunk, *sent = fuse("gradient_sum", pair_sum, even, *[swap(part, "row", 1) for part in odd])
    from_rows = [swap(part, "row", k) for part, k in zip(sent, evens[1:])]
    (chunk,) = fuse("chunk_sum", wide_sum, chunk, *from_rows)
    chunks = [chunk, swap(chunk, "col", 2)]

    (large,) = fuse("stack", stack, backs[0], beyond[0])
    (small,) = fuse("with_chunk", with_chunk, backs[1], after(beyond[1], large), *chunks)
    large_received, small_received = swap(large, "col", 1), swap(small, "col", 1)
    (chunk,) = fuse("chunk_sum", functools.partial(chunk_sum, depth), small, small_received)

    mine, *sent = backward(
        col,
        count,
        rows,
        cols,
        tile,
        [*backs, *beyond, after(large_received, chunk), small_received],
        [[(0, 0), (1, 0)], [(4, 0), (5, 0)], [(2, 0), (3, 0)], [(4, cuts[0]), (5, cuts[1])]],
        cuts,
        [n_all // 2] + [n_all // 4] * 2,
        col_blocks,
    )
    from_sibling = [swap(part, "row", 1) for part in sent]
    sibling_chunk = swap(chunk, "row", 1)
    own_sum, *sums = fuse(
        "row_payloads", functools.partial(row_payloads, depth), chunk, sibling_chunk, mine, *from_sibling
    )
    received = [swap(part, "row", k) for part, k in zip(sums, evens[1:])]
    grad_features, grad_weight = finish(row, chunk, sibling_chunk, own_sum, received)
    return output, grad_weight, grad_features.T


def shards_gathered(features, weight, adj_values, block_rows, block_cols, block_counts, cotangent):
    n_row = lax.axis_size("row")
    n_col = lax.axis_size("col")
    adj = adj_values[0, 0]
    rows = block_rows[0, 0]
    cols = block_cols[0, 0]
    count = block_counts
    size = adj.shape[1]
    nodes = cotangent.shape[0] * n_row * n_col
    row_blocks = cotangent.shape[0] * n_col // size
    col_blocks = features.shape[0] // size
    zero = jnp.zeros((1,), jnp.int32)
    panels = lax.all_gather(features.T, "row", axis=0, tiled=True)
    (terms,) = forward(zero, count, rows, cols, adj, [panels], row_blocks, [panels.shape[0]], [(0,)])
    part = lax.psum_scatter(terms, "col", scatter_dimension=1, tiled=True)
    output, deltas, aggregated, back = middle(1, zero, weight, cotangent, [[part]], (0,), [weight.shape[0]])
    slab = lax.all_gather(back, "col", axis=1, tiled=True)
    (column_terms,) = backward(zero, count, rows, cols, adj, [slab], [[(0, 0)]], [slab.shape[0]], [slab.shape[0]], col_blocks)
    grad_features = lax.psum_scatter(column_terms, "row", scatter_dimension=0, tiled=True).T
    (part,) = gradient(1.0 / math.sqrt(nodes), [(0,)], aggregated, deltas)
    grad_weight = lax.psum(part[0], ("row", "col"))
    return output, grad_weight, grad_features


def solution(mesh):
    n_row = mesh.shape["row"]
    n_col = mesh.shape["col"]
    exchanged = n_row == 8 and n_col == 4
    return jax.shard_map(
        shards_exchanged if exchanged else shards_gathered,
        mesh=mesh,
        in_specs=(
            P("col", "row"),
            P(),
            P("row", "col", None, None, None),
            P("row", "col", None),
            P("row", "col", None),
            P("row", "col"),
            P(("row", "col"), None),
        ),
        out_specs=(P(("row", "col"), None), P(), P("col", "row")),
        check_vma=False,
    )
```

```python
import functools
import math

import jax
import jax.numpy as jnp
from jax import lax
from jax.experimental import pallas as pl
from jax.experimental.pallas import tpu as pltpu
from jax.sharding import PartitionSpec as P

VMEM = pl.BlockSpec(memory_space=pltpu.VMEM)
SMEM = pl.BlockSpec(memory_space=pltpu.SMEM)
HBM = pl.BlockSpec(memory_space=pltpu.HBM)
MIB = 1024 * 1024
NT = (((1,), (1,)), ((), ()))
NN = (((1,), (0,)), ((), ()))


COST = pl.CostEstimate(flops=1, bytes_accessed=1, transcendentals=0)


def params(mib):
    return pltpu.CompilerParams(vmem_limit_bytes=mib * MIB)


def fuse(name, function, *values):
    shapes = jax.eval_shape(function, *values)

    def kernel(*refs):
        results = function(*[ref[...] for ref in refs[: len(values)]])
        for ref, result in zip(refs[len(values) :], results):
            ref[...] = result

    return pl.pallas_call(
        kernel,
        out_shape=shapes,
        in_specs=[VMEM] * len(values),
        out_specs=[VMEM] * len(shapes),
        compiler_params=params(4),
        cost_estimate=COST,
        name=name,
    )(*values)


def turn_of(slots):
    return math.gcd(slots, 8)


def product_loop(count, source_ids, target_ids, adj, source, total, dims):
    turn = turn_of(adj.shape[0])
    spare = total.shape[0] - 1
    total[...] = jnp.zeros_like(total)

    def step(index, carry):
        first = index * turn
        for k in range(turn):
            slot = first + k
            product = lax.dot_general(
                source[source_ids[slot]], adj[slot], dims, preferred_element_type=jnp.float32
            )
            target = jnp.where(slot < count, target_ids[slot], spare)
            total[target] += product
        return carry

    lax.fori_loop(0, (count + turn - 1) // turn, step, 0)


def fetch_kernel(count, rows, cols, features, tile, *refs):
    outs, (sem, small_sem) = refs[:5], refs[5:]
    half = features.shape[0] // 2
    sources = (rows, cols, features.at[pl.ds(0, half)], features.at[pl.ds(half, half)])
    small = [
        pltpu.make_async_copy(source, target, small_sem.at[n])
        for n, (source, target) in enumerate(zip(sources, outs))
    ]
    for copy in small:
        copy.start()
    turn = turn_of(tile.shape[0])

    def copy_turn(index):
        blocks = pl.ds(index * turn, turn)
        return pltpu.make_async_copy(tile.at[blocks], outs[4].at[blocks], sem.at[index])

    def begin(index, carry):
        copy_turn(index).start()
        return carry

    def wait(index, carry):
        copy_turn(index).wait()
        return carry

    turns = (count[0, 0] + turn - 1) // turn
    lax.fori_loop(0, turns, begin, 0)
    lax.fori_loop(0, turns, wait, 0)
    for copy in small:
        copy.wait()


def fetch(count, rows, cols, features, tile):
    arrays = (rows, cols, features, tile)
    half = jax.ShapeDtypeStruct((features.shape[0] // 2, features.shape[1]), features.dtype)
    outs = [jax.ShapeDtypeStruct(array.shape, array.dtype) for array in (rows, cols)] + [half] * 2
    return pl.pallas_call(
        fetch_kernel,
        out_shape=outs + [jax.ShapeDtypeStruct(tile.shape, tile.dtype)],
        in_specs=[SMEM] + [HBM] * 4,
        out_specs=[VMEM] * 5,
        scratch_shapes=[
            pltpu.SemaphoreType.DMA((tile.shape[0] // turn_of(tile.shape[0]),)),
            pltpu.SemaphoreType.DMA((4,)),
        ],
        compiler_params=params(4),
        cost_estimate=COST,
        name="fetch",
    )(count, *[pltpu.with_memory_space_constraint(array, pltpu.HBM) for array in arrays])


def forward_kernel(n_parts, depths, layout, place, count, rows, cols, adj, *refs):
    parts = refs[:n_parts]
    outs = refs[n_parts:-2]
    source, total = refs[-2:]
    size = adj.shape[1]
    row = 0
    for part in parts:
        depth = part.shape[0]
        for c in range(source.shape[0]):
            source[c, row : row + depth, :] = part[:, c * size : (c + 1) * size]
        row += depth
    product_loop(count[0, 0], cols, rows, adj, source, total, NT)
    blocks = outs[0].shape[1] // size
    outs = iter(outs)
    row = 0
    for depth in depths:
        for chunks in layout:
            out = next(outs)
            for n, k in enumerate(chunks):
                first = (place[0] ^ k) * blocks
                for i in range(blocks):
                    out[n * depth : (n + 1) * depth, i * size : (i + 1) * size] = total[
                        first + i, row : row + depth, :
                    ].astype(out.dtype)
        row += depth


def forward(place, count, rows, cols, adj, parts, row_blocks, depths, layout):
    size = adj.shape[1]
    col_blocks = parts[0].shape[1] // size
    wide = row_blocks * size // sum(len(chunks) for chunks in layout)
    outs = [
        jax.ShapeDtypeStruct((len(chunks) * depth, wide), jnp.bfloat16)
        for depth in depths
        for chunks in layout
    ]
    return pl.pallas_call(
        functools.partial(forward_kernel, len(parts), depths, layout),
        out_shape=outs,
        in_specs=[SMEM] * 4 + [VMEM] * (1 + len(parts)),
        out_specs=[VMEM] * len(outs),
        scratch_shapes=[
            pltpu.VMEM((col_blocks, sum(depths), size), jnp.bfloat16),
            pltpu.VMEM((row_blocks + 1, sum(depths), size), jnp.float32),
        ],
        compiler_params=params(14),
        cost_estimate=COST,
        name="forward_products",
    )(place, count, rows, cols, adj, *parts)


def backward_kernel(spots, depths, place, count, rows, cols, adj, *refs):
    n_parts = 1 + max(part for places in spots for part, _ in places)
    parts = refs[:n_parts]
    outs = refs[n_parts:-2]
    source, total = refs[-2:]
    size = adj.shape[1]
    blocks = parts[0].shape[1] // size
    for k, places in enumerate(spots):
        first = (place[0] ^ k) * blocks
        row = 0
        for (part, offset), depth in zip(places, depths):
            for i in range(blocks):
                source[first + i, row : row + depth, :] = parts[part][
                    offset : offset + depth, i * size : (i + 1) * size
                ]
            row += depth
    product_loop(count[0, 0], rows, cols, adj, source, total, NN)
    row = 0
    for out in outs:
        depth = out.shape[0]
        for c in range(total.shape[0] - 1):
            out[:, c * size : (c + 1) * size] = total[c, row : row + depth, :].astype(out.dtype)
        row += depth


def backward(place, count, rows, cols, adj, parts, spots, depths, out_depths, col_blocks):
    size = adj.shape[1]
    row_blocks = len(spots) * parts[0].shape[1] // size
    return pl.pallas_call(
        functools.partial(backward_kernel, spots, depths),
        out_shape=[jax.ShapeDtypeStruct((depth, col_blocks * size), jnp.bfloat16) for depth in out_depths],
        in_specs=[SMEM] * 4 + [VMEM] * (1 + len(parts)),
        out_specs=[VMEM] * len(out_depths),
        scratch_shapes=[
            pltpu.VMEM((row_blocks, sum(out_depths), size), jnp.bfloat16),
            pltpu.VMEM((col_blocks + 1, sum(out_depths), size), jnp.float32),
        ],
        compiler_params=params(14),
        cost_estimate=COST,
        name="backward_products",
    )(place, count, rows, cols, adj, *parts)


def middle_kernel(sizes, order, n_sum, n_row, row, weight, cotangent, *refs):
    terms = refs[: n_sum * len(sizes)]
    outs = refs[n_sum * len(sizes) : -1]
    output, deltas, aggregated, *backs = outs
    ordered = refs[-1]
    depth = weight.shape[0] // n_row
    for j in range(n_row):
        first = pl.multiple_of((row[0] ^ j) * depth, depth)
        ordered[j * depth : (j + 1) * depth, :] = weight[pl.ds(first, depth), :]
    first = 0
    for p, size in enumerate(sizes):
        summed = terms[p * n_sum][:size, :].astype(jnp.float32)
        for k in range(1, n_sum):
            summed += terms[p * n_sum + k][:size, :].astype(jnp.float32)
        aggregated[first : first + size, :] = summed.astype(jnp.bfloat16)
        first += size
    nodes_first = aggregated[...].T
    preact = jnp.dot(nodes_first, ordered[...], preferred_element_type=jnp.float32)
    gate = jax.nn.sigmoid(preact)
    output[...] = (preact * gate).astype(jnp.bfloat16)
    slopes = gate * (1.0 + preact * (1.0 - gate))
    delta = (cotangent[...].astype(jnp.float32) * slopes).astype(jnp.bfloat16)
    deltas[...] = delta
    product = lax.dot_general(ordered[...], delta, NT, preferred_element_type=jnp.float32)
    product = product.astype(jnp.bfloat16)
    rows = [product[k * depth : (k + 1) * depth, :] for k in order]
    product = jnp.concatenate(rows)
    first = 0
    for back in backs:
        first %= product.shape[0]
        back[...] = product[first : first + back.shape[0], :]
        first += back.shape[0]


def middle(n_row, row, weight, cotangent, pieces, order, depths):
    sizes = [piece[0].shape[0] for piece in pieces]
    nodes = cotangent.shape[0]
    features = weight.shape[0]
    shape = jax.ShapeDtypeStruct
    outs = [
        shape((nodes, features), jnp.bfloat16),
        shape((nodes, features), jnp.bfloat16),
        shape((features, nodes), jnp.bfloat16),
    ] + [shape((depth, nodes), jnp.bfloat16) for depth in depths]
    flat = [term for piece in pieces for term in piece]
    return pl.pallas_call(
        functools.partial(middle_kernel, sizes, order, len(pieces[0]), n_row),
        out_shape=outs,
        in_specs=[SMEM] + [VMEM] * (2 + len(flat)),
        out_specs=[VMEM] * len(outs),
        scratch_shapes=[pltpu.VMEM(weight.shape, jnp.bfloat16)],
        compiler_params=params(10),
        cost_estimate=COST,
        name="layer",
    )(row, weight, cotangent, *flat)


def gradient_kernel(scale, order, aggregated, deltas, *outs):
    product = jnp.dot(aggregated[...], deltas[...], preferred_element_type=jnp.float32) * scale
    for out, chunks in zip(outs, order):
        depth = out.shape[1]
        for n, k in enumerate(chunks):
            out[n] = product[k * depth : (k + 1) * depth, :]


def gradient(scale, order, aggregated, deltas):
    depth = aggregated.shape[0] // sum(len(chunks) for chunks in order)
    outs = [jax.ShapeDtypeStruct((len(chunks), depth, deltas.shape[1]), jnp.float32) for chunks in order]
    return pl.pallas_call(
        functools.partial(gradient_kernel, scale, order),
        out_shape=outs,
        in_specs=[VMEM] * 2,
        out_specs=[VMEM] * len(outs),
        compiler_params=params(6),
        cost_estimate=COST,
        name="weight_gradient",
    )(aggregated, deltas)


def swap(value, axis, k):
    size = lax.axis_size(axis)
    return lax.ppermute(value, axis, [(i, i ^ k) for i in range(size)])


def wide_sum(*values):
    total = values[0].astype(jnp.float32)
    for value in values[1:]:
        total = total + value.astype(jnp.float32)
    return (total.astype(values[0].dtype),)


def after(value, *earlier):
    return lax.optimization_barrier((value, *earlier))[0]


def with_chunk(rows, *parts):
    total = functools.reduce(jnp.add, parts)
    high = total.astype(jnp.bfloat16)
    low = (total - high.astype(jnp.float32)).astype(jnp.bfloat16)
    return (jnp.concatenate([rows, jnp.concatenate([high, low], axis=1)]),)


def chunk_sum(depth, *values):
    total = None
    for value in values:
        halves = value[-depth:].astype(jnp.float32)
        wide = halves.shape[1] // 2
        chunk = halves[:, :wide] + halves[:, wide:]
        total = chunk if total is None else total + chunk
    return (total,)


def pair_sum(mine, *received):
    return tuple(mine + jnp.concatenate(received))


def row_sums(depth, mine, *received):
    total = mine.astype(jnp.float32) + jnp.concatenate(received).astype(jnp.float32)
    total = jnp.concatenate([total, total[:, :128]], axis=1).astype(mine.dtype)
    return tuple(total[first : first + depth] for first in range(0, total.shape[0], depth))


def row_payloads(depth, chunk, sibling, mine, *received):
    chunks = jnp.concatenate([chunk.astype(mine.dtype), sibling.astype(mine.dtype)], axis=1)
    total = mine.astype(jnp.float32) + jnp.concatenate(received).astype(jnp.float32)
    total = total.astype(mine.dtype)
    own, *sums = [total[first : first + depth] for first in range(0, total.shape[0], depth)]
    return chunks, own, *[jnp.concatenate([part, chunks], axis=1) for part in sums]


def finish_kernel(keys, row, *refs):
    grad_features, grad_weight = refs[-2:]
    parts, chunks = refs[: len(keys)], refs[len(keys) : -2]
    depth, nodes = grad_features.shape
    wide = grad_weight.shape[1]
    total = parts[0][...].astype(jnp.float32)
    for part in parts[1:]:
        total += part[:, :nodes].astype(jnp.float32)
    grad_features[...] = total.astype(grad_features.dtype)
    values = [ref[...] for ref in chunks] + [part[:, nodes:] for part in parts[len(chunks) :]]
    for key, value in zip(keys, values):
        for k in range(2):
            first = pl.multiple_of((row[0] ^ (key + k)) * depth, depth)
            grad_weight[pl.ds(first, depth), :] = value[:, k * wide : (k + 1) * wide].astype(jnp.float32)


def finish(row, keys, parts, chunks):
    depth, nodes = parts[0].shape
    return pl.pallas_call(
        functools.partial(finish_kernel, keys),
        out_shape=[
            jax.ShapeDtypeStruct((depth, nodes), jnp.bfloat16),
            jax.ShapeDtypeStruct((2 * len(keys) * depth, chunks[0].shape[1] // 2), jnp.float32),
        ],
        in_specs=[SMEM] + [VMEM] * (len(parts) + len(chunks)),
        out_specs=[VMEM] * 2,
        compiler_params=params(8),
        cost_estimate=COST,
        name="finish",
    )(row, *parts, *chunks)


def shards_exchanged(features, weight, adj_values, block_rows, block_cols, block_counts, cotangent):
    n_row = lax.axis_size("row")
    n_col = lax.axis_size("col")
    adj = adj_values[0, 0]
    rows = block_rows[0, 0]
    cols = block_cols[0, 0]
    count = block_counts
    size = adj.shape[1]
    nodes = cotangent.shape[0] * n_row * n_col
    row_blocks = cotangent.shape[0] * n_col // size
    col_blocks = features.shape[0] // size
    row = lax.axis_index("row").reshape(1)
    col = lax.axis_index("col").reshape(1)
    own = after(features.T, row, col)

    depth = features.shape[1]
    near = [k for k in range(2, n_row, 2) if k & (k - 1) == 0]
    far = [k for k in range(2, n_row, 2) if k & (k - 1) != 0]
    sibling = swap(own, "row", 1)
    from_near = [swap(own, "row", k) for k in near]
    rows, cols, *halves, tile = fetch(count, rows, cols, own, adj)
    from_near = [after(part, tile) for part in from_near]
    from_far = [swap(half, "row", k) for k in far for half in halves]

    def pass_on(beyond, received):
        return wide_sum(beyond, received[beyond.shape[0] :])

    def forward_pieces(parts, depths):
        outs = forward(col, count, rows, cols, tile, parts, row_blocks, depths, [(0,), (2,), (1, 3)])
        outs = [outs[n : n + 3] for n in range(0, len(outs), 3)]
        return [(kept, beyond, swap(sent, "col", 1)) for kept, beyond, sent in outs]

    def fold(piece, *earlier):
        kept, beyond, received = piece
        received = after(received, *earlier)
        (passed,) = fuse("pass_on", pass_on, beyond, received)
        return [kept, received, swap(passed, "col", 2)]

    n_near = 2 * depth * (1 + len(near))
    cut = n_near // 2 + 16
    parts = [own, sibling] + [piece for part in from_near for piece in (part, swap(part, "row", 1))]
    pieces = forward_pieces(parts, [cut, n_near - cut])
    from_far = [after(part, pieces[0][0]) for part in from_far]
    parts = []
    for n in range(0, len(from_far), 2):
        halves = from_far[n : n + 2]
        parts += halves + [swap(half, "row", 1) for half in halves]
    pieces += forward_pieces(parts, [2 * depth * len(far)])
    sums = []
    for piece in pieces:
        sums.append(fold(piece, *(sums[-1][1:2] if sums else ())))

    groups = [near, [0] + far]
    order = [k + side for group in groups for side in range(2) for k in group]
    cuts = [2 * depth * len(group) for group in groups]
    output, deltas, aggregated, back, *backs = middle(
        n_row, row, weight, cotangent, sums, order, [sum(cuts)] + cuts
    )
    beside = swap(back, "col", 1)
    beyond = [swap(part, "col", 2) for part in backs]

    evens = tuple(range(0, n_row, 2))
    odds = tuple(range(1, n_row, 2))
    even, *odd = gradient(1.0 / math.sqrt(nodes), [evens, odds[:2], odds[2:]], aggregated, deltas)
    chunk, *sent = fuse("gradient_sum", pair_sum, even, *[swap(part, "row", 1) for part in odd])
    from_rows = [swap(part, "row", k) for part, k in zip(sent, evens[1:])]
    (chunk,) = fuse("chunk_sum", wide_sum, after(chunk, beside), *from_rows)
    chunks = [chunk, swap(chunk, "col", 2)]

    beyond[0] = after(beyond[0], chunk)
    (second,) = fuse("with_chunk", with_chunk, after(beyond[1], beyond[0]), *chunks)
    received = [swap(beyond[0], "col", 1), swap(second, "col", 1)]

    def columns(n, *earlier):
        parts = [back, beside, after(beyond[n], *earlier), received[n]]
        spots = [[(0, n * cuts[0])], [(1, n * cuts[0])], [(2, 0)], [(3, 0)]]
        out_depths = [cuts[n] // 2] + [cuts[n] // (8 - 4 * n)] * (4 - 2 * n)
        mine, *sent = backward(
            col, count, rows, cols, tile, parts, spots, cuts[n : n + 1], out_depths, col_blocks
        )
        return [mine] + [swap(part, "row", 1) for part in sent]

    sums = fuse("row_sums", functools.partial(row_sums, depth), *columns(0, second))
    near_sums = [swap(part, "row", k) for part, k in zip(sums, near)]
    received[1] = after(received[1], *sums)
    (chunk,) = fuse("chunk_sum", functools.partial(chunk_sum, depth), second, received[1])
    mine, *from_sibling = columns(1, chunk)
    mine = after(mine, *near_sums)
    chunks, own_sum, *sums = fuse(
        "row_payloads", functools.partial(row_payloads, depth), chunk, swap(chunk, "row", 1), mine, *from_sibling
    )
    far_sums = [swap(part, "row", k) for part, k in zip(sums, far)]
    near_chunks = [swap(chunks, "row", k) for k in near]
    grad_features, grad_weight = finish(
        row, [0] + near + far, [own_sum] + near_sums + far_sums, [chunks] + near_chunks
    )
    return output, grad_weight, grad_features.T


def shards_gathered(features, weight, adj_values, block_rows, block_cols, block_counts, cotangent):
    n_row = lax.axis_size("row")
    n_col = lax.axis_size("col")
    adj = adj_values[0, 0]
    rows = block_rows[0, 0]
    cols = block_cols[0, 0]
    count = block_counts
    size = adj.shape[1]
    nodes = cotangent.shape[0] * n_row * n_col
    row_blocks = cotangent.shape[0] * n_col // size
    col_blocks = features.shape[0] // size
    zero = jnp.zeros((1,), jnp.int32)
    panels = lax.all_gather(features.T, "row", axis=0, tiled=True)
    (terms,) = forward(zero, count, rows, cols, adj, [panels], row_blocks, [panels.shape[0]], [(0,)])
    part = lax.psum_scatter(terms, "col", scatter_dimension=1, tiled=True)
    output, deltas, aggregated, back = middle(1, zero, weight, cotangent, [[part]], (0,), [weight.shape[0]])
    slab = lax.all_gather(back, "col", axis=1, tiled=True)
    (column_terms,) = backward(zero, count, rows, cols, adj, [slab], [[(0, 0)]], [slab.shape[0]], [slab.shape[0]], col_blocks)
    grad_features = lax.psum_scatter(column_terms, "row", scatter_dimension=0, tiled=True).T
    (part,) = gradient(1.0 / math.sqrt(nodes), [(0,)], aggregated, deltas)
    grad_weight = lax.psum(part[0], ("row", "col"))
    return output, grad_weight, grad_features


def solution(mesh):
    n_row = mesh.shape["row"]
    n_col = mesh.shape["col"]
    exchanged = n_row == 8 and n_col == 4
    return jax.shard_map(
        shards_exchanged if exchanged else shards_gathered,
        mesh=mesh,
        in_specs=(
            P("col", "row"),
            P(),
            P("row", "col", None, None, None),
            P("row", "col", None),
            P("row", "col", None),
            P("row", "col"),
            P(("row", "col"), None),
        ),
        out_specs=(P(("row", "col"), None), P(), P("col", "row")),
        check_vma=False,
    )
```

```python
import functools
import math

import jax
import jax.numpy as jnp
from jax import lax
from jax.experimental import pallas as pl
from jax.experimental.pallas import tpu as pltpu
from jax.sharding import PartitionSpec as P

VMEM = pl.BlockSpec(memory_space=pltpu.VMEM)
SMEM = pl.BlockSpec(memory_space=pltpu.SMEM)
HBM = pl.BlockSpec(memory_space=pltpu.HBM)
MIB = 1024 * 1024
NT = (((1,), (1,)), ((), ()))
NN = (((1,), (0,)), ((), ()))


COST = pl.CostEstimate(flops=1, bytes_accessed=1, transcendentals=0)


def params(mib):
    return pltpu.CompilerParams(vmem_limit_bytes=mib * MIB)


def fuse(name, function, *values):
    shapes = jax.eval_shape(function, *values)

    def kernel(*refs):
        results = function(*[ref[...] for ref in refs[: len(values)]])
        for ref, result in zip(refs[len(values) :], results):
            ref[...] = result

    return pl.pallas_call(
        kernel,
        out_shape=shapes,
        in_specs=[VMEM] * len(values),
        out_specs=[VMEM] * len(shapes),
        compiler_params=params(4),
        cost_estimate=COST,
        name=name,
    )(*values)


def turn_of(slots):
    return math.gcd(slots, 8)


def product_loop(count, source_ids, target_ids, adj, source, total, dims):
    turn = turn_of(adj.shape[0])
    spare = total.shape[0] - 1
    total[...] = jnp.zeros_like(total)

    def step(index, carry):
        first = index * turn
        for k in range(turn):
            slot = first + k
            product = lax.dot_general(
                source[source_ids[slot]], adj[slot], dims, preferred_element_type=jnp.float32
            )
            target = jnp.where(slot < count, target_ids[slot], spare)
            total[target] += product
        return carry

    lax.fori_loop(0, (count + turn - 1) // turn, step, 0)


def fetch_kernel(count, rows, cols, features, tile, *refs):
    outs, (sem, small_sem) = refs[:5], refs[5:]
    half = features.shape[0] // 2
    sources = (rows, cols, features.at[pl.ds(0, half)], features.at[pl.ds(half, half)])
    small = [
        pltpu.make_async_copy(source, target, small_sem.at[n])
        for n, (source, target) in enumerate(zip(sources, outs))
    ]
    for copy in small:
        copy.start()
    turn = turn_of(tile.shape[0])

    def copy_turn(index):
        blocks = pl.ds(index * turn, turn)
        return pltpu.make_async_copy(tile.at[blocks], outs[4].at[blocks], sem.at[index])

    def begin(index, carry):
        copy_turn(index).start()
        return carry

    def wait(index, carry):
        copy_turn(index).wait()
        return carry

    turns = (count[0, 0] + turn - 1) // turn
    lax.fori_loop(0, turns, begin, 0)
    lax.fori_loop(0, turns, wait, 0)
    for copy in small:
        copy.wait()


def fetch(count, rows, cols, features, tile):
    arrays = (rows, cols, features, tile)
    half = jax.ShapeDtypeStruct((features.shape[0] // 2, features.shape[1]), features.dtype)
    outs = [jax.ShapeDtypeStruct(array.shape, array.dtype) for array in (rows, cols)] + [half] * 2
    return pl.pallas_call(
        fetch_kernel,
        out_shape=outs + [jax.ShapeDtypeStruct(tile.shape, tile.dtype)],
        in_specs=[SMEM] + [HBM] * 4,
        out_specs=[VMEM] * 5,
        scratch_shapes=[
            pltpu.SemaphoreType.DMA((tile.shape[0] // turn_of(tile.shape[0]),)),
            pltpu.SemaphoreType.DMA((4,)),
        ],
        compiler_params=params(4),
        cost_estimate=COST,
        name="fetch",
    )(count, *[pltpu.with_memory_space_constraint(array, pltpu.HBM) for array in arrays])


def forward_kernel(n_parts, depths, layout, place, count, rows, cols, adj, *refs):
    parts, refs = refs[:n_parts], refs[n_parts:]
    source, total = refs[-2:]
    outs = refs[-2 - len(depths) * len(layout) : -2]
    carried = refs[: len(refs) - 2 - len(outs)]
    size = adj.shape[1]
    row = 0
    for part in parts:
        depth = part.shape[0]
        for c in range(source.shape[0]):
            source[c, row : row + depth, :] = part[:, c * size : (c + 1) * size]
        row += depth
    product_loop(count[0, 0], cols, rows, adj, source, total, NT)
    blocks = outs[0].shape[1] // size
    ahead = carried[0].shape[0] // len(layout[0]) if carried else 0
    outs = iter(outs)
    row = 0
    for depth in depths:
        for m, chunks in enumerate(layout):
            out = next(outs)
            for n, k in enumerate(chunks):
                begin = n * (ahead + depth)
                if ahead:
                    out[begin : begin + ahead, :] = carried[m][n * ahead : (n + 1) * ahead, :]
                first = (place[0] ^ k) * blocks
                for i in range(blocks):
                    out[begin + ahead : begin + ahead + depth, i * size : (i + 1) * size] = total[
                        first + i, row : row + depth, :
                    ].astype(out.dtype)
        row += depth


def forward(place, count, rows, cols, adj, parts, row_blocks, depths, layout, carried=()):
    size = adj.shape[1]
    col_blocks = parts[0].shape[1] // size
    wide = row_blocks * size // sum(len(chunks) for chunks in layout)
    ahead = carried[0].shape[0] // len(layout[0]) if carried else 0
    outs = [
        jax.ShapeDtypeStruct((len(chunks) * (ahead + depth), wide), jnp.bfloat16)
        for depth in depths
        for chunks in layout
    ]
    return pl.pallas_call(
        functools.partial(forward_kernel, len(parts), depths, layout),
        out_shape=outs,
        in_specs=[SMEM] * 4 + [VMEM] * (1 + len(parts) + len(carried)),
        out_specs=[VMEM] * len(outs),
        scratch_shapes=[
            pltpu.VMEM((col_blocks, sum(depths), size), jnp.bfloat16),
            pltpu.VMEM((row_blocks + 1, sum(depths), size), jnp.float32),
        ],
        compiler_params=params(14),
        cost_estimate=COST,
        name="forward_products",
    )(place, count, rows, cols, adj, *parts, *carried)


def backward_kernel(spots, depths, place, count, rows, cols, adj, *refs):
    n_parts = 1 + max(part for places in spots for part, _ in places)
    parts = refs[:n_parts]
    outs = refs[n_parts:-2]
    source, total = refs[-2:]
    size = adj.shape[1]
    blocks = parts[0].shape[1] // size
    for k, places in enumerate(spots):
        first = (place[0] ^ k) * blocks
        row = 0
        for (part, offset), depth in zip(places, depths):
            for i in range(blocks):
                source[first + i, row : row + depth, :] = parts[part][
                    offset : offset + depth, i * size : (i + 1) * size
                ]
            row += depth
    product_loop(count[0, 0], rows, cols, adj, source, total, NN)
    row = 0
    for out in outs:
        depth = out.shape[0]
        for c in range(total.shape[0] - 1):
            out[:, c * size : (c + 1) * size] = total[c, row : row + depth, :].astype(out.dtype)
        row += depth


def backward(place, count, rows, cols, adj, parts, spots, depths, out_depths, col_blocks):
    size = adj.shape[1]
    row_blocks = len(spots) * parts[0].shape[1] // size
    return pl.pallas_call(
        functools.partial(backward_kernel, spots, depths),
        out_shape=[jax.ShapeDtypeStruct((depth, col_blocks * size), jnp.bfloat16) for depth in out_depths],
        in_specs=[SMEM] * 4 + [VMEM] * (1 + len(parts)),
        out_specs=[VMEM] * len(out_depths),
        scratch_shapes=[
            pltpu.VMEM((row_blocks, sum(out_depths), size), jnp.bfloat16),
            pltpu.VMEM((col_blocks + 1, sum(out_depths), size), jnp.float32),
        ],
        compiler_params=params(14),
        cost_estimate=COST,
        name="backward_products",
    )(place, count, rows, cols, adj, *parts)


def middle_kernel(sizes, order, n_sum, n_row, row, weight, cotangent, *refs):
    terms = refs[: n_sum * len(sizes)]
    outs = refs[n_sum * len(sizes) : -1]
    output, deltas, aggregated, back = outs
    ordered = refs[-1]
    depth = weight.shape[0] // n_row
    for j in range(n_row):
        first = pl.multiple_of((row[0] ^ j) * depth, depth)
        ordered[j * depth : (j + 1) * depth, :] = weight[pl.ds(first, depth), :]
    first = 0
    for p, size in enumerate(sizes):
        summed = terms[p * n_sum][:size, :].astype(jnp.float32)
        for k in range(1, n_sum):
            summed += terms[p * n_sum + k][:size, :].astype(jnp.float32)
        aggregated[first : first + size, :] = summed.astype(jnp.bfloat16)
        first += size
    nodes_first = aggregated[...].T
    preact = jnp.dot(nodes_first, ordered[...], preferred_element_type=jnp.float32)
    gate = jax.nn.sigmoid(preact)
    output[...] = (preact * gate).astype(jnp.bfloat16)
    slopes = gate * (1.0 + preact * (1.0 - gate))
    delta = (cotangent[...].astype(jnp.float32) * slopes).astype(jnp.bfloat16)
    deltas[...] = delta
    product = lax.dot_general(ordered[...], delta, NT, preferred_element_type=jnp.float32)
    for n, k in enumerate(order):
        back[n * depth : (n + 1) * depth, :] = product[k * depth : (k + 1) * depth, :].astype(jnp.bfloat16)


def middle(n_row, row, weight, cotangent, pieces, order):
    sizes = [piece[0].shape[0] for piece in pieces]
    nodes = cotangent.shape[0]
    features = weight.shape[0]
    shape = jax.ShapeDtypeStruct
    outs = [
        shape((nodes, features), jnp.bfloat16),
        shape((nodes, features), jnp.bfloat16),
        shape((features, nodes), jnp.bfloat16),
        shape((features, nodes), jnp.bfloat16),
    ]
    flat = [term for piece in pieces for term in piece]
    return pl.pallas_call(
        functools.partial(middle_kernel, sizes, order, len(pieces[0]), n_row),
        out_shape=outs,
        in_specs=[SMEM] + [VMEM] * (2 + len(flat)),
        out_specs=[VMEM] * len(outs),
        scratch_shapes=[pltpu.VMEM(weight.shape, jnp.bfloat16)],
        compiler_params=params(10),
        cost_estimate=COST,
        name="layer",
    )(row, weight, cotangent, *flat)


def gradient_kernel(scale, order, aggregated, deltas, *outs):
    product = jnp.dot(aggregated[...], deltas[...], preferred_element_type=jnp.float32) * scale
    for out, chunks in zip(outs, order):
        depth = out.shape[1]
        for n, k in enumerate(chunks):
            out[n] = product[k * depth : (k + 1) * depth, :]


def gradient(scale, order, aggregated, deltas):
    depth = aggregated.shape[0] // sum(len(chunks) for chunks in order)
    outs = [jax.ShapeDtypeStruct((len(chunks), depth, deltas.shape[1]), jnp.float32) for chunks in order]
    return pl.pallas_call(
        functools.partial(gradient_kernel, scale, order),
        out_shape=outs,
        in_specs=[VMEM] * 2,
        out_specs=[VMEM] * len(outs),
        compiler_params=params(6),
        cost_estimate=COST,
        name="weight_gradient",
    )(aggregated, deltas)


def swap(value, axis, k):
    size = lax.axis_size(axis)
    return lax.ppermute(value, axis, [(i, i ^ k) for i in range(size)])


def wide_sum(*values):
    total = values[0].astype(jnp.float32)
    for value in values[1:]:
        total = total + value.astype(jnp.float32)
    return (total.astype(values[0].dtype),)


def after(value, *earlier):
    return lax.optimization_barrier((value, *earlier))[0]


def with_chunk(first, rows, *parts):
    total = functools.reduce(jnp.add, parts)
    high = total.astype(jnp.bfloat16)
    low = (total - high.astype(jnp.float32)).astype(jnp.bfloat16)
    return (jnp.concatenate([rows[first:], jnp.concatenate([high, low], axis=1)]),)


def chunk_sum(depth, *values):
    total = None
    for value in values:
        halves = value[-depth:].astype(jnp.float32)
        wide = halves.shape[1] // 2
        chunk = halves[:, :wide] + halves[:, wide:]
        total = chunk if total is None else total + chunk
    return (total,)


def halves_sum(mine, *received):
    total = mine + jnp.concatenate(received)
    half = total.shape[0] // 2
    return total[:half], total[half:]


def far_sums(depth, mine, *received):
    total = mine.astype(jnp.float32) + jnp.concatenate(received).astype(jnp.float32)
    total = total.astype(mine.dtype)
    own, far = total[:depth], total[depth:]
    return own, jnp.concatenate([far, far[:, :128]], axis=1)


def near_kernel(row, chunk, sibling, half_way, mine, *refs):
    received, (chunks, *sums) = refs[: -1 - 2], refs[-1 - 2 :]
    depth = half_way.shape[0]
    nodes = mine.shape[1]
    for k, ref in enumerate((chunk, sibling)):
        wide = ref.shape[1]
        chunks[:, k * wide : (k + 1) * wide] = ref[...].astype(chunks.dtype)
    passed = half_way[:, :nodes].astype(jnp.float32)
    odd = row[0] % 2
    for n, out in enumerate(sums):
        total = mine[n * depth : (n + 1) * depth, :].astype(jnp.float32) + received[n][...].astype(jnp.float32)
        total += jnp.where(odd == 1 - n, passed, 0.0)
        out[:, :nodes] = total.astype(out.dtype)
        out[:, nodes:] = chunks[...]


def near_payloads(row, chunk, sibling, half_way, mine, received):
    depth, nodes = received[0].shape
    wide = 2 * chunk.shape[1]
    shape = jax.ShapeDtypeStruct
    return pl.pallas_call(
        near_kernel,
        out_shape=[shape((depth, wide), mine.dtype)]
        + [shape((depth, nodes + wide), mine.dtype)] * len(received),
        in_specs=[SMEM] + [VMEM] * (4 + len(received)),
        out_specs=[VMEM] * (1 + len(received)),
        compiler_params=params(8),
        cost_estimate=COST,
        name="near_payloads",
    )(row, chunk, sibling, half_way, mine, *received)


def finish_kernel(keys, row, *refs):
    grad_features, grad_weight = refs[-2:]
    depth, nodes = grad_features.shape
    wide = grad_weight.shape[1]
    parts = [ref for ref in refs[:-2] if ref.shape[1] >= nodes]
    values = [ref[...] for ref in refs[:-2] if ref.shape[1] < nodes] + [part[:, nodes:] for part in parts[1:]]
    total = parts[0][...].astype(jnp.float32)
    for part in parts[1:]:
        total += part[:, :nodes].astype(jnp.float32)
    grad_features[...] = total.astype(grad_features.dtype)
    for key, value in zip(keys, values):
        for k in range(2):
            first = pl.multiple_of((row[0] ^ (key + k)) * depth, depth)
            grad_weight[pl.ds(first, depth), :] = value[:, k * wide : (k + 1) * wide].astype(jnp.float32)


def finish(row, keys, parts, chunks):
    depth, nodes = parts[0].shape
    return pl.pallas_call(
        functools.partial(finish_kernel, keys),
        out_shape=[
            jax.ShapeDtypeStruct((depth, nodes), jnp.bfloat16),
            jax.ShapeDtypeStruct((2 * len(keys) * depth, chunks[0].shape[1] // 2), jnp.float32),
        ],
        in_specs=[SMEM] + [VMEM] * (len(parts) + len(chunks)),
        out_specs=[VMEM] * 2,
        compiler_params=params(8),
        cost_estimate=COST,
        name="finish",
    )(row, *parts, *chunks)


def shards_exchanged(features, weight, adj_values, block_rows, block_cols, block_counts, cotangent):
    n_row = lax.axis_size("row")
    n_col = lax.axis_size("col")
    adj = adj_values[0, 0]
    rows = block_rows[0, 0]
    cols = block_cols[0, 0]
    count = block_counts
    size = adj.shape[1]
    nodes = cotangent.shape[0] * n_row * n_col
    row_blocks = cotangent.shape[0] * n_col // size
    col_blocks = features.shape[0] // size
    row = lax.axis_index("row").reshape(1)
    col = lax.axis_index("col").reshape(1)
    own = after(features.T, row, col)

    depth = features.shape[1]
    near = [k for k in range(2, n_row, 2) if k & (k - 1) == 0]
    far = [k for k in range(2, n_row, 2) if k & (k - 1) != 0]
    sibling = swap(own, "row", 1)
    from_near = [swap(own, "row", k) for k in near]
    rows, cols, *halves, tile = fetch(count, rows, cols, own, adj)
    from_near = [after(part, tile) for part in from_near]
    from_far = [swap(half, "row", k) for k in far for half in halves]

    def pass_on(beyond, received):
        return wide_sum(beyond, received[beyond.shape[0] :])

    layout = [(0,), (2,), (1, 3)]

    def fold(kept, beyond, received):
        (passed,) = fuse("pass_on", pass_on, beyond, received)
        return [kept, received, swap(passed, "col", 2)]

    n_near = 2 * depth * (1 + len(near))
    cut = n_near * 5 // 6
    parts = [own, sibling] + [piece for part in from_near for piece in (part, swap(part, "row", 1))]
    kept, beyond, sent, *carried = forward(
        col, count, rows, cols, tile, parts, row_blocks, [cut, n_near - cut], layout
    )
    received = swap(sent, "col", 1)
    from_far = [after(part, kept) for part in from_far]
    parts = []
    for n in range(0, len(from_far), 2):
        halves = from_far[n : n + 2]
        parts += halves + [swap(half, "row", 1) for half in halves]
    far_piece = forward(
        col, count, rows, cols, tile, parts, row_blocks, [2 * depth * len(far)], layout, carried
    )
    far_received = swap(far_piece[2], "col", 1)
    first = fold(kept, beyond, after(received, far_piece[0]))
    second = fold(*far_piece[:2], after(far_received, first[1]))
    sums = [first, second]

    groups = [[0] + far, near]
    order = [k + side for group in groups for side in range(2) for k in group]
    cuts = [2 * depth * len(group) for group in groups]
    output, deltas, aggregated, back = middle(n_row, row, weight, cotangent, sums, order)
    beside = swap(back, "col", 1)
    beyond = swap(back, "col", 2)

    even, *odd = gradient(1.0 / math.sqrt(nodes), [(0, 4, 2, 6), (1, 5), (3, 7)], aggregated, deltas)
    even, sent = fuse("gradient_sum", halves_sum, even, *[swap(part, "row", 1) for part in odd])
    even, sent = fuse("gradient_sum", halves_sum, even, swap(sent, "row", 2))
    (chunk,) = fuse("gradient_sum", lambda a, b: ((a + b)[0],), after(even, beside), swap(sent, "row", 4))
    chunks = [chunk, swap(chunk, "col", 2)]

    cut = cuts[0]
    (first,) = fuse("first_rows", lambda rows: (rows[:cut],), after(beyond, *chunks))
    (second,) = fuse("with_chunk", functools.partial(with_chunk, cut), after(beyond, first), *chunks)
    received = [swap(first, "col", 1), swap(second, "col", 1)]

    def columns(n, *earlier):
        parts = [back, beside, after(beyond, *earlier), received[n]]
        spots = [[(part, n * cut)] for part in range(3)] + [[(3, 0)]]
        out_depths = [cuts[n] // 2] + [cuts[n] // (8 - 4 * n)] * (4 - 2 * n)
        mine, *sent = backward(
            col, count, rows, cols, tile, parts, spots, cuts[n : n + 1], out_depths, col_blocks
        )
        return [mine] + [swap(part, "row", 1) for part in sent]

    own_sum, far_sum = fuse("far_sums", functools.partial(far_sums, depth), *columns(0, second))
    half_way = lax.ppermute(far_sum, "row", [(i, i ^ (4 if i % 2 else 2)) for i in range(n_row)])
    received[1] = after(received[1], far_sum)
    (chunk,) = fuse("chunk_sum", functools.partial(chunk_sum, depth), second, received[1])
    mine, *from_sibling = columns(1, chunk)
    chunks, *near_sums = near_payloads(row, chunk, swap(chunk, "row", 1), half_way, mine, from_sibling)
    near_sums = [swap(part, "row", k) for part, k in zip(near_sums, near)]
    far_chunks = [swap(chunks, "row", k) for k in far]
    grad_features, grad_weight = finish(row, [0] + far + near, [own_sum] + near_sums, [chunks] + far_chunks)
    return output, grad_weight, grad_features.T


def shards_gathered(features, weight, adj_values, block_rows, block_cols, block_counts, cotangent):
    n_row = lax.axis_size("row")
    n_col = lax.axis_size("col")
    adj = adj_values[0, 0]
    rows = block_rows[0, 0]
    cols = block_cols[0, 0]
    count = block_counts
    size = adj.shape[1]
    nodes = cotangent.shape[0] * n_row * n_col
    row_blocks = cotangent.shape[0] * n_col // size
    col_blocks = features.shape[0] // size
    zero = jnp.zeros((1,), jnp.int32)
    panels = lax.all_gather(features.T, "row", axis=0, tiled=True)
    (terms,) = forward(zero, count, rows, cols, adj, [panels], row_blocks, [panels.shape[0]], [(0,)])
    part = lax.psum_scatter(terms, "col", scatter_dimension=1, tiled=True)
    output, deltas, aggregated, back = middle(1, zero, weight, cotangent, [[part]], (0,))
    slab = lax.all_gather(back, "col", axis=1, tiled=True)
    (column_terms,) = backward(zero, count, rows, cols, adj, [slab], [[(0, 0)]], [slab.shape[0]], [slab.shape[0]], col_blocks)
    grad_features = lax.psum_scatter(column_terms, "row", scatter_dimension=0, tiled=True).T
    (part,) = gradient(1.0 / math.sqrt(nodes), [(0,)], aggregated, deltas)
    grad_weight = lax.psum(part[0], ("row", "col"))
    return output, grad_weight, grad_features


def solution(mesh):
    n_row = mesh.shape["row"]
    n_col = mesh.shape["col"]
    exchanged = n_row == 8 and n_col == 4
    return jax.shard_map(
        shards_exchanged if exchanged else shards_gathered,
        mesh=mesh,
        in_specs=(
            P("col", "row"),
            P(),
            P("row", "col", None, None, None),
            P("row", "col", None),
            P("row", "col", None),
            P("row", "col"),
            P(("row", "col"), None),
        ),
        out_specs=(P(("row", "col"), None), P(), P("col", "row")),
        check_vma=False,
    )
```

```python
import functools
import math

import jax
import jax.numpy as jnp
from jax import lax
from jax.experimental import pallas as pl
from jax.experimental.pallas import tpu as pltpu
from jax.sharding import PartitionSpec as P

VMEM = pl.BlockSpec(memory_space=pltpu.VMEM)
SMEM = pl.BlockSpec(memory_space=pltpu.SMEM)
HBM = pl.BlockSpec(memory_space=pltpu.HBM)
MIB = 1024 * 1024
NT = (((1,), (1,)), ((), ()))
NN = (((1,), (0,)), ((), ()))


COST = pl.CostEstimate(flops=1, bytes_accessed=1, transcendentals=0)


def params(mib):
    return pltpu.CompilerParams(vmem_limit_bytes=mib * MIB)


def fuse(name, function, *values):
    shapes = jax.eval_shape(function, *values)

    def kernel(*refs):
        results = function(*[ref[...] for ref in refs[: len(values)]])
        for ref, result in zip(refs[len(values) :], results):
            ref[...] = result

    return pl.pallas_call(
        kernel,
        out_shape=shapes,
        in_specs=[VMEM] * len(values),
        out_specs=[VMEM] * len(shapes),
        compiler_params=params(4),
        cost_estimate=COST,
        name=name,
    )(*values)


def turn_of(slots):
    return math.gcd(slots, 8)


def product_loop(count, source_ids, target_ids, adj, source, total, dims):
    turn = turn_of(adj.shape[0])
    spare = total.shape[0] - 1
    total[...] = jnp.zeros_like(total)

    def step(index, carry):
        first = index * turn
        for k in range(turn):
            slot = first + k
            product = lax.dot_general(
                source[source_ids[slot]], adj[slot], dims, preferred_element_type=jnp.float32
            )
            target = jnp.where(slot < count, target_ids[slot], spare)
            total[target] += product
        return carry

    lax.fori_loop(0, (count + turn - 1) // turn, step, 0)


def fetch_kernel(count, rows, cols, features, tile, *refs):
    outs, (sem, small_sem) = refs[:5], refs[5:]
    half = features.shape[0] // 2
    sources = (rows, cols, features.at[pl.ds(0, half)], features.at[pl.ds(half, half)])
    small = [
        pltpu.make_async_copy(source, target, small_sem.at[n])
        for n, (source, target) in enumerate(zip(sources, outs))
    ]
    for copy in small:
        copy.start()
    turn = turn_of(tile.shape[0])

    def copy_turn(index):
        blocks = pl.ds(index * turn, turn)
        return pltpu.make_async_copy(tile.at[blocks], outs[4].at[blocks], sem.at[index])

    def begin(index, carry):
        copy_turn(index).start()
        return carry

    def wait(index, carry):
        copy_turn(index).wait()
        return carry

    turns = (count[0, 0] + turn - 1) // turn
    lax.fori_loop(0, turns, begin, 0)
    lax.fori_loop(0, turns, wait, 0)
    for copy in small:
        copy.wait()


def fetch(count, rows, cols, features, tile):
    arrays = (rows, cols, features, tile)
    half = jax.ShapeDtypeStruct((features.shape[0] // 2, features.shape[1]), features.dtype)
    outs = [jax.ShapeDtypeStruct(array.shape, array.dtype) for array in (rows, cols)] + [half] * 2
    return pl.pallas_call(
        fetch_kernel,
        out_shape=outs + [jax.ShapeDtypeStruct(tile.shape, tile.dtype)],
        in_specs=[SMEM] + [HBM] * 4,
        out_specs=[VMEM] * 5,
        scratch_shapes=[
            pltpu.SemaphoreType.DMA((tile.shape[0] // turn_of(tile.shape[0]),)),
            pltpu.SemaphoreType.DMA((4,)),
        ],
        compiler_params=params(4),
        cost_estimate=COST,
        name="fetch",
    )(count, *[pltpu.with_memory_space_constraint(array, pltpu.HBM) for array in arrays])


def forward_kernel(n_parts, depths, layout, place, count, rows, cols, adj, *refs):
    parts, refs = refs[:n_parts], refs[n_parts:]
    source, total = refs[-2:]
    outs = refs[-2 - len(depths) * len(layout) : -2]
    carried = refs[: len(refs) - 2 - len(outs)]
    size = adj.shape[1]
    row = 0
    for part in parts:
        depth = part.shape[0]
        for c in range(source.shape[0]):
            source[c, row : row + depth, :] = part[:, c * size : (c + 1) * size]
        row += depth
    product_loop(count[0, 0], cols, rows, adj, source, total, NT)
    blocks = outs[0].shape[1] // size
    ahead = carried[0].shape[0] // len(layout[0]) if carried else 0
    outs = iter(outs)
    row = 0
    for depth in depths:
        for m, chunks in enumerate(layout):
            out = next(outs)
            for n, k in enumerate(chunks):
                begin = n * (ahead + depth)
                if ahead:
                    out[begin : begin + ahead, :] = carried[m][n * ahead : (n + 1) * ahead, :]
                first = (place[0] ^ k) * blocks
                for i in range(blocks):
                    out[begin + ahead : begin + ahead + depth, i * size : (i + 1) * size] = total[
                        first + i, row : row + depth, :
                    ].astype(out.dtype)
        row += depth


def forward(place, count, rows, cols, adj, parts, row_blocks, depths, layout, carried=()):
    size = adj.shape[1]
    col_blocks = parts[0].shape[1] // size
    wide = row_blocks * size // sum(len(chunks) for chunks in layout)
    ahead = carried[0].shape[0] // len(layout[0]) if carried else 0
    outs = [
        jax.ShapeDtypeStruct((len(chunks) * (ahead + depth), wide), jnp.bfloat16)
        for depth in depths
        for chunks in layout
    ]
    return pl.pallas_call(
        functools.partial(forward_kernel, len(parts), depths, layout),
        out_shape=outs,
        in_specs=[SMEM] * 4 + [VMEM] * (1 + len(parts) + len(carried)),
        out_specs=[VMEM] * len(outs),
        scratch_shapes=[
            pltpu.VMEM((col_blocks, sum(depths), size), jnp.bfloat16),
            pltpu.VMEM((row_blocks + 1, sum(depths), size), jnp.float32),
        ],
        compiler_params=params(14),
        cost_estimate=COST,
        name="forward_products",
    )(place, count, rows, cols, adj, *parts, *carried)


def backward_kernel(spots, depths, place, count, rows, cols, adj, *refs):
    n_parts = 1 + max(part for places in spots for part, _ in places)
    parts = refs[:n_parts]
    outs = refs[n_parts:-2]
    source, total = refs[-2:]
    size = adj.shape[1]
    blocks = parts[0].shape[1] // size
    for k, places in enumerate(spots):
        first = (place[0] ^ k) * blocks
        row = 0
        for (part, offset), depth in zip(places, depths):
            for i in range(blocks):
                source[first + i, row : row + depth, :] = parts[part][
                    offset : offset + depth, i * size : (i + 1) * size
                ]
            row += depth
    product_loop(count[0, 0], rows, cols, adj, source, total, NN)
    row = 0
    for out in outs:
        depth = out.shape[0]
        for c in range(total.shape[0] - 1):
            out[:, c * size : (c + 1) * size] = total[c, row : row + depth, :].astype(out.dtype)
        row += depth


def backward(place, count, rows, cols, adj, parts, spots, depths, out_depths, col_blocks):
    size = adj.shape[1]
    row_blocks = len(spots) * parts[0].shape[1] // size
    return pl.pallas_call(
        functools.partial(backward_kernel, spots, depths),
        out_shape=[jax.ShapeDtypeStruct((depth, col_blocks * size), jnp.bfloat16) for depth in out_depths],
        in_specs=[SMEM] * 4 + [VMEM] * (1 + len(parts)),
        out_specs=[VMEM] * len(out_depths),
        scratch_shapes=[
            pltpu.VMEM((row_blocks, sum(out_depths), size), jnp.bfloat16),
            pltpu.VMEM((col_blocks + 1, sum(out_depths), size), jnp.float32),
        ],
        compiler_params=params(14),
        cost_estimate=COST,
        name="backward_products",
    )(place, count, rows, cols, adj, *parts)


def middle_kernel(sizes, order, n_sum, n_row, row, weight, cotangent, *refs):
    terms = refs[: n_sum * len(sizes)]
    outs = refs[n_sum * len(sizes) : -1]
    output, deltas, aggregated, *backs = outs
    ordered = refs[-1]
    depth = weight.shape[0] // n_row
    for j in range(n_row):
        first = pl.multiple_of((row[0] ^ j) * depth, depth)
        ordered[j * depth : (j + 1) * depth, :] = weight[pl.ds(first, depth), :]
    first = 0
    for p, size in enumerate(sizes):
        summed = terms[p * n_sum][:size, :].astype(jnp.float32)
        for k in range(1, n_sum):
            summed += terms[p * n_sum + k][:size, :].astype(jnp.float32)
        aggregated[first : first + size, :] = summed.astype(jnp.bfloat16)
        first += size
    nodes_first = aggregated[...].T
    preact = jnp.dot(nodes_first, ordered[...], preferred_element_type=jnp.float32)
    gate = jax.nn.sigmoid(preact)
    output[...] = (preact * gate).astype(jnp.bfloat16)
    slopes = gate * (1.0 + preact * (1.0 - gate))
    delta = (cotangent[...].astype(jnp.float32) * slopes).astype(jnp.bfloat16)
    deltas[...] = delta
    product = lax.dot_general(ordered[...], delta, NT, preferred_element_type=jnp.float32)
    product = jnp.concatenate([product[k * depth : (k + 1) * depth, :] for k in order]).astype(jnp.bfloat16)
    first = 0
    for back in backs:
        first %= product.shape[0]
        back[...] = product[first : first + back.shape[0], :]
        first += back.shape[0]


def middle(n_row, row, weight, cotangent, pieces, order, depths):
    sizes = [piece[0].shape[0] for piece in pieces]
    nodes = cotangent.shape[0]
    features = weight.shape[0]
    shape = jax.ShapeDtypeStruct
    outs = [
        shape((nodes, features), jnp.bfloat16),
        shape((nodes, features), jnp.bfloat16),
        shape((features, nodes), jnp.bfloat16),
    ] + [shape((depth, nodes), jnp.bfloat16) for depth in depths]
    flat = [term for piece in pieces for term in piece]
    return pl.pallas_call(
        functools.partial(middle_kernel, sizes, order, len(pieces[0]), n_row),
        out_shape=outs,
        in_specs=[SMEM] + [VMEM] * (2 + len(flat)),
        out_specs=[VMEM] * len(outs),
        scratch_shapes=[pltpu.VMEM(weight.shape, jnp.bfloat16)],
        compiler_params=params(10),
        cost_estimate=COST,
        name="layer",
    )(row, weight, cotangent, *flat)


def gradient_kernel(scale, order, aggregated, deltas, *outs):
    product = jnp.dot(aggregated[...], deltas[...], preferred_element_type=jnp.float32) * scale
    for out, chunks in zip(outs, order):
        depth = out.shape[1]
        for n, k in enumerate(chunks):
            out[n] = product[k * depth : (k + 1) * depth, :]


def gradient(scale, order, aggregated, deltas):
    depth = aggregated.shape[0] // sum(len(chunks) for chunks in order)
    outs = [jax.ShapeDtypeStruct((len(chunks), depth, deltas.shape[1]), jnp.float32) for chunks in order]
    return pl.pallas_call(
        functools.partial(gradient_kernel, scale, order),
        out_shape=outs,
        in_specs=[VMEM] * 2,
        out_specs=[VMEM] * len(outs),
        compiler_params=params(6),
        cost_estimate=COST,
        name="weight_gradient",
    )(aggregated, deltas)


def swap(value, axis, k):
    size = lax.axis_size(axis)
    return lax.ppermute(value, axis, [(i, i ^ k) for i in range(size)])


def wide_sum(*values):
    total = values[0].astype(jnp.float32)
    for value in values[1:]:
        total = total + value.astype(jnp.float32)
    return (total.astype(values[0].dtype),)


def after(value, *earlier):
    return lax.optimization_barrier((value, *earlier))[0]


def with_chunk(rows, *parts):
    total = functools.reduce(jnp.add, parts)
    high = total.astype(jnp.bfloat16)
    low = (total - high.astype(jnp.float32)).astype(jnp.bfloat16)
    return (jnp.concatenate([rows, jnp.concatenate([high, low], axis=1)]),)


def chunk_sum(depth, *values):
    total = None
    for value in values:
        halves = value[-depth:].astype(jnp.float32)
        wide = halves.shape[1] // 2
        chunk = halves[:, :wide] + halves[:, wide:]
        total = chunk if total is None else total + chunk
    return (total,)


def halves_sum(mine, *received):
    total = mine + jnp.concatenate(received)
    half = total.shape[0] // 2
    return total[:half], total[half:]


def far_sums(mine, *received):
    total = mine.astype(jnp.float32) + jnp.concatenate(received).astype(jnp.float32)
    total = total.astype(mine.dtype)
    return (jnp.concatenate([total, total[:, :128]], axis=1),)


def near_kernel(row, chunk, sibling, half_way, mine, *refs):
    n_sums = mine.shape[0] // half_way.shape[0]
    received, (chunks, *sums) = refs[:n_sums], refs[n_sums:]
    depth = half_way.shape[0]
    nodes = mine.shape[1]
    for k, ref in enumerate((chunk, sibling)):
        wide = ref.shape[1]
        chunks[:, k * wide : (k + 1) * wide] = ref[...].astype(chunks.dtype)
    passed = half_way[:, :nodes].astype(jnp.float32)
    odd = row[0] % 2
    for n, out in enumerate(sums):
        total = mine[n * depth : (n + 1) * depth, :].astype(jnp.float32) + received[n][...].astype(jnp.float32)
        if n:
            total += jnp.where(odd == 2 - n, passed, 0.0)
            out[:, nodes:] = chunks[...]
        out[:, :nodes] = total.astype(out.dtype)


def near_payloads(row, chunk, sibling, half_way, mine, received):
    depth, nodes = received[0].shape
    wide = 2 * chunk.shape[1]
    shapes = [(depth, wide), (depth, nodes)] + [(depth, nodes + wide)] * (len(received) - 1)
    return pl.pallas_call(
        near_kernel,
        out_shape=[jax.ShapeDtypeStruct(shape, mine.dtype) for shape in shapes],
        in_specs=[SMEM] + [VMEM] * (4 + len(received)),
        out_specs=[VMEM] * len(shapes),
        compiler_params=params(8),
        cost_estimate=COST,
        name="near_payloads",
    )(row, chunk, sibling, half_way, mine, *received)


def finish_kernel(keys, row, *refs):
    grad_features, grad_weight = refs[-2:]
    depth, nodes = grad_features.shape
    wide = grad_weight.shape[1]
    parts = [ref for ref in refs[:-2] if ref.shape[1] >= nodes]
    values = [ref[...] for ref in refs[:-2] if ref.shape[1] < nodes] + [part[:, nodes:] for part in parts[1:]]
    total = parts[0][...].astype(jnp.float32)
    for part in parts[1:]:
        total += part[:, :nodes].astype(jnp.float32)
    grad_features[...] = total.astype(grad_features.dtype)
    for key, value in zip(keys, values):
        for k in range(2):
            first = pl.multiple_of((row[0] ^ (key + k)) * depth, depth)
            grad_weight[pl.ds(first, depth), :] = value[:, k * wide : (k + 1) * wide].astype(jnp.float32)


def finish(row, keys, parts, chunks):
    depth, nodes = parts[0].shape
    return pl.pallas_call(
        functools.partial(finish_kernel, keys),
        out_shape=[
            jax.ShapeDtypeStruct((depth, nodes), jnp.bfloat16),
            jax.ShapeDtypeStruct((2 * len(keys) * depth, chunks[0].shape[1] // 2), jnp.float32),
        ],
        in_specs=[SMEM] + [VMEM] * (len(parts) + len(chunks)),
        out_specs=[VMEM] * 2,
        compiler_params=params(8),
        cost_estimate=COST,
        name="finish",
    )(row, *parts, *chunks)


def shards_exchanged(features, weight, adj_values, block_rows, block_cols, block_counts, cotangent):
    n_row = lax.axis_size("row")
    n_col = lax.axis_size("col")
    adj = adj_values[0, 0]
    rows = block_rows[0, 0]
    cols = block_cols[0, 0]
    count = block_counts
    size = adj.shape[1]
    nodes = cotangent.shape[0] * n_row * n_col
    row_blocks = cotangent.shape[0] * n_col // size
    col_blocks = features.shape[0] // size
    row = lax.axis_index("row").reshape(1)
    col = lax.axis_index("col").reshape(1)
    own = after(features.T, row, col)

    depth = features.shape[1]
    near = [k for k in range(2, n_row, 2) if k & (k - 1) == 0]
    far = [k for k in range(2, n_row, 2) if k & (k - 1) != 0]
    sibling = swap(own, "row", 1)
    from_near = [swap(own, "row", k) for k in near]
    rows, cols, *halves, tile = fetch(count, rows, cols, own, adj)
    from_near = [after(part, tile) for part in from_near]
    from_far = [swap(half, "row", k) for k in far for half in halves]

    def pass_on(beyond, received):
        return wide_sum(beyond, received[beyond.shape[0] :])

    layout = [(0,), (2,), (1, 3)]

    def fold(kept, beyond, received):
        (passed,) = fuse("pass_on", pass_on, beyond, received)
        return [kept, received, swap(passed, "col", 2)]

    n_near = 2 * depth * (1 + len(near))
    cut = n_near * 5 // 6
    parts = [own, sibling] + [piece for part in from_near for piece in (part, swap(part, "row", 1))]
    kept, beyond, sent, *carried = forward(
        col, count, rows, cols, tile, parts, row_blocks, [cut, n_near - cut], layout
    )
    received = swap(sent, "col", 1)
    from_far = [after(part, kept) for part in from_far]
    parts = []
    for n in range(0, len(from_far), 2):
        halves = from_far[n : n + 2]
        parts += halves + [swap(half, "row", 1) for half in halves]
    far_piece = forward(
        col, count, rows, cols, tile, parts, row_blocks, [2 * depth * len(far)], layout, carried
    )
    far_received = swap(far_piece[2], "col", 1)
    first = fold(kept, beyond, after(received, far_piece[0]))
    second = fold(*far_piece[:2], after(far_received, first[1]))
    sums = [first, second]

    groups = [far, [0] + near]
    order = [k + side for group in groups for side in range(2) for k in group]
    cuts = [2 * depth * len(group) for group in groups]
    output, deltas, aggregated, back, *backs = middle(
        n_row, row, weight, cotangent, sums, order, [sum(cuts)] + cuts
    )

    even, *odd = gradient(1.0 / math.sqrt(nodes), [(0, 4, 2, 6), (1, 5), (3, 7)], aggregated, deltas)
    even, sent = fuse("gradient_sum", halves_sum, even, *[swap(part, "row", 1) for part in odd])
    beyond = [swap(backs[0], "col", 2)]
    beyond.append(swap(after(backs[1], beyond[0]), "col", 2))
    beside = swap(after(back, beyond[0]), "col", 1)
    received = [swap(beyond[0], "col", 1)]
    even, sent = fuse("gradient_sum", halves_sum, even, swap(sent, "row", 2))
    even = after(even, received[0])
    (chunk,) = fuse("gradient_sum", lambda a, b: ((a + b)[0],), even, swap(sent, "row", 4))
    chunks = [chunk, swap(chunk, "col", 2)]

    (second,) = fuse("with_chunk", with_chunk, beyond[1], *chunks)
    received.append(swap(second, "col", 1))

    def columns(n, *earlier):
        parts = [backs[n], beside, after(beyond[n], *earlier), received[n]]
        spots = [[(0, 0)], [(1, n * cuts[0])], [(2, 0)], [(3, 0)]]
        step = depth if n else depth // 2
        out_depths = [cuts[n] // 2] + [step] * (cuts[n] // 2 // step)
        mine, *sent = backward(
            col, count, rows, cols, tile, parts, spots, cuts[n : n + 1], out_depths, col_blocks
        )
        return [mine] + [swap(part, "row", 1) for part in sent]

    (far_sum,) = fuse("far_sums", far_sums, *columns(0, chunks[1]))
    half_way = lax.ppermute(far_sum, "row", [(i, i ^ (4 if i % 2 else 2)) for i in range(n_row)])
    received[1] = after(received[1], far_sum)
    (chunk,) = fuse("chunk_sum", functools.partial(chunk_sum, depth), second, received[1])
    mine, *from_sibling = columns(1, chunk)
    chunks, own_sum, *near_sums = near_payloads(row, chunk, swap(chunk, "row", 1), half_way, mine, from_sibling)
    near_sums = [swap(part, "row", k) for part, k in zip(near_sums, near)]
    far_chunks = [swap(chunks, "row", k) for k in far]
    grad_features, grad_weight = finish(row, [0] + far + near, [own_sum] + near_sums, [chunks] + far_chunks)
    return output, grad_weight, grad_features.T


def shards_gathered(features, weight, adj_values, block_rows, block_cols, block_counts, cotangent):
    n_row = lax.axis_size("row")
    n_col = lax.axis_size("col")
    adj = adj_values[0, 0]
    rows = block_rows[0, 0]
    cols = block_cols[0, 0]
    count = block_counts
    size = adj.shape[1]
    nodes = cotangent.shape[0] * n_row * n_col
    row_blocks = cotangent.shape[0] * n_col // size
    col_blocks = features.shape[0] // size
    zero = jnp.zeros((1,), jnp.int32)
    panels = lax.all_gather(features.T, "row", axis=0, tiled=True)
    (terms,) = forward(zero, count, rows, cols, adj, [panels], row_blocks, [panels.shape[0]], [(0,)])
    part = lax.psum_scatter(terms, "col", scatter_dimension=1, tiled=True)
    output, deltas, aggregated, back = middle(1, zero, weight, cotangent, [[part]], (0,), [weight.shape[0]])
    slab = lax.all_gather(back, "col", axis=1, tiled=True)
    (column_terms,) = backward(zero, count, rows, cols, adj, [slab], [[(0, 0)]], [slab.shape[0]], [slab.shape[0]], col_blocks)
    grad_features = lax.psum_scatter(column_terms, "row", scatter_dimension=0, tiled=True).T
    (part,) = gradient(1.0 / math.sqrt(nodes), [(0,)], aggregated, deltas)
    grad_weight = lax.psum(part[0], ("row", "col"))
    return output, grad_weight, grad_features


def solution(mesh):
    n_row = mesh.shape["row"]
    n_col = mesh.shape["col"]
    exchanged = n_row == 8 and n_col == 4
    return jax.shard_map(
        shards_exchanged if exchanged else shards_gathered,
        mesh=mesh,
        in_specs=(
            P("col", "row"),
            P(),
            P("row", "col", None, None, None),
            P("row", "col", None),
            P("row", "col", None),
            P("row", "col"),
            P(("row", "col"), None),
        ),
        out_specs=(P(("row", "col"), None), P(), P("col", "row")),
        check_vma=False,
    )
```

```python
import functools
import math

import jax
import jax.numpy as jnp
from jax import lax
from jax.experimental import pallas as pl
from jax.experimental.pallas import tpu as pltpu
from jax.sharding import PartitionSpec as P

VMEM = pl.BlockSpec(memory_space=pltpu.VMEM)
SMEM = pl.BlockSpec(memory_space=pltpu.SMEM)
HBM = pl.BlockSpec(memory_space=pltpu.HBM)
MIB = 1024 * 1024
NT = (((1,), (1,)), ((), ()))
NN = (((1,), (0,)), ((), ()))


COST = pl.CostEstimate(flops=1, bytes_accessed=1, transcendentals=0)


def params(mib):
    return pltpu.CompilerParams(vmem_limit_bytes=mib * MIB)


def fuse(name, function, *values):
    shapes = jax.eval_shape(function, *values)

    def kernel(*refs):
        results = function(*[ref[...] for ref in refs[: len(values)]])
        for ref, result in zip(refs[len(values) :], results):
            ref[...] = result

    return pl.pallas_call(
        kernel,
        out_shape=shapes,
        in_specs=[VMEM] * len(values),
        out_specs=[VMEM] * len(shapes),
        compiler_params=params(4),
        cost_estimate=COST,
        name=name,
    )(*values)


def turn_of(slots):
    return math.gcd(slots, 8)


def product_loop(count, source_ids, target_ids, adj, source, total, dims):
    turn = turn_of(adj.shape[0])
    spare = total.shape[0] - 1
    total[...] = jnp.zeros_like(total)

    def step(index, carry):
        first = index * turn
        for k in range(turn):
            slot = first + k
            product = lax.dot_general(
                source[source_ids[slot]], adj[slot], dims, preferred_element_type=jnp.float32
            )
            target = jnp.where(slot < count, target_ids[slot], spare)
            total[target] += product
        return carry

    lax.fori_loop(0, (count + turn - 1) // turn, step, 0)


def fetch_kernel(count, rows, cols, features, tile, *refs):
    outs, (sem, small_sem) = refs[:5], refs[5:]
    half = features.shape[0] // 2
    sources = (rows, cols, features.at[pl.ds(0, half)], features.at[pl.ds(half, half)])
    small = [
        pltpu.make_async_copy(source, target, small_sem.at[n])
        for n, (source, target) in enumerate(zip(sources, outs))
    ]
    for copy in small:
        copy.start()
    turn = turn_of(tile.shape[0])

    def copy_turn(index):
        blocks = pl.ds(index * turn, turn)
        return pltpu.make_async_copy(tile.at[blocks], outs[4].at[blocks], sem.at[index])

    def begin(index, carry):
        copy_turn(index).start()
        return carry

    def wait(index, carry):
        copy_turn(index).wait()
        return carry

    turns = (count[0, 0] + turn - 1) // turn
    lax.fori_loop(0, turns, begin, 0)
    lax.fori_loop(0, turns, wait, 0)
    for copy in small:
        copy.wait()


def fetch(count, rows, cols, features, tile):
    arrays = (rows, cols, features, tile)
    half = jax.ShapeDtypeStruct((features.shape[0] // 2, features.shape[1]), features.dtype)
    outs = [jax.ShapeDtypeStruct(array.shape, array.dtype) for array in (rows, cols)] + [half] * 2
    return pl.pallas_call(
        fetch_kernel,
        out_shape=outs + [jax.ShapeDtypeStruct(tile.shape, tile.dtype)],
        in_specs=[SMEM] + [HBM] * 4,
        out_specs=[VMEM] * 5,
        scratch_shapes=[
            pltpu.SemaphoreType.DMA((tile.shape[0] // turn_of(tile.shape[0]),)),
            pltpu.SemaphoreType.DMA((4,)),
        ],
        compiler_params=params(4),
        cost_estimate=COST,
        name="fetch",
    )(count, *[pltpu.with_memory_space_constraint(array, pltpu.HBM) for array in arrays])


def forward_kernel(n_parts, depths, layout, place, count, rows, cols, adj, *refs):
    parts, refs = refs[:n_parts], refs[n_parts:]
    source, total = refs[-2:]
    outs = refs[-2 - len(depths) * len(layout) : -2]
    carried = refs[: len(refs) - 2 - len(outs)]
    size = adj.shape[1]
    row = 0
    for part in parts:
        depth = part.shape[0]
        for c in range(source.shape[0]):
            source[c, row : row + depth, :] = part[:, c * size : (c + 1) * size]
        row += depth
    product_loop(count[0, 0], cols, rows, adj, source, total, NT)
    blocks = outs[0].shape[1] // size
    ahead = carried[0].shape[0] // len(layout[0]) if carried else 0
    outs = iter(outs)
    row = 0
    for depth in depths:
        for m, chunks in enumerate(layout):
            out = next(outs)
            for n, k in enumerate(chunks):
                begin = n * (ahead + depth)
                if ahead:
                    out[begin : begin + ahead, :] = carried[m][n * ahead : (n + 1) * ahead, :]
                first = (place[0] ^ k) * blocks
                for i in range(blocks):
                    out[begin + ahead : begin + ahead + depth, i * size : (i + 1) * size] = total[
                        first + i, row : row + depth, :
                    ].astype(out.dtype)
        row += depth


def forward(place, count, rows, cols, adj, parts, row_blocks, depths, layout, carried=()):
    size = adj.shape[1]
    col_blocks = parts[0].shape[1] // size
    wide = row_blocks * size // sum(len(chunks) for chunks in layout)
    ahead = carried[0].shape[0] // len(layout[0]) if carried else 0
    outs = [
        jax.ShapeDtypeStruct((len(chunks) * (ahead + depth), wide), jnp.bfloat16)
        for depth in depths
        for chunks in layout
    ]
    return pl.pallas_call(
        functools.partial(forward_kernel, len(parts), depths, layout),
        out_shape=outs,
        in_specs=[SMEM] * 4 + [VMEM] * (1 + len(parts) + len(carried)),
        out_specs=[VMEM] * len(outs),
        scratch_shapes=[
            pltpu.VMEM((col_blocks, sum(depths), size), jnp.bfloat16),
            pltpu.VMEM((row_blocks + 1, sum(depths), size), jnp.float32),
        ],
        compiler_params=params(14),
        cost_estimate=COST,
        name="forward_products",
    )(place, count, rows, cols, adj, *parts, *carried)


def backward_kernel(spots, depths, place, count, rows, cols, adj, *refs):
    n_parts = 1 + max(part for places in spots for part, _ in places)
    parts = refs[:n_parts]
    outs = refs[n_parts:-2]
    source, total = refs[-2:]
    size = adj.shape[1]
    blocks = parts[0].shape[1] // size
    for k, places in enumerate(spots):
        first = (place[0] ^ k) * blocks
        row = 0
        for (part, offset), depth in zip(places, depths):
            for i in range(blocks):
                source[first + i, row : row + depth, :] = parts[part][
                    offset : offset + depth, i * size : (i + 1) * size
                ]
            row += depth
    product_loop(count[0, 0], rows, cols, adj, source, total, NN)
    row = 0
    for out in outs:
        depth = out.shape[0]
        for c in range(total.shape[0] - 1):
            out[:, c * size : (c + 1) * size] = total[c, row : row + depth, :].astype(out.dtype)
        row += depth


def backward(place, count, rows, cols, adj, parts, spots, depths, out_depths, col_blocks):
    size = adj.shape[1]
    row_blocks = len(spots) * parts[0].shape[1] // size
    return pl.pallas_call(
        functools.partial(backward_kernel, spots, depths),
        out_shape=[jax.ShapeDtypeStruct((depth, col_blocks * size), jnp.bfloat16) for depth in out_depths],
        in_specs=[SMEM] * 4 + [VMEM] * (1 + len(parts)),
        out_specs=[VMEM] * len(out_depths),
        scratch_shapes=[
            pltpu.VMEM((row_blocks, sum(out_depths), size), jnp.bfloat16),
            pltpu.VMEM((col_blocks + 1, sum(out_depths), size), jnp.float32),
        ],
        compiler_params=params(14),
        cost_estimate=COST,
        name="backward_products",
    )(place, count, rows, cols, adj, *parts)


def middle_kernel(sizes, order, n_sum, n_row, row, weight, cotangent, *refs):
    terms = refs[: n_sum * len(sizes)]
    outs = refs[n_sum * len(sizes) : -1]
    output, deltas, aggregated, *backs = outs
    ordered = refs[-1]
    depth = weight.shape[0] // n_row
    for j in range(n_row):
        first = pl.multiple_of((row[0] ^ j) * depth, depth)
        ordered[j * depth : (j + 1) * depth, :] = weight[pl.ds(first, depth), :]
    first = 0
    for p, size in enumerate(sizes):
        summed = terms[p * n_sum][:size, :].astype(jnp.float32)
        for k in range(1, n_sum):
            summed += terms[p * n_sum + k][:size, :].astype(jnp.float32)
        aggregated[first : first + size, :] = summed.astype(jnp.bfloat16)
        first += size
    nodes_first = aggregated[...].T
    preact = jnp.dot(nodes_first, ordered[...], preferred_element_type=jnp.float32)
    gate = jax.nn.sigmoid(preact)
    output[...] = (preact * gate).astype(jnp.bfloat16)
    slopes = gate * (1.0 + preact * (1.0 - gate))
    delta = (cotangent[...].astype(jnp.float32) * slopes).astype(jnp.bfloat16)
    deltas[...] = delta
    product = lax.dot_general(ordered[...], delta, NT, preferred_element_type=jnp.float32)
    product = jnp.concatenate([product[k * depth : (k + 1) * depth, :] for k in order]).astype(jnp.bfloat16)
    first = 0
    for back in backs:
        first %= product.shape[0]
        back[...] = product[first : first + back.shape[0], :]
        first += back.shape[0]


def middle(n_row, row, weight, cotangent, pieces, order, depths):
    sizes = [piece[0].shape[0] for piece in pieces]
    nodes = cotangent.shape[0]
    features = weight.shape[0]
    shape = jax.ShapeDtypeStruct
    outs = [
        shape((nodes, features), jnp.bfloat16),
        shape((nodes, features), jnp.bfloat16),
        shape((features, nodes), jnp.bfloat16),
    ] + [shape((depth, nodes), jnp.bfloat16) for depth in depths]
    flat = [term for piece in pieces for term in piece]
    return pl.pallas_call(
        functools.partial(middle_kernel, sizes, order, len(pieces[0]), n_row),
        out_shape=outs,
        in_specs=[SMEM] + [VMEM] * (2 + len(flat)),
        out_specs=[VMEM] * len(outs),
        scratch_shapes=[pltpu.VMEM(weight.shape, jnp.bfloat16)],
        compiler_params=params(10),
        cost_estimate=COST,
        name="layer",
    )(row, weight, cotangent, *flat)


def gradient_kernel(scale, order, aggregated, deltas, *outs):
    product = jnp.dot(aggregated[...], deltas[...], preferred_element_type=jnp.float32) * scale
    for out, chunks in zip(outs, order):
        depth = out.shape[1]
        for n, k in enumerate(chunks):
            out[n] = product[k * depth : (k + 1) * depth, :]


def gradient(scale, order, aggregated, deltas):
    depth = aggregated.shape[0] // sum(len(chunks) for chunks in order)
    outs = [jax.ShapeDtypeStruct((len(chunks), depth, deltas.shape[1]), jnp.float32) for chunks in order]
    return pl.pallas_call(
        functools.partial(gradient_kernel, scale, order),
        out_shape=outs,
        in_specs=[VMEM] * 2,
        out_specs=[VMEM] * len(outs),
        compiler_params=params(6),
        cost_estimate=COST,
        name="weight_gradient",
    )(aggregated, deltas)


def swap(value, axis, k):
    size = lax.axis_size(axis)
    return lax.ppermute(value, axis, [(i, i ^ k) for i in range(size)])


def wide_sum(*values):
    total = values[0].astype(jnp.float32)
    for value in values[1:]:
        total = total + value.astype(jnp.float32)
    return (total.astype(values[0].dtype),)


def after(value, *earlier):
    return lax.optimization_barrier((value, *earlier))[0]


def with_chunk(rows, *parts):
    total = functools.reduce(jnp.add, parts)
    high = total.astype(jnp.bfloat16)
    low = (total - high.astype(jnp.float32)).astype(jnp.bfloat16)
    return (jnp.concatenate([rows, jnp.concatenate([high, low], axis=1)]),)


def chunk_sum(depth, *values):
    total = None
    for value in values:
        halves = value[-depth:].astype(jnp.float32)
        wide = halves.shape[1] // 2
        chunk = halves[:, :wide] + halves[:, wide:]
        total = chunk if total is None else total + chunk
    return (total,)


def halves_sum(mine, *received):
    total = mine + jnp.concatenate(received)
    half = total.shape[0] // 2
    return total[:half], total[half:]


def far_sums(depth, mine, *received):
    total = mine.astype(jnp.float32) + jnp.concatenate(received).astype(jnp.float32)
    total = total.astype(mine.dtype)
    own, far = total[:depth], total[depth:]
    return own, jnp.concatenate([far, far[:, :128]], axis=1)


def near_kernel(row, chunk, sibling, half_way, mine, *refs):
    received, (chunks, *sums) = refs[: -1 - 2], refs[-1 - 2 :]
    depth = half_way.shape[0]
    nodes = mine.shape[1]
    for k, ref in enumerate((chunk, sibling)):
        wide = ref.shape[1]
        chunks[:, k * wide : (k + 1) * wide] = ref[...].astype(chunks.dtype)
    passed = half_way[:, :nodes].astype(jnp.float32)
    odd = row[0] % 2
    for n, out in enumerate(sums):
        total = mine[n * depth : (n + 1) * depth, :].astype(jnp.float32) + received[n][...].astype(jnp.float32)
        total += jnp.where(odd == 1 - n, passed, 0.0)
        out[:, :nodes] = total.astype(out.dtype)
        out[:, nodes:] = chunks[...]


def near_payloads(row, chunk, sibling, half_way, mine, received):
    depth, nodes = received[0].shape
    wide = 2 * chunk.shape[1]
    shape = jax.ShapeDtypeStruct
    return pl.pallas_call(
        near_kernel,
        out_shape=[shape((depth, wide), mine.dtype)]
        + [shape((depth, nodes + wide), mine.dtype)] * len(received),
        in_specs=[SMEM] + [VMEM] * (4 + len(received)),
        out_specs=[VMEM] * (1 + len(received)),
        compiler_params=params(8),
        cost_estimate=COST,
        name="near_payloads",
    )(row, chunk, sibling, half_way, mine, *received)


def finish_kernel(keys, row, *refs):
    grad_features, grad_weight = refs[-2:]
    depth, nodes = grad_features.shape
    wide = grad_weight.shape[1]
    parts = [ref for ref in refs[:-2] if ref.shape[1] >= nodes]
    values = [ref[...] for ref in refs[:-2] if ref.shape[1] < nodes] + [part[:, nodes:] for part in parts[1:]]
    total = parts[0][...].astype(jnp.float32)
    for part in parts[1:]:
        total += part[:, :nodes].astype(jnp.float32)
    grad_features[...] = total.astype(grad_features.dtype)
    for key, value in zip(keys, values):
        for k in range(2):
            first = pl.multiple_of((row[0] ^ (key + k)) * depth, depth)
            grad_weight[pl.ds(first, depth), :] = value[:, k * wide : (k + 1) * wide].astype(jnp.float32)


def finish(row, keys, parts, chunks):
    depth, nodes = parts[0].shape
    return pl.pallas_call(
        functools.partial(finish_kernel, keys),
        out_shape=[
            jax.ShapeDtypeStruct((depth, nodes), jnp.bfloat16),
            jax.ShapeDtypeStruct((2 * len(keys) * depth, chunks[0].shape[1] // 2), jnp.float32),
        ],
        in_specs=[SMEM] + [VMEM] * (len(parts) + len(chunks)),
        out_specs=[VMEM] * 2,
        compiler_params=params(8),
        cost_estimate=COST,
        name="finish",
    )(row, *parts, *chunks)


def shards_exchanged(features, weight, adj_values, block_rows, block_cols, block_counts, cotangent):
    n_row = lax.axis_size("row")
    n_col = lax.axis_size("col")
    adj = adj_values[0, 0]
    rows = block_rows[0, 0]
    cols = block_cols[0, 0]
    count = block_counts
    size = adj.shape[1]
    nodes = cotangent.shape[0] * n_row * n_col
    row_blocks = cotangent.shape[0] * n_col // size
    col_blocks = features.shape[0] // size
    row = lax.axis_index("row").reshape(1)
    col = lax.axis_index("col").reshape(1)
    own = after(features.T, row, col)

    depth = features.shape[1]
    near = [k for k in range(2, n_row, 2) if k & (k - 1) == 0]
    far = [k for k in range(2, n_row, 2) if k & (k - 1) != 0]
    sibling = swap(own, "row", 1)
    from_near = [swap(own, "row", k) for k in near]
    rows, cols, *halves, tile = fetch(count, rows, cols, own, adj)
    from_near = [after(part, tile) for part in from_near]
    from_far = [swap(half, "row", k) for k in far for half in halves]

    def pass_on(beyond, received):
        return wide_sum(beyond, received[beyond.shape[0] :])

    layout = [(0,), (2,), (1, 3)]

    def fold(kept, beyond, received):
        (passed,) = fuse("pass_on", pass_on, beyond, received)
        return [kept, received, swap(passed, "col", 2)]

    n_near = 2 * depth * (1 + len(near))
    cut = n_near * 5 // 6
    parts = [own, sibling] + [piece for part in from_near for piece in (part, swap(part, "row", 1))]
    kept, beyond, sent, *carried = forward(
        col, count, rows, cols, tile, parts, row_blocks, [cut, n_near - cut], layout
    )
    received = swap(sent, "col", 1)
    from_far = [after(part, kept) for part in from_far]
    parts = []
    for n in range(0, len(from_far), 2):
        halves = from_far[n : n + 2]
        parts += halves + [swap(half, "row", 1) for half in halves]
    far_piece = forward(
        col, count, rows, cols, tile, parts, row_blocks, [2 * depth * len(far)], layout, carried
    )
    far_received = swap(far_piece[2], "col", 1)
    first = fold(kept, beyond, after(received, far_piece[0]))
    second = fold(*far_piece[:2], after(far_received, first[1]))
    sums = [first, second]

    groups = [[0] + far, near]
    order = [k + side for group in groups for side in range(2) for k in group]
    cuts = [2 * depth * len(group) for group in groups]
    ahead = depth // 2
    output, deltas, aggregated, back, *backs = middle(
        n_row, row, weight, cotangent, sums, order, [sum(cuts), cuts[0] + ahead, cuts[1] - ahead]
    )
    beside = swap(back, "col", 1)
    beyond = [swap(part, "col", 2) for part in backs]

    even, *odd = gradient(1.0 / math.sqrt(nodes), [(0, 4, 2, 6), (1, 5), (3, 7)], aggregated, deltas)
    even, sent = fuse("gradient_sum", halves_sum, even, *[swap(part, "row", 1) for part in odd])
    even, sent = fuse("gradient_sum", halves_sum, even, swap(sent, "row", 2))
    beyond[0] = after(beyond[0], sent)
    even = after(even, beyond[1])
    (chunk,) = fuse("gradient_sum", lambda a, b: ((a + b)[0],), even, swap(sent, "row", 4))
    chunks = [chunk, swap(chunk, "col", 2)]

    (second,) = fuse("with_chunk", with_chunk, beyond[1], *chunks)
    received = [swap(beyond[0], "col", 1), swap(second, "col", 1)]

    def columns(n, *earlier):
        parts = [back, beside, after(beyond[0], *earlier), received[0], beyond[1], received[1]]
        if n == 0:
            depths = cuts[:1]
            parts = parts[:4]
            spots = [[(part, 0)] for part in range(4)]
        else:
            depths = [ahead, cuts[1] - ahead]
            spots = [[(part, cuts[0]), (part, cuts[0] + ahead)] for part in range(2)]
            spots += [[(part, cuts[0]), (part + 2, 0)] for part in (2, 3)]
        out_depths = [cuts[n] // 2] + [cuts[n] // (8 - 4 * n)] * (4 - 2 * n)
        mine, *sent = backward(
            col, count, rows, cols, tile, parts, spots, depths, out_depths, col_blocks
        )
        return [mine] + [swap(part, "row", 1) for part in sent]

    own_sum, far_sum = fuse("far_sums", functools.partial(far_sums, depth), *columns(0, second))
    half_way = lax.ppermute(far_sum, "row", [(i, i ^ (4 if i % 2 else 2)) for i in range(n_row)])
    received[1] = after(received[1], far_sum)
    (chunk,) = fuse("chunk_sum", functools.partial(chunk_sum, depth), second, received[1])
    mine, *from_sibling = columns(1, chunk)
    chunks, *near_sums = near_payloads(row, chunk, swap(chunk, "row", 1), half_way, mine, from_sibling)
    near_sums = [swap(part, "row", k) for part, k in zip(near_sums, near)]
    far_chunks = [swap(chunks, "row", k) for k in far]
    grad_features, grad_weight = finish(row, [0] + far + near, [own_sum] + near_sums, [chunks] + far_chunks)
    return output, grad_weight, grad_features.T


def shards_gathered(features, weight, adj_values, block_rows, block_cols, block_counts, cotangent):
    n_row = lax.axis_size("row")
    n_col = lax.axis_size("col")
    adj = adj_values[0, 0]
    rows = block_rows[0, 0]
    cols = block_cols[0, 0]
    count = block_counts
    size = adj.shape[1]
    nodes = cotangent.shape[0] * n_row * n_col
    row_blocks = cotangent.shape[0] * n_col // size
    col_blocks = features.shape[0] // size
    zero = jnp.zeros((1,), jnp.int32)
    panels = lax.all_gather(features.T, "row", axis=0, tiled=True)
    (terms,) = forward(zero, count, rows, cols, adj, [panels], row_blocks, [panels.shape[0]], [(0,)])
    part = lax.psum_scatter(terms, "col", scatter_dimension=1, tiled=True)
    output, deltas, aggregated, back = middle(1, zero, weight, cotangent, [[part]], (0,), [weight.shape[0]])
    slab = lax.all_gather(back, "col", axis=1, tiled=True)
    (column_terms,) = backward(zero, count, rows, cols, adj, [slab], [[(0, 0)]], [slab.shape[0]], [slab.shape[0]], col_blocks)
    grad_features = lax.psum_scatter(column_terms, "row", scatter_dimension=0, tiled=True).T
    (part,) = gradient(1.0 / math.sqrt(nodes), [(0,)], aggregated, deltas)
    grad_weight = lax.psum(part[0], ("row", "col"))
    return output, grad_weight, grad_features


def solution(mesh):
    n_row = mesh.shape["row"]
    n_col = mesh.shape["col"]
    exchanged = n_row == 8 and n_col == 4
    return jax.shard_map(
        shards_exchanged if exchanged else shards_gathered,
        mesh=mesh,
        in_specs=(
            P("col", "row"),
            P(),
            P("row", "col", None, None, None),
            P("row", "col", None),
            P("row", "col", None),
            P("row", "col"),
            P(("row", "col"), None),
        ),
        out_specs=(P(("row", "col"), None), P(), P("col", "row")),
        check_vma=False,
    )
```

```python
import functools
import math

import jax
import jax.numpy as jnp
from jax import lax
from jax.experimental import pallas as pl
from jax.experimental.pallas import tpu as pltpu
from jax.sharding import PartitionSpec as P

VMEM = pl.BlockSpec(memory_space=pltpu.VMEM)
SMEM = pl.BlockSpec(memory_space=pltpu.SMEM)
HBM = pl.BlockSpec(memory_space=pltpu.HBM)
MIB = 1024 * 1024
NT = (((1,), (1,)), ((), ()))
NN = (((1,), (0,)), ((), ()))


COST = pl.CostEstimate(flops=1, bytes_accessed=1, transcendentals=0)


def params(mib):
    return pltpu.CompilerParams(vmem_limit_bytes=mib * MIB)


def fuse(name, function, *values):
    shapes = jax.eval_shape(function, *values)

    def kernel(*refs):
        results = function(*[ref[...] for ref in refs[: len(values)]])
        for ref, result in zip(refs[len(values) :], results):
            ref[...] = result

    return pl.pallas_call(
        kernel,
        out_shape=shapes,
        in_specs=[VMEM] * len(values),
        out_specs=[VMEM] * len(shapes),
        compiler_params=params(4),
        cost_estimate=COST,
        name=name,
    )(*values)


def turn_of(slots):
    return math.gcd(slots, 8)


def product_loop(count, source_ids, target_ids, adj, source, total, dims):
    turn = turn_of(adj.shape[0])
    spare = total.shape[0] - 1
    total[...] = jnp.zeros_like(total)

    def step(index, carry):
        first = index * turn
        for k in range(turn):
            slot = first + k
            product = lax.dot_general(
                source[source_ids[slot]], adj[slot], dims, preferred_element_type=jnp.float32
            )
            target = jnp.where(slot < count, target_ids[slot], spare)
            total[target] += product
        return carry

    lax.fori_loop(0, (count + turn - 1) // turn, step, 0)


def fetch_kernel(count, rows, cols, features, tile, *refs):
    outs, (sem, small_sem) = refs[:5], refs[5:]
    half = features.shape[0] // 2
    sources = (rows, cols, features.at[pl.ds(0, half)], features.at[pl.ds(half, half)])
    small = [
        pltpu.make_async_copy(source, target, small_sem.at[n])
        for n, (source, target) in enumerate(zip(sources, outs))
    ]
    for copy in small:
        copy.start()
    turn = turn_of(tile.shape[0])

    def copy_turn(index):
        blocks = pl.ds(index * turn, turn)
        return pltpu.make_async_copy(tile.at[blocks], outs[4].at[blocks], sem.at[index])

    def begin(index, carry):
        copy_turn(index).start()
        return carry

    def wait(index, carry):
        copy_turn(index).wait()
        return carry

    turns = (count[0, 0] + turn - 1) // turn
    lax.fori_loop(0, turns, begin, 0)
    lax.fori_loop(0, turns, wait, 0)
    for copy in small:
        copy.wait()


def fetch(count, rows, cols, features, tile):
    arrays = (rows, cols, features, tile)
    half = jax.ShapeDtypeStruct((features.shape[0] // 2, features.shape[1]), features.dtype)
    outs = [jax.ShapeDtypeStruct(array.shape, array.dtype) for array in (rows, cols)] + [half] * 2
    return pl.pallas_call(
        fetch_kernel,
        out_shape=outs + [jax.ShapeDtypeStruct(tile.shape, tile.dtype)],
        in_specs=[SMEM] + [HBM] * 4,
        out_specs=[VMEM] * 5,
        scratch_shapes=[
            pltpu.SemaphoreType.DMA((tile.shape[0] // turn_of(tile.shape[0]),)),
            pltpu.SemaphoreType.DMA((4,)),
        ],
        compiler_params=params(4),
        cost_estimate=COST,
        name="fetch",
    )(count, *[pltpu.with_memory_space_constraint(array, pltpu.HBM) for array in arrays])


def forward_kernel(n_parts, depths, layout, place, count, rows, cols, adj, *refs):
    parts, refs = refs[:n_parts], refs[n_parts:]
    source, total = refs[-2:]
    outs = refs[-2 - len(depths) * len(layout) : -2]
    carried = refs[: len(refs) - 2 - len(outs)]
    size = adj.shape[1]
    row = 0
    for part in parts:
        depth = part.shape[0]
        for c in range(source.shape[0]):
            source[c, row : row + depth, :] = part[:, c * size : (c + 1) * size]
        row += depth
    product_loop(count[0, 0], cols, rows, adj, source, total, NT)
    blocks = outs[0].shape[1] // size
    ahead = carried[0].shape[0] // len(layout[0]) if carried else 0
    outs = iter(outs)
    row = 0
    for depth in depths:
        for m, chunks in enumerate(layout):
            out = next(outs)
            for n, k in enumerate(chunks):
                begin = n * (ahead + depth)
                if ahead:
                    out[begin : begin + ahead, :] = carried[m][n * ahead : (n + 1) * ahead, :]
                first = (place[0] ^ k) * blocks
                for i in range(blocks):
                    out[begin + ahead : begin + ahead + depth, i * size : (i + 1) * size] = total[
                        first + i, row : row + depth, :
                    ].astype(out.dtype)
        row += depth


def forward(place, count, rows, cols, adj, parts, row_blocks, depths, layout, carried=()):
    size = adj.shape[1]
    col_blocks = parts[0].shape[1] // size
    wide = row_blocks * size // sum(len(chunks) for chunks in layout)
    ahead = carried[0].shape[0] // len(layout[0]) if carried else 0
    outs = [
        jax.ShapeDtypeStruct((len(chunks) * (ahead + depth), wide), jnp.bfloat16)
        for depth in depths
        for chunks in layout
    ]
    return pl.pallas_call(
        functools.partial(forward_kernel, len(parts), depths, layout),
        out_shape=outs,
        in_specs=[SMEM] * 4 + [VMEM] * (1 + len(parts) + len(carried)),
        out_specs=[VMEM] * len(outs),
        scratch_shapes=[
            pltpu.VMEM((col_blocks, sum(depths), size), jnp.bfloat16),
            pltpu.VMEM((row_blocks + 1, sum(depths), size), jnp.float32),
        ],
        compiler_params=params(14),
        cost_estimate=COST,
        name="forward_products",
    )(place, count, rows, cols, adj, *parts, *carried)


def backward_kernel(spots, depths, place, count, rows, cols, adj, *refs):
    n_parts = 1 + max(part for places in spots for part, _ in places)
    parts = refs[:n_parts]
    outs = refs[n_parts:-2]
    source, total = refs[-2:]
    size = adj.shape[1]
    blocks = parts[0].shape[1] // size
    for k, places in enumerate(spots):
        first = (place[0] ^ k) * blocks
        row = 0
        for (part, offset), depth in zip(places, depths):
            for i in range(blocks):
                source[first + i, row : row + depth, :] = parts[part][
                    offset : offset + depth, i * size : (i + 1) * size
                ]
            row += depth
    product_loop(count[0, 0], rows, cols, adj, source, total, NN)
    row = 0
    for out in outs:
        depth = out.shape[0]
        for c in range(total.shape[0] - 1):
            out[:, c * size : (c + 1) * size] = total[c, row : row + depth, :].astype(out.dtype)
        row += depth


def backward(place, count, rows, cols, adj, parts, spots, depths, out_depths, col_blocks):
    size = adj.shape[1]
    row_blocks = len(spots) * parts[0].shape[1] // size
    return pl.pallas_call(
        functools.partial(backward_kernel, spots, depths),
        out_shape=[jax.ShapeDtypeStruct((depth, col_blocks * size), jnp.bfloat16) for depth in out_depths],
        in_specs=[SMEM] * 4 + [VMEM] * (1 + len(parts)),
        out_specs=[VMEM] * len(out_depths),
        scratch_shapes=[
            pltpu.VMEM((row_blocks, sum(out_depths), size), jnp.bfloat16),
            pltpu.VMEM((col_blocks + 1, sum(out_depths), size), jnp.float32),
        ],
        compiler_params=params(14),
        cost_estimate=COST,
        name="backward_products",
    )(place, count, rows, cols, adj, *parts)


def middle_kernel(sizes, order, n_sum, n_row, row, weight, cotangent, *refs):
    terms = refs[: n_sum * len(sizes)]
    outs = refs[n_sum * len(sizes) : -1]
    output, deltas, aggregated, *backs = outs
    ordered = refs[-1]
    depth = weight.shape[0] // n_row
    for j in range(n_row):
        first = pl.multiple_of((row[0] ^ j) * depth, depth)
        ordered[j * depth : (j + 1) * depth, :] = weight[pl.ds(first, depth), :]
    first = 0
    for p, size in enumerate(sizes):
        summed = terms[p * n_sum][:size, :].astype(jnp.float32)
        for k in range(1, n_sum):
            summed += terms[p * n_sum + k][:size, :].astype(jnp.float32)
        aggregated[first : first + size, :] = summed.astype(jnp.bfloat16)
        first += size
    nodes_first = aggregated[...].T
    preact = jnp.dot(nodes_first, ordered[...], preferred_element_type=jnp.float32)
    gate = jax.nn.sigmoid(preact)
    output[...] = (preact * gate).astype(jnp.bfloat16)
    slopes = gate * (1.0 + preact * (1.0 - gate))
    delta = (cotangent[...].astype(jnp.float32) * slopes).astype(jnp.bfloat16)
    deltas[...] = delta
    product = lax.dot_general(ordered[...], delta, NT, preferred_element_type=jnp.float32)
    product = jnp.concatenate([product[k * depth : (k + 1) * depth, :] for k in order]).astype(jnp.bfloat16)
    first = 0
    for back in backs:
        first %= product.shape[0]
        back[...] = product[first : first + back.shape[0], :]
        first += back.shape[0]


def middle(n_row, row, weight, cotangent, pieces, order, depths):
    sizes = [piece[0].shape[0] for piece in pieces]
    nodes = cotangent.shape[0]
    features = weight.shape[0]
    shape = jax.ShapeDtypeStruct
    outs = [
        shape((nodes, features), jnp.bfloat16),
        shape((nodes, features), jnp.bfloat16),
        shape((features, nodes), jnp.bfloat16),
    ] + [shape((depth, nodes), jnp.bfloat16) for depth in depths]
    flat = [term for piece in pieces for term in piece]
    return pl.pallas_call(
        functools.partial(middle_kernel, sizes, order, len(pieces[0]), n_row),
        out_shape=outs,
        in_specs=[SMEM] + [VMEM] * (2 + len(flat)),
        out_specs=[VMEM] * len(outs),
        scratch_shapes=[pltpu.VMEM(weight.shape, jnp.bfloat16)],
        compiler_params=params(10),
        cost_estimate=COST,
        name="layer",
    )(row, weight, cotangent, *flat)


def gradient_kernel(scale, order, aggregated, deltas, *outs):
    product = jnp.dot(aggregated[...], deltas[...], preferred_element_type=jnp.float32) * scale
    for out, chunks in zip(outs, order):
        depth = out.shape[1]
        for n, k in enumerate(chunks):
            out[n] = product[k * depth : (k + 1) * depth, :]


def gradient(scale, order, aggregated, deltas):
    depth = aggregated.shape[0] // sum(len(chunks) for chunks in order)
    outs = [jax.ShapeDtypeStruct((len(chunks), depth, deltas.shape[1]), jnp.float32) for chunks in order]
    return pl.pallas_call(
        functools.partial(gradient_kernel, scale, order),
        out_shape=outs,
        in_specs=[VMEM] * 2,
        out_specs=[VMEM] * len(outs),
        compiler_params=params(6),
        cost_estimate=COST,
        name="weight_gradient",
    )(aggregated, deltas)


def swap(value, axis, k):
    size = lax.axis_size(axis)
    return lax.ppermute(value, axis, [(i, i ^ k) for i in range(size)])


def wide_sum(*values):
    total = values[0].astype(jnp.float32)
    for value in values[1:]:
        total = total + value.astype(jnp.float32)
    return (total.astype(values[0].dtype),)


def after(value, *earlier):
    return lax.optimization_barrier((value, *earlier))[0]


def with_chunk(rows, *parts):
    total = functools.reduce(jnp.add, parts)
    high = total.astype(jnp.bfloat16)
    low = (total - high.astype(jnp.float32)).astype(jnp.bfloat16)
    return (jnp.concatenate([rows, jnp.concatenate([high, low], axis=1)]),)


def chunk_sum(depth, *values):
    total = None
    for value in values:
        halves = value[-depth:].astype(jnp.float32)
        wide = halves.shape[1] // 2
        chunk = halves[:, :wide] + halves[:, wide:]
        total = chunk if total is None else total + chunk
    return (total,)


def halves_sum(mine, *received):
    total = mine + jnp.concatenate(received)
    half = total.shape[0] // 2
    return total[:half], total[half:]


def far_sums(depth, mine, *received):
    total = mine.astype(jnp.float32) + jnp.concatenate(received).astype(jnp.float32)
    total = total.astype(mine.dtype)
    own, far = total[:depth], total[depth:]
    return own, jnp.concatenate([far, far[:, :128]], axis=1)


def near_kernel(row, chunk, sibling, half_way, mine, *refs):
    received, (chunks, *sums) = refs[: -1 - 2], refs[-1 - 2 :]
    depth = half_way.shape[0]
    nodes = mine.shape[1]
    for k, ref in enumerate((chunk, sibling)):
        wide = ref.shape[1]
        chunks[:, k * wide : (k + 1) * wide] = ref[...].astype(chunks.dtype)
    passed = half_way[:, :nodes].astype(jnp.float32)
    odd = row[0] % 2
    for n, out in enumerate(sums):
        total = mine[n * depth : (n + 1) * depth, :].astype(jnp.float32) + received[n][...].astype(jnp.float32)
        total += jnp.where(odd == 1 - n, passed, 0.0)
        out[:, :nodes] = total.astype(out.dtype)
        out[:, nodes:] = chunks[...]


def near_payloads(row, chunk, sibling, half_way, mine, received):
    depth, nodes = received[0].shape
    wide = 2 * chunk.shape[1]
    shape = jax.ShapeDtypeStruct
    return pl.pallas_call(
        near_kernel,
        out_shape=[shape((depth, wide), mine.dtype)]
        + [shape((depth, nodes + wide), mine.dtype)] * len(received),
        in_specs=[SMEM] + [VMEM] * (4 + len(received)),
        out_specs=[VMEM] * (1 + len(received)),
        compiler_params=params(8),
        cost_estimate=COST,
        name="near_payloads",
    )(row, chunk, sibling, half_way, mine, *received)


def finish_kernel(keys, row, *refs):
    grad_features, grad_weight = refs[-2:]
    depth, nodes = grad_features.shape
    wide = grad_weight.shape[1]
    parts = [ref for ref in refs[:-2] if ref.shape[1] >= nodes]
    values = [ref[...] for ref in refs[:-2] if ref.shape[1] < nodes] + [part[:, nodes:] for part in parts[1:]]
    total = parts[0][...].astype(jnp.float32)
    for part in parts[1:]:
        total += part[:, :nodes].astype(jnp.float32)
    grad_features[...] = total.astype(grad_features.dtype)
    for key, value in zip(keys, values):
        for k in range(2):
            first = pl.multiple_of((row[0] ^ (key + k)) * depth, depth)
            grad_weight[pl.ds(first, depth), :] = value[:, k * wide : (k + 1) * wide].astype(jnp.float32)


def finish(row, keys, parts, chunks):
    depth, nodes = parts[0].shape
    return pl.pallas_call(
        functools.partial(finish_kernel, keys),
        out_shape=[
            jax.ShapeDtypeStruct((depth, nodes), jnp.bfloat16),
            jax.ShapeDtypeStruct((2 * len(keys) * depth, chunks[0].shape[1] // 2), jnp.float32),
        ],
        in_specs=[SMEM] + [VMEM] * (len(parts) + len(chunks)),
        out_specs=[VMEM] * 2,
        compiler_params=params(8),
        cost_estimate=COST,
        name="finish",
    )(row, *parts, *chunks)


def shards_exchanged(features, weight, adj_values, block_rows, block_cols, block_counts, cotangent):
    n_row = lax.axis_size("row")
    n_col = lax.axis_size("col")
    adj = adj_values[0, 0]
    rows = block_rows[0, 0]
    cols = block_cols[0, 0]
    count = block_counts
    size = adj.shape[1]
    nodes = cotangent.shape[0] * n_row * n_col
    row_blocks = cotangent.shape[0] * n_col // size
    col_blocks = features.shape[0] // size
    row = lax.axis_index("row").reshape(1)
    col = lax.axis_index("col").reshape(1)
    own = after(features.T, row, col)

    depth = features.shape[1]
    near = [k for k in range(2, n_row, 2) if k & (k - 1) == 0]
    far = [k for k in range(2, n_row, 2) if k & (k - 1) != 0]
    sibling = swap(own, "row", 1)
    from_near = [swap(own, "row", k) for k in near]
    rows, cols, *halves, tile = fetch(count, rows, cols, own, adj)
    from_near = [after(part, tile) for part in from_near]
    from_far = [swap(half, "row", k) for k in far for half in halves]

    def pass_on(beyond, received):
        return wide_sum(beyond, received[beyond.shape[0] :])

    layout = [(0,), (2,), (1, 3)]

    def fold(kept, beyond, received):
        (passed,) = fuse("pass_on", pass_on, beyond, received)
        return [kept, received, swap(passed, "col", 2)]

    n_near = 2 * depth * (1 + len(near))
    cut = n_near * 5 // 6
    parts = [own, sibling] + [piece for part in from_near for piece in (part, swap(part, "row", 1))]
    kept, beyond, sent, *carried = forward(
        col, count, rows, cols, tile, parts, row_blocks, [cut, n_near - cut], layout
    )
    received = swap(sent, "col", 1)
    from_far = [after(part, kept) for part in from_far]
    parts = []
    for n in range(0, len(from_far), 2):
        halves = from_far[n : n + 2]
        parts += halves + [swap(half, "row", 1) for half in halves]
    far_piece = forward(
        col, count, rows, cols, tile, parts, row_blocks, [2 * depth * len(far)], layout, carried
    )
    far_received = swap(far_piece[2], "col", 1)
    first = fold(kept, beyond, after(received, far_piece[0]))
    second = fold(*far_piece[:2], after(far_received, first[1]))
    sums = [first, second]

    groups = [[0] + far, near]
    order = [k + side for group in groups for side in range(2) for k in group]
    cuts = [2 * depth * len(group) for group in groups]
    ahead = depth // 2
    output, deltas, aggregated, *backs = middle(
        n_row, row, weight, cotangent, sums, order, [cuts[0] + ahead, cuts[1] - ahead]
    )
    beside = [swap(backs[0], "col", 1)]
    beyond = [swap(part, "col", 2) for part in backs]

    even, *odd = gradient(1.0 / math.sqrt(nodes), [(0, 4, 2, 6), (1, 5), (3, 7)], aggregated, deltas)
    even, sent = fuse("gradient_sum", halves_sum, even, *[swap(part, "row", 1) for part in odd])
    even, sent = fuse("gradient_sum", halves_sum, after(even, beside[0]), swap(sent, "row", 2))
    beyond[0] = after(beyond[0], sent)
    beside.append(swap(after(backs[1], beyond[0]), "col", 1))
    even = after(even, beyond[1])
    (chunk,) = fuse("gradient_sum", lambda a, b: ((a + b)[0],), even, swap(sent, "row", 4))
    chunks = [chunk, swap(chunk, "col", 2)]

    (second,) = fuse("with_chunk", with_chunk, beyond[1], *chunks)
    received = [swap(beyond[0], "col", 1), swap(second, "col", 1)]

    def columns(n, *earlier):
        parts = [backs[0], beside[0], after(beyond[0], *earlier), received[0]]
        if n == 0:
            depths = cuts[:1]
            spots = [[(part, 0)] for part in range(4)]
        else:
            depths = [ahead, cuts[1] - ahead]
            parts += [backs[1], beside[1], beyond[1], received[1]]
            spots = [[(part, cuts[0]), (part + 4, 0)] for part in range(4)]
        out_depths = [cuts[n] // 2] + [cuts[n] // (8 - 4 * n)] * (4 - 2 * n)
        mine, *sent = backward(
            col, count, rows, cols, tile, parts, spots, depths, out_depths, col_blocks
        )
        return [mine] + [swap(part, "row", 1) for part in sent]

    own_sum, far_sum = fuse("far_sums", functools.partial(far_sums, depth), *columns(0, second, beside[1]))
    half_way = lax.ppermute(far_sum, "row", [(i, i ^ (4 if i % 2 else 2)) for i in range(n_row)])
    received[1] = after(received[1], far_sum)
    (chunk,) = fuse("chunk_sum", functools.partial(chunk_sum, depth), second, received[1])
    mine, *from_sibling = columns(1, chunk)
    chunks, *near_sums = near_payloads(row, chunk, swap(chunk, "row", 1), half_way, mine, from_sibling)
    near_sums = [swap(part, "row", k) for part, k in zip(near_sums, near)]
    far_chunks = [swap(chunks, "row", k) for k in far]
    grad_features, grad_weight = finish(row, [0] + far + near, [own_sum] + near_sums, [chunks] + far_chunks)
    return output, grad_weight, grad_features.T


def shards_gathered(features, weight, adj_values, block_rows, block_cols, block_counts, cotangent):
    n_row = lax.axis_size("row")
    n_col = lax.axis_size("col")
    adj = adj_values[0, 0]
    rows = block_rows[0, 0]
    cols = block_cols[0, 0]
    count = block_counts
    size = adj.shape[1]
    nodes = cotangent.shape[0] * n_row * n_col
    row_blocks = cotangent.shape[0] * n_col // size
    col_blocks = features.shape[0] // size
    zero = jnp.zeros((1,), jnp.int32)
    panels = lax.all_gather(features.T, "row", axis=0, tiled=True)
    (terms,) = forward(zero, count, rows, cols, adj, [panels], row_blocks, [panels.shape[0]], [(0,)])
    part = lax.psum_scatter(terms, "col", scatter_dimension=1, tiled=True)
    output, deltas, aggregated, back = middle(1, zero, weight, cotangent, [[part]], (0,), [weight.shape[0]])
    slab = lax.all_gather(back, "col", axis=1, tiled=True)
    (column_terms,) = backward(zero, count, rows, cols, adj, [slab], [[(0, 0)]], [slab.shape[0]], [slab.shape[0]], col_blocks)
    grad_features = lax.psum_scatter(column_terms, "row", scatter_dimension=0, tiled=True).T
    (part,) = gradient(1.0 / math.sqrt(nodes), [(0,)], aggregated, deltas)
    grad_weight = lax.psum(part[0], ("row", "col"))
    return output, grad_weight, grad_features


def solution(mesh):
    n_row = mesh.shape["row"]
    n_col = mesh.shape["col"]
    exchanged = n_row == 8 and n_col == 4
    return jax.shard_map(
        shards_exchanged if exchanged else shards_gathered,
        mesh=mesh,
        in_specs=(
            P("col", "row"),
            P(),
            P("row", "col", None, None, None),
            P("row", "col", None),
            P("row", "col", None),
            P("row", "col"),
            P(("row", "col"), None),
        ),
        out_specs=(P(("row", "col"), None), P(), P("col", "row")),
        check_vma=False,
    )
```

```python
import functools
import math

import jax
import jax.numpy as jnp
from jax import lax
from jax.experimental import pallas as pl
from jax.experimental.pallas import tpu as pltpu
from jax.sharding import PartitionSpec as P

VMEM = pl.BlockSpec(memory_space=pltpu.VMEM)
SMEM = pl.BlockSpec(memory_space=pltpu.SMEM)
HBM = pl.BlockSpec(memory_space=pltpu.HBM)
MIB = 1024 * 1024
NT = (((1,), (1,)), ((), ()))
NN = (((1,), (0,)), ((), ()))


COST = pl.CostEstimate(flops=1, bytes_accessed=1, transcendentals=0)


def params(mib):
    return pltpu.CompilerParams(vmem_limit_bytes=mib * MIB)


def fuse(name, function, *values):
    shapes = jax.eval_shape(function, *values)

    def kernel(*refs):
        results = function(*[ref[...] for ref in refs[: len(values)]])
        for ref, result in zip(refs[len(values) :], results):
            ref[...] = result

    return pl.pallas_call(
        kernel,
        out_shape=shapes,
        in_specs=[VMEM] * len(values),
        out_specs=[VMEM] * len(shapes),
        compiler_params=params(4),
        cost_estimate=COST,
        name=name,
    )(*values)


def turn_of(slots):
    return math.gcd(slots, 8)


def list_size(slots, groups):
    return (slots + groups) // 2 + 8


def pair_up(count, ids, groups, pending, lists, base):
    size = list_size(ids.shape[0], groups)
    for group in range(groups):
        pending[group] = -1

    def visit(slot, entries):
        group = ids[slot]
        partner = pending[group]
        found = partner >= 0
        lists[base + entries] = partner
        lists[base + size + entries] = slot
        pending[group] = jnp.where(found, -1, slot)
        return entries + jnp.where(found, 1, 0)

    def leave(group, entries):
        slot = pending[group]
        lists[base + entries] = slot
        lists[base + size + entries] = slot
        return entries + jnp.where(slot >= 0, 1, 0)

    pairs = lax.fori_loop(0, count, visit, 0)
    lists[base + 2 * size] = lax.fori_loop(0, groups, leave, pairs)
    lists[base + 2 * size + 1] = pairs


def lists_size(slots, groups):
    return sum(2 * list_size(slots, n) + 2 for n in groups)


def product_loop(lists, base, groups, source_ids, target_ids, adj, source, total, dims, axis):
    size = list_size(adj.shape[0], groups)
    width = adj.shape[1]
    spare = total.shape[0] - 1
    turn = 4
    entries = lists[base + 2 * size]
    pairs = lists[base + 2 * size + 1]
    total[...] = jnp.zeros_like(total)

    def step(index, carry):
        for k in range(turn):
            n = index * turn + k
            first = jnp.where(n < entries, lists[base + n], 0)
            second = jnp.where(n < pairs, lists[base + size + n], first)
            blocks = jnp.concatenate([adj[first], adj[second]], axis=axis)
            product = lax.dot_general(
                source[source_ids[first]], blocks, dims, preferred_element_type=jnp.float32
            )
            total[jnp.where(n < entries, target_ids[first], spare)] += product[:, :width]
            total[jnp.where(n < pairs, target_ids[second], spare)] += product[:, width:]
        return carry

    lax.fori_loop(0, (entries + turn - 1) // turn, step, 0)


def fetch_kernel(groups, count, rows, cols, features, tile, *refs):
    outs, lists = refs[:5], refs[5]
    row_ids, col_ids, pending, sem, small_sem = refs[6:]
    half = features.shape[0] // 2
    sources = (rows, cols, rows, cols, features.at[pl.ds(0, half)], features.at[pl.ds(half, half)])
    targets = (row_ids, col_ids, *outs[:4])
    small = [
        pltpu.make_async_copy(source, target, small_sem.at[n])
        for n, (source, target) in enumerate(zip(sources, targets))
    ]
    for copy in small:
        copy.start()
    turn = turn_of(tile.shape[0])

    def copy_turn(index):
        blocks = pl.ds(index * turn, turn)
        return pltpu.make_async_copy(tile.at[blocks], outs[4].at[blocks], sem.at[index])

    def begin(index, carry):
        copy_turn(index).start()
        return carry

    def wait(index, carry):
        copy_turn(index).wait()
        return carry

    turns = (count[0, 0] + turn - 1) // turn
    lax.fori_loop(0, turns, begin, 0)
    for copy in small[:2]:
        copy.wait()
    list_pairs(groups, count[0, 0], row_ids, col_ids, pending, lists)
    lax.fori_loop(0, turns, wait, 0)
    for copy in small[2:]:
        copy.wait()


def list_pairs(groups, count, rows, cols, pending, lists):
    pair_up(count, cols, groups[0], pending, lists, 0)
    pair_up(count, rows, groups[1], pending, lists, 2 * list_size(rows.shape[0], groups[0]) + 2)


def pairs_kernel(groups, count, rows, cols, lists, pending):
    list_pairs(groups, count[0, 0], rows, cols, pending, lists)


def pair_lists(groups, count, rows, cols):
    return pl.pallas_call(
        functools.partial(pairs_kernel, groups),
        out_shape=jax.ShapeDtypeStruct((lists_size(rows.shape[0], groups),), jnp.int32),
        in_specs=[SMEM] * 3,
        out_specs=SMEM,
        scratch_shapes=[pltpu.SMEM((max(groups),), jnp.int32)],
        compiler_params=params(4),
        cost_estimate=COST,
        name="pair_lists",
    )(count, rows, cols)


def fetch(groups, count, rows, cols, features, tile):
    arrays = (rows, cols, features, tile)
    half = jax.ShapeDtypeStruct((features.shape[0] // 2, features.shape[1]), features.dtype)
    outs = [jax.ShapeDtypeStruct(array.shape, array.dtype) for array in (rows, cols)] + [half] * 2
    outs.append(jax.ShapeDtypeStruct(tile.shape, tile.dtype))
    outs.append(jax.ShapeDtypeStruct((lists_size(rows.shape[0], groups),), jnp.int32))
    return pl.pallas_call(
        functools.partial(fetch_kernel, groups),
        out_shape=outs,
        in_specs=[SMEM] + [HBM] * 4,
        out_specs=[VMEM] * 5 + [SMEM],
        scratch_shapes=[
            pltpu.SMEM(rows.shape, rows.dtype),
            pltpu.SMEM(cols.shape, cols.dtype),
            pltpu.SMEM((max(groups),), jnp.int32),
            pltpu.SemaphoreType.DMA((tile.shape[0] // turn_of(tile.shape[0]),)),
            pltpu.SemaphoreType.DMA((6,)),
        ],
        compiler_params=params(4),
        cost_estimate=COST,
        name="fetch",
    )(count, *[pltpu.with_memory_space_constraint(array, pltpu.HBM) for array in arrays])


def forward_kernel(n_parts, depths, layout, place, lists, rows, cols, adj, *refs):
    parts, refs = refs[:n_parts], refs[n_parts:]
    source, total = refs[-2:]
    outs = refs[-2 - len(depths) * len(layout) : -2]
    carried = refs[: len(refs) - 2 - len(outs)]
    size = adj.shape[1]
    row = 0
    for part in parts:
        depth = part.shape[0]
        for c in range(source.shape[0]):
            source[c, row : row + depth, :] = part[:, c * size : (c + 1) * size]
        row += depth
    product_loop(lists, 0, source.shape[0], cols, rows, adj, source, total, NT, 0)
    blocks = outs[0].shape[1] // size
    ahead = carried[0].shape[0] // len(layout[0]) if carried else 0
    outs = iter(outs)
    row = 0
    for depth in depths:
        for m, chunks in enumerate(layout):
            out = next(outs)
            for n, k in enumerate(chunks):
                begin = n * (ahead + depth)
                if ahead:
                    out[begin : begin + ahead, :] = carried[m][n * ahead : (n + 1) * ahead, :]
                first = (place[0] ^ k) * blocks
                for i in range(blocks):
                    out[begin + ahead : begin + ahead + depth, i * size : (i + 1) * size] = total[
                        first + i, row : row + depth, :
                    ].astype(out.dtype)
        row += depth


def forward(place, lists, rows, cols, adj, parts, row_blocks, depths, layout, carried=()):
    size = adj.shape[1]
    col_blocks = parts[0].shape[1] // size
    wide = row_blocks * size // sum(len(chunks) for chunks in layout)
    ahead = carried[0].shape[0] // len(layout[0]) if carried else 0
    outs = [
        jax.ShapeDtypeStruct((len(chunks) * (ahead + depth), wide), jnp.bfloat16)
        for depth in depths
        for chunks in layout
    ]
    return pl.pallas_call(
        functools.partial(forward_kernel, len(parts), depths, layout),
        out_shape=outs,
        in_specs=[SMEM] * 4 + [VMEM] * (1 + len(parts) + len(carried)),
        out_specs=[VMEM] * len(outs),
        scratch_shapes=[
            pltpu.VMEM((col_blocks, sum(depths), size), jnp.bfloat16),
            pltpu.VMEM((row_blocks + 1, sum(depths), size), jnp.float32),
        ],
        compiler_params=params(14),
        cost_estimate=COST,
        name="forward_products",
    )(place, lists, rows, cols, adj, *parts, *carried)


def backward_kernel(spots, depths, place, lists, rows, cols, adj, *refs):
    n_parts = 1 + max(part for places in spots for part, _ in places)
    parts = refs[:n_parts]
    outs = refs[n_parts:-2]
    source, total = refs[-2:]
    size = adj.shape[1]
    blocks = parts[0].shape[1] // size
    for k, places in enumerate(spots):
        first = (place[0] ^ k) * blocks
        row = 0
        for (part, offset), depth in zip(places, depths):
            for i in range(blocks):
                source[first + i, row : row + depth, :] = parts[part][
                    offset : offset + depth, i * size : (i + 1) * size
                ]
            row += depth
    base = 2 * list_size(adj.shape[0], total.shape[0] - 1) + 2
    product_loop(lists, base, source.shape[0], rows, cols, adj, source, total, NN, 1)
    row = 0
    for out in outs:
        depth = out.shape[0]
        for c in range(total.shape[0] - 1):
            out[:, c * size : (c + 1) * size] = total[c, row : row + depth, :].astype(out.dtype)
        row += depth


def backward(place, lists, rows, cols, adj, parts, spots, depths, out_depths, col_blocks):
    size = adj.shape[1]
    row_blocks = len(spots) * parts[0].shape[1] // size
    return pl.pallas_call(
        functools.partial(backward_kernel, spots, depths),
        out_shape=[jax.ShapeDtypeStruct((depth, col_blocks * size), jnp.bfloat16) for depth in out_depths],
        in_specs=[SMEM] * 4 + [VMEM] * (1 + len(parts)),
        out_specs=[VMEM] * len(out_depths),
        scratch_shapes=[
            pltpu.VMEM((row_blocks, sum(out_depths), size), jnp.bfloat16),
            pltpu.VMEM((col_blocks + 1, sum(out_depths), size), jnp.float32),
        ],
        compiler_params=params(14),
        cost_estimate=COST,
        name="backward_products",
    )(place, lists, rows, cols, adj, *parts)


def middle_kernel(sizes, order, n_sum, n_row, row, weight, cotangent, *refs):
    terms = refs[: n_sum * len(sizes)]
    outs = refs[n_sum * len(sizes) : -1]
    output, deltas, aggregated, *backs = outs
    ordered = refs[-1]
    depth = weight.shape[0] // n_row
    for j in range(n_row):
        first = pl.multiple_of((row[0] ^ j) * depth, depth)
        ordered[j * depth : (j + 1) * depth, :] = weight[pl.ds(first, depth), :]
    first = 0
    for p, size in enumerate(sizes):
        summed = terms[p * n_sum][:size, :].astype(jnp.float32)
        for k in range(1, n_sum):
            summed += terms[p * n_sum + k][:size, :].astype(jnp.float32)
        aggregated[first : first + size, :] = summed.astype(jnp.bfloat16)
        first += size
    nodes_first = aggregated[...].T
    preact = jnp.dot(nodes_first, ordered[...], preferred_element_type=jnp.float32)
    gate = jax.nn.sigmoid(preact)
    output[...] = (preact * gate).astype(jnp.bfloat16)
    slopes = gate * (1.0 + preact * (1.0 - gate))
    delta = (cotangent[...].astype(jnp.float32) * slopes).astype(jnp.bfloat16)
    deltas[...] = delta
    product = lax.dot_general(ordered[...], delta, NT, preferred_element_type=jnp.float32)
    product = jnp.concatenate([product[k * depth : (k + 1) * depth, :] for k in order]).astype(jnp.bfloat16)
    first = 0
    for back in backs:
        first %= product.shape[0]
        back[...] = product[first : first + back.shape[0], :]
        first += back.shape[0]


def middle(n_row, row, weight, cotangent, pieces, order, depths):
    sizes = [piece[0].shape[0] for piece in pieces]
    nodes = cotangent.shape[0]
    features = weight.shape[0]
    shape = jax.ShapeDtypeStruct
    outs = [
        shape((nodes, features), jnp.bfloat16),
        shape((nodes, features), jnp.bfloat16),
        shape((features, nodes), jnp.bfloat16),
    ] + [shape((depth, nodes), jnp.bfloat16) for depth in depths]
    flat = [term for piece in pieces for term in piece]
    return pl.pallas_call(
        functools.partial(middle_kernel, sizes, order, len(pieces[0]), n_row),
        out_shape=outs,
        in_specs=[SMEM] + [VMEM] * (2 + len(flat)),
        out_specs=[VMEM] * len(outs),
        scratch_shapes=[pltpu.VMEM(weight.shape, jnp.bfloat16)],
        compiler_params=params(10),
        cost_estimate=COST,
        name="layer",
    )(row, weight, cotangent, *flat)


def gradient_kernel(scale, order, aggregated, deltas, *outs):
    product = jnp.dot(aggregated[...], deltas[...], preferred_element_type=jnp.float32) * scale
    for out, chunks in zip(outs, order):
        depth = out.shape[1]
        for n, k in enumerate(chunks):
            out[n] = product[k * depth : (k + 1) * depth, :]


def gradient(scale, order, aggregated, deltas):
    depth = aggregated.shape[0] // sum(len(chunks) for chunks in order)
    outs = [jax.ShapeDtypeStruct((len(chunks), depth, deltas.shape[1]), jnp.float32) for chunks in order]
    return pl.pallas_call(
        functools.partial(gradient_kernel, scale, order),
        out_shape=outs,
        in_specs=[VMEM] * 2,
        out_specs=[VMEM] * len(outs),
        compiler_params=params(6),
        cost_estimate=COST,
        name="weight_gradient",
    )(aggregated, deltas)


def swap(value, axis, k):
    size = lax.axis_size(axis)
    return lax.ppermute(value, axis, [(i, i ^ k) for i in range(size)])


def wide_sum(*values):
    total = values[0].astype(jnp.float32)
    for value in values[1:]:
        total = total + value.astype(jnp.float32)
    return (total.astype(values[0].dtype),)


def after(value, *earlier):
    return lax.optimization_barrier((value, *earlier))[0]


def with_chunk(rows, *parts):
    total = functools.reduce(jnp.add, parts)
    high = total.astype(jnp.bfloat16)
    low = (total - high.astype(jnp.float32)).astype(jnp.bfloat16)
    return (jnp.concatenate([rows, jnp.concatenate([high, low], axis=1)]),)


def chunk_sum(depth, *values):
    total = None
    for value in values:
        halves = value[-depth:].astype(jnp.float32)
        wide = halves.shape[1] // 2
        chunk = halves[:, :wide] + halves[:, wide:]
        total = chunk if total is None else total + chunk
    return (total,)


def halves_sum(mine, *received):
    total = mine + jnp.concatenate(received)
    half = total.shape[0] // 2
    return total[:half], total[half:]


def far_sums(depth, mine, *received):
    total = mine.astype(jnp.float32) + jnp.concatenate(received).astype(jnp.float32)
    total = total.astype(mine.dtype)
    own, far = total[:depth], total[depth:]
    return own, jnp.concatenate([far, far[:, :128]], axis=1)


def near_kernel(row, chunk, sibling, half_way, mine, *refs):
    received, (chunks, *sums) = refs[: -1 - 2], refs[-1 - 2 :]
    depth = half_way.shape[0]
    nodes = mine.shape[1]
    for k, ref in enumerate((chunk, sibling)):
        wide = ref.shape[1]
        chunks[:, k * wide : (k + 1) * wide] = ref[...].astype(chunks.dtype)
    passed = half_way[:, :nodes].astype(jnp.float32)
    odd = row[0] % 2
    for n, out in enumerate(sums):
        total = mine[n * depth : (n + 1) * depth, :].astype(jnp.float32) + received[n][...].astype(jnp.float32)
        total += jnp.where(odd == 1 - n, passed, 0.0)
        out[:, :nodes] = total.astype(out.dtype)
        out[:, nodes:] = chunks[...]


def near_payloads(row, chunk, sibling, half_way, mine, received):
    depth, nodes = received[0].shape
    wide = 2 * chunk.shape[1]
    shape = jax.ShapeDtypeStruct
    return pl.pallas_call(
        near_kernel,
        out_shape=[shape((depth, wide), mine.dtype)]
        + [shape((depth, nodes + wide), mine.dtype)] * len(received),
        in_specs=[SMEM] + [VMEM] * (4 + len(received)),
        out_specs=[VMEM] * (1 + len(received)),
        compiler_params=params(8),
        cost_estimate=COST,
        name="near_payloads",
    )(row, chunk, sibling, half_way, mine, *received)


def finish_kernel(keys, row, *refs):
    grad_features, grad_weight = refs[-2:]
    depth, nodes = grad_features.shape
    wide = grad_weight.shape[1]
    parts = [ref for ref in refs[:-2] if ref.shape[1] >= nodes]
    values = [ref[...] for ref in refs[:-2] if ref.shape[1] < nodes] + [part[:, nodes:] for part in parts[1:]]
    total = parts[0][...].astype(jnp.float32)
    for part in parts[1:]:
        total += part[:, :nodes].astype(jnp.float32)
    grad_features[...] = total.astype(grad_features.dtype)
    for key, value in zip(keys, values):
        for k in range(2):
            first = pl.multiple_of((row[0] ^ (key + k)) * depth, depth)
            grad_weight[pl.ds(first, depth), :] = value[:, k * wide : (k + 1) * wide].astype(jnp.float32)


def finish(row, keys, parts, chunks):
    depth, nodes = parts[0].shape
    return pl.pallas_call(
        functools.partial(finish_kernel, keys),
        out_shape=[
            jax.ShapeDtypeStruct((depth, nodes), jnp.bfloat16),
            jax.ShapeDtypeStruct((2 * len(keys) * depth, chunks[0].shape[1] // 2), jnp.float32),
        ],
        in_specs=[SMEM] + [VMEM] * (len(parts) + len(chunks)),
        out_specs=[VMEM] * 2,
        compiler_params=params(8),
        cost_estimate=COST,
        name="finish",
    )(row, *parts, *chunks)


def shards_exchanged(features, weight, adj_values, block_rows, block_cols, block_counts, cotangent):
    n_row = lax.axis_size("row")
    n_col = lax.axis_size("col")
    adj = adj_values[0, 0]
    rows = block_rows[0, 0]
    cols = block_cols[0, 0]
    count = block_counts
    size = adj.shape[1]
    nodes = cotangent.shape[0] * n_row * n_col
    row_blocks = cotangent.shape[0] * n_col // size
    col_blocks = features.shape[0] // size
    row = lax.axis_index("row").reshape(1)
    col = lax.axis_index("col").reshape(1)
    own = after(features.T, row, col)

    depth = features.shape[1]
    near = [k for k in range(2, n_row, 2) if k & (k - 1) == 0]
    far = [k for k in range(2, n_row, 2) if k & (k - 1) != 0]
    sibling = swap(own, "row", 1)
    from_near = [swap(own, "row", k) for k in near]
    rows, cols, *halves, tile, lists = fetch((col_blocks, row_blocks), count, rows, cols, own, adj)
    from_near = [after(part, tile) for part in from_near]
    from_far = [swap(half, "row", k) for k in far for half in halves]

    def pass_on(beyond, received):
        return wide_sum(beyond, received[beyond.shape[0] :])

    layout = [(0,), (2,), (1, 3)]

    def fold(kept, beyond, received):
        (passed,) = fuse("pass_on", pass_on, beyond, received)
        return [kept, received, swap(passed, "col", 2)]

    n_near = 2 * depth * (1 + len(near))
    cut = n_near * 5 // 6
    parts = [own, sibling] + [piece for part in from_near for piece in (part, swap(part, "row", 1))]
    kept, beyond, sent, *carried = forward(
        col, lists, rows, cols, tile, parts, row_blocks, [cut, n_near - cut], layout
    )
    received = swap(sent, "col", 1)
    from_far = [after(part, kept) for part in from_far]
    parts = []
    for n in range(0, len(from_far), 2):
        halves = from_far[n : n + 2]
        parts += halves + [swap(half, "row", 1) for half in halves]
    far_piece = forward(
        col, lists, rows, cols, tile, parts, row_blocks, [2 * depth * len(far)], layout, carried
    )
    far_received = swap(far_piece[2], "col", 1)
    first = fold(kept, beyond, after(received, far_piece[0]))
    second = fold(*far_piece[:2], after(far_received, first[1]))
    sums = [first, second]

    groups = [[0] + far, near]
    order = [k + side for group in groups for side in range(2) for k in group]
    cuts = [2 * depth * len(group) for group in groups]
    ahead = depth // 2
    output, deltas, aggregated, back, *backs = middle(
        n_row, row, weight, cotangent, sums, order, [sum(cuts), cuts[0] + ahead, cuts[1] - ahead]
    )
    beside = swap(back, "col", 1)
    beyond = [swap(part, "col", 2) for part in backs]

    even, *odd = gradient(1.0 / math.sqrt(nodes), [(0, 4, 2, 6), (1, 5), (3, 7)], aggregated, deltas)
    even, sent = fuse("gradient_sum", halves_sum, even, *[swap(part, "row", 1) for part in odd])
    even, sent = fuse("gradient_sum", halves_sum, even, swap(sent, "row", 2))
    beyond[0] = after(beyond[0], sent)
    even = after(even, beyond[1])
    (chunk,) = fuse("gradient_sum", lambda a, b: ((a + b)[0],), even, swap(sent, "row", 4))
    chunks = [chunk, swap(chunk, "col", 2)]

    (second,) = fuse("with_chunk", with_chunk, beyond[1], *chunks)
    received = [swap(beyond[0], "col", 1), swap(second, "col", 1)]

    def columns(n, *earlier):
        parts = [back, beside, after(beyond[0], *earlier), received[0], beyond[1], received[1]]
        if n == 0:
            depths = cuts[:1]
            parts = parts[:4]
            spots = [[(part, 0)] for part in range(4)]
        else:
            depths = [ahead, cuts[1] - ahead]
            spots = [[(part, cuts[0]), (part, cuts[0] + ahead)] for part in range(2)]
            spots += [[(part, cuts[0]), (part + 2, 0)] for part in (2, 3)]
        out_depths = [cuts[n] // 2] + [cuts[n] // (8 - 4 * n)] * (4 - 2 * n)
        mine, *sent = backward(
            col, lists, rows, cols, tile, parts, spots, depths, out_depths, col_blocks
        )
        return [mine] + [swap(part, "row", 1) for part in sent]

    own_sum, far_sum = fuse("far_sums", functools.partial(far_sums, depth), *columns(0, second))
    half_way = lax.ppermute(far_sum, "row", [(i, i ^ (4 if i % 2 else 2)) for i in range(n_row)])
    received[1] = after(received[1], far_sum)
    (chunk,) = fuse("chunk_sum", functools.partial(chunk_sum, depth), second, received[1])
    mine, *from_sibling = columns(1, chunk)
    chunks, *near_sums = near_payloads(row, chunk, swap(chunk, "row", 1), half_way, mine, from_sibling)
    near_sums = [swap(part, "row", k) for part, k in zip(near_sums, near)]
    far_chunks = [swap(chunks, "row", k) for k in far]
    grad_features, grad_weight = finish(row, [0] + far + near, [own_sum] + near_sums, [chunks] + far_chunks)
    return output, grad_weight, grad_features.T


def shards_gathered(features, weight, adj_values, block_rows, block_cols, block_counts, cotangent):
    n_row = lax.axis_size("row")
    n_col = lax.axis_size("col")
    adj = adj_values[0, 0]
    rows = block_rows[0, 0]
    cols = block_cols[0, 0]
    count = block_counts
    size = adj.shape[1]
    nodes = cotangent.shape[0] * n_row * n_col
    row_blocks = cotangent.shape[0] * n_col // size
    col_blocks = features.shape[0] // size
    zero = jnp.zeros((1,), jnp.int32)
    lists = pair_lists((col_blocks, row_blocks), count, rows, cols)
    panels = lax.all_gather(features.T, "row", axis=0, tiled=True)
    (terms,) = forward(zero, lists, rows, cols, adj, [panels], row_blocks, [panels.shape[0]], [(0,)])
    part = lax.psum_scatter(terms, "col", scatter_dimension=1, tiled=True)
    output, deltas, aggregated, back = middle(1, zero, weight, cotangent, [[part]], (0,), [weight.shape[0]])
    slab = lax.all_gather(back, "col", axis=1, tiled=True)
    (column_terms,) = backward(zero, lists, rows, cols, adj, [slab], [[(0, 0)]], [slab.shape[0]], [slab.shape[0]], col_blocks)
    grad_features = lax.psum_scatter(column_terms, "row", scatter_dimension=0, tiled=True).T
    (part,) = gradient(1.0 / math.sqrt(nodes), [(0,)], aggregated, deltas)
    grad_weight = lax.psum(part[0], ("row", "col"))
    return output, grad_weight, grad_features


def solution(mesh):
    n_row = mesh.shape["row"]
    n_col = mesh.shape["col"]
    exchanged = n_row == 8 and n_col == 4
    return jax.shard_map(
        shards_exchanged if exchanged else shards_gathered,
        mesh=mesh,
        in_specs=(
            P("col", "row"),
            P(),
            P("row", "col", None, None, None),
            P("row", "col", None),
            P("row", "col", None),
            P("row", "col"),
            P(("row", "col"), None),
        ),
        out_specs=(P(("row", "col"), None), P(), P("col", "row")),
        check_vma=False,
    )
```

```python
import functools
import math

import jax
import jax.numpy as jnp
from jax import lax
from jax.experimental import pallas as pl
from jax.experimental.pallas import tpu as pltpu
from jax.sharding import PartitionSpec as P

VMEM = pl.BlockSpec(memory_space=pltpu.VMEM)
SMEM = pl.BlockSpec(memory_space=pltpu.SMEM)
HBM = pl.BlockSpec(memory_space=pltpu.HBM)
MIB = 1024 * 1024
NT = (((1,), (1,)), ((), ()))
NN = (((1,), (0,)), ((), ()))


COST = pl.CostEstimate(flops=1, bytes_accessed=1, transcendentals=0)


def params(mib):
    return pltpu.CompilerParams(vmem_limit_bytes=mib * MIB)


def fuse(name, function, *values):
    shapes = jax.eval_shape(function, *values)

    def kernel(*refs):
        results = function(*[ref[...] for ref in refs[: len(values)]])
        for ref, result in zip(refs[len(values) :], results):
            ref[...] = result

    return pl.pallas_call(
        kernel,
        out_shape=shapes,
        in_specs=[VMEM] * len(values),
        out_specs=[VMEM] * len(shapes),
        compiler_params=params(4),
        cost_estimate=COST,
        name=name,
    )(*values)


def turn_of(slots):
    return math.gcd(slots, 8)


def list_size(slots, groups):
    return (slots + groups) // 2 + 8


def pair_up(count, ids, groups, pending, lists, base):
    size = list_size(ids.shape[0], groups)
    for group in range(groups):
        pending[group] = -1

    def visit(slot, entries):
        group = ids[slot]
        partner = pending[group]
        found = partner >= 0
        lists[base + entries] = partner
        lists[base + size + entries] = slot
        pending[group] = jnp.where(found, -1, slot)
        return entries + jnp.where(found, 1, 0)

    def leave(group, entries):
        slot = pending[group]
        lists[base + entries] = slot
        lists[base + size + entries] = slot
        return entries + jnp.where(slot >= 0, 1, 0)

    pairs = lax.fori_loop(0, count, visit, 0)
    lists[base + 2 * size] = lax.fori_loop(0, groups, leave, pairs)
    lists[base + 2 * size + 1] = pairs


def lists_size(slots, groups):
    return sum(2 * list_size(slots, n) + 2 for n in groups)


def product_loop(lists, base, groups, source_ids, target_ids, adj, source, total, dims, axis):
    size = list_size(adj.shape[0], groups)
    width = adj.shape[1]
    spare = total.shape[0] - 1
    turn = 4
    entries = lists[base + 2 * size]
    pairs = lists[base + 2 * size + 1]
    total[...] = jnp.zeros_like(total)

    def step(index, carry):
        for k in range(turn):
            n = index * turn + k
            first = jnp.where(n < entries, lists[base + n], 0)
            second = jnp.where(n < pairs, lists[base + size + n], first)
            blocks = jnp.concatenate([adj[first], adj[second]], axis=axis)
            product = lax.dot_general(
                source[source_ids[first]], blocks, dims, preferred_element_type=jnp.float32
            )
            total[jnp.where(n < entries, target_ids[first], spare)] += product[:, :width]
            total[jnp.where(n < pairs, target_ids[second], spare)] += product[:, width:]
        return carry

    lax.fori_loop(0, (entries + turn - 1) // turn, step, 0)


def fetch_kernel(groups, count, rows, cols, features, tile, *refs):
    outs, lists = refs[:5], refs[5]
    row_ids, col_ids, pending, sem, small_sem = refs[6:]
    half = features.shape[0] // 2
    sources = (rows, cols, rows, cols, features.at[pl.ds(0, half)], features.at[pl.ds(half, half)])
    targets = (row_ids, col_ids, *outs[:4])
    small = [
        pltpu.make_async_copy(source, target, small_sem.at[n])
        for n, (source, target) in enumerate(zip(sources, targets))
    ]
    for copy in small:
        copy.start()
    turn = turn_of(tile.shape[0])

    def copy_turn(index):
        blocks = pl.ds(index * turn, turn)
        return pltpu.make_async_copy(tile.at[blocks], outs[4].at[blocks], sem.at[index])

    def begin(index, carry):
        copy_turn(index).start()
        return carry

    def wait(index, carry):
        copy_turn(index).wait()
        return carry

    turns = (count[0, 0] + turn - 1) // turn
    lax.fori_loop(0, turns, begin, 0)
    for copy in small[:2]:
        copy.wait()
    list_pairs(groups, count[0, 0], row_ids, col_ids, pending, lists)
    lax.fori_loop(0, turns, wait, 0)
    for copy in small[2:]:
        copy.wait()


def list_pairs(groups, count, rows, cols, pending, lists):
    pair_up(count, cols, groups[0], pending, lists, 0)
    pair_up(count, rows, groups[1], pending, lists, 2 * list_size(rows.shape[0], groups[0]) + 2)


def pairs_kernel(groups, count, rows, cols, lists, pending):
    list_pairs(groups, count[0, 0], rows, cols, pending, lists)


def pair_lists(groups, count, rows, cols):
    return pl.pallas_call(
        functools.partial(pairs_kernel, groups),
        out_shape=jax.ShapeDtypeStruct((lists_size(rows.shape[0], groups),), jnp.int32),
        in_specs=[SMEM] * 3,
        out_specs=SMEM,
        scratch_shapes=[pltpu.SMEM((max(groups),), jnp.int32)],
        compiler_params=params(4),
        cost_estimate=COST,
        name="pair_lists",
    )(count, rows, cols)


def fetch(groups, count, rows, cols, features, tile):
    arrays = (rows, cols, features, tile)
    half = jax.ShapeDtypeStruct((features.shape[0] // 2, features.shape[1]), features.dtype)
    outs = [jax.ShapeDtypeStruct(array.shape, array.dtype) for array in (rows, cols)] + [half] * 2
    outs.append(jax.ShapeDtypeStruct(tile.shape, tile.dtype))
    outs.append(jax.ShapeDtypeStruct((lists_size(rows.shape[0], groups),), jnp.int32))
    return pl.pallas_call(
        functools.partial(fetch_kernel, groups),
        out_shape=outs,
        in_specs=[SMEM] + [HBM] * 4,
        out_specs=[VMEM] * 5 + [SMEM],
        scratch_shapes=[
            pltpu.SMEM(rows.shape, rows.dtype),
            pltpu.SMEM(cols.shape, cols.dtype),
            pltpu.SMEM((max(groups),), jnp.int32),
            pltpu.SemaphoreType.DMA((tile.shape[0] // turn_of(tile.shape[0]),)),
            pltpu.SemaphoreType.DMA((6,)),
        ],
        compiler_params=params(4),
        cost_estimate=COST,
        name="fetch",
    )(count, *[pltpu.with_memory_space_constraint(array, pltpu.HBM) for array in arrays])


def forward_kernel(n_parts, depths, layout, place, lists, rows, cols, adj, *refs):
    parts, refs = refs[:n_parts], refs[n_parts:]
    source, total = refs[-2:]
    outs = refs[-2 - len(depths) * len(layout) : -2]
    carried = refs[: len(refs) - 2 - len(outs)]
    size = adj.shape[1]
    row = 0
    for part in parts:
        depth = part.shape[0]
        for c in range(source.shape[0]):
            source[c, row : row + depth, :] = part[:, c * size : (c + 1) * size]
        row += depth
    product_loop(lists, 0, source.shape[0], cols, rows, adj, source, total, NT, 0)
    blocks = outs[0].shape[1] // size
    ahead = carried[0].shape[0] // len(layout[0]) if carried else 0
    outs = iter(outs)
    row = 0
    for depth in depths:
        for m, chunks in enumerate(layout):
            out = next(outs)
            for n, k in enumerate(chunks):
                begin = n * (ahead + depth)
                if ahead:
                    out[begin : begin + ahead, :] = carried[m][n * ahead : (n + 1) * ahead, :]
                first = (place[0] ^ k) * blocks
                for i in range(blocks):
                    out[begin + ahead : begin + ahead + depth, i * size : (i + 1) * size] = total[
                        first + i, row : row + depth, :
                    ].astype(out.dtype)
        row += depth


def forward(place, lists, rows, cols, adj, parts, row_blocks, depths, layout, carried=()):
    size = adj.shape[1]
    col_blocks = parts[0].shape[1] // size
    wide = row_blocks * size // sum(len(chunks) for chunks in layout)
    ahead = carried[0].shape[0] // len(layout[0]) if carried else 0
    outs = [
        jax.ShapeDtypeStruct((len(chunks) * (ahead + depth), wide), jnp.bfloat16)
        for depth in depths
        for chunks in layout
    ]
    return pl.pallas_call(
        functools.partial(forward_kernel, len(parts), depths, layout),
        out_shape=outs,
        in_specs=[SMEM] * 4 + [VMEM] * (1 + len(parts) + len(carried)),
        out_specs=[VMEM] * len(outs),
        scratch_shapes=[
            pltpu.VMEM((col_blocks, sum(depths), size), jnp.bfloat16),
            pltpu.VMEM((row_blocks + 1, sum(depths), size), jnp.float32),
        ],
        compiler_params=params(14),
        cost_estimate=COST,
        name="forward_products",
    )(place, lists, rows, cols, adj, *parts, *carried)


def backward_kernel(spots, depths, place, lists, rows, cols, adj, *refs):
    n_parts = 1 + max(part for places in spots for part, _ in places)
    parts = refs[:n_parts]
    outs = refs[n_parts:-2]
    source, total = refs[-2:]
    size = adj.shape[1]
    blocks = parts[0].shape[1] // size
    for k, places in enumerate(spots):
        first = (place[0] ^ k) * blocks
        row = 0
        for (part, offset), depth in zip(places, depths):
            for i in range(blocks):
                source[first + i, row : row + depth, :] = parts[part][
                    offset : offset + depth, i * size : (i + 1) * size
                ]
            row += depth
    base = 2 * list_size(adj.shape[0], total.shape[0] - 1) + 2
    product_loop(lists, base, source.shape[0], rows, cols, adj, source, total, NN, 1)
    row = 0
    for out in outs:
        depth = out.shape[0]
        for c in range(total.shape[0] - 1):
            out[:, c * size : (c + 1) * size] = total[c, row : row + depth, :].astype(out.dtype)
        row += depth


def backward(place, lists, rows, cols, adj, parts, spots, depths, out_depths, col_blocks):
    size = adj.shape[1]
    row_blocks = len(spots) * parts[0].shape[1] // size
    return pl.pallas_call(
        functools.partial(backward_kernel, spots, depths),
        out_shape=[jax.ShapeDtypeStruct((depth, col_blocks * size), jnp.bfloat16) for depth in out_depths],
        in_specs=[SMEM] * 4 + [VMEM] * (1 + len(parts)),
        out_specs=[VMEM] * len(out_depths),
        scratch_shapes=[
            pltpu.VMEM((row_blocks, sum(out_depths), size), jnp.bfloat16),
            pltpu.VMEM((col_blocks + 1, sum(out_depths), size), jnp.float32),
        ],
        compiler_params=params(14),
        cost_estimate=COST,
        name="backward_products",
    )(place, lists, rows, cols, adj, *parts)


def middle_kernel(sizes, order, n_sum, n_row, row, weight, cotangent, *refs):
    terms = refs[: n_sum * len(sizes)]
    outs = refs[n_sum * len(sizes) : -1]
    output, deltas, aggregated, *backs = outs
    ordered = refs[-1]
    depth = weight.shape[0] // n_row
    for j in range(n_row):
        first = pl.multiple_of((row[0] ^ j) * depth, depth)
        ordered[j * depth : (j + 1) * depth, :] = weight[pl.ds(first, depth), :]
    first = 0
    for p, size in enumerate(sizes):
        summed = terms[p * n_sum][:size, :].astype(jnp.float32)
        for k in range(1, n_sum):
            summed += terms[p * n_sum + k][:size, :].astype(jnp.float32)
        aggregated[first : first + size, :] = summed.astype(jnp.bfloat16)
        first += size
    nodes_first = aggregated[...].T
    preact = jnp.dot(nodes_first, ordered[...], preferred_element_type=jnp.float32)
    gate = jax.nn.sigmoid(preact)
    output[...] = (preact * gate).astype(jnp.bfloat16)
    slopes = gate * (1.0 + preact * (1.0 - gate))
    delta = (cotangent[...].astype(jnp.float32) * slopes).astype(jnp.bfloat16)
    deltas[...] = delta
    product = lax.dot_general(ordered[...], delta, NT, preferred_element_type=jnp.float32)
    product = jnp.concatenate([product[k * depth : (k + 1) * depth, :] for k in order]).astype(jnp.bfloat16)
    first = 0
    for back in backs:
        first %= product.shape[0]
        back[...] = product[first : first + back.shape[0], :]
        first += back.shape[0]


def middle(n_row, row, weight, cotangent, pieces, order, depths):
    sizes = [piece[0].shape[0] for piece in pieces]
    nodes = cotangent.shape[0]
    features = weight.shape[0]
    shape = jax.ShapeDtypeStruct
    outs = [
        shape((nodes, features), jnp.bfloat16),
        shape((nodes, features), jnp.bfloat16),
        shape((features, nodes), jnp.bfloat16),
    ] + [shape((depth, nodes), jnp.bfloat16) for depth in depths]
    flat = [term for piece in pieces for term in piece]
    return pl.pallas_call(
        functools.partial(middle_kernel, sizes, order, len(pieces[0]), n_row),
        out_shape=outs,
        in_specs=[SMEM] + [VMEM] * (2 + len(flat)),
        out_specs=[VMEM] * len(outs),
        scratch_shapes=[pltpu.VMEM(weight.shape, jnp.bfloat16)],
        compiler_params=params(10),
        cost_estimate=COST,
        name="layer",
    )(row, weight, cotangent, *flat)


def gradient_kernel(scale, order, aggregated, deltas, *outs):
    product = jnp.dot(aggregated[...], deltas[...], preferred_element_type=jnp.float32) * scale
    for out, chunks in zip(outs, order):
        depth = out.shape[1]
        for n, k in enumerate(chunks):
            out[n] = product[k * depth : (k + 1) * depth, :]


def gradient(scale, order, aggregated, deltas):
    depth = aggregated.shape[0] // sum(len(chunks) for chunks in order)
    outs = [jax.ShapeDtypeStruct((len(chunks), depth, deltas.shape[1]), jnp.float32) for chunks in order]
    return pl.pallas_call(
        functools.partial(gradient_kernel, scale, order),
        out_shape=outs,
        in_specs=[VMEM] * 2,
        out_specs=[VMEM] * len(outs),
        compiler_params=params(6),
        cost_estimate=COST,
        name="weight_gradient",
    )(aggregated, deltas)


def swap(value, axis, k):
    size = lax.axis_size(axis)
    return lax.ppermute(value, axis, [(i, i ^ k) for i in range(size)])


def wide_sum(*values):
    total = values[0].astype(jnp.float32)
    for value in values[1:]:
        total = total + value.astype(jnp.float32)
    return (total.astype(values[0].dtype),)


def after(value, *earlier):
    return lax.optimization_barrier((value, *earlier))[0]


def with_chunk(rows, chunk):
    high = chunk.astype(jnp.bfloat16)
    low = (chunk - high.astype(jnp.float32)).astype(jnp.bfloat16)
    return (jnp.concatenate([rows, jnp.concatenate([high, low], axis=1)]),)


def chunk_sum(depth, *values):
    total = None
    for value in values:
        halves = value[-depth:].astype(jnp.float32)
        wide = halves.shape[1] // 2
        chunk = halves[:, :wide] + halves[:, wide:]
        total = chunk if total is None else total + chunk
    return (total,)


def halves_sum(mine, *received):
    total = mine + jnp.concatenate(received)
    half = total.shape[0] // 2
    return total[:half], total[half:]


def far_sums(depth, mine, *received):
    total = mine.astype(jnp.float32) + jnp.concatenate(received).astype(jnp.float32)
    total = total.astype(mine.dtype)
    own, far = total[:depth], total[depth:]
    return own, jnp.concatenate([far, far[:, :128]], axis=1)


def near_kernel(row, chunk, sibling, half_way, mine, *refs):
    received, (chunks, *sums) = refs[: -1 - 2], refs[-1 - 2 :]
    depth = half_way.shape[0]
    nodes = mine.shape[1]
    for k, ref in enumerate((chunk, sibling)):
        wide = ref.shape[1]
        chunks[:, k * wide : (k + 1) * wide] = ref[...].astype(chunks.dtype)
    passed = half_way[:, :nodes].astype(jnp.float32)
    odd = row[0] % 2
    for n, out in enumerate(sums):
        total = mine[n * depth : (n + 1) * depth, :].astype(jnp.float32) + received[n][...].astype(jnp.float32)
        total += jnp.where(odd == 1 - n, passed, 0.0)
        out[:, :nodes] = total.astype(out.dtype)
        out[:, nodes:] = chunks[...]


def near_payloads(row, chunk, sibling, half_way, mine, received):
    depth, nodes = received[0].shape
    wide = 2 * chunk.shape[1]
    shape = jax.ShapeDtypeStruct
    return pl.pallas_call(
        near_kernel,
        out_shape=[shape((depth, wide), mine.dtype)]
        + [shape((depth, nodes + wide), mine.dtype)] * len(received),
        in_specs=[SMEM] + [VMEM] * (4 + len(received)),
        out_specs=[VMEM] * (1 + len(received)),
        compiler_params=params(8),
        cost_estimate=COST,
        name="near_payloads",
    )(row, chunk, sibling, half_way, mine, *received)


def finish_kernel(keys, row, *refs):
    grad_features, grad_weight = refs[-2:]
    depth, nodes = grad_features.shape
    wide = grad_weight.shape[1]
    parts = [ref for ref in refs[:-2] if ref.shape[1] >= nodes]
    values = [ref[...] for ref in refs[:-2] if ref.shape[1] < nodes] + [part[:, nodes:] for part in parts[1:]]
    total = parts[0][...].astype(jnp.float32)
    for part in parts[1:]:
        total += part[:, :nodes].astype(jnp.float32)
    grad_features[...] = total.astype(grad_features.dtype)
    for key, value in zip(keys, values):
        for k in range(2):
            first = pl.multiple_of((row[0] ^ (key + k)) * depth, depth)
            grad_weight[pl.ds(first, depth), :] = value[:, k * wide : (k + 1) * wide].astype(jnp.float32)


def finish(row, keys, parts, chunks):
    depth, nodes = parts[0].shape
    return pl.pallas_call(
        functools.partial(finish_kernel, keys),
        out_shape=[
            jax.ShapeDtypeStruct((depth, nodes), jnp.bfloat16),
            jax.ShapeDtypeStruct((2 * len(keys) * depth, chunks[0].shape[1] // 2), jnp.float32),
        ],
        in_specs=[SMEM] + [VMEM] * (len(parts) + len(chunks)),
        out_specs=[VMEM] * 2,
        compiler_params=params(8),
        cost_estimate=COST,
        name="finish",
    )(row, *parts, *chunks)


def shards_exchanged(features, weight, adj_values, block_rows, block_cols, block_counts, cotangent):
    n_row = lax.axis_size("row")
    n_col = lax.axis_size("col")
    adj = adj_values[0, 0]
    rows = block_rows[0, 0]
    cols = block_cols[0, 0]
    count = block_counts
    size = adj.shape[1]
    nodes = cotangent.shape[0] * n_row * n_col
    row_blocks = cotangent.shape[0] * n_col // size
    col_blocks = features.shape[0] // size
    row = lax.axis_index("row").reshape(1)
    col = lax.axis_index("col").reshape(1)
    own = after(features.T, row, col)

    depth = features.shape[1]
    near = [k for k in range(2, n_row, 2) if k & (k - 1) == 0]
    far = [k for k in range(2, n_row, 2) if k & (k - 1) != 0]
    sibling = swap(own, "row", 1)
    from_near = [swap(own, "row", k) for k in near]
    rows, cols, *halves, tile, lists = fetch((col_blocks, row_blocks), count, rows, cols, own, adj)
    from_near = [after(part, tile) for part in from_near]
    from_far = [swap(half, "row", k) for k in far for half in halves]

    def pass_on(beyond, received):
        return wide_sum(beyond, received[beyond.shape[0] :])

    layout = [(0,), (2,), (1, 3)]

    def fold(kept, beyond, received):
        (passed,) = fuse("pass_on", pass_on, beyond, received)
        return [kept, received, swap(passed, "col", 2)]

    n_near = 2 * depth * (1 + len(near))
    cut = n_near * 5 // 6
    parts = [own, sibling] + [piece for part in from_near for piece in (part, swap(part, "row", 1))]
    kept, beyond, sent, *carried = forward(
        col, lists, rows, cols, tile, parts, row_blocks, [cut, n_near - cut], layout
    )
    received = swap(sent, "col", 1)
    from_far = [after(part, kept) for part in from_far]
    parts = []
    for n in range(0, len(from_far), 2):
        halves = from_far[n : n + 2]
        parts += halves + [swap(half, "row", 1) for half in halves]
    far_piece = forward(
        col, lists, rows, cols, tile, parts, row_blocks, [2 * depth * len(far)], layout, carried
    )
    far_received = swap(far_piece[2], "col", 1)
    first = fold(kept, beyond, after(received, far_piece[0]))
    second = fold(*far_piece[:2], after(far_received, first[1]))
    sums = [first, second]

    groups = [[0] + far, near]
    order = [k + side for group in groups for side in range(2) for k in group]
    cuts = [2 * depth * len(group) for group in groups]
    ahead = depth // 2
    output, deltas, aggregated, back, *backs = middle(
        n_row, row, weight, cotangent, sums, order, [sum(cuts), cuts[0] + ahead, cuts[1] - ahead]
    )
    beside = swap(back, "col", 1)
    beyond = [swap(part, "col", 2) for part in backs]

    even, *odd = gradient(1.0 / math.sqrt(nodes), [(0, 4, 2, 6), (1, 5), (3, 7)], aggregated, deltas)
    even, sent = fuse("gradient_sum", halves_sum, even, *[swap(part, "row", 1) for part in odd])
    even, sent = fuse("gradient_sum", halves_sum, even, swap(sent, "row", 2))
    beyond[0] = after(beyond[0], sent)
    even = after(even, beyond[1])
    (chunk,) = fuse("gradient_sum", lambda a, b: ((a + b)[0],), even, swap(sent, "row", 4))
    (second,) = fuse("with_chunk", with_chunk, beyond[1], chunk)
    received = [swap(beyond[0], "col", 1), swap(second, "col", 1)]

    def columns(n, *earlier):
        parts = [back, beside, after(beyond[0], *earlier), received[0], beyond[1], received[1]]
        if n == 0:
            depths = cuts[:1]
            parts = parts[:4]
            spots = [[(part, 0)] for part in range(4)]
        else:
            depths = [ahead, cuts[1] - ahead]
            spots = [[(part, cuts[0]), (part, cuts[0] + ahead)] for part in range(2)]
            spots += [[(part, cuts[0]), (part + 2, 0)] for part in (2, 3)]
        out_depths = [cuts[n] // 2] + [cuts[n] // (8 - 4 * n)] * (4 - 2 * n)
        mine, *sent = backward(
            col, lists, rows, cols, tile, parts, spots, depths, out_depths, col_blocks
        )
        return [mine] + [swap(part, "row", 1) for part in sent]

    own_sum, far_sum = fuse("far_sums", functools.partial(far_sums, depth), *columns(0, second))
    half_way = lax.ppermute(far_sum, "row", [(i, i ^ (4 if i % 2 else 2)) for i in range(n_row)])
    (chunk,) = fuse("chunk_sum", functools.partial(chunk_sum, depth), second, received[1])
    (chunk,) = fuse("chunk_sum", wide_sum, chunk, swap(chunk, "col", 2))
    mine, *from_sibling = columns(1, chunk, far_sum)
    chunks, *near_sums = near_payloads(row, chunk, swap(chunk, "row", 1), half_way, mine, from_sibling)
    near_sums = [swap(part, "row", k) for part, k in zip(near_sums, near)]
    far_chunks = [swap(chunks, "row", k) for k in far]
    grad_features, grad_weight = finish(row, [0] + far + near, [own_sum] + near_sums, [chunks] + far_chunks)
    return output, grad_weight, grad_features.T


def shards_gathered(features, weight, adj_values, block_rows, block_cols, block_counts, cotangent):
    n_row = lax.axis_size("row")
    n_col = lax.axis_size("col")
    adj = adj_values[0, 0]
    rows = block_rows[0, 0]
    cols = block_cols[0, 0]
    count = block_counts
    size = adj.shape[1]
    nodes = cotangent.shape[0] * n_row * n_col
    row_blocks = cotangent.shape[0] * n_col // size
    col_blocks = features.shape[0] // size
    zero = jnp.zeros((1,), jnp.int32)
    lists = pair_lists((col_blocks, row_blocks), count, rows, cols)
    panels = lax.all_gather(features.T, "row", axis=0, tiled=True)
    (terms,) = forward(zero, lists, rows, cols, adj, [panels], row_blocks, [panels.shape[0]], [(0,)])
    part = lax.psum_scatter(terms, "col", scatter_dimension=1, tiled=True)
    output, deltas, aggregated, back = middle(1, zero, weight, cotangent, [[part]], (0,), [weight.shape[0]])
    slab = lax.all_gather(back, "col", axis=1, tiled=True)
    (column_terms,) = backward(zero, lists, rows, cols, adj, [slab], [[(0, 0)]], [slab.shape[0]], [slab.shape[0]], col_blocks)
    grad_features = lax.psum_scatter(column_terms, "row", scatter_dimension=0, tiled=True).T
    (part,) = gradient(1.0 / math.sqrt(nodes), [(0,)], aggregated, deltas)
    grad_weight = lax.psum(part[0], ("row", "col"))
    return output, grad_weight, grad_features


def solution(mesh):
    n_row = mesh.shape["row"]
    n_col = mesh.shape["col"]
    exchanged = n_row == 8 and n_col == 4
    return jax.shard_map(
        shards_exchanged if exchanged else shards_gathered,
        mesh=mesh,
        in_specs=(
            P("col", "row"),
            P(),
            P("row", "col", None, None, None),
            P("row", "col", None),
            P("row", "col", None),
            P("row", "col"),
            P(("row", "col"), None),
        ),
        out_specs=(P(("row", "col"), None), P(), P("col", "row")),
        check_vma=False,
    )
```

```python
import functools
import math

import jax
import jax.numpy as jnp
from jax import lax
from jax.experimental import pallas as pl
from jax.experimental.pallas import tpu as pltpu
from jax.sharding import PartitionSpec as P

VMEM = pl.BlockSpec(memory_space=pltpu.VMEM)
SMEM = pl.BlockSpec(memory_space=pltpu.SMEM)
HBM = pl.BlockSpec(memory_space=pltpu.HBM)
MIB = 1024 * 1024
NT = (((1,), (1,)), ((), ()))
NN = (((1,), (0,)), ((), ()))


COST = pl.CostEstimate(flops=1, bytes_accessed=1, transcendentals=0)


def params(mib):
    return pltpu.CompilerParams(vmem_limit_bytes=mib * MIB)


def fuse(name, function, *values):
    shapes = jax.eval_shape(function, *values)

    def kernel(*refs):
        results = function(*[ref[...] for ref in refs[: len(values)]])
        for ref, result in zip(refs[len(values) :], results):
            ref[...] = result

    return pl.pallas_call(
        kernel,
        out_shape=shapes,
        in_specs=[VMEM] * len(values),
        out_specs=[VMEM] * len(shapes),
        compiler_params=params(4),
        cost_estimate=COST,
        name=name,
    )(*values)


def turn_of(slots):
    return math.gcd(slots, 8)


def product_loop(count, source_ids, target_ids, adj, source, total, dims):
    turn = turn_of(adj.shape[0])
    spare = total.shape[0] - 1
    total[...] = jnp.zeros_like(total)

    def step(index, carry):
        first = index * turn
        for k in range(turn):
            slot = first + k
            product = lax.dot_general(
                source[source_ids[slot]], adj[slot], dims, preferred_element_type=jnp.float32
            )
            target = jnp.where(slot < count, target_ids[slot], spare)
            total[target] += product
        return carry

    lax.fori_loop(0, (count + turn - 1) // turn, step, 0)


def fetch_kernel(count, rows, cols, features, tile, *refs):
    outs, (sem, small_sem) = refs[:5], refs[5:]
    half = features.shape[0] // 2
    sources = (rows, cols, features.at[pl.ds(0, half)], features.at[pl.ds(half, half)])
    small = [
        pltpu.make_async_copy(source, target, small_sem.at[n])
        for n, (source, target) in enumerate(zip(sources, outs))
    ]
    for copy in small:
        copy.start()
    turn = turn_of(tile.shape[0])

    def copy_turn(index):
        blocks = pl.ds(index * turn, turn)
        return pltpu.make_async_copy(tile.at[blocks], outs[4].at[blocks], sem.at[index])

    def begin(index, carry):
        copy_turn(index).start()
        return carry

    def wait(index, carry):
        copy_turn(index).wait()
        return carry

    turns = (count[0, 0] + turn - 1) // turn
    lax.fori_loop(0, turns, begin, 0)
    lax.fori_loop(0, turns, wait, 0)
    for copy in small:
        copy.wait()


def fetch(count, rows, cols, features, tile):
    arrays = (rows, cols, features, tile)
    half = jax.ShapeDtypeStruct((features.shape[0] // 2, features.shape[1]), features.dtype)
    outs = [jax.ShapeDtypeStruct(array.shape, array.dtype) for array in (rows, cols)] + [half] * 2
    return pl.pallas_call(
        fetch_kernel,
        out_shape=outs + [jax.ShapeDtypeStruct(tile.shape, tile.dtype)],
        in_specs=[SMEM] + [HBM] * 4,
        out_specs=[VMEM] * 5,
        scratch_shapes=[
            pltpu.SemaphoreType.DMA((tile.shape[0] // turn_of(tile.shape[0]),)),
            pltpu.SemaphoreType.DMA((4,)),
        ],
        compiler_params=params(4),
        cost_estimate=COST,
        name="fetch",
    )(count, *[pltpu.with_memory_space_constraint(array, pltpu.HBM) for array in arrays])


def forward_kernel(n_parts, depths, layout, place, count, rows, cols, adj, *refs):
    parts, refs = refs[:n_parts], refs[n_parts:]
    source, total = refs[-2:]
    outs = refs[-2 - len(depths) * len(layout) : -2]
    carried = refs[: len(refs) - 2 - len(outs)]
    size = adj.shape[1]
    row = 0
    for part in parts:
        depth = part.shape[0]
        for c in range(source.shape[0]):
            source[c, row : row + depth, :] = part[:, c * size : (c + 1) * size]
        row += depth
    product_loop(count[0, 0], cols, rows, adj, source, total, NT)
    blocks = outs[0].shape[1] // size
    ahead = carried[0].shape[0] // len(layout[0]) if carried else 0
    outs = iter(outs)
    row = 0
    for depth in depths:
        for m, chunks in enumerate(layout):
            out = next(outs)
            for n, k in enumerate(chunks):
                begin = n * (ahead + depth)
                if ahead:
                    out[begin : begin + ahead, :] = carried[m][n * ahead : (n + 1) * ahead, :]
                first = (place[0] ^ k) * blocks
                for i in range(blocks):
                    out[begin + ahead : begin + ahead + depth, i * size : (i + 1) * size] = total[
                        first + i, row : row + depth, :
                    ].astype(out.dtype)
        row += depth


def forward(place, count, rows, cols, adj, parts, row_blocks, depths, layout, carried=()):
    size = adj.shape[1]
    col_blocks = parts[0].shape[1] // size
    wide = row_blocks * size // sum(len(chunks) for chunks in layout)
    ahead = carried[0].shape[0] // len(layout[0]) if carried else 0
    outs = [
        jax.ShapeDtypeStruct((len(chunks) * (ahead + depth), wide), jnp.bfloat16)
        for depth in depths
        for chunks in layout
    ]
    return pl.pallas_call(
        functools.partial(forward_kernel, len(parts), depths, layout),
        out_shape=outs,
        in_specs=[SMEM] * 4 + [VMEM] * (1 + len(parts) + len(carried)),
        out_specs=[VMEM] * len(outs),
        scratch_shapes=[
            pltpu.VMEM((col_blocks, sum(depths), size), jnp.bfloat16),
            pltpu.VMEM((row_blocks + 1, sum(depths), size), jnp.float32),
        ],
        compiler_params=params(14),
        cost_estimate=COST,
        name="forward_products",
    )(place, count, rows, cols, adj, *parts, *carried)


def backward_kernel(spots, depths, place, count, rows, cols, adj, *refs):
    n_parts = 1 + max(part for places in spots for part, _ in places)
    parts = refs[:n_parts]
    outs = refs[n_parts:-2]
    source, total = refs[-2:]
    size = adj.shape[1]
    blocks = parts[0].shape[1] // size
    for k, places in enumerate(spots):
        first = (place[0] ^ k) * blocks
        row = 0
        for (part, offset), depth in zip(places, depths):
            for i in range(blocks):
                source[first + i, row : row + depth, :] = parts[part][
                    offset : offset + depth, i * size : (i + 1) * size
                ]
            row += depth
    product_loop(count[0, 0], rows, cols, adj, source, total, NN)
    row = 0
    for out in outs:
        depth = out.shape[0]
        for c in range(total.shape[0] - 1):
            out[:, c * size : (c + 1) * size] = total[c, row : row + depth, :].astype(out.dtype)
        row += depth


def backward(place, count, rows, cols, adj, parts, spots, depths, out_depths, col_blocks):
    size = adj.shape[1]
    row_blocks = len(spots) * parts[0].shape[1] // size
    return pl.pallas_call(
        functools.partial(backward_kernel, spots, depths),
        out_shape=[jax.ShapeDtypeStruct((depth, col_blocks * size), jnp.bfloat16) for depth in out_depths],
        in_specs=[SMEM] * 4 + [VMEM] * (1 + len(parts)),
        out_specs=[VMEM] * len(out_depths),
        scratch_shapes=[
            pltpu.VMEM((row_blocks, sum(out_depths), size), jnp.bfloat16),
            pltpu.VMEM((col_blocks + 1, sum(out_depths), size), jnp.float32),
        ],
        compiler_params=params(14),
        cost_estimate=COST,
        name="backward_products",
    )(place, count, rows, cols, adj, *parts)


def middle_kernel(sizes, order, n_sum, n_row, row, weight, cotangent, *refs):
    terms = refs[: n_sum * len(sizes)]
    outs = refs[n_sum * len(sizes) : -1]
    output, deltas, aggregated, *backs = outs
    ordered = refs[-1]
    depth = weight.shape[0] // n_row
    for j in range(n_row):
        first = pl.multiple_of((row[0] ^ j) * depth, depth)
        ordered[j * depth : (j + 1) * depth, :] = weight[pl.ds(first, depth), :]
    first = 0
    for p, size in enumerate(sizes):
        summed = terms[p * n_sum][:size, :].astype(jnp.float32)
        for k in range(1, n_sum):
            summed += terms[p * n_sum + k][:size, :].astype(jnp.float32)
        aggregated[first : first + size, :] = summed.astype(jnp.bfloat16)
        first += size
    nodes_first = aggregated[...].T
    preact = jnp.dot(nodes_first, ordered[...], preferred_element_type=jnp.float32)
    gate = jax.nn.sigmoid(preact)
    output[...] = (preact * gate).astype(jnp.bfloat16)
    slopes = gate * (1.0 + preact * (1.0 - gate))
    delta = (cotangent[...].astype(jnp.float32) * slopes).astype(jnp.bfloat16)
    deltas[...] = delta
    product = lax.dot_general(ordered[...], delta, NT, preferred_element_type=jnp.float32)
    product = jnp.concatenate([product[k * depth : (k + 1) * depth, :] for k in order]).astype(jnp.bfloat16)
    first = 0
    for back in backs:
        first %= product.shape[0]
        back[...] = product[first : first + back.shape[0], :]
        first += back.shape[0]


def middle(n_row, row, weight, cotangent, pieces, order, depths):
    sizes = [piece[0].shape[0] for piece in pieces]
    nodes = cotangent.shape[0]
    features = weight.shape[0]
    shape = jax.ShapeDtypeStruct
    outs = [
        shape((nodes, features), jnp.bfloat16),
        shape((nodes, features), jnp.bfloat16),
        shape((features, nodes), jnp.bfloat16),
    ] + [shape((depth, nodes), jnp.bfloat16) for depth in depths]
    flat = [term for piece in pieces for term in piece]
    return pl.pallas_call(
        functools.partial(middle_kernel, sizes, order, len(pieces[0]), n_row),
        out_shape=outs,
        in_specs=[SMEM] + [VMEM] * (2 + len(flat)),
        out_specs=[VMEM] * len(outs),
        scratch_shapes=[pltpu.VMEM(weight.shape, jnp.bfloat16)],
        compiler_params=params(10),
        cost_estimate=COST,
        name="layer",
    )(row, weight, cotangent, *flat)


def gradient_kernel(scale, order, aggregated, deltas, *outs):
    product = jnp.dot(aggregated[...], deltas[...], preferred_element_type=jnp.float32) * scale
    for out, chunks in zip(outs, order):
        depth = out.shape[1]
        for n, k in enumerate(chunks):
            out[n] = product[k * depth : (k + 1) * depth, :]


def gradient(scale, order, aggregated, deltas):
    depth = aggregated.shape[0] // sum(len(chunks) for chunks in order)
    outs = [jax.ShapeDtypeStruct((len(chunks), depth, deltas.shape[1]), jnp.float32) for chunks in order]
    return pl.pallas_call(
        functools.partial(gradient_kernel, scale, order),
        out_shape=outs,
        in_specs=[VMEM] * 2,
        out_specs=[VMEM] * len(outs),
        compiler_params=params(6),
        cost_estimate=COST,
        name="weight_gradient",
    )(aggregated, deltas)


def swap(value, axis, k):
    size = lax.axis_size(axis)
    return lax.ppermute(value, axis, [(i, i ^ k) for i in range(size)])


def wide_sum(*values):
    total = values[0].astype(jnp.float32)
    for value in values[1:]:
        total = total + value.astype(jnp.float32)
    return (total.astype(values[0].dtype),)


def after(value, *earlier):
    return lax.optimization_barrier((value, *earlier))[0]


def with_chunk(rows, chunk):
    high = chunk.astype(jnp.bfloat16)
    low = (chunk - high.astype(jnp.float32)).astype(jnp.bfloat16)
    return (jnp.concatenate([rows, jnp.concatenate([high, low], axis=1)]),)


def chunk_sum(depth, *values):
    total = None
    for value in values:
        halves = value[-depth:].astype(jnp.float32)
        wide = halves.shape[1] // 2
        chunk = halves[:, :wide] + halves[:, wide:]
        total = chunk if total is None else total + chunk
    return (total,)


def halves_sum(mine, *received):
    total = mine + jnp.concatenate(received)
    half = total.shape[0] // 2
    return total[:half], total[half:]


def far_sums(mine, received):
    total = mine[: received.shape[0]].astype(jnp.float32) + received.astype(jnp.float32)
    total = total.astype(mine.dtype)
    return (jnp.concatenate([total, total[:, :128]], axis=1),)


def near_kernel(row, chunk, sibling, half_way, mine, *refs):
    depth, nodes = half_way.shape[0], mine.shape[1]
    n_sums = mine.shape[0] // depth - 1
    received, (chunks, *sums) = refs[:n_sums], refs[n_sums:]
    for k, ref in enumerate((chunk, sibling)):
        wide = ref.shape[1]
        chunks[:, k * wide : (k + 1) * wide] = ref[...].astype(chunks.dtype)
    passed = half_way[:, :nodes].astype(jnp.float32)
    odd = row[0] % 2
    for n, out in enumerate(sums):
        first = (n + 1) * depth
        total = mine[first : first + depth, :].astype(jnp.float32) + received[n][...].astype(jnp.float32)
        if n:
            total += jnp.where(odd == 2 - n, passed, 0.0)
            out[:, nodes:] = chunks[...]
        out[:, :nodes] = total.astype(out.dtype)


def near_payloads(row, chunk, sibling, half_way, mine, received):
    depth, nodes = received[0].shape
    wide = 2 * chunk.shape[1]
    shapes = [(depth, wide), (depth, nodes)] + [(depth, nodes + wide)] * (len(received) - 1)
    return pl.pallas_call(
        near_kernel,
        out_shape=[jax.ShapeDtypeStruct(shape, mine.dtype) for shape in shapes],
        in_specs=[SMEM] + [VMEM] * (4 + len(received)),
        out_specs=[VMEM] * len(shapes),
        compiler_params=params(8),
        cost_estimate=COST,
        name="near_payloads",
    )(row, chunk, sibling, half_way, mine, *received)


def finish_kernel(keys, row, *refs):
    grad_features, grad_weight = refs[-2:]
    depth, nodes = grad_features.shape
    wide = grad_weight.shape[1]
    parts = [ref for ref in refs[:-2] if ref.shape[1] >= nodes]
    values = [ref[...] for ref in refs[:-2] if ref.shape[1] < nodes] + [part[:, nodes:] for part in parts[1:]]
    total = parts[0][...].astype(jnp.float32)
    for part in parts[1:]:
        total += part[:, :nodes].astype(jnp.float32)
    grad_features[...] = total.astype(grad_features.dtype)
    for key, value in zip(keys, values):
        for k in range(2):
            first = pl.multiple_of((row[0] ^ (key + k)) * depth, depth)
            grad_weight[pl.ds(first, depth), :] = value[:, k * wide : (k + 1) * wide].astype(jnp.float32)


def finish(row, keys, parts, chunks):
    depth, nodes = parts[0].shape
    return pl.pallas_call(
        functools.partial(finish_kernel, keys),
        out_shape=[
            jax.ShapeDtypeStruct((depth, nodes), jnp.bfloat16),
            jax.ShapeDtypeStruct((2 * len(keys) * depth, chunks[0].shape[1] // 2), jnp.float32),
        ],
        in_specs=[SMEM] + [VMEM] * (len(parts) + len(chunks)),
        out_specs=[VMEM] * 2,
        compiler_params=params(8),
        cost_estimate=COST,
        name="finish",
    )(row, *parts, *chunks)


def shards_exchanged(features, weight, adj_values, block_rows, block_cols, block_counts, cotangent):
    n_row = lax.axis_size("row")
    n_col = lax.axis_size("col")
    adj = adj_values[0, 0]
    rows = block_rows[0, 0]
    cols = block_cols[0, 0]
    count = block_counts
    size = adj.shape[1]
    nodes = cotangent.shape[0] * n_row * n_col
    row_blocks = cotangent.shape[0] * n_col // size
    col_blocks = features.shape[0] // size
    row = lax.axis_index("row").reshape(1)
    col = lax.axis_index("col").reshape(1)
    own = after(features.T, row, col)

    depth = features.shape[1]
    near = [k for k in range(2, n_row, 2) if k & (k - 1) == 0]
    far = [k for k in range(2, n_row, 2) if k & (k - 1) != 0]
    sibling = swap(own, "row", 1)
    from_near = [swap(own, "row", k) for k in near]
    rows, cols, *halves, tile = fetch(count, rows, cols, own, adj)
    from_near = [after(part, tile) for part in from_near]
    from_far = [swap(half, "row", k) for k in far for half in halves]

    def pass_on(beyond, received):
        return wide_sum(beyond, received[beyond.shape[0] :])

    layout = [(0,), (2,), (1, 3)]

    def fold(kept, beyond, received):
        (passed,) = fuse("pass_on", pass_on, beyond, received)
        return [kept, received, swap(passed, "col", 2)]

    n_near = 2 * depth * (1 + len(near))
    cut = n_near * 5 // 6
    parts = [own, sibling] + [piece for part in from_near for piece in (part, swap(part, "row", 1))]
    kept, beyond, sent, *carried = forward(
        col, count, rows, cols, tile, parts, row_blocks, [cut, n_near - cut], layout
    )
    received = swap(sent, "col", 1)
    from_far = [after(part, kept) for part in from_far]
    parts = []
    for n in range(0, len(from_far), 2):
        halves = from_far[n : n + 2]
        parts += halves + [swap(half, "row", 1) for half in halves]
    far_piece = forward(
        col, count, rows, cols, tile, parts, row_blocks, [2 * depth * len(far)], layout, carried
    )
    far_received = swap(far_piece[2], "col", 1)
    first = fold(kept, beyond, after(received, far_piece[0]))
    second = fold(*far_piece[:2], after(far_received, first[1]))
    sums = [first, second]

    keys = far + [0] + near
    order = keys + [k + 1 for k in keys]
    cut = weight.shape[0] // 2 + depth
    cuts = [cut, weight.shape[0] - cut]
    output, deltas, aggregated, back, *backs = middle(
        n_row, row, weight, cotangent, sums, order, [sum(cuts)] + cuts
    )
    beside = swap(back, "col", 1)
    beyond = [swap(part, "col", 2) for part in backs]

    even, *odd = gradient(1.0 / math.sqrt(nodes), [(0, 4, 2, 6), (1, 5), (3, 7)], aggregated, deltas)
    even, sent = fuse("gradient_sum", halves_sum, even, *[swap(part, "row", 1) for part in odd])
    even, sent = fuse("gradient_sum", halves_sum, even, swap(sent, "row", 2))
    beyond[0] = after(beyond[0], sent)
    even = after(even, beyond[1])
    (chunk,) = fuse("gradient_sum", lambda a, b: ((a + b)[0],), even, swap(sent, "row", 4))
    (second,) = fuse("with_chunk", with_chunk, beyond[1], chunk)
    received = [swap(beyond[0], "col", 1), swap(second, "col", 1)]

    (chunk,) = fuse("chunk_sum", functools.partial(chunk_sum, depth), second, received[1])

    parts = [back, beside, beyond[0], received[0], beyond[1], after(received[1], chunk)]
    spots = [[(part, 0), (part, cut)] for part in range(2)] + [[(part, 0), (part + 2, 0)] for part in (2, 3)]
    out_depths = [depth * len(keys)] + [depth] * len(keys)
    mine, *sent = backward(col, count, rows, cols, tile, parts, spots, cuts, out_depths, col_blocks)
    from_sibling = [swap(part, "row", 1) for part in sent]
    (chunk,) = fuse("chunk_sum", wide_sum, chunk, swap(chunk, "col", 2))

    (far_sum,) = fuse("far_sums", far_sums, mine, from_sibling[0])
    half_way = lax.ppermute(far_sum, "row", [(i, i ^ (4 if i % 2 else 2)) for i in range(n_row)])
    chunks, own_sum, *near_sums = near_payloads(
        row, chunk, swap(chunk, "row", 1), half_way, mine, from_sibling[1:]
    )
    near_sums = [swap(part, "row", k) for part, k in zip(near_sums, near)]
    far_chunks = [swap(chunks, "row", k) for k in far]
    grad_features, grad_weight = finish(row, [0] + far + near, [own_sum] + near_sums, [chunks] + far_chunks)
    return output, grad_weight, grad_features.T


def shards_gathered(features, weight, adj_values, block_rows, block_cols, block_counts, cotangent):
    n_row = lax.axis_size("row")
    n_col = lax.axis_size("col")
    adj = adj_values[0, 0]
    rows = block_rows[0, 0]
    cols = block_cols[0, 0]
    count = block_counts
    size = adj.shape[1]
    nodes = cotangent.shape[0] * n_row * n_col
    row_blocks = cotangent.shape[0] * n_col // size
    col_blocks = features.shape[0] // size
    zero = jnp.zeros((1,), jnp.int32)
    panels = lax.all_gather(features.T, "row", axis=0, tiled=True)
    (terms,) = forward(zero, count, rows, cols, adj, [panels], row_blocks, [panels.shape[0]], [(0,)])
    part = lax.psum_scatter(terms, "col", scatter_dimension=1, tiled=True)
    output, deltas, aggregated, back = middle(1, zero, weight, cotangent, [[part]], (0,), [weight.shape[0]])
    slab = lax.all_gather(back, "col", axis=1, tiled=True)
    (column_terms,) = backward(zero, count, rows, cols, adj, [slab], [[(0, 0)]], [slab.shape[0]], [slab.shape[0]], col_blocks)
    grad_features = lax.psum_scatter(column_terms, "row", scatter_dimension=0, tiled=True).T
    (part,) = gradient(1.0 / math.sqrt(nodes), [(0,)], aggregated, deltas)
    grad_weight = lax.psum(part[0], ("row", "col"))
    return output, grad_weight, grad_features


def solution(mesh):
    n_row = mesh.shape["row"]
    n_col = mesh.shape["col"]
    exchanged = n_row == 8 and n_col == 4
    return jax.shard_map(
        shards_exchanged if exchanged else shards_gathered,
        mesh=mesh,
        in_specs=(
            P("col", "row"),
            P(),
            P("row", "col", None, None, None),
            P("row", "col", None),
            P("row", "col", None),
            P("row", "col"),
            P(("row", "col"), None),
        ),
        out_specs=(P(("row", "col"), None), P(), P("col", "row")),
        check_vma=False,
    )
```

```python
import functools
import math

import jax
import jax.numpy as jnp
from jax import lax
from jax.experimental import pallas as pl
from jax.experimental.pallas import tpu as pltpu
from jax.sharding import PartitionSpec as P

VMEM = pl.BlockSpec(memory_space=pltpu.VMEM)
SMEM = pl.BlockSpec(memory_space=pltpu.SMEM)
HBM = pl.BlockSpec(memory_space=pltpu.HBM)
MIB = 1024 * 1024
NT = (((1,), (1,)), ((), ()))
NN = (((1,), (0,)), ((), ()))


COST = pl.CostEstimate(flops=1, bytes_accessed=1, transcendentals=0)


def params(mib):
    return pltpu.CompilerParams(vmem_limit_bytes=mib * MIB)


def fuse(name, function, *values):
    shapes = jax.eval_shape(function, *values)

    def kernel(*refs):
        results = function(*[ref[...] for ref in refs[: len(values)]])
        for ref, result in zip(refs[len(values) :], results):
            ref[...] = result

    return pl.pallas_call(
        kernel,
        out_shape=shapes,
        in_specs=[VMEM] * len(values),
        out_specs=[VMEM] * len(shapes),
        compiler_params=params(4),
        cost_estimate=COST,
        name=name,
    )(*values)


def turn_of(slots):
    return math.gcd(slots, 8)


def product_loop(count, source_ids, target_ids, adj, source, total, dims):
    turn = turn_of(adj.shape[0])
    spare = total.shape[0] - 1
    total[...] = jnp.zeros_like(total)

    def step(index, carry):
        first = index * turn
        for k in range(turn):
            slot = first + k
            product = lax.dot_general(
                source[source_ids[slot]], adj[slot], dims, preferred_element_type=jnp.float32
            )
            target = jnp.where(slot < count, target_ids[slot], spare)
            total[target] += product
        return carry

    lax.fori_loop(0, (count + turn - 1) // turn, step, 0)


def fetch_kernel(count, rows, cols, features, tile, *refs):
    outs, (sem, small_sem) = refs[:5], refs[5:]
    half = features.shape[0] // 2
    sources = (rows, cols, features.at[pl.ds(0, half)], features.at[pl.ds(half, half)])
    small = [
        pltpu.make_async_copy(source, target, small_sem.at[n])
        for n, (source, target) in enumerate(zip(sources, outs))
    ]
    for copy in small:
        copy.start()
    turn = turn_of(tile.shape[0])

    def copy_turn(index):
        blocks = pl.ds(index * turn, turn)
        return pltpu.make_async_copy(tile.at[blocks], outs[4].at[blocks], sem.at[index])

    def begin(index, carry):
        copy_turn(index).start()
        return carry

    def wait(index, carry):
        copy_turn(index).wait()
        return carry

    turns = (count[0, 0] + turn - 1) // turn
    lax.fori_loop(0, turns, begin, 0)
    lax.fori_loop(0, turns, wait, 0)
    for copy in small:
        copy.wait()


def fetch(count, rows, cols, features, tile):
    arrays = (rows, cols, features, tile)
    half = jax.ShapeDtypeStruct((features.shape[0] // 2, features.shape[1]), features.dtype)
    outs = [jax.ShapeDtypeStruct(array.shape, array.dtype) for array in (rows, cols)] + [half] * 2
    return pl.pallas_call(
        fetch_kernel,
        out_shape=outs + [jax.ShapeDtypeStruct(tile.shape, tile.dtype)],
        in_specs=[SMEM] + [HBM] * 4,
        out_specs=[VMEM] * 5,
        scratch_shapes=[
            pltpu.SemaphoreType.DMA((tile.shape[0] // turn_of(tile.shape[0]),)),
            pltpu.SemaphoreType.DMA((4,)),
        ],
        compiler_params=params(4),
        cost_estimate=COST,
        name="fetch",
    )(count, *[pltpu.with_memory_space_constraint(array, pltpu.HBM) for array in arrays])


def forward_kernel(n_parts, depths, layout, place, count, rows, cols, adj, *refs):
    parts, refs = refs[:n_parts], refs[n_parts:]
    source, total = refs[-2:]
    outs = refs[-2 - len(depths) * len(layout) : -2]
    carried = refs[: len(refs) - 2 - len(outs)]
    size = adj.shape[1]
    row = 0
    for part in parts:
        depth = part.shape[0]
        for c in range(source.shape[0]):
            source[c, row : row + depth, :] = part[:, c * size : (c + 1) * size]
        row += depth
    product_loop(count[0, 0], cols, rows, adj, source, total, NT)
    blocks = outs[0].shape[1] // size
    ahead = carried[0].shape[0] // len(layout[0]) if carried else 0
    outs = iter(outs)
    row = 0
    for depth in depths:
        for m, chunks in enumerate(layout):
            out = next(outs)
            for n, k in enumerate(chunks):
                begin = n * (ahead + depth)
                if ahead:
                    out[begin : begin + ahead, :] = carried[m][n * ahead : (n + 1) * ahead, :]
                first = (place[0] ^ k) * blocks
                for i in range(blocks):
                    out[begin + ahead : begin + ahead + depth, i * size : (i + 1) * size] = total[
                        first + i, row : row + depth, :
                    ].astype(out.dtype)
        row += depth


def forward(place, count, rows, cols, adj, parts, row_blocks, depths, layout, carried=()):
    size = adj.shape[1]
    col_blocks = parts[0].shape[1] // size
    wide = row_blocks * size // sum(len(chunks) for chunks in layout)
    ahead = carried[0].shape[0] // len(layout[0]) if carried else 0
    outs = [
        jax.ShapeDtypeStruct((len(chunks) * (ahead + depth), wide), jnp.bfloat16)
        for depth in depths
        for chunks in layout
    ]
    return pl.pallas_call(
        functools.partial(forward_kernel, len(parts), depths, layout),
        out_shape=outs,
        in_specs=[SMEM] * 4 + [VMEM] * (1 + len(parts) + len(carried)),
        out_specs=[VMEM] * len(outs),
        scratch_shapes=[
            pltpu.VMEM((col_blocks, sum(depths), size), jnp.bfloat16),
            pltpu.VMEM((row_blocks + 1, sum(depths), size), jnp.float32),
        ],
        compiler_params=params(14),
        cost_estimate=COST,
        name="forward_products",
    )(place, count, rows, cols, adj, *parts, *carried)


def backward_kernel(spots, depths, place, count, rows, cols, adj, *refs):
    n_parts = 1 + max(part for places in spots for part, _ in places)
    parts = refs[:n_parts]
    outs = refs[n_parts:-2]
    source, total = refs[-2:]
    size = adj.shape[1]
    blocks = parts[0].shape[1] // size
    for k, places in enumerate(spots):
        first = (place[0] ^ k) * blocks
        row = 0
        for (part, offset), depth in zip(places, depths):
            for i in range(blocks):
                source[first + i, row : row + depth, :] = parts[part][
                    offset : offset + depth, i * size : (i + 1) * size
                ]
            row += depth
    product_loop(count[0, 0], rows, cols, adj, source, total, NN)
    row = 0
    for out in outs:
        depth = out.shape[0]
        for c in range(total.shape[0] - 1):
            out[:, c * size : (c + 1) * size] = total[c, row : row + depth, :].astype(out.dtype)
        row += depth


def backward(place, count, rows, cols, adj, parts, spots, depths, out_depths, col_blocks):
    size = adj.shape[1]
    row_blocks = len(spots) * parts[0].shape[1] // size
    return pl.pallas_call(
        functools.partial(backward_kernel, spots, depths),
        out_shape=[jax.ShapeDtypeStruct((depth, col_blocks * size), jnp.bfloat16) for depth in out_depths],
        in_specs=[SMEM] * 4 + [VMEM] * (1 + len(parts)),
        out_specs=[VMEM] * len(out_depths),
        scratch_shapes=[
            pltpu.VMEM((row_blocks, sum(out_depths), size), jnp.bfloat16),
            pltpu.VMEM((col_blocks + 1, sum(out_depths), size), jnp.float32),
        ],
        compiler_params=params(14),
        cost_estimate=COST,
        name="backward_products",
    )(place, count, rows, cols, adj, *parts)


def middle_kernel(sizes, order, n_sum, n_row, row, weight, cotangent, *refs):
    terms = refs[: n_sum * len(sizes)]
    outs = refs[n_sum * len(sizes) : -1]
    output, deltas, aggregated, *backs = outs
    ordered = refs[-1]
    depth = weight.shape[0] // n_row
    for j in range(n_row):
        first = pl.multiple_of((row[0] ^ j) * depth, depth)
        ordered[j * depth : (j + 1) * depth, :] = weight[pl.ds(first, depth), :]
    first = 0
    for p, size in enumerate(sizes):
        summed = terms[p * n_sum][:size, :].astype(jnp.float32)
        for k in range(1, n_sum):
            summed += terms[p * n_sum + k][:size, :].astype(jnp.float32)
        aggregated[first : first + size, :] = summed.astype(jnp.bfloat16)
        first += size
    nodes_first = aggregated[...].T
    preact = jnp.dot(nodes_first, ordered[...], preferred_element_type=jnp.float32)
    gate = jax.nn.sigmoid(preact)
    output[...] = (preact * gate).astype(jnp.bfloat16)
    slopes = gate * (1.0 + preact * (1.0 - gate))
    delta = (cotangent[...].astype(jnp.float32) * slopes).astype(jnp.bfloat16)
    deltas[...] = delta
    product = lax.dot_general(ordered[...], delta, NT, preferred_element_type=jnp.float32)
    product = jnp.concatenate([product[k * depth : (k + 1) * depth, :] for k in order]).astype(jnp.bfloat16)
    first = 0
    for back in backs:
        first %= product.shape[0]
        back[...] = product[first : first + back.shape[0], :]
        first += back.shape[0]


def middle(n_row, row, weight, cotangent, pieces, order, depths):
    sizes = [piece[0].shape[0] for piece in pieces]
    nodes = cotangent.shape[0]
    features = weight.shape[0]
    shape = jax.ShapeDtypeStruct
    outs = [
        shape((nodes, features), jnp.bfloat16),
        shape((nodes, features), jnp.bfloat16),
        shape((features, nodes), jnp.bfloat16),
    ] + [shape((depth, nodes), jnp.bfloat16) for depth in depths]
    flat = [term for piece in pieces for term in piece]
    return pl.pallas_call(
        functools.partial(middle_kernel, sizes, order, len(pieces[0]), n_row),
        out_shape=outs,
        in_specs=[SMEM] + [VMEM] * (2 + len(flat)),
        out_specs=[VMEM] * len(outs),
        scratch_shapes=[pltpu.VMEM(weight.shape, jnp.bfloat16)],
        compiler_params=params(10),
        cost_estimate=COST,
        name="layer",
    )(row, weight, cotangent, *flat)


def gradient_kernel(scale, order, aggregated, deltas, *outs):
    product = jnp.dot(aggregated[...], deltas[...], preferred_element_type=jnp.float32) * scale
    for out, chunks in zip(outs, order):
        depth = out.shape[1]
        for n, k in enumerate(chunks):
            out[n] = product[k * depth : (k + 1) * depth, :]


def gradient(scale, order, aggregated, deltas):
    depth = aggregated.shape[0] // sum(len(chunks) for chunks in order)
    outs = [jax.ShapeDtypeStruct((len(chunks), depth, deltas.shape[1]), jnp.float32) for chunks in order]
    return pl.pallas_call(
        functools.partial(gradient_kernel, scale, order),
        out_shape=outs,
        in_specs=[VMEM] * 2,
        out_specs=[VMEM] * len(outs),
        compiler_params=params(6),
        cost_estimate=COST,
        name="weight_gradient",
    )(aggregated, deltas)


def swap(value, axis, k):
    size = lax.axis_size(axis)
    return lax.ppermute(value, axis, [(i, i ^ k) for i in range(size)])


def wide_sum(*values):
    total = values[0].astype(jnp.float32)
    for value in values[1:]:
        total = total + value.astype(jnp.float32)
    return (total.astype(values[0].dtype),)


def after(value, *earlier):
    return lax.optimization_barrier((value, *earlier))[0]


def with_chunk(rows, chunk):
    high = chunk.astype(jnp.bfloat16)
    low = (chunk - high.astype(jnp.float32)).astype(jnp.bfloat16)
    return (jnp.concatenate([rows, jnp.concatenate([high, low], axis=1)]),)


def chunk_sum(depth, *values):
    total = None
    for value in values:
        halves = value[-depth:].astype(jnp.float32)
        wide = halves.shape[1] // 2
        chunk = halves[:, :wide] + halves[:, wide:]
        total = chunk if total is None else total + chunk
    return (total,)


def halves_sum(mine, *received):
    total = mine + jnp.concatenate(received)
    half = total.shape[0] // 2
    return total[:half], total[half:]


def far_sums(mine, received):
    total = mine[: received.shape[0]].astype(jnp.float32) + received.astype(jnp.float32)
    total = total.astype(mine.dtype)
    return (jnp.concatenate([total, total[:, :128]], axis=1),)


def near_kernel(row, chunk, sibling, half_way, mine, *refs):
    depth, nodes = half_way.shape[0], mine.shape[1]
    n_sums = mine.shape[0] // depth - 1
    received, (chunks, *sums) = refs[:n_sums], refs[n_sums:]
    for k, ref in enumerate((chunk, sibling)):
        wide = ref.shape[1]
        chunks[:, k * wide : (k + 1) * wide] = ref[...].astype(chunks.dtype)
    passed = half_way[:, :nodes].astype(jnp.float32)
    odd = row[0] % 2
    for n, out in enumerate(sums):
        first = (n + 1) * depth
        total = mine[first : first + depth, :].astype(jnp.float32) + received[n][...].astype(jnp.float32)
        if n:
            total += jnp.where(odd == 2 - n, passed, 0.0)
            out[:, nodes:] = chunks[...]
        out[:, :nodes] = total.astype(out.dtype)


def near_payloads(row, chunk, sibling, half_way, mine, received):
    depth, nodes = received[0].shape
    wide = 2 * chunk.shape[1]
    shapes = [(depth, wide), (depth, nodes)] + [(depth, nodes + wide)] * (len(received) - 1)
    return pl.pallas_call(
        near_kernel,
        out_shape=[jax.ShapeDtypeStruct(shape, mine.dtype) for shape in shapes],
        in_specs=[SMEM] + [VMEM] * (4 + len(received)),
        out_specs=[VMEM] * len(shapes),
        compiler_params=params(8),
        cost_estimate=COST,
        name="near_payloads",
    )(row, chunk, sibling, half_way, mine, *received)


def finish_kernel(keys, row, *refs):
    grad_features, grad_weight = refs[-2:]
    depth, nodes = grad_features.shape
    wide = grad_weight.shape[1]
    parts = [ref for ref in refs[:-2] if ref.shape[1] >= nodes]
    values = [ref[...] for ref in refs[:-2] if ref.shape[1] < nodes] + [part[:, nodes:] for part in parts[1:]]
    total = parts[0][...].astype(jnp.float32)
    for part in parts[1:]:
        total += part[:, :nodes].astype(jnp.float32)
    grad_features[...] = total.astype(grad_features.dtype)
    for key, value in zip(keys, values):
        for k in range(2):
            first = pl.multiple_of((row[0] ^ (key + k)) * depth, depth)
            grad_weight[pl.ds(first, depth), :] = value[:, k * wide : (k + 1) * wide].astype(jnp.float32)


def finish(row, keys, parts, chunks):
    depth, nodes = parts[0].shape
    return pl.pallas_call(
        functools.partial(finish_kernel, keys),
        out_shape=[
            jax.ShapeDtypeStruct((depth, nodes), jnp.bfloat16),
            jax.ShapeDtypeStruct((2 * len(keys) * depth, chunks[0].shape[1] // 2), jnp.float32),
        ],
        in_specs=[SMEM] + [VMEM] * (len(parts) + len(chunks)),
        out_specs=[VMEM] * 2,
        compiler_params=params(8),
        cost_estimate=COST,
        name="finish",
    )(row, *parts, *chunks)


def shards_exchanged(features, weight, adj_values, block_rows, block_cols, block_counts, cotangent):
    n_row = lax.axis_size("row")
    n_col = lax.axis_size("col")
    adj = adj_values[0, 0]
    rows = block_rows[0, 0]
    cols = block_cols[0, 0]
    count = block_counts
    size = adj.shape[1]
    nodes = cotangent.shape[0] * n_row * n_col
    row_blocks = cotangent.shape[0] * n_col // size
    col_blocks = features.shape[0] // size
    row = lax.axis_index("row").reshape(1)
    col = lax.axis_index("col").reshape(1)
    own = after(features.T, row, col)

    depth = features.shape[1]
    near = [k for k in range(2, n_row, 2) if k & (k - 1) == 0]
    far = [k for k in range(2, n_row, 2) if k & (k - 1) != 0]
    sibling = swap(own, "row", 1)
    from_near = [swap(own, "row", k) for k in near]
    rows, cols, *halves, tile = fetch(count, rows, cols, own, adj)
    from_near = [after(part, tile) for part in from_near]
    from_far = [swap(half, "row", k) for k in far for half in halves]

    def pass_on(beyond, received):
        return wide_sum(beyond, received[beyond.shape[0] :])

    layout = [(0,), (2,), (1, 3)]

    def fold(kept, beyond, received):
        (passed,) = fuse("pass_on", pass_on, beyond, received)
        return [kept, received, swap(passed, "col", 2)]

    n_near = 2 * depth * (1 + len(near))
    cut = n_near * 5 // 6
    parts = [own, sibling] + [piece for part in from_near for piece in (part, swap(part, "row", 1))]
    kept, beyond, sent, *carried = forward(
        col, count, rows, cols, tile, parts, row_blocks, [cut, n_near - cut], layout
    )
    received = swap(sent, "col", 1)
    from_far = [after(part, kept) for part in from_far]
    parts = []
    for n in range(0, len(from_far), 2):
        halves = from_far[n : n + 2]
        parts += halves + [swap(half, "row", 1) for half in halves]
    far_piece = forward(
        col, count, rows, cols, tile, parts, row_blocks, [2 * depth * len(far)], layout, carried
    )
    far_received = swap(far_piece[2], "col", 1)
    first = fold(kept, beyond, after(received, far_piece[0]))
    second = fold(*far_piece[:2], after(far_received, first[1]))
    sums = [first, second]

    keys = far + [0] + near
    order = keys + [k + 1 for k in keys]
    cut = weight.shape[0] // 2 + depth
    cuts = [cut, weight.shape[0] - cut]
    output, deltas, aggregated, back, *backs = middle(
        n_row, row, weight, cotangent, sums, order, [sum(cuts)] + cuts
    )
    beside = swap(back, "col", 1)
    beyond = [swap(part, "col", 2) for part in backs]

    even, *odd = gradient(1.0 / math.sqrt(nodes), [(0, 4, 2, 6), (1, 5), (3, 7)], aggregated, deltas)
    even, sent = fuse("gradient_sum", halves_sum, even, *[swap(part, "row", 1) for part in odd])
    even, sent = fuse("gradient_sum", halves_sum, even, swap(sent, "row", 2))
    beyond[0] = after(beyond[0], sent)
    received = [swap(beyond[0], "col", 1)]
    even = after(even, beyond[1], beside)
    (chunk,) = fuse("gradient_sum", lambda a, b: ((a + b)[0],), even, swap(sent, "row", 4))
    (second,) = fuse("with_chunk", with_chunk, beyond[1], chunk)
    received.append(swap(second, "col", 1))

    (chunk,) = fuse("chunk_sum", functools.partial(chunk_sum, depth), second, received[1])

    parts = [back, beside, beyond[0], received[0], beyond[1], after(received[1], chunk)]
    spots = [[(part, 0), (part, cut)] for part in range(2)] + [[(part, 0), (part + 2, 0)] for part in (2, 3)]
    out_depths = [depth * len(keys)] + [depth] * len(keys)
    mine, *sent = backward(col, count, rows, cols, tile, parts, spots, cuts, out_depths, col_blocks)
    from_sibling = [swap(part, "row", 1) for part in sent]
    (chunk,) = fuse("chunk_sum", wide_sum, chunk, swap(chunk, "col", 2))

    mine = after(mine, chunk)
    (far_sum,) = fuse("far_sums", far_sums, mine, from_sibling[0])
    half_way = lax.ppermute(far_sum, "row", [(i, i ^ (4 if i % 2 else 2)) for i in range(n_row)])
    chunks, own_sum, *near_sums = near_payloads(
        row, chunk, swap(chunk, "row", 1), half_way, mine, from_sibling[1:]
    )
    near_sums = [swap(part, "row", k) for part, k in zip(near_sums, near)]
    far_chunks = [swap(chunks, "row", k) for k in far]
    grad_features, grad_weight = finish(row, [0] + far + near, [own_sum] + near_sums, [chunks] + far_chunks)
    return output, grad_weight, grad_features.T


def shards_gathered(features, weight, adj_values, block_rows, block_cols, block_counts, cotangent):
    n_row = lax.axis_size("row")
    n_col = lax.axis_size("col")
    adj = adj_values[0, 0]
    rows = block_rows[0, 0]
    cols = block_cols[0, 0]
    count = block_counts
    size = adj.shape[1]
    nodes = cotangent.shape[0] * n_row * n_col
    row_blocks = cotangent.shape[0] * n_col // size
    col_blocks = features.shape[0] // size
    zero = jnp.zeros((1,), jnp.int32)
    panels = lax.all_gather(features.T, "row", axis=0, tiled=True)
    (terms,) = forward(zero, count, rows, cols, adj, [panels], row_blocks, [panels.shape[0]], [(0,)])
    part = lax.psum_scatter(terms, "col", scatter_dimension=1, tiled=True)
    output, deltas, aggregated, back = middle(1, zero, weight, cotangent, [[part]], (0,), [weight.shape[0]])
    slab = lax.all_gather(back, "col", axis=1, tiled=True)
    (column_terms,) = backward(zero, count, rows, cols, adj, [slab], [[(0, 0)]], [slab.shape[0]], [slab.shape[0]], col_blocks)
    grad_features = lax.psum_scatter(column_terms, "row", scatter_dimension=0, tiled=True).T
    (part,) = gradient(1.0 / math.sqrt(nodes), [(0,)], aggregated, deltas)
    grad_weight = lax.psum(part[0], ("row", "col"))
    return output, grad_weight, grad_features


def solution(mesh):
    n_row = mesh.shape["row"]
    n_col = mesh.shape["col"]
    exchanged = n_row == 8 and n_col == 4
    return jax.shard_map(
        shards_exchanged if exchanged else shards_gathered,
        mesh=mesh,
        in_specs=(
            P("col", "row"),
            P(),
            P("row", "col", None, None, None),
            P("row", "col", None),
            P("row", "col", None),
            P("row", "col"),
            P(("row", "col"), None),
        ),
        out_specs=(P(("row", "col"), None), P(), P("col", "row")),
        check_vma=False,
    )
```

```python
import functools
import math

import jax
import jax.numpy as jnp
from jax import lax
from jax.experimental import pallas as pl
from jax.experimental.pallas import tpu as pltpu
from jax.sharding import PartitionSpec as P

VMEM = pl.BlockSpec(memory_space=pltpu.VMEM)
SMEM = pl.BlockSpec(memory_space=pltpu.SMEM)
HBM = pl.BlockSpec(memory_space=pltpu.HBM)
MIB = 1024 * 1024
NT = (((1,), (1,)), ((), ()))
NN = (((1,), (0,)), ((), ()))


COST = pl.CostEstimate(flops=1, bytes_accessed=1, transcendentals=0)


def params(mib):
    return pltpu.CompilerParams(vmem_limit_bytes=mib * MIB)


def fuse(name, function, *values):
    shapes = jax.eval_shape(function, *values)

    def kernel(*refs):
        results = function(*[ref[...] for ref in refs[: len(values)]])
        for ref, result in zip(refs[len(values) :], results):
            ref[...] = result

    return pl.pallas_call(
        kernel,
        out_shape=shapes,
        in_specs=[VMEM] * len(values),
        out_specs=[VMEM] * len(shapes),
        compiler_params=params(4),
        cost_estimate=COST,
        name=name,
    )(*values)


def turn_of(slots):
    return math.gcd(slots, 8)


def product_loop(count, source_ids, target_ids, adj, source, total, dims):
    turn = turn_of(adj.shape[0])
    spare = total.shape[0] - 1
    total[...] = jnp.zeros_like(total)

    def step(index, carry):
        first = index * turn
        for k in range(turn):
            slot = first + k
            product = lax.dot_general(
                source[source_ids[slot]], adj[slot], dims, preferred_element_type=jnp.float32
            )
            target = jnp.where(slot < count, target_ids[slot], spare)
            total[target] += product
        return carry

    lax.fori_loop(0, (count + turn - 1) // turn, step, 0)


def fetch_kernel(count, rows, cols, features, tile, *refs):
    outs, (sem, small_sem) = refs[:5], refs[5:]
    half = features.shape[0] // 2
    sources = (rows, cols, features.at[pl.ds(0, half)], features.at[pl.ds(half, half)])
    small = [
        pltpu.make_async_copy(source, target, small_sem.at[n])
        for n, (source, target) in enumerate(zip(sources, outs))
    ]
    for copy in small:
        copy.start()
    turn = turn_of(tile.shape[0])

    def copy_turn(index):
        blocks = pl.ds(index * turn, turn)
        return pltpu.make_async_copy(tile.at[blocks], outs[4].at[blocks], sem.at[index])

    def begin(index, carry):
        copy_turn(index).start()
        return carry

    def wait(index, carry):
        copy_turn(index).wait()
        return carry

    turns = (count[0, 0] + turn - 1) // turn
    lax.fori_loop(0, turns, begin, 0)
    lax.fori_loop(0, turns, wait, 0)
    for copy in small:
        copy.wait()


def fetch(count, rows, cols, features, tile):
    arrays = (rows, cols, features, tile)
    half = jax.ShapeDtypeStruct((features.shape[0] // 2, features.shape[1]), features.dtype)
    outs = [jax.ShapeDtypeStruct(array.shape, array.dtype) for array in (rows, cols)] + [half] * 2
    return pl.pallas_call(
        fetch_kernel,
        out_shape=outs + [jax.ShapeDtypeStruct(tile.shape, tile.dtype)],
        in_specs=[SMEM] + [HBM] * 4,
        out_specs=[VMEM] * 5,
        scratch_shapes=[
            pltpu.SemaphoreType.DMA((tile.shape[0] // turn_of(tile.shape[0]),)),
            pltpu.SemaphoreType.DMA((4,)),
        ],
        compiler_params=params(4),
        cost_estimate=COST,
        name="fetch",
    )(count, *[pltpu.with_memory_space_constraint(array, pltpu.HBM) for array in arrays])


def forward_kernel(n_parts, depths, layout, place, count, rows, cols, adj, *refs):
    parts, refs = refs[:n_parts], refs[n_parts:]
    source, total = refs[-2:]
    outs = refs[-2 - len(depths) * len(layout) : -2]
    carried = refs[: len(refs) - 2 - len(outs)]
    size = adj.shape[1]
    row = 0
    for part in parts:
        depth = part.shape[0]
        for c in range(source.shape[0]):
            source[c, row : row + depth, :] = part[:, c * size : (c + 1) * size]
        row += depth
    product_loop(count[0, 0], cols, rows, adj, source, total, NT)
    blocks = outs[0].shape[1] // size
    ahead = carried[0].shape[0] // len(layout[0]) if carried else 0
    outs = iter(outs)
    row = 0
    for depth in depths:
        for m, chunks in enumerate(layout):
            out = next(outs)
            for n, k in enumerate(chunks):
                begin = n * (ahead + depth)
                if ahead:
                    out[begin : begin + ahead, :] = carried[m][n * ahead : (n + 1) * ahead, :]
                first = (place[0] ^ k) * blocks
                for i in range(blocks):
                    out[begin + ahead : begin + ahead + depth, i * size : (i + 1) * size] = total[
                        first + i, row : row + depth, :
                    ].astype(out.dtype)
        row += depth


def forward(place, count, rows, cols, adj, parts, row_blocks, depths, layout, carried=()):
    size = adj.shape[1]
    col_blocks = parts[0].shape[1] // size
    wide = row_blocks * size // sum(len(chunks) for chunks in layout)
    ahead = carried[0].shape[0] // len(layout[0]) if carried else 0
    outs = [
        jax.ShapeDtypeStruct((len(chunks) * (ahead + depth), wide), jnp.bfloat16)
        for depth in depths
        for chunks in layout
    ]
    return pl.pallas_call(
        functools.partial(forward_kernel, len(parts), depths, layout),
        out_shape=outs,
        in_specs=[SMEM] * 4 + [VMEM] * (1 + len(parts) + len(carried)),
        out_specs=[VMEM] * len(outs),
        scratch_shapes=[
            pltpu.VMEM((col_blocks, sum(depths), size), jnp.bfloat16),
            pltpu.VMEM((row_blocks + 1, sum(depths), size), jnp.float32),
        ],
        compiler_params=params(14),
        cost_estimate=COST,
        name="forward_products",
    )(place, count, rows, cols, adj, *parts, *carried)


def backward_kernel(spots, depths, place, count, rows, cols, adj, *refs):
    n_parts = 1 + max(part for places in spots for part, _ in places)
    parts = refs[:n_parts]
    outs = refs[n_parts:-2]
    source, total = refs[-2:]
    size = adj.shape[1]
    blocks = parts[0].shape[1] // size
    for k, places in enumerate(spots):
        first = (place[0] ^ k) * blocks
        row = 0
        for (part, offset), depth in zip(places, depths):
            for i in range(blocks):
                source[first + i, row : row + depth, :] = parts[part][
                    offset : offset + depth, i * size : (i + 1) * size
                ]
            row += depth
    product_loop(count[0, 0], rows, cols, adj, source, total, NN)
    row = 0
    for out in outs:
        depth = out.shape[0]
        for c in range(total.shape[0] - 1):
            out[:, c * size : (c + 1) * size] = total[c, row : row + depth, :].astype(out.dtype)
        row += depth


def backward(place, count, rows, cols, adj, parts, spots, depths, out_depths, col_blocks):
    size = adj.shape[1]
    row_blocks = len(spots) * parts[0].shape[1] // size
    return pl.pallas_call(
        functools.partial(backward_kernel, spots, depths),
        out_shape=[jax.ShapeDtypeStruct((depth, col_blocks * size), jnp.bfloat16) for depth in out_depths],
        in_specs=[SMEM] * 4 + [VMEM] * (1 + len(parts)),
        out_specs=[VMEM] * len(out_depths),
        scratch_shapes=[
            pltpu.VMEM((row_blocks, sum(out_depths), size), jnp.bfloat16),
            pltpu.VMEM((col_blocks + 1, sum(out_depths), size), jnp.float32),
        ],
        compiler_params=params(14),
        cost_estimate=COST,
        name="backward_products",
    )(place, count, rows, cols, adj, *parts)


def middle_kernel(sizes, order, n_sum, n_row, row, weight, cotangent, *refs):
    terms = refs[: n_sum * len(sizes)]
    outs = refs[n_sum * len(sizes) : -1]
    output, deltas, aggregated, *backs = outs
    ordered = refs[-1]
    depth = weight.shape[0] // n_row
    for j in range(n_row):
        first = pl.multiple_of((row[0] ^ j) * depth, depth)
        ordered[j * depth : (j + 1) * depth, :] = weight[pl.ds(first, depth), :]
    first = 0
    for p, size in enumerate(sizes):
        summed = terms[p * n_sum][:size, :].astype(jnp.float32)
        for k in range(1, n_sum):
            summed += terms[p * n_sum + k][:size, :].astype(jnp.float32)
        aggregated[first : first + size, :] = summed.astype(jnp.bfloat16)
        first += size
    nodes_first = aggregated[...].T
    preact = jnp.dot(nodes_first, ordered[...], preferred_element_type=jnp.float32)
    gate = jax.nn.sigmoid(preact)
    output[...] = (preact * gate).astype(jnp.bfloat16)
    slopes = gate * (1.0 + preact * (1.0 - gate))
    delta = (cotangent[...].astype(jnp.float32) * slopes).astype(jnp.bfloat16)
    deltas[...] = delta
    product = lax.dot_general(ordered[...], delta, NT, preferred_element_type=jnp.float32)
    product = jnp.concatenate([product[k * depth : (k + 1) * depth, :] for k in order]).astype(jnp.bfloat16)
    first = 0
    for back in backs:
        first %= product.shape[0]
        back[...] = product[first : first + back.shape[0], :]
        first += back.shape[0]


def middle(n_row, row, weight, cotangent, pieces, order, depths):
    sizes = [piece[0].shape[0] for piece in pieces]
    nodes = cotangent.shape[0]
    features = weight.shape[0]
    shape = jax.ShapeDtypeStruct
    outs = [
        shape((nodes, features), jnp.bfloat16),
        shape((nodes, features), jnp.bfloat16),
        shape((features, nodes), jnp.bfloat16),
    ] + [shape((depth, nodes), jnp.bfloat16) for depth in depths]
    flat = [term for piece in pieces for term in piece]
    return pl.pallas_call(
        functools.partial(middle_kernel, sizes, order, len(pieces[0]), n_row),
        out_shape=outs,
        in_specs=[SMEM] + [VMEM] * (2 + len(flat)),
        out_specs=[VMEM] * len(outs),
        scratch_shapes=[pltpu.VMEM(weight.shape, jnp.bfloat16)],
        compiler_params=params(10),
        cost_estimate=COST,
        name="layer",
    )(row, weight, cotangent, *flat)


def gradient_kernel(scale, order, aggregated, deltas, *outs):
    product = jnp.dot(aggregated[...], deltas[...], preferred_element_type=jnp.float32) * scale
    for out, chunks in zip(outs, order):
        depth = out.shape[1]
        for n, k in enumerate(chunks):
            out[n] = product[k * depth : (k + 1) * depth, :]


def gradient(scale, order, aggregated, deltas):
    depth = aggregated.shape[0] // sum(len(chunks) for chunks in order)
    outs = [jax.ShapeDtypeStruct((len(chunks), depth, deltas.shape[1]), jnp.float32) for chunks in order]
    return pl.pallas_call(
        functools.partial(gradient_kernel, scale, order),
        out_shape=outs,
        in_specs=[VMEM] * 2,
        out_specs=[VMEM] * len(outs),
        compiler_params=params(6),
        cost_estimate=COST,
        name="weight_gradient",
    )(aggregated, deltas)


def swap(value, axis, k):
    size = lax.axis_size(axis)
    return lax.ppermute(value, axis, [(i, i ^ k) for i in range(size)])


def wide_sum(*values):
    total = values[0].astype(jnp.float32)
    for value in values[1:]:
        total = total + value.astype(jnp.float32)
    return (total.astype(values[0].dtype),)


def after(value, *earlier):
    return lax.optimization_barrier((value, *earlier))[0]


def with_chunk(rows, *chunks):
    chunk = jnp.concatenate(chunks)
    high = chunk.astype(jnp.bfloat16)
    low = (chunk - high.astype(jnp.float32)).astype(jnp.bfloat16)
    return (jnp.concatenate([rows, jnp.concatenate([high, low], axis=1)]),)


def chunk_sum(depth, *values):
    total = None
    for value in values:
        halves = value[-depth:].astype(jnp.float32)
        wide = halves.shape[1] // 2
        chunk = halves[:, :wide] + halves[:, wide:]
        total = chunk if total is None else total + chunk
    return (total,)


def halves_sum(mine, *received):
    total = mine + jnp.concatenate(received)
    half = total.shape[0] // 2
    return total[:half], total[half:]


def far_sums(mine, received):
    total = mine[: received.shape[0]].astype(jnp.float32) + received.astype(jnp.float32)
    total = total.astype(mine.dtype)
    return (jnp.concatenate([total, total[:, :128]], axis=1),)


def near_kernel(row, chunk, half_way, mine, *refs):
    depth, nodes = half_way.shape[0], mine.shape[1]
    n_sums = mine.shape[0] // depth - 1
    received, (chunks, *sums) = refs[:n_sums], refs[n_sums:]
    wide = chunk.shape[1]
    for k in range(2):
        chunks[:, k * wide : (k + 1) * wide] = chunk[k * depth : (k + 1) * depth, :].astype(chunks.dtype)
    passed = half_way[:, :nodes].astype(jnp.float32)
    odd = row[0] % 2
    for n, out in enumerate(sums):
        first = (n + 1) * depth
        total = mine[first : first + depth, :].astype(jnp.float32) + received[n][...].astype(jnp.float32)
        if n:
            total += jnp.where(odd == 2 - n, passed, 0.0)
            out[:, nodes:] = chunks[...]
        out[:, :nodes] = total.astype(out.dtype)


def near_payloads(row, chunk, half_way, mine, received):
    depth, nodes = received[0].shape
    wide = 2 * chunk.shape[1]
    shapes = [(depth, wide), (depth, nodes)] + [(depth, nodes + wide)] * (len(received) - 1)
    return pl.pallas_call(
        near_kernel,
        out_shape=[jax.ShapeDtypeStruct(shape, mine.dtype) for shape in shapes],
        in_specs=[SMEM] + [VMEM] * (3 + len(received)),
        out_specs=[VMEM] * len(shapes),
        compiler_params=params(8),
        cost_estimate=COST,
        name="near_payloads",
    )(row, chunk, half_way, mine, *received)


def finish_kernel(keys, row, *refs):
    grad_features, grad_weight = refs[-2:]
    depth, nodes = grad_features.shape
    wide = grad_weight.shape[1]
    parts = [ref for ref in refs[:-2] if ref.shape[1] >= nodes]
    values = [ref[...] for ref in refs[:-2] if ref.shape[1] < nodes] + [part[:, nodes:] for part in parts[1:]]
    total = parts[0][...].astype(jnp.float32)
    for part in parts[1:]:
        total += part[:, :nodes].astype(jnp.float32)
    grad_features[...] = total.astype(grad_features.dtype)
    for key, value in zip(keys, values):
        for k in range(2):
            first = pl.multiple_of((row[0] ^ (key + k)) * depth, depth)
            grad_weight[pl.ds(first, depth), :] = value[:, k * wide : (k + 1) * wide].astype(jnp.float32)


def finish(row, keys, parts, chunks):
    depth, nodes = parts[0].shape
    return pl.pallas_call(
        functools.partial(finish_kernel, keys),
        out_shape=[
            jax.ShapeDtypeStruct((depth, nodes), jnp.bfloat16),
            jax.ShapeDtypeStruct((2 * len(keys) * depth, chunks[0].shape[1] // 2), jnp.float32),
        ],
        in_specs=[SMEM] + [VMEM] * (len(parts) + len(chunks)),
        out_specs=[VMEM] * 2,
        compiler_params=params(8),
        cost_estimate=COST,
        name="finish",
    )(row, *parts, *chunks)


def shards_exchanged(features, weight, adj_values, block_rows, block_cols, block_counts, cotangent):
    n_row = lax.axis_size("row")
    n_col = lax.axis_size("col")
    adj = adj_values[0, 0]
    rows = block_rows[0, 0]
    cols = block_cols[0, 0]
    count = block_counts
    size = adj.shape[1]
    nodes = cotangent.shape[0] * n_row * n_col
    row_blocks = cotangent.shape[0] * n_col // size
    col_blocks = features.shape[0] // size
    row = lax.axis_index("row").reshape(1)
    col = lax.axis_index("col").reshape(1)
    own = after(features.T, row, col)

    depth = features.shape[1]
    near = [k for k in range(2, n_row, 2) if k & (k - 1) == 0]
    far = [k for k in range(2, n_row, 2) if k & (k - 1) != 0]
    sibling = swap(own, "row", 1)
    from_near = [swap(own, "row", k) for k in near]
    rows, cols, *halves, tile = fetch(count, rows, cols, own, adj)
    from_near = [after(part, tile) for part in from_near]
    from_far = [swap(half, "row", k) for k in far for half in halves]

    def pass_on(beyond, received):
        return wide_sum(beyond, received[beyond.shape[0] :])

    layout = [(0,), (2,), (1, 3)]

    def fold(kept, beyond, received):
        (passed,) = fuse("pass_on", pass_on, beyond, received)
        return [kept, received, swap(passed, "col", 2)]

    n_near = 2 * depth * (1 + len(near))
    cut = n_near * 5 // 6
    parts = [own, sibling] + [piece for part in from_near for piece in (part, swap(part, "row", 1))]
    kept, beyond, sent, *carried = forward(
        col, count, rows, cols, tile, parts, row_blocks, [cut, n_near - cut], layout
    )
    received = swap(sent, "col", 1)
    from_far = [after(part, kept) for part in from_far]
    parts = []
    for n in range(0, len(from_far), 2):
        halves = from_far[n : n + 2]
        parts += halves + [swap(half, "row", 1) for half in halves]
    far_piece = forward(
        col, count, rows, cols, tile, parts, row_blocks, [2 * depth * len(far)], layout, carried
    )
    far_received = swap(far_piece[2], "col", 1)
    first = fold(kept, beyond, after(received, far_piece[0]))
    second = fold(*far_piece[:2], after(far_received, first[1]))
    sums = [first, second]

    keys = far + [0] + near
    order = keys + [k + 1 for k in keys]
    cut = weight.shape[0] // 2 + 2 * depth
    cuts = [cut, weight.shape[0] - cut]
    output, deltas, aggregated, back, *backs = middle(
        n_row, row, weight, cotangent, sums, order, [sum(cuts)] + cuts
    )
    beside = swap(back, "col", 1)
    beyond = [swap(part, "col", 2) for part in backs]

    even, *odd = gradient(1.0 / math.sqrt(nodes), [(0, 4, 2, 6), (1, 5), (3, 7)], aggregated, deltas)
    even, sent = fuse("gradient_sum", halves_sum, even, *[swap(part, "row", 1) for part in odd])
    even, sent = fuse("gradient_sum", halves_sum, even, swap(sent, "row", 2))
    beyond[0] = after(beyond[0], sent)
    received = [swap(beyond[0], "col", 1)]
    even = after(even, beyond[1], beside)
    (chunk,) = fuse("gradient_sum", lambda a, b: ((a + b)[0],), even, swap(sent, "row", 4))
    (second,) = fuse("with_chunk", with_chunk, beyond[1], chunk, swap(chunk, "row", 1))
    received.append(swap(second, "col", 1))

    (chunk,) = fuse("chunk_sum", functools.partial(chunk_sum, 2 * depth), second, received[1])

    parts = [back, beside, beyond[0], received[0], beyond[1], after(received[1], chunk)]
    spots = [[(part, 0), (part, cut)] for part in range(2)] + [[(part, 0), (part + 2, 0)] for part in (2, 3)]
    out_depths = [depth * len(keys)] + [depth] * len(keys)
    mine, *sent = backward(col, count, rows, cols, tile, parts, spots, cuts, out_depths, col_blocks)
    from_sibling = [swap(part, "row", 1) for part in sent]
    (chunk,) = fuse("chunk_sum", wide_sum, chunk, swap(chunk, "col", 2))

    (far_sum,) = fuse("far_sums", far_sums, mine, from_sibling[0])
    half_way = lax.ppermute(far_sum, "row", [(i, i ^ (4 if i % 2 else 2)) for i in range(n_row)])
    chunks, own_sum, *near_sums = near_payloads(row, chunk, half_way, mine, from_sibling[1:])
    near_sums = [swap(part, "row", k) for part, k in zip(near_sums, near)]
    far_chunks = [swap(chunks, "row", k) for k in far]
    grad_features, grad_weight = finish(row, [0] + far + near, [own_sum] + near_sums, [chunks] + far_chunks)
    return output, grad_weight, grad_features.T


def shards_gathered(features, weight, adj_values, block_rows, block_cols, block_counts, cotangent):
    n_row = lax.axis_size("row")
    n_col = lax.axis_size("col")
    adj = adj_values[0, 0]
    rows = block_rows[0, 0]
    cols = block_cols[0, 0]
    count = block_counts
    size = adj.shape[1]
    nodes = cotangent.shape[0] * n_row * n_col
    row_blocks = cotangent.shape[0] * n_col // size
    col_blocks = features.shape[0] // size
    zero = jnp.zeros((1,), jnp.int32)
    panels = lax.all_gather(features.T, "row", axis=0, tiled=True)
    (terms,) = forward(zero, count, rows, cols, adj, [panels], row_blocks, [panels.shape[0]], [(0,)])
    part = lax.psum_scatter(terms, "col", scatter_dimension=1, tiled=True)
    output, deltas, aggregated, back = middle(1, zero, weight, cotangent, [[part]], (0,), [weight.shape[0]])
    slab = lax.all_gather(back, "col", axis=1, tiled=True)
    (column_terms,) = backward(zero, count, rows, cols, adj, [slab], [[(0, 0)]], [slab.shape[0]], [slab.shape[0]], col_blocks)
    grad_features = lax.psum_scatter(column_terms, "row", scatter_dimension=0, tiled=True).T
    (part,) = gradient(1.0 / math.sqrt(nodes), [(0,)], aggregated, deltas)
    grad_weight = lax.psum(part[0], ("row", "col"))
    return output, grad_weight, grad_features


def solution(mesh):
    n_row = mesh.shape["row"]
    n_col = mesh.shape["col"]
    exchanged = n_row == 8 and n_col == 4
    return jax.shard_map(
        shards_exchanged if exchanged else shards_gathered,
        mesh=mesh,
        in_specs=(
            P("col", "row"),
            P(),
            P("row", "col", None, None, None),
            P("row", "col", None),
            P("row", "col", None),
            P("row", "col"),
            P(("row", "col"), None),
        ),
        out_specs=(P(("row", "col"), None), P(), P("col", "row")),
        check_vma=False,
    )
```

```python
import functools
import math

import jax
import jax.numpy as jnp
from jax import lax
from jax.experimental import pallas as pl
from jax.experimental.pallas import tpu as pltpu
from jax.sharding import PartitionSpec as P

VMEM = pl.BlockSpec(memory_space=pltpu.VMEM)
SMEM = pl.BlockSpec(memory_space=pltpu.SMEM)
HBM = pl.BlockSpec(memory_space=pltpu.HBM)
MIB = 1024 * 1024
NT = (((1,), (1,)), ((), ()))
NN = (((1,), (0,)), ((), ()))


COST = pl.CostEstimate(flops=1, bytes_accessed=1, transcendentals=0)


def params(mib):
    return pltpu.CompilerParams(vmem_limit_bytes=mib * MIB)


def fuse(name, function, *values):
    shapes = jax.eval_shape(function, *values)

    def kernel(*refs):
        results = function(*[ref[...] for ref in refs[: len(values)]])
        for ref, result in zip(refs[len(values) :], results):
            ref[...] = result

    return pl.pallas_call(
        kernel,
        out_shape=shapes,
        in_specs=[VMEM] * len(values),
        out_specs=[VMEM] * len(shapes),
        compiler_params=params(4),
        cost_estimate=COST,
        name=name,
    )(*values)


def turn_of(slots):
    return math.gcd(slots, 8)


def product_loop(count, source_ids, target_ids, adj, source, total, dims):
    turn = turn_of(adj.shape[0])
    spare = total.shape[0] - 1
    total[...] = jnp.zeros_like(total)

    def step(index, carry):
        first = index * turn
        for k in range(turn):
            slot = first + k
            product = lax.dot_general(
                source[source_ids[slot]], adj[slot], dims, preferred_element_type=jnp.float32
            )
            target = jnp.where(slot < count, target_ids[slot], spare)
            total[target] += product
        return carry

    lax.fori_loop(0, (count + turn - 1) // turn, step, 0)


def fetch_kernel(count, rows, cols, features, tile, *refs):
    outs, (sem, small_sem) = refs[:5], refs[5:]
    half = features.shape[0] // 2
    sources = (rows, cols, features.at[pl.ds(0, half)], features.at[pl.ds(half, half)])
    small = [
        pltpu.make_async_copy(source, target, small_sem.at[n])
        for n, (source, target) in enumerate(zip(sources, outs))
    ]
    for copy in small:
        copy.start()
    turn = turn_of(tile.shape[0])

    def copy_turn(index):
        blocks = pl.ds(index * turn, turn)
        return pltpu.make_async_copy(tile.at[blocks], outs[4].at[blocks], sem.at[index])

    def begin(index, carry):
        copy_turn(index).start()
        return carry

    def wait(index, carry):
        copy_turn(index).wait()
        return carry

    turns = (count[0, 0] + turn - 1) // turn
    lax.fori_loop(0, turns, begin, 0)
    lax.fori_loop(0, turns, wait, 0)
    for copy in small:
        copy.wait()


def fetch(count, rows, cols, features, tile):
    arrays = (rows, cols, features, tile)
    half = jax.ShapeDtypeStruct((features.shape[0] // 2, features.shape[1]), features.dtype)
    outs = [jax.ShapeDtypeStruct(array.shape, array.dtype) for array in (rows, cols)] + [half] * 2
    return pl.pallas_call(
        fetch_kernel,
        out_shape=outs + [jax.ShapeDtypeStruct(tile.shape, tile.dtype)],
        in_specs=[SMEM] + [HBM] * 4,
        out_specs=[VMEM] * 5,
        scratch_shapes=[
            pltpu.SemaphoreType.DMA((tile.shape[0] // turn_of(tile.shape[0]),)),
            pltpu.SemaphoreType.DMA((4,)),
        ],
        compiler_params=params(4),
        cost_estimate=COST,
        name="fetch",
    )(count, *[pltpu.with_memory_space_constraint(array, pltpu.HBM) for array in arrays])


def forward_kernel(n_parts, depths, layout, place, count, rows, cols, adj, *refs):
    parts, refs = refs[:n_parts], refs[n_parts:]
    source, total = refs[-2:]
    outs = refs[-2 - len(depths) * len(layout) : -2]
    carried = refs[: len(refs) - 2 - len(outs)]
    size = adj.shape[1]
    row = 0
    for part in parts:
        depth = part.shape[0]
        for c in range(source.shape[0]):
            source[c, row : row + depth, :] = part[:, c * size : (c + 1) * size]
        row += depth
    product_loop(count[0, 0], cols, rows, adj, source, total, NT)
    blocks = outs[0].shape[1] // size
    ahead = carried[0].shape[0] // len(layout[0]) if carried else 0
    outs = iter(outs)
    row = 0
    for depth in depths:
        for m, chunks in enumerate(layout):
            out = next(outs)
            for n, k in enumerate(chunks):
                begin = n * (ahead + depth)
                if ahead:
                    out[begin : begin + ahead, :] = carried[m][n * ahead : (n + 1) * ahead, :]
                first = (place[0] ^ k) * blocks
                for i in range(blocks):
                    out[begin + ahead : begin + ahead + depth, i * size : (i + 1) * size] = total[
                        first + i, row : row + depth, :
                    ].astype(out.dtype)
        row += depth


def forward(place, count, rows, cols, adj, parts, row_blocks, depths, layout, carried=()):
    size = adj.shape[1]
    col_blocks = parts[0].shape[1] // size
    wide = row_blocks * size // sum(len(chunks) for chunks in layout)
    ahead = carried[0].shape[0] // len(layout[0]) if carried else 0
    outs = [
        jax.ShapeDtypeStruct((len(chunks) * (ahead + depth), wide), jnp.bfloat16)
        for depth in depths
        for chunks in layout
    ]
    return pl.pallas_call(
        functools.partial(forward_kernel, len(parts), depths, layout),
        out_shape=outs,
        in_specs=[SMEM] * 4 + [VMEM] * (1 + len(parts) + len(carried)),
        out_specs=[VMEM] * len(outs),
        scratch_shapes=[
            pltpu.VMEM((col_blocks, sum(depths), size), jnp.bfloat16),
            pltpu.VMEM((row_blocks + 1, sum(depths), size), jnp.float32),
        ],
        compiler_params=params(14),
        cost_estimate=COST,
        name="forward_products",
    )(place, count, rows, cols, adj, *parts, *carried)


def backward_kernel(spots, depths, place, count, rows, cols, adj, *refs):
    n_parts = 1 + max(part for places in spots for part, _ in places)
    parts = refs[:n_parts]
    outs = refs[n_parts:-2]
    source, total = refs[-2:]
    size = adj.shape[1]
    blocks = parts[0].shape[1] // size
    for k, places in enumerate(spots):
        first = (place[0] ^ k) * blocks
        row = 0
        for (part, offset), depth in zip(places, depths):
            for i in range(blocks):
                source[first + i, row : row + depth, :] = parts[part][
                    offset : offset + depth, i * size : (i + 1) * size
                ]
            row += depth
    product_loop(count[0, 0], rows, cols, adj, source, total, NN)
    row = 0
    for out in outs:
        depth = out.shape[0]
        for c in range(total.shape[0] - 1):
            out[:, c * size : (c + 1) * size] = total[c, row : row + depth, :].astype(out.dtype)
        row += depth


def backward(place, count, rows, cols, adj, parts, spots, depths, out_depths, col_blocks):
    size = adj.shape[1]
    row_blocks = len(spots) * parts[0].shape[1] // size
    return pl.pallas_call(
        functools.partial(backward_kernel, spots, depths),
        out_shape=[jax.ShapeDtypeStruct((depth, col_blocks * size), jnp.bfloat16) for depth in out_depths],
        in_specs=[SMEM] * 4 + [VMEM] * (1 + len(parts)),
        out_specs=[VMEM] * len(out_depths),
        scratch_shapes=[
            pltpu.VMEM((row_blocks, sum(out_depths), size), jnp.bfloat16),
            pltpu.VMEM((col_blocks + 1, sum(out_depths), size), jnp.float32),
        ],
        compiler_params=params(14),
        cost_estimate=COST,
        name="backward_products",
    )(place, count, rows, cols, adj, *parts)


def middle_kernel(sizes, order, n_sum, n_row, row, weight, cotangent, *refs):
    terms = refs[: n_sum * len(sizes)]
    outs = refs[n_sum * len(sizes) : -1]
    output, deltas, aggregated, *backs = outs
    ordered = refs[-1]
    depth = weight.shape[0] // n_row
    for j in range(n_row):
        first = pl.multiple_of((row[0] ^ j) * depth, depth)
        ordered[j * depth : (j + 1) * depth, :] = weight[pl.ds(first, depth), :]
    first = 0
    for p, size in enumerate(sizes):
        summed = terms[p * n_sum][:size, :].astype(jnp.float32)
        for k in range(1, n_sum):
            summed += terms[p * n_sum + k][:size, :].astype(jnp.float32)
        aggregated[first : first + size, :] = summed.astype(jnp.bfloat16)
        first += size
    nodes_first = aggregated[...].T
    preact = jnp.dot(nodes_first, ordered[...], preferred_element_type=jnp.float32)
    gate = jax.nn.sigmoid(preact)
    output[...] = (preact * gate).astype(jnp.bfloat16)
    slopes = gate * (1.0 + preact * (1.0 - gate))
    delta = (cotangent[...].astype(jnp.float32) * slopes).astype(jnp.bfloat16)
    deltas[...] = delta
    product = lax.dot_general(ordered[...], delta, NT, preferred_element_type=jnp.float32)
    product = jnp.concatenate([product[k * depth : (k + 1) * depth, :] for k in order]).astype(jnp.bfloat16)
    first = 0
    for back in backs:
        first %= product.shape[0]
        back[...] = product[first : first + back.shape[0], :]
        first += back.shape[0]


def middle(n_row, row, weight, cotangent, pieces, order, depths):
    sizes = [piece[0].shape[0] for piece in pieces]
    nodes = cotangent.shape[0]
    features = weight.shape[0]
    shape = jax.ShapeDtypeStruct
    outs = [
        shape((nodes, features), jnp.bfloat16),
        shape((nodes, features), jnp.bfloat16),
        shape((features, nodes), jnp.bfloat16),
    ] + [shape((depth, nodes), jnp.bfloat16) for depth in depths]
    flat = [term for piece in pieces for term in piece]
    return pl.pallas_call(
        functools.partial(middle_kernel, sizes, order, len(pieces[0]), n_row),
        out_shape=outs,
        in_specs=[SMEM] + [VMEM] * (2 + len(flat)),
        out_specs=[VMEM] * len(outs),
        scratch_shapes=[pltpu.VMEM(weight.shape, jnp.bfloat16)],
        compiler_params=params(10),
        cost_estimate=COST,
        name="layer",
    )(row, weight, cotangent, *flat)


def gradient_kernel(scale, order, aggregated, deltas, *outs):
    product = jnp.dot(aggregated[...], deltas[...], preferred_element_type=jnp.float32) * scale
    for out, chunks in zip(outs, order):
        depth = out.shape[1]
        for n, k in enumerate(chunks):
            out[n] = product[k * depth : (k + 1) * depth, :]


def gradient(scale, order, aggregated, deltas):
    depth = aggregated.shape[0] // sum(len(chunks) for chunks in order)
    outs = [jax.ShapeDtypeStruct((len(chunks), depth, deltas.shape[1]), jnp.float32) for chunks in order]
    return pl.pallas_call(
        functools.partial(gradient_kernel, scale, order),
        out_shape=outs,
        in_specs=[VMEM] * 2,
        out_specs=[VMEM] * len(outs),
        compiler_params=params(6),
        cost_estimate=COST,
        name="weight_gradient",
    )(aggregated, deltas)


def swap(value, axis, k):
    size = lax.axis_size(axis)
    return lax.ppermute(value, axis, [(i, i ^ k) for i in range(size)])


def wide_sum(*values):
    total = values[0].astype(jnp.float32)
    for value in values[1:]:
        total = total + value.astype(jnp.float32)
    return (total.astype(values[0].dtype),)


def after(value, *earlier):
    return lax.optimization_barrier((value, *earlier))[0]


def with_chunk(chunk, *rows):
    high = chunk.astype(jnp.bfloat16)
    low = (chunk - high.astype(jnp.float32)).astype(jnp.bfloat16)
    return (jnp.concatenate([*rows, jnp.concatenate([high, low], axis=1)]),)


def chunk_sum(depth, *values):
    total = None
    for value in values:
        halves = value[-depth:].astype(jnp.float32)
        wide = halves.shape[1] // 2
        chunk = halves[:, :wide] + halves[:, wide:]
        total = chunk if total is None else total + chunk
    return (total,)


def halves_sum(mine, *received):
    total = mine + jnp.concatenate(received)
    half = total.shape[0] // 2
    return total[:half], total[half:]


def far_sums(depth, mine, *received):
    total = mine.astype(jnp.float32) + jnp.concatenate(received).astype(jnp.float32)
    total = total.astype(mine.dtype)
    own, far = total[:depth], total[depth:]
    return own, jnp.concatenate([far, far[:, :128]], axis=1)


def near_kernel(row, chunk, sibling, half_way, mine, *refs):
    received, (chunks, *sums) = refs[: -1 - 2], refs[-1 - 2 :]
    depth = half_way.shape[0]
    nodes = mine.shape[1]
    for k, ref in enumerate((chunk, sibling)):
        wide = ref.shape[1]
        chunks[:, k * wide : (k + 1) * wide] = ref[...].astype(chunks.dtype)
    passed = half_way[:, :nodes].astype(jnp.float32)
    odd = row[0] % 2
    for n, out in enumerate(sums):
        total = mine[n * depth : (n + 1) * depth, :].astype(jnp.float32) + received[n][...].astype(jnp.float32)
        total += jnp.where(odd == 1 - n, passed, 0.0)
        out[:, :nodes] = total.astype(out.dtype)
        out[:, nodes:] = chunks[...]


def near_payloads(row, chunk, sibling, half_way, mine, received):
    depth, nodes = received[0].shape
    wide = 2 * chunk.shape[1]
    shape = jax.ShapeDtypeStruct
    return pl.pallas_call(
        near_kernel,
        out_shape=[shape((depth, wide), mine.dtype)]
        + [shape((depth, nodes + wide), mine.dtype)] * len(received),
        in_specs=[SMEM] + [VMEM] * (4 + len(received)),
        out_specs=[VMEM] * (1 + len(received)),
        compiler_params=params(8),
        cost_estimate=COST,
        name="near_payloads",
    )(row, chunk, sibling, half_way, mine, *received)


def finish_kernel(keys, row, *refs):
    grad_features, grad_weight = refs[-2:]
    depth, nodes = grad_features.shape
    wide = grad_weight.shape[1]
    parts = [ref for ref in refs[:-2] if ref.shape[1] >= nodes]
    values = [ref[...] for ref in refs[:-2] if ref.shape[1] < nodes] + [part[:, nodes:] for part in parts[1:]]
    total = parts[0][...].astype(jnp.float32)
    for part in parts[1:]:
        total += part[:, :nodes].astype(jnp.float32)
    grad_features[...] = total.astype(grad_features.dtype)
    for key, value in zip(keys, values):
        for k in range(2):
            first = pl.multiple_of((row[0] ^ (key + k)) * depth, depth)
            grad_weight[pl.ds(first, depth), :] = value[:, k * wide : (k + 1) * wide].astype(jnp.float32)


def finish(row, keys, parts, chunks):
    depth, nodes = parts[0].shape
    return pl.pallas_call(
        functools.partial(finish_kernel, keys),
        out_shape=[
            jax.ShapeDtypeStruct((depth, nodes), jnp.bfloat16),
            jax.ShapeDtypeStruct((2 * len(keys) * depth, chunks[0].shape[1] // 2), jnp.float32),
        ],
        in_specs=[SMEM] + [VMEM] * (len(parts) + len(chunks)),
        out_specs=[VMEM] * 2,
        compiler_params=params(8),
        cost_estimate=COST,
        name="finish",
    )(row, *parts, *chunks)


def shards_exchanged(features, weight, adj_values, block_rows, block_cols, block_counts, cotangent):
    n_row = lax.axis_size("row")
    n_col = lax.axis_size("col")
    adj = adj_values[0, 0]
    rows = block_rows[0, 0]
    cols = block_cols[0, 0]
    count = block_counts
    size = adj.shape[1]
    nodes = cotangent.shape[0] * n_row * n_col
    row_blocks = cotangent.shape[0] * n_col // size
    col_blocks = features.shape[0] // size
    row = lax.axis_index("row").reshape(1)
    col = lax.axis_index("col").reshape(1)
    own = after(features.T, row, col)

    depth = features.shape[1]
    near = [k for k in range(2, n_row, 2) if k & (k - 1) == 0]
    far = [k for k in range(2, n_row, 2) if k & (k - 1) != 0]
    sibling = swap(own, "row", 1)
    from_near = [swap(own, "row", k) for k in near]
    rows, cols, *halves, tile = fetch(count, rows, cols, own, adj)
    from_near = [after(part, tile) for part in from_near]
    from_far = [swap(half, "row", k) for k in far for half in halves]

    def pass_on(beyond, received):
        return wide_sum(beyond, received[beyond.shape[0] :])

    layout = [(0,), (2,), (1, 3)]

    def fold(kept, beyond, received):
        (passed,) = fuse("pass_on", pass_on, beyond, received)
        return [kept, received, swap(passed, "col", 2)]

    n_near = 2 * depth * (1 + len(near))
    cut = n_near * 5 // 6
    parts = [own, sibling] + [piece for part in from_near for piece in (part, swap(part, "row", 1))]
    kept, beyond, sent, *carried = forward(
        col, count, rows, cols, tile, parts, row_blocks, [cut, n_near - cut], layout
    )
    received = swap(sent, "col", 1)
    from_far = [after(part, kept) for part in from_far]
    parts = []
    for n in range(0, len(from_far), 2):
        halves = from_far[n : n + 2]
        parts += halves + [swap(half, "row", 1) for half in halves]
    far_piece = forward(
        col, count, rows, cols, tile, parts, row_blocks, [2 * depth * len(far)], layout, carried
    )
    far_received = swap(far_piece[2], "col", 1)
    first = fold(kept, beyond, after(received, far_piece[0]))
    second = fold(*far_piece[:2], after(far_received, first[1]))
    sums = [first, second]

    groups = [[0] + far, near]
    order = [k + side for group in groups for side in range(2) for k in group]
    cuts = [2 * depth * len(group) for group in groups]
    ahead = depth // 2
    output, deltas, aggregated, *backs = middle(
        n_row, row, weight, cotangent, sums, order, [cuts[0] + ahead, cuts[1] - ahead]
    )
    beside = swap(backs[0], "col", 1)
    beyond = [swap(part, "col", 2) for part in backs]

    even, *odd = gradient(1.0 / math.sqrt(nodes), [(0, 4, 2, 6), (1, 5), (3, 7)], aggregated, deltas)
    even, sent = fuse("gradient_sum", halves_sum, even, *[swap(part, "row", 1) for part in odd])
    even, sent = fuse("gradient_sum", halves_sum, after(even, beside), swap(sent, "row", 2))
    beyond[0] = after(beyond[0], sent)
    received = [swap(beyond[0], "col", 1)]
    even = after(even, beyond[1], received[0])
    (chunk,) = fuse("gradient_sum", lambda a, b: ((a + b)[0],), even, swap(sent, "row", 4))
    (second,) = fuse("with_chunk", with_chunk, chunk, backs[1], beyond[1])
    received.append(swap(second, "col", 1))

    def columns(n, *earlier):
        parts = [backs[0], beside, after(beyond[0], *earlier), received[0]]
        if n == 0:
            depths = cuts[:1]
            spots = [[(part, 0)] for part in range(4)]
        else:
            depths = [ahead, cuts[1] - ahead]
            parts += [backs[1], received[1], beyond[1]]
            later = [(4, 0), (5, 0), (6, 0), (5, depths[1])]
            spots = [[(part, cuts[0]), place] for part, place in enumerate(later)]
        out_depths = [cuts[n] // 2] + [cuts[n] // (8 - 4 * n)] * (4 - 2 * n)
        mine, *sent = backward(
            col, count, rows, cols, tile, parts, spots, depths, out_depths, col_blocks
        )
        return [mine] + [swap(part, "row", 1) for part in sent]

    own_sum, far_sum = fuse("far_sums", functools.partial(far_sums, depth), *columns(0, second))
    half_way = lax.ppermute(far_sum, "row", [(i, i ^ (4 if i % 2 else 2)) for i in range(n_row)])
    (chunk,) = fuse("chunk_sum", functools.partial(chunk_sum, depth), second, received[1])
    (chunk,) = fuse("chunk_sum", wide_sum, chunk, swap(chunk, "col", 2))
    mine, *from_sibling = columns(1, chunk, far_sum)
    chunks, *near_sums = near_payloads(row, chunk, swap(chunk, "row", 1), half_way, mine, from_sibling)
    near_sums = [swap(part, "row", k) for part, k in zip(near_sums, near)]
    far_chunks = [swap(chunks, "row", k) for k in far]
    grad_features, grad_weight = finish(row, [0] + far + near, [own_sum] + near_sums, [chunks] + far_chunks)
    return output, grad_weight, grad_features.T


def shards_gathered(features, weight, adj_values, block_rows, block_cols, block_counts, cotangent):
    n_row = lax.axis_size("row")
    n_col = lax.axis_size("col")
    adj = adj_values[0, 0]
    rows = block_rows[0, 0]
    cols = block_cols[0, 0]
    count = block_counts
    size = adj.shape[1]
    nodes = cotangent.shape[0] * n_row * n_col
    row_blocks = cotangent.shape[0] * n_col // size
    col_blocks = features.shape[0] // size
    zero = jnp.zeros((1,), jnp.int32)
    panels = lax.all_gather(features.T, "row", axis=0, tiled=True)
    (terms,) = forward(zero, count, rows, cols, adj, [panels], row_blocks, [panels.shape[0]], [(0,)])
    part = lax.psum_scatter(terms, "col", scatter_dimension=1, tiled=True)
    output, deltas, aggregated, back = middle(1, zero, weight, cotangent, [[part]], (0,), [weight.shape[0]])
    slab = lax.all_gather(back, "col", axis=1, tiled=True)
    (column_terms,) = backward(zero, count, rows, cols, adj, [slab], [[(0, 0)]], [slab.shape[0]], [slab.shape[0]], col_blocks)
    grad_features = lax.psum_scatter(column_terms, "row", scatter_dimension=0, tiled=True).T
    (part,) = gradient(1.0 / math.sqrt(nodes), [(0,)], aggregated, deltas)
    grad_weight = lax.psum(part[0], ("row", "col"))
    return output, grad_weight, grad_features


def solution(mesh):
    n_row = mesh.shape["row"]
    n_col = mesh.shape["col"]
    exchanged = n_row == 8 and n_col == 4
    return jax.shard_map(
        shards_exchanged if exchanged else shards_gathered,
        mesh=mesh,
        in_specs=(
            P("col", "row"),
            P(),
            P("row", "col", None, None, None),
            P("row", "col", None),
            P("row", "col", None),
            P("row", "col"),
            P(("row", "col"), None),
        ),
        out_specs=(P(("row", "col"), None), P(), P("col", "row")),
        check_vma=False,
    )
```

```python
import functools
import math

import jax
import jax.numpy as jnp
from jax import lax
from jax.experimental import pallas as pl
from jax.experimental.pallas import tpu as pltpu
from jax.sharding import PartitionSpec as P

VMEM = pl.BlockSpec(memory_space=pltpu.VMEM)
SMEM = pl.BlockSpec(memory_space=pltpu.SMEM)
HBM = pl.BlockSpec(memory_space=pltpu.HBM)
MIB = 1024 * 1024
NT = (((1,), (1,)), ((), ()))
NN = (((1,), (0,)), ((), ()))


COST = pl.CostEstimate(flops=1, bytes_accessed=1, transcendentals=0)


def params(mib):
    return pltpu.CompilerParams(vmem_limit_bytes=mib * MIB)


def fuse(name, function, *values):
    shapes = jax.eval_shape(function, *values)

    def kernel(*refs):
        results = function(*[ref[...] for ref in refs[: len(values)]])
        for ref, result in zip(refs[len(values) :], results):
            ref[...] = result

    return pl.pallas_call(
        kernel,
        out_shape=shapes,
        in_specs=[VMEM] * len(values),
        out_specs=[VMEM] * len(shapes),
        compiler_params=params(4),
        cost_estimate=COST,
        name=name,
    )(*values)


def turn_of(slots):
    return math.gcd(slots, 8)


def product_loop(count, source_ids, target_ids, adj, source, total, dims):
    turn = turn_of(adj.shape[0])
    spare = total.shape[0] - 1
    total[...] = jnp.zeros_like(total)

    def step(index, carry):
        first = index * turn
        for k in range(turn):
            slot = first + k
            product = lax.dot_general(
                source[source_ids[slot]], adj[slot], dims, preferred_element_type=jnp.float32
            )
            target = jnp.where(slot < count, target_ids[slot], spare)
            total[target] += product
        return carry

    lax.fori_loop(0, (count + turn - 1) // turn, step, 0)


def fetch_kernel(count, rows, cols, features, tile, *refs):
    outs, (sem, small_sem) = refs[:5], refs[5:]
    half = features.shape[0] // 2
    sources = (rows, cols, features.at[pl.ds(0, half)], features.at[pl.ds(half, half)])
    small = [
        pltpu.make_async_copy(source, target, small_sem.at[n])
        for n, (source, target) in enumerate(zip(sources, outs))
    ]
    for copy in small:
        copy.start()
    turn = turn_of(tile.shape[0])

    def copy_turn(index):
        blocks = pl.ds(index * turn, turn)
        return pltpu.make_async_copy(tile.at[blocks], outs[4].at[blocks], sem.at[index])

    def begin(index, carry):
        copy_turn(index).start()
        return carry

    def wait(index, carry):
        copy_turn(index).wait()
        return carry

    turns = (count[0, 0] + turn - 1) // turn
    lax.fori_loop(0, turns, begin, 0)
    lax.fori_loop(0, turns, wait, 0)
    for copy in small:
        copy.wait()


def fetch(count, rows, cols, features, tile):
    arrays = (rows, cols, features, tile)
    half = jax.ShapeDtypeStruct((features.shape[0] // 2, features.shape[1]), features.dtype)
    outs = [jax.ShapeDtypeStruct(array.shape, array.dtype) for array in (rows, cols)] + [half] * 2
    return pl.pallas_call(
        fetch_kernel,
        out_shape=outs + [jax.ShapeDtypeStruct(tile.shape, tile.dtype)],
        in_specs=[SMEM] + [HBM] * 4,
        out_specs=[VMEM] * 5,
        scratch_shapes=[
            pltpu.SemaphoreType.DMA((tile.shape[0] // turn_of(tile.shape[0]),)),
            pltpu.SemaphoreType.DMA((4,)),
        ],
        compiler_params=params(4),
        cost_estimate=COST,
        name="fetch",
    )(count, *[pltpu.with_memory_space_constraint(array, pltpu.HBM) for array in arrays])


def forward_kernel(n_parts, depths, layout, place, count, rows, cols, adj, *refs):
    parts, refs = refs[:n_parts], refs[n_parts:]
    source, total = refs[-2:]
    outs = refs[-2 - len(depths) * len(layout) : -2]
    carried = refs[: len(refs) - 2 - len(outs)]
    size = adj.shape[1]
    row = 0
    for part in parts:
        depth = part.shape[0]
        for c in range(source.shape[0]):
            source[c, row : row + depth, :] = part[:, c * size : (c + 1) * size]
        row += depth
    product_loop(count[0, 0], cols, rows, adj, source, total, NT)
    blocks = outs[0].shape[1] // size
    ahead = carried[0].shape[0] // len(layout[0]) if carried else 0
    outs = iter(outs)
    row = 0
    for depth in depths:
        for m, chunks in enumerate(layout):
            out = next(outs)
            for n, k in enumerate(chunks):
                begin = n * (ahead + depth)
                if ahead:
                    out[begin : begin + ahead, :] = carried[m][n * ahead : (n + 1) * ahead, :]
                first = (place[0] ^ k) * blocks
                for i in range(blocks):
                    out[begin + ahead : begin + ahead + depth, i * size : (i + 1) * size] = total[
                        first + i, row : row + depth, :
                    ].astype(out.dtype)
        row += depth


def forward(place, count, rows, cols, adj, parts, row_blocks, depths, layout, carried=()):
    size = adj.shape[1]
    col_blocks = parts[0].shape[1] // size
    wide = row_blocks * size // sum(len(chunks) for chunks in layout)
    ahead = carried[0].shape[0] // len(layout[0]) if carried else 0
    outs = [
        jax.ShapeDtypeStruct((len(chunks) * (ahead + depth), wide), jnp.bfloat16)
        for depth in depths
        for chunks in layout
    ]
    return pl.pallas_call(
        functools.partial(forward_kernel, len(parts), depths, layout),
        out_shape=outs,
        in_specs=[SMEM] * 4 + [VMEM] * (1 + len(parts) + len(carried)),
        out_specs=[VMEM] * len(outs),
        scratch_shapes=[
            pltpu.VMEM((col_blocks, sum(depths), size), jnp.bfloat16),
            pltpu.VMEM((row_blocks + 1, sum(depths), size), jnp.float32),
        ],
        compiler_params=params(14),
        cost_estimate=COST,
        name="forward_products",
    )(place, count, rows, cols, adj, *parts, *carried)


def backward_kernel(spots, depths, place, count, rows, cols, adj, *refs):
    n_parts = 1 + max(part for places in spots for part, _ in places)
    parts = refs[:n_parts]
    outs = refs[n_parts:-2]
    source, total = refs[-2:]
    size = adj.shape[1]
    blocks = parts[0].shape[1] // size
    for k, places in enumerate(spots):
        first = (place[0] ^ k) * blocks
        row = 0
        for (part, offset), depth in zip(places, depths):
            for i in range(blocks):
                source[first + i, row : row + depth, :] = parts[part][
                    offset : offset + depth, i * size : (i + 1) * size
                ]
            row += depth
    product_loop(count[0, 0], rows, cols, adj, source, total, NN)
    row = 0
    for out in outs:
        depth = out.shape[0]
        for c in range(total.shape[0] - 1):
            out[:, c * size : (c + 1) * size] = total[c, row : row + depth, :].astype(out.dtype)
        row += depth


def backward(place, count, rows, cols, adj, parts, spots, depths, out_depths, col_blocks):
    size = adj.shape[1]
    row_blocks = len(spots) * parts[0].shape[1] // size
    return pl.pallas_call(
        functools.partial(backward_kernel, spots, depths),
        out_shape=[jax.ShapeDtypeStruct((depth, col_blocks * size), jnp.bfloat16) for depth in out_depths],
        in_specs=[SMEM] * 4 + [VMEM] * (1 + len(parts)),
        out_specs=[VMEM] * len(out_depths),
        scratch_shapes=[
            pltpu.VMEM((row_blocks, sum(out_depths), size), jnp.bfloat16),
            pltpu.VMEM((col_blocks + 1, sum(out_depths), size), jnp.float32),
        ],
        compiler_params=params(14),
        cost_estimate=COST,
        name="backward_products",
    )(place, count, rows, cols, adj, *parts)


def middle_kernel(sizes, order, n_sum, n_row, row, weight, cotangent, *refs):
    terms = refs[: n_sum * len(sizes)]
    outs = refs[n_sum * len(sizes) : -1]
    output, deltas, aggregated, *backs = outs
    ordered = refs[-1]
    depth = weight.shape[0] // n_row
    for j in range(n_row):
        first = pl.multiple_of((row[0] ^ j) * depth, depth)
        ordered[j * depth : (j + 1) * depth, :] = weight[pl.ds(first, depth), :]
    first = 0
    for p, size in enumerate(sizes):
        summed = terms[p * n_sum][:size, :].astype(jnp.float32)
        for k in range(1, n_sum):
            summed += terms[p * n_sum + k][:size, :].astype(jnp.float32)
        aggregated[first : first + size, :] = summed.astype(jnp.bfloat16)
        first += size
    nodes_first = aggregated[...].T
    preact = jnp.dot(nodes_first, ordered[...], preferred_element_type=jnp.float32)
    gate = jax.nn.sigmoid(preact)
    output[...] = (preact * gate).astype(jnp.bfloat16)
    slopes = gate * (1.0 + preact * (1.0 - gate))
    delta = (cotangent[...].astype(jnp.float32) * slopes).astype(jnp.bfloat16)
    deltas[...] = delta
    product = lax.dot_general(ordered[...], delta, NT, preferred_element_type=jnp.float32)
    product = jnp.concatenate([product[k * depth : (k + 1) * depth, :] for k in order]).astype(jnp.bfloat16)
    first = 0
    for back in backs:
        first %= product.shape[0]
        back[...] = product[first : first + back.shape[0], :]
        first += back.shape[0]


def middle(n_row, row, weight, cotangent, pieces, order, depths):
    sizes = [piece[0].shape[0] for piece in pieces]
    nodes = cotangent.shape[0]
    features = weight.shape[0]
    shape = jax.ShapeDtypeStruct
    outs = [
        shape((nodes, features), jnp.bfloat16),
        shape((nodes, features), jnp.bfloat16),
        shape((features, nodes), jnp.bfloat16),
    ] + [shape((depth, nodes), jnp.bfloat16) for depth in depths]
    flat = [term for piece in pieces for term in piece]
    return pl.pallas_call(
        functools.partial(middle_kernel, sizes, order, len(pieces[0]), n_row),
        out_shape=outs,
        in_specs=[SMEM] + [VMEM] * (2 + len(flat)),
        out_specs=[VMEM] * len(outs),
        scratch_shapes=[pltpu.VMEM(weight.shape, jnp.bfloat16)],
        compiler_params=params(10),
        cost_estimate=COST,
        name="layer",
    )(row, weight, cotangent, *flat)


def gradient_kernel(scale, order, aggregated, deltas, *outs):
    product = jnp.dot(aggregated[...], deltas[...], preferred_element_type=jnp.float32) * scale
    for out, chunks in zip(outs, order):
        depth = out.shape[1]
        for n, k in enumerate(chunks):
            out[n] = product[k * depth : (k + 1) * depth, :]


def gradient(scale, order, aggregated, deltas):
    depth = aggregated.shape[0] // sum(len(chunks) for chunks in order)
    outs = [jax.ShapeDtypeStruct((len(chunks), depth, deltas.shape[1]), jnp.float32) for chunks in order]
    return pl.pallas_call(
        functools.partial(gradient_kernel, scale, order),
        out_shape=outs,
        in_specs=[VMEM] * 2,
        out_specs=[VMEM] * len(outs),
        compiler_params=params(6),
        cost_estimate=COST,
        name="weight_gradient",
    )(aggregated, deltas)


def swap(value, axis, k):
    size = lax.axis_size(axis)
    return lax.ppermute(value, axis, [(i, i ^ k) for i in range(size)])


def wide_sum(*values):
    total = values[0].astype(jnp.float32)
    for value in values[1:]:
        total = total + value.astype(jnp.float32)
    return (total.astype(values[0].dtype),)


def after(value, *earlier):
    return lax.optimization_barrier((value, *earlier))[0]


def with_chunk(rows, chunk):
    high = chunk.astype(jnp.bfloat16)
    low = (chunk - high.astype(jnp.float32)).astype(jnp.bfloat16)
    return (jnp.concatenate([rows, jnp.concatenate([high, low], axis=1)]),)


def chunk_sum(depth, *values):
    total = None
    for value in values:
        halves = value[-depth:].astype(jnp.float32)
        wide = halves.shape[1] // 2
        chunk = halves[:, :wide] + halves[:, wide:]
        total = chunk if total is None else total + chunk
    return (total,)


def halves_sum(mine, *received):
    total = mine + jnp.concatenate(received)
    half = total.shape[0] // 2
    return total[:half], total[half:]


def far_sums(depth, mine, *received):
    total = mine.astype(jnp.float32) + jnp.concatenate(received).astype(jnp.float32)
    total = total.astype(mine.dtype)
    own, far = total[:depth], total[depth:]
    return own, jnp.concatenate([far, far[:, :128]], axis=1)


def near_kernel(row, chunk, sibling, half_way, mine, *refs):
    received, (chunks, *sums) = refs[: -1 - 2], refs[-1 - 2 :]
    depth = half_way.shape[0]
    nodes = mine.shape[1]
    for k, ref in enumerate((chunk, sibling)):
        wide = ref.shape[1]
        chunks[:, k * wide : (k + 1) * wide] = ref[...].astype(chunks.dtype)
    passed = half_way[:, :nodes].astype(jnp.float32)
    odd = row[0] % 2
    for n, out in enumerate(sums):
        total = mine[n * depth : (n + 1) * depth, :].astype(jnp.float32) + received[n][...].astype(jnp.float32)
        total += jnp.where(odd == 1 - n, passed, 0.0)
        out[:, :nodes] = total.astype(out.dtype)
        out[:, nodes:] = chunks[...]


def near_payloads(row, chunk, sibling, half_way, mine, received):
    depth, nodes = received[0].shape
    wide = 2 * chunk.shape[1]
    shape = jax.ShapeDtypeStruct
    return pl.pallas_call(
        near_kernel,
        out_shape=[shape((depth, wide), mine.dtype)]
        + [shape((depth, nodes + wide), mine.dtype)] * len(received),
        in_specs=[SMEM] + [VMEM] * (4 + len(received)),
        out_specs=[VMEM] * (1 + len(received)),
        compiler_params=params(8),
        cost_estimate=COST,
        name="near_payloads",
    )(row, chunk, sibling, half_way, mine, *received)


def finish_kernel(keys, row, *refs):
    grad_features, grad_weight = refs[-2:]
    depth, nodes = grad_features.shape
    wide = grad_weight.shape[1]
    parts = [ref for ref in refs[:-2] if ref.shape[1] >= nodes]
    values = [ref[...] for ref in refs[:-2] if ref.shape[1] < nodes] + [part[:, nodes:] for part in parts[1:]]
    total = parts[0][...].astype(jnp.float32)
    for part in parts[1:]:
        total += part[:, :nodes].astype(jnp.float32)
    grad_features[...] = total.astype(grad_features.dtype)
    for key, value in zip(keys, values):
        for k in range(2):
            first = pl.multiple_of((row[0] ^ (key + k)) * depth, depth)
            grad_weight[pl.ds(first, depth), :] = value[:, k * wide : (k + 1) * wide].astype(jnp.float32)


def finish(row, keys, parts, chunks):
    depth, nodes = parts[0].shape
    return pl.pallas_call(
        functools.partial(finish_kernel, keys),
        out_shape=[
            jax.ShapeDtypeStruct((depth, nodes), jnp.bfloat16),
            jax.ShapeDtypeStruct((2 * len(keys) * depth, chunks[0].shape[1] // 2), jnp.float32),
        ],
        in_specs=[SMEM] + [VMEM] * (len(parts) + len(chunks)),
        out_specs=[VMEM] * 2,
        compiler_params=params(8),
        cost_estimate=COST,
        name="finish",
    )(row, *parts, *chunks)


def shards_exchanged(features, weight, adj_values, block_rows, block_cols, block_counts, cotangent):
    n_row = lax.axis_size("row")
    n_col = lax.axis_size("col")
    adj = adj_values[0, 0]
    rows = block_rows[0, 0]
    cols = block_cols[0, 0]
    count = block_counts
    size = adj.shape[1]
    nodes = cotangent.shape[0] * n_row * n_col
    row_blocks = cotangent.shape[0] * n_col // size
    col_blocks = features.shape[0] // size
    row = lax.axis_index("row").reshape(1)
    col = lax.axis_index("col").reshape(1)
    own = after(features.T, row, col)

    depth = features.shape[1]
    near = [k for k in range(2, n_row, 2) if k & (k - 1) == 0]
    far = [k for k in range(2, n_row, 2) if k & (k - 1) != 0]
    sibling = swap(own, "row", 1)
    from_near = [swap(own, "row", k) for k in near]
    rows, cols, *halves, tile = fetch(count, rows, cols, own, adj)
    from_near = [after(part, tile) for part in from_near]
    from_far = [swap(half, "row", k) for k in far for half in halves]

    def pass_on(beyond, received):
        return wide_sum(beyond, received[beyond.shape[0] :])

    layout = [(0,), (2,), (1, 3)]

    def fold(kept, beyond, received):
        (passed,) = fuse("pass_on", pass_on, beyond, received)
        return [kept, received, swap(passed, "col", 2)]

    n_near = 2 * depth * (1 + len(near))
    cut = n_near * 5 // 6
    parts = [own, sibling] + [piece for part in from_near for piece in (part, swap(part, "row", 1))]
    kept, beyond, sent, *carried = forward(
        col, count, rows, cols, tile, parts, row_blocks, [cut, n_near - cut], layout
    )
    received = swap(sent, "col", 1)
    from_far = [after(part, kept) for part in from_far]
    parts = []
    for n in range(0, len(from_far), 2):
        halves = from_far[n : n + 2]
        parts += halves + [swap(half, "row", 1) for half in halves]
    far_piece = forward(
        col, count, rows, cols, tile, parts, row_blocks, [2 * depth * len(far)], layout, carried
    )
    far_received = swap(far_piece[2], "col", 1)
    first = fold(kept, beyond, after(received, far_piece[0]))
    second = fold(*far_piece[:2], after(far_received, first[1]))
    sums = [first, second]

    groups = [[0] + far, near]
    order = [k + side for group in groups for side in range(2) for k in group]
    cuts = [2 * depth * len(group) for group in groups]
    ahead = depth // 2
    output, deltas, aggregated, back, *backs = middle(
        n_row, row, weight, cotangent, sums, order, [sum(cuts), cuts[0] + ahead, cuts[1] - ahead]
    )
    beside = swap(back, "col", 1)
    beyond = [swap(part, "col", 2) for part in backs]

    even, *odd = gradient(1.0 / math.sqrt(nodes), [(0, 4, 2, 6), (1, 5), (3, 7)], aggregated, deltas)
    even, sent = fuse("gradient_sum", halves_sum, even, *[swap(part, "row", 1) for part in odd])
    even, sent = fuse("gradient_sum", halves_sum, even, swap(sent, "row", 2))
    beyond[0] = after(beyond[0], sent)
    even = after(even, beyond[1], beside)
    (chunk,) = fuse("gradient_sum", lambda a, b: ((a + b)[0],), even, swap(sent, "row", 4))
    (second,) = fuse("with_chunk", with_chunk, beyond[1], chunk)
    received = [swap(beyond[0], "col", 1), swap(second, "col", 1)]

    def columns(n, *earlier):
        parts = [back, beside, after(beyond[0], *earlier), received[0], beyond[1], received[1]]
        if n == 0:
            depths = cuts[:1]
            parts = parts[:4]
            spots = [[(part, 0)] for part in range(4)]
        else:
            depths = [ahead, cuts[1] - ahead]
            spots = [[(part, cuts[0]), (part, cuts[0] + ahead)] for part in range(2)]
            spots += [[(part, cuts[0]), (part + 2, 0)] for part in (2, 3)]
        out_depths = [cuts[n] // 2] + [cuts[n] // (8 - 4 * n)] * (4 - 2 * n)
        mine, *sent = backward(
            col, count, rows, cols, tile, parts, spots, depths, out_depths, col_blocks
        )
        return [mine] + [swap(part, "row", 1) for part in sent]

    own_sum, far_sum = fuse("far_sums", functools.partial(far_sums, depth), *columns(0, second))
    half_way = lax.ppermute(far_sum, "row", [(i, i ^ (4 if i % 2 else 2)) for i in range(n_row)])
    (chunk,) = fuse("chunk_sum", functools.partial(chunk_sum, depth), second, received[1])
    (chunk,) = fuse("chunk_sum", wide_sum, chunk, swap(chunk, "col", 2))
    mine, *from_sibling = columns(1, chunk, far_sum)
    chunks, *near_sums = near_payloads(row, chunk, swap(chunk, "row", 1), half_way, mine, from_sibling)
    near_sums = [swap(part, "row", k) for part, k in zip(near_sums, near)]
    far_chunks = [swap(chunks, "row", k) for k in far]
    grad_features, grad_weight = finish(row, [0] + far + near, [own_sum] + near_sums, [chunks] + far_chunks)
    return output, grad_weight, grad_features.T


def shards_gathered(features, weight, adj_values, block_rows, block_cols, block_counts, cotangent):
    n_row = lax.axis_size("row")
    n_col = lax.axis_size("col")
    adj = adj_values[0, 0]
    rows = block_rows[0, 0]
    cols = block_cols[0, 0]
    count = block_counts
    size = adj.shape[1]
    nodes = cotangent.shape[0] * n_row * n_col
    row_blocks = cotangent.shape[0] * n_col // size
    col_blocks = features.shape[0] // size
    zero = jnp.zeros((1,), jnp.int32)
    panels = lax.all_gather(features.T, "row", axis=0, tiled=True)
    (terms,) = forward(zero, count, rows, cols, adj, [panels], row_blocks, [panels.shape[0]], [(0,)])
    part = lax.psum_scatter(terms, "col", scatter_dimension=1, tiled=True)
    output, deltas, aggregated, back = middle(1, zero, weight, cotangent, [[part]], (0,), [weight.shape[0]])
    slab = lax.all_gather(back, "col", axis=1, tiled=True)
    (column_terms,) = backward(zero, count, rows, cols, adj, [slab], [[(0, 0)]], [slab.shape[0]], [slab.shape[0]], col_blocks)
    grad_features = lax.psum_scatter(column_terms, "row", scatter_dimension=0, tiled=True).T
    (part,) = gradient(1.0 / math.sqrt(nodes), [(0,)], aggregated, deltas)
    grad_weight = lax.psum(part[0], ("row", "col"))
    return output, grad_weight, grad_features


def solution(mesh):
    n_row = mesh.shape["row"]
    n_col = mesh.shape["col"]
    exchanged = n_row == 8 and n_col == 4
    return jax.shard_map(
        shards_exchanged if exchanged else shards_gathered,
        mesh=mesh,
        in_specs=(
            P("col", "row"),
            P(),
            P("row", "col", None, None, None),
            P("row", "col", None),
            P("row", "col", None),
            P("row", "col"),
            P(("row", "col"), None),
        ),
        out_specs=(P(("row", "col"), None), P(), P("col", "row")),
        check_vma=False,
    )
```

```python
import functools
import math

import jax
import jax.numpy as jnp
from jax import lax
from jax.experimental import pallas as pl
from jax.experimental.pallas import tpu as pltpu
from jax.sharding import PartitionSpec as P

VMEM = pl.BlockSpec(memory_space=pltpu.VMEM)
SMEM = pl.BlockSpec(memory_space=pltpu.SMEM)
HBM = pl.BlockSpec(memory_space=pltpu.HBM)
MIB = 1024 * 1024
NT = (((1,), (1,)), ((), ()))
NN = (((1,), (0,)), ((), ()))


COST = pl.CostEstimate(flops=1, bytes_accessed=1, transcendentals=0)


def params(mib):
    return pltpu.CompilerParams(vmem_limit_bytes=mib * MIB)


def fuse(name, function, *values):
    shapes = jax.eval_shape(function, *values)

    def kernel(*refs):
        results = function(*[ref[...] for ref in refs[: len(values)]])
        for ref, result in zip(refs[len(values) :], results):
            ref[...] = result

    return pl.pallas_call(
        kernel,
        out_shape=shapes,
        in_specs=[VMEM] * len(values),
        out_specs=[VMEM] * len(shapes),
        compiler_params=params(4),
        cost_estimate=COST,
        name=name,
    )(*values)


def turn_of(slots):
    return math.gcd(slots, 8)


def product_loop(count, source_ids, target_ids, adj, source, total, dims):
    turn = turn_of(adj.shape[0])
    spare = total.shape[0] - 1
    total[...] = jnp.zeros_like(total)

    def step(index, carry):
        first = index * turn
        for k in range(turn):
            slot = first + k
            product = lax.dot_general(
                source[source_ids[slot]], adj[slot], dims, preferred_element_type=jnp.float32
            )
            target = jnp.where(slot < count, target_ids[slot], spare)
            total[target] += product
        return carry

    lax.fori_loop(0, (count + turn - 1) // turn, step, 0)


def fetch_kernel(count, rows, cols, features, tile, *refs):
    outs, (sem, small_sem) = refs[:5], refs[5:]
    half = features.shape[0] // 2
    sources = (rows, cols, features.at[pl.ds(0, half)], features.at[pl.ds(half, half)])
    small = [
        pltpu.make_async_copy(source, target, small_sem.at[n])
        for n, (source, target) in enumerate(zip(sources, outs))
    ]
    for copy in small:
        copy.start()
    turn = turn_of(tile.shape[0])

    def copy_turn(index):
        blocks = pl.ds(index * turn, turn)
        return pltpu.make_async_copy(tile.at[blocks], outs[4].at[blocks], sem.at[index])

    def begin(index, carry):
        copy_turn(index).start()
        return carry

    def wait(index, carry):
        copy_turn(index).wait()
        return carry

    turns = (count[0, 0] + turn - 1) // turn
    lax.fori_loop(0, turns, begin, 0)
    lax.fori_loop(0, turns, wait, 0)
    for copy in small:
        copy.wait()


def fetch(count, rows, cols, features, tile):
    arrays = (rows, cols, features, tile)
    half = jax.ShapeDtypeStruct((features.shape[0] // 2, features.shape[1]), features.dtype)
    outs = [jax.ShapeDtypeStruct(array.shape, array.dtype) for array in (rows, cols)] + [half] * 2
    return pl.pallas_call(
        fetch_kernel,
        out_shape=outs + [jax.ShapeDtypeStruct(tile.shape, tile.dtype)],
        in_specs=[SMEM] + [HBM] * 4,
        out_specs=[VMEM] * 5,
        scratch_shapes=[
            pltpu.SemaphoreType.DMA((tile.shape[0] // turn_of(tile.shape[0]),)),
            pltpu.SemaphoreType.DMA((4,)),
        ],
        compiler_params=params(4),
        cost_estimate=COST,
        name="fetch",
    )(count, *[pltpu.with_memory_space_constraint(array, pltpu.HBM) for array in arrays])


def forward_kernel(n_parts, depths, layout, place, count, rows, cols, adj, *refs):
    parts, refs = refs[:n_parts], refs[n_parts:]
    source, total = refs[-2:]
    outs = refs[-2 - len(depths) * len(layout) : -2]
    carried = refs[: len(refs) - 2 - len(outs)]
    size = adj.shape[1]
    row = 0
    for part in parts:
        depth = part.shape[0]
        for c in range(source.shape[0]):
            source[c, row : row + depth, :] = part[:, c * size : (c + 1) * size]
        row += depth
    product_loop(count[0, 0], cols, rows, adj, source, total, NT)
    blocks = outs[0].shape[1] // size
    ahead = carried[0].shape[0] // len(layout[0]) if carried else 0
    outs = iter(outs)
    row = 0
    for depth in depths:
        for m, chunks in enumerate(layout):
            out = next(outs)
            for n, k in enumerate(chunks):
                begin = n * (ahead + depth)
                if ahead:
                    out[begin : begin + ahead, :] = carried[m][n * ahead : (n + 1) * ahead, :]
                first = (place[0] ^ k) * blocks
                for i in range(blocks):
                    out[begin + ahead : begin + ahead + depth, i * size : (i + 1) * size] = total[
                        first + i, row : row + depth, :
                    ].astype(out.dtype)
        row += depth


def forward(place, count, rows, cols, adj, parts, row_blocks, depths, layout, carried=()):
    size = adj.shape[1]
    col_blocks = parts[0].shape[1] // size
    wide = row_blocks * size // sum(len(chunks) for chunks in layout)
    ahead = carried[0].shape[0] // len(layout[0]) if carried else 0
    outs = [
        jax.ShapeDtypeStruct((len(chunks) * (ahead + depth), wide), jnp.bfloat16)
        for depth in depths
        for chunks in layout
    ]
    return pl.pallas_call(
        functools.partial(forward_kernel, len(parts), depths, layout),
        out_shape=outs,
        in_specs=[SMEM] * 4 + [VMEM] * (1 + len(parts) + len(carried)),
        out_specs=[VMEM] * len(outs),
        scratch_shapes=[
            pltpu.VMEM((col_blocks, sum(depths), size), jnp.bfloat16),
            pltpu.VMEM((row_blocks + 1, sum(depths), size), jnp.float32),
        ],
        compiler_params=params(14),
        cost_estimate=COST,
        name="forward_products",
    )(place, count, rows, cols, adj, *parts, *carried)


def backward_kernel(spots, depths, place, count, rows, cols, adj, *refs):
    n_parts = 1 + max(part for places in spots for part, _ in places)
    parts = refs[:n_parts]
    outs = refs[n_parts:-2]
    source, total = refs[-2:]
    size = adj.shape[1]
    blocks = parts[0].shape[1] // size
    for k, places in enumerate(spots):
        first = (place[0] ^ k) * blocks
        row = 0
        for (part, offset), depth in zip(places, depths):
            for i in range(blocks):
                source[first + i, row : row + depth, :] = parts[part][
                    offset : offset + depth, i * size : (i + 1) * size
                ]
            row += depth
    product_loop(count[0, 0], rows, cols, adj, source, total, NN)
    row = 0
    for out in outs:
        depth = out.shape[0]
        for c in range(total.shape[0] - 1):
            out[:, c * size : (c + 1) * size] = total[c, row : row + depth, :].astype(out.dtype)
        row += depth


def backward(place, count, rows, cols, adj, parts, spots, depths, out_depths, col_blocks):
    size = adj.shape[1]
    row_blocks = len(spots) * parts[0].shape[1] // size
    return pl.pallas_call(
        functools.partial(backward_kernel, spots, depths),
        out_shape=[jax.ShapeDtypeStruct((depth, col_blocks * size), jnp.bfloat16) for depth in out_depths],
        in_specs=[SMEM] * 4 + [VMEM] * (1 + len(parts)),
        out_specs=[VMEM] * len(out_depths),
        scratch_shapes=[
            pltpu.VMEM((row_blocks, sum(out_depths), size), jnp.bfloat16),
            pltpu.VMEM((col_blocks + 1, sum(out_depths), size), jnp.float32),
        ],
        compiler_params=params(14),
        cost_estimate=COST,
        name="backward_products",
    )(place, count, rows, cols, adj, *parts)


def middle_kernel(sizes, order, n_sum, n_row, row, weight, cotangent, *refs):
    terms = refs[: n_sum * len(sizes)]
    outs = refs[n_sum * len(sizes) : -1]
    output, deltas, aggregated, *backs = outs
    ordered = refs[-1]
    depth = weight.shape[0] // n_row
    for j in range(n_row):
        first = pl.multiple_of((row[0] ^ j) * depth, depth)
        ordered[j * depth : (j + 1) * depth, :] = weight[pl.ds(first, depth), :]
    first = 0
    for p, size in enumerate(sizes):
        summed = terms[p * n_sum][:size, :].astype(jnp.float32)
        for k in range(1, n_sum):
            summed += terms[p * n_sum + k][:size, :].astype(jnp.float32)
        aggregated[first : first + size, :] = summed.astype(jnp.bfloat16)
        first += size
    nodes_first = aggregated[...].T
    preact = jnp.dot(nodes_first, ordered[...], preferred_element_type=jnp.float32)
    gate = jax.nn.sigmoid(preact)
    output[...] = (preact * gate).astype(jnp.bfloat16)
    slopes = gate * (1.0 + preact * (1.0 - gate))
    delta = (cotangent[...].astype(jnp.float32) * slopes).astype(jnp.bfloat16)
    deltas[...] = delta
    product = lax.dot_general(ordered[...], delta, NT, preferred_element_type=jnp.float32)
    product = jnp.concatenate([product[k * depth : (k + 1) * depth, :] for k in order]).astype(jnp.bfloat16)
    first = 0
    for back in backs:
        first %= product.shape[0]
        back[...] = product[first : first + back.shape[0], :]
        first += back.shape[0]


def middle(n_row, row, weight, cotangent, pieces, order, depths):
    sizes = [piece[0].shape[0] for piece in pieces]
    nodes = cotangent.shape[0]
    features = weight.shape[0]
    shape = jax.ShapeDtypeStruct
    outs = [
        shape((nodes, features), jnp.bfloat16),
        shape((nodes, features), jnp.bfloat16),
        shape((features, nodes), jnp.bfloat16),
    ] + [shape((depth, nodes), jnp.bfloat16) for depth in depths]
    flat = [term for piece in pieces for term in piece]
    return pl.pallas_call(
        functools.partial(middle_kernel, sizes, order, len(pieces[0]), n_row),
        out_shape=outs,
        in_specs=[SMEM] + [VMEM] * (2 + len(flat)),
        out_specs=[VMEM] * len(outs),
        scratch_shapes=[pltpu.VMEM(weight.shape, jnp.bfloat16)],
        compiler_params=params(10),
        cost_estimate=COST,
        name="layer",
    )(row, weight, cotangent, *flat)


def gradient_kernel(scale, order, aggregated, deltas, *outs):
    product = jnp.dot(aggregated[...], deltas[...], preferred_element_type=jnp.float32) * scale
    for out, chunks in zip(outs, order):
        depth = out.shape[1]
        for n, k in enumerate(chunks):
            out[n] = product[k * depth : (k + 1) * depth, :]


def gradient(scale, order, aggregated, deltas):
    depth = aggregated.shape[0] // sum(len(chunks) for chunks in order)
    outs = [jax.ShapeDtypeStruct((len(chunks), depth, deltas.shape[1]), jnp.float32) for chunks in order]
    return pl.pallas_call(
        functools.partial(gradient_kernel, scale, order),
        out_shape=outs,
        in_specs=[VMEM] * 2,
        out_specs=[VMEM] * len(outs),
        compiler_params=params(6),
        cost_estimate=COST,
        name="weight_gradient",
    )(aggregated, deltas)


def swap(value, axis, k):
    size = lax.axis_size(axis)
    return lax.ppermute(value, axis, [(i, i ^ k) for i in range(size)])


def wide_sum(*values):
    total = values[0].astype(jnp.float32)
    for value in values[1:]:
        total = total + value.astype(jnp.float32)
    return (total.astype(values[0].dtype),)


def after(value, *earlier):
    return lax.optimization_barrier((value, *earlier))[0]


def with_chunk(rows, *chunks):
    chunk = jnp.concatenate(chunks)
    high = chunk.astype(jnp.bfloat16)
    low = (chunk - high.astype(jnp.float32)).astype(jnp.bfloat16)
    return (jnp.concatenate([rows, jnp.concatenate([high, low], axis=1)]),)


def chunk_sum(depth, *values):
    total = None
    for value in values:
        halves = value[-depth:].astype(jnp.float32)
        wide = halves.shape[1] // 2
        chunk = halves[:, :wide] + halves[:, wide:]
        total = chunk if total is None else total + chunk
    return (total,)


def halves_sum(mine, *received):
    total = mine + jnp.concatenate(received)
    half = total.shape[0] // 2
    return total[:half], total[half:]


def far_sums(depth, mine, *received):
    total = mine.astype(jnp.float32) + jnp.concatenate(received).astype(jnp.float32)
    total = total.astype(mine.dtype)
    own, far = total[:depth], total[depth:]
    return own, jnp.concatenate([far, far[:, :128]], axis=1)


def near_kernel(row, chunk, half_way, mine, *refs):
    received, (chunks, *sums) = refs[: -1 - 2], refs[-1 - 2 :]
    depth = half_way.shape[0]
    nodes = mine.shape[1]
    wide = chunk.shape[1]
    for k in range(2):
        chunks[:, k * wide : (k + 1) * wide] = chunk[k * depth : (k + 1) * depth, :].astype(chunks.dtype)
    passed = half_way[:, :nodes].astype(jnp.float32)
    odd = row[0] % 2
    for n, out in enumerate(sums):
        total = mine[n * depth : (n + 1) * depth, :].astype(jnp.float32) + received[n][...].astype(jnp.float32)
        total += jnp.where(odd == 1 - n, passed, 0.0)
        out[:, :nodes] = total.astype(out.dtype)
        out[:, nodes:] = chunks[...]


def near_payloads(row, chunk, half_way, mine, received):
    depth, nodes = received[0].shape
    wide = 2 * chunk.shape[1]
    shape = jax.ShapeDtypeStruct
    return pl.pallas_call(
        near_kernel,
        out_shape=[shape((depth, wide), mine.dtype)]
        + [shape((depth, nodes + wide), mine.dtype)] * len(received),
        in_specs=[SMEM] + [VMEM] * (3 + len(received)),
        out_specs=[VMEM] * (1 + len(received)),
        compiler_params=params(8),
        cost_estimate=COST,
        name="near_payloads",
    )(row, chunk, half_way, mine, *received)


def finish_kernel(keys, row, *refs):
    grad_features, grad_weight = refs[-2:]
    depth, nodes = grad_features.shape
    wide = grad_weight.shape[1]
    parts = [ref for ref in refs[:-2] if ref.shape[1] >= nodes]
    values = [ref[...] for ref in refs[:-2] if ref.shape[1] < nodes] + [part[:, nodes:] for part in parts[1:]]
    total = parts[0][...].astype(jnp.float32)
    for part in parts[1:]:
        total += part[:, :nodes].astype(jnp.float32)
    grad_features[...] = total.astype(grad_features.dtype)
    for key, value in zip(keys, values):
        for k in range(2):
            first = pl.multiple_of((row[0] ^ (key + k)) * depth, depth)
            grad_weight[pl.ds(first, depth), :] = value[:, k * wide : (k + 1) * wide].astype(jnp.float32)


def finish(row, keys, parts, chunks):
    depth, nodes = parts[0].shape
    return pl.pallas_call(
        functools.partial(finish_kernel, keys),
        out_shape=[
            jax.ShapeDtypeStruct((depth, nodes), jnp.bfloat16),
            jax.ShapeDtypeStruct((2 * len(keys) * depth, chunks[0].shape[1] // 2), jnp.float32),
        ],
        in_specs=[SMEM] + [VMEM] * (len(parts) + len(chunks)),
        out_specs=[VMEM] * 2,
        compiler_params=params(8),
        cost_estimate=COST,
        name="finish",
    )(row, *parts, *chunks)


def shards_exchanged(features, weight, adj_values, block_rows, block_cols, block_counts, cotangent):
    n_row = lax.axis_size("row")
    n_col = lax.axis_size("col")
    adj = adj_values[0, 0]
    rows = block_rows[0, 0]
    cols = block_cols[0, 0]
    count = block_counts
    size = adj.shape[1]
    nodes = cotangent.shape[0] * n_row * n_col
    row_blocks = cotangent.shape[0] * n_col // size
    col_blocks = features.shape[0] // size
    row = lax.axis_index("row").reshape(1)
    col = lax.axis_index("col").reshape(1)
    own = after(features.T, row, col)

    depth = features.shape[1]
    near = [k for k in range(2, n_row, 2) if k & (k - 1) == 0]
    far = [k for k in range(2, n_row, 2) if k & (k - 1) != 0]
    sibling = swap(own, "row", 1)
    from_near = [swap(own, "row", k) for k in near]
    rows, cols, *halves, tile = fetch(count, rows, cols, own, adj)
    from_near = [after(part, tile) for part in from_near]
    from_far = [swap(half, "row", k) for k in far for half in halves]

    def pass_on(beyond, received):
        return wide_sum(beyond, received[beyond.shape[0] :])

    layout = [(0,), (2,), (1, 3)]

    def fold(kept, beyond, received):
        (passed,) = fuse("pass_on", pass_on, beyond, received)
        return [kept, received, swap(passed, "col", 2)]

    n_near = 2 * depth * (1 + len(near))
    cut = n_near * 5 // 6
    parts = [own, sibling] + [piece for part in from_near for piece in (part, swap(part, "row", 1))]
    kept, beyond, sent, *carried = forward(
        col, count, rows, cols, tile, parts, row_blocks, [cut, n_near - cut], layout
    )
    received = swap(sent, "col", 1)
    from_far = [after(part, kept) for part in from_far]
    parts = []
    for n in range(0, len(from_far), 2):
        halves = from_far[n : n + 2]
        parts += halves + [swap(half, "row", 1) for half in halves]
    far_piece = forward(
        col, count, rows, cols, tile, parts, row_blocks, [2 * depth * len(far)], layout, carried
    )
    far_received = swap(far_piece[2], "col", 1)
    first = fold(kept, beyond, after(received, far_piece[0]))
    second = fold(*far_piece[:2], after(far_received, first[1]))
    sums = [first, second]

    groups = [[0] + far, near]
    order = [k + side for group in groups for side in range(2) for k in group]
    cuts = [2 * depth * len(group) for group in groups]
    ahead = depth // 2
    output, deltas, aggregated, back, *backs = middle(
        n_row, row, weight, cotangent, sums, order, [sum(cuts), cuts[0] + ahead, cuts[1] - ahead]
    )
    beside = swap(back, "col", 1)
    beyond = [swap(part, "col", 2) for part in backs]

    even, *odd = gradient(1.0 / math.sqrt(nodes), [(0, 4, 2, 6), (1, 5), (3, 7)], aggregated, deltas)
    even, sent = fuse("gradient_sum", halves_sum, even, *[swap(part, "row", 1) for part in odd])
    even, sent = fuse("gradient_sum", halves_sum, even, swap(sent, "row", 2))
    beyond[0] = after(beyond[0], sent)
    even = after(even, beside)
    (chunk,) = fuse("gradient_sum", lambda a, b: ((a + b)[0],), even, swap(sent, "row", 4))
    (second,) = fuse("with_chunk", with_chunk, beyond[1], chunk, swap(chunk, "row", 1))
    received = [swap(beyond[0], "col", 1), swap(second, "col", 1)]

    def columns(n, *earlier):
        parts = [back, beside, after(beyond[0], *earlier), received[0], beyond[1], received[1]]
        if n == 0:
            depths = cuts[:1]
            parts = parts[:4]
            spots = [[(part, 0)] for part in range(4)]
        else:
            depths = [ahead, cuts[1] - ahead]
            spots = [[(part, cuts[0]), (part, cuts[0] + ahead)] for part in range(2)]
            spots += [[(part, cuts[0]), (part + 2, 0)] for part in (2, 3)]
        out_depths = [cuts[n] // 2] + [cuts[n] // (8 - 4 * n)] * (4 - 2 * n)
        mine, *sent = backward(
            col, count, rows, cols, tile, parts, spots, depths, out_depths, col_blocks
        )
        return [mine] + [swap(part, "row", 1) for part in sent]

    own_sum, far_sum = fuse("far_sums", functools.partial(far_sums, depth), *columns(0, second))
    half_way = lax.ppermute(far_sum, "row", [(i, i ^ (4 if i % 2 else 2)) for i in range(n_row)])
    (chunk,) = fuse("chunk_sum", functools.partial(chunk_sum, 2 * depth), second, received[1])
    (chunk,) = fuse("chunk_sum", wide_sum, chunk, swap(chunk, "col", 2))
    mine, *from_sibling = columns(1, far_sum)
    chunks, *near_sums = near_payloads(row, chunk, half_way, mine, from_sibling)
    near_sums = [swap(part, "row", k) for part, k in zip(near_sums, near)]
    far_chunks = [swap(chunks, "row", k) for k in far]
    grad_features, grad_weight = finish(row, [0] + far + near, [own_sum] + near_sums, [chunks] + far_chunks)
    return output, grad_weight, grad_features.T


def shards_gathered(features, weight, adj_values, block_rows, block_cols, block_counts, cotangent):
    n_row = lax.axis_size("row")
    n_col = lax.axis_size("col")
    adj = adj_values[0, 0]
    rows = block_rows[0, 0]
    cols = block_cols[0, 0]
    count = block_counts
    size = adj.shape[1]
    nodes = cotangent.shape[0] * n_row * n_col
    row_blocks = cotangent.shape[0] * n_col // size
    col_blocks = features.shape[0] // size
    zero = jnp.zeros((1,), jnp.int32)
    panels = lax.all_gather(features.T, "row", axis=0, tiled=True)
    (terms,) = forward(zero, count, rows, cols, adj, [panels], row_blocks, [panels.shape[0]], [(0,)])
    part = lax.psum_scatter(terms, "col", scatter_dimension=1, tiled=True)
    output, deltas, aggregated, back = middle(1, zero, weight, cotangent, [[part]], (0,), [weight.shape[0]])
    slab = lax.all_gather(back, "col", axis=1, tiled=True)
    (column_terms,) = backward(zero, count, rows, cols, adj, [slab], [[(0, 0)]], [slab.shape[0]], [slab.shape[0]], col_blocks)
    grad_features = lax.psum_scatter(column_terms, "row", scatter_dimension=0, tiled=True).T
    (part,) = gradient(1.0 / math.sqrt(nodes), [(0,)], aggregated, deltas)
    grad_weight = lax.psum(part[0], ("row", "col"))
    return output, grad_weight, grad_features


def solution(mesh):
    n_row = mesh.shape["row"]
    n_col = mesh.shape["col"]
    exchanged = n_row == 8 and n_col == 4
    return jax.shard_map(
        shards_exchanged if exchanged else shards_gathered,
        mesh=mesh,
        in_specs=(
            P("col", "row"),
            P(),
            P("row", "col", None, None, None),
            P("row", "col", None),
            P("row", "col", None),
            P("row", "col"),
            P(("row", "col"), None),
        ),
        out_specs=(P(("row", "col"), None), P(), P("col", "row")),
        check_vma=False,
    )
```

```python
import functools
import math

import jax
import jax.numpy as jnp
from jax import lax
from jax.experimental import pallas as pl
from jax.experimental.pallas import tpu as pltpu
from jax.sharding import PartitionSpec as P

VMEM = pl.BlockSpec(memory_space=pltpu.VMEM)
SMEM = pl.BlockSpec(memory_space=pltpu.SMEM)
HBM = pl.BlockSpec(memory_space=pltpu.HBM)
MIB = 1024 * 1024
NT = (((1,), (1,)), ((), ()))
NN = (((1,), (0,)), ((), ()))


COST = pl.CostEstimate(flops=1, bytes_accessed=1, transcendentals=0)


def params(mib):
    return pltpu.CompilerParams(vmem_limit_bytes=mib * MIB)


def fuse(name, function, *values):
    shapes = jax.eval_shape(function, *values)

    def kernel(*refs):
        results = function(*[ref[...] for ref in refs[: len(values)]])
        for ref, result in zip(refs[len(values) :], results):
            ref[...] = result

    return pl.pallas_call(
        kernel,
        out_shape=shapes,
        in_specs=[VMEM] * len(values),
        out_specs=[VMEM] * len(shapes),
        compiler_params=params(4),
        cost_estimate=COST,
        name=name,
    )(*values)


def turn_of(slots):
    return math.gcd(slots, 8)


def product_loop(count, source_ids, target_ids, adj, source, total, dims):
    turn = math.gcd(adj.shape[0], 24)
    spare = total.shape[0] - 1
    total[...] = jnp.zeros_like(total)

    def step(index, carry):
        first = index * turn
        for k in range(turn):
            slot = first + k
            product = lax.dot_general(
                source[source_ids[slot]], adj[slot], dims, preferred_element_type=jnp.float32
            )
            target = jnp.where(slot < count, target_ids[slot], spare)
            total[target] += product
        return carry

    lax.fori_loop(0, (count + turn - 1) // turn, step, 0)


def fetch_kernel(count, rows, cols, features, tile, *refs):
    outs, (sem, small_sem) = refs[:5], refs[5:]
    half = features.shape[0] // 2
    sources = (rows, cols, features.at[pl.ds(0, half)], features.at[pl.ds(half, half)])
    small = [
        pltpu.make_async_copy(source, target, small_sem.at[n])
        for n, (source, target) in enumerate(zip(sources, outs))
    ]
    for copy in small:
        copy.start()
    turn = turn_of(tile.shape[0])

    def copy_turn(index):
        blocks = pl.ds(index * turn, turn)
        return pltpu.make_async_copy(tile.at[blocks], outs[4].at[blocks], sem.at[index])

    def begin(index, carry):
        copy_turn(index).start()
        return carry

    def wait(index, carry):
        copy_turn(index).wait()
        return carry

    turns = (count[0, 0] + turn - 1) // turn
    lax.fori_loop(0, turns, begin, 0)
    lax.fori_loop(0, turns, wait, 0)
    for copy in small:
        copy.wait()


def fetch(count, rows, cols, features, tile):
    arrays = (rows, cols, features, tile)
    half = jax.ShapeDtypeStruct((features.shape[0] // 2, features.shape[1]), features.dtype)
    outs = [jax.ShapeDtypeStruct(array.shape, array.dtype) for array in (rows, cols)] + [half] * 2
    return pl.pallas_call(
        fetch_kernel,
        out_shape=outs + [jax.ShapeDtypeStruct(tile.shape, tile.dtype)],
        in_specs=[SMEM] + [HBM] * 4,
        out_specs=[VMEM] * 5,
        scratch_shapes=[
            pltpu.SemaphoreType.DMA((tile.shape[0] // turn_of(tile.shape[0]),)),
            pltpu.SemaphoreType.DMA((4,)),
        ],
        compiler_params=params(4),
        cost_estimate=COST,
        name="fetch",
    )(count, *[pltpu.with_memory_space_constraint(array, pltpu.HBM) for array in arrays])


def forward_kernel(n_parts, depths, layout, place, count, rows, cols, adj, *refs):
    parts, refs = refs[:n_parts], refs[n_parts:]
    source, total = refs[-2:]
    outs = refs[-2 - len(depths) * len(layout) : -2]
    carried = refs[: len(refs) - 2 - len(outs)]
    size = adj.shape[1]
    row = 0
    for part in parts:
        depth = part.shape[0]
        for c in range(source.shape[0]):
            source[c, row : row + depth, :] = part[:, c * size : (c + 1) * size]
        row += depth
    product_loop(count[0, 0], cols, rows, adj, source, total, NT)
    blocks = outs[0].shape[1] // size
    ahead = carried[0].shape[0] // len(layout[0]) if carried else 0
    outs = iter(outs)
    row = 0
    for depth in depths:
        for m, chunks in enumerate(layout):
            out = next(outs)
            for n, k in enumerate(chunks):
                begin = n * (ahead + depth)
                if ahead:
                    out[begin : begin + ahead, :] = carried[m][n * ahead : (n + 1) * ahead, :]
                first = (place[0] ^ k) * blocks
                for i in range(blocks):
                    out[begin + ahead : begin + ahead + depth, i * size : (i + 1) * size] = total[
                        first + i, row : row + depth, :
                    ].astype(out.dtype)
        row += depth


def forward(place, count, rows, cols, adj, parts, row_blocks, depths, layout, carried=()):
    size = adj.shape[1]
    col_blocks = parts[0].shape[1] // size
    wide = row_blocks * size // sum(len(chunks) for chunks in layout)
    ahead = carried[0].shape[0] // len(layout[0]) if carried else 0
    outs = [
        jax.ShapeDtypeStruct((len(chunks) * (ahead + depth), wide), jnp.bfloat16)
        for depth in depths
        for chunks in layout
    ]
    return pl.pallas_call(
        functools.partial(forward_kernel, len(parts), depths, layout),
        out_shape=outs,
        in_specs=[SMEM] * 4 + [VMEM] * (1 + len(parts) + len(carried)),
        out_specs=[VMEM] * len(outs),
        scratch_shapes=[
            pltpu.VMEM((col_blocks, sum(depths), size), jnp.bfloat16),
            pltpu.VMEM((row_blocks + 1, sum(depths), size), jnp.float32),
        ],
        compiler_params=params(14),
        cost_estimate=COST,
        name="forward_products",
    )(place, count, rows, cols, adj, *parts, *carried)


def backward_kernel(spots, depths, place, count, rows, cols, adj, *refs):
    n_parts = 1 + max(part for places in spots for part, _ in places)
    parts = refs[:n_parts]
    outs = refs[n_parts:-2]
    source, total = refs[-2:]
    size = adj.shape[1]
    blocks = parts[0].shape[1] // size
    for k, places in enumerate(spots):
        first = (place[0] ^ k) * blocks
        row = 0
        for (part, offset), depth in zip(places, depths):
            for i in range(blocks):
                source[first + i, row : row + depth, :] = parts[part][
                    offset : offset + depth, i * size : (i + 1) * size
                ]
            row += depth
    product_loop(count[0, 0], rows, cols, adj, source, total, NN)
    row = 0
    for out in outs:
        depth = out.shape[0]
        for c in range(total.shape[0] - 1):
            out[:, c * size : (c + 1) * size] = total[c, row : row + depth, :].astype(out.dtype)
        row += depth


def backward(place, count, rows, cols, adj, parts, spots, depths, out_depths, col_blocks):
    size = adj.shape[1]
    row_blocks = len(spots) * parts[0].shape[1] // size
    return pl.pallas_call(
        functools.partial(backward_kernel, spots, depths),
        out_shape=[jax.ShapeDtypeStruct((depth, col_blocks * size), jnp.bfloat16) for depth in out_depths],
        in_specs=[SMEM] * 4 + [VMEM] * (1 + len(parts)),
        out_specs=[VMEM] * len(out_depths),
        scratch_shapes=[
            pltpu.VMEM((row_blocks, sum(out_depths), size), jnp.bfloat16),
            pltpu.VMEM((col_blocks + 1, sum(out_depths), size), jnp.float32),
        ],
        compiler_params=params(14),
        cost_estimate=COST,
        name="backward_products",
    )(place, count, rows, cols, adj, *parts)


def middle_kernel(sizes, order, n_sum, n_row, row, weight, cotangent, *refs):
    terms = refs[: n_sum * len(sizes)]
    outs = refs[n_sum * len(sizes) : -1]
    output, deltas, aggregated, *backs = outs
    ordered = refs[-1]
    depth = weight.shape[0] // n_row
    for j in range(n_row):
        first = pl.multiple_of((row[0] ^ j) * depth, depth)
        ordered[j * depth : (j + 1) * depth, :] = weight[pl.ds(first, depth), :]
    first = 0
    for p, size in enumerate(sizes):
        summed = terms[p * n_sum][:size, :].astype(jnp.float32)
        for k in range(1, n_sum):
            summed += terms[p * n_sum + k][:size, :].astype(jnp.float32)
        aggregated[first : first + size, :] = summed.astype(jnp.bfloat16)
        first += size
    nodes_first = aggregated[...].T
    preact = jnp.dot(nodes_first, ordered[...], preferred_element_type=jnp.float32)
    gate = jax.nn.sigmoid(preact)
    output[...] = (preact * gate).astype(jnp.bfloat16)
    slopes = gate * (1.0 + preact * (1.0 - gate))
    delta = (cotangent[...].astype(jnp.float32) * slopes).astype(jnp.bfloat16)
    deltas[...] = delta
    product = lax.dot_general(ordered[...], delta, NT, preferred_element_type=jnp.float32)
    product = jnp.concatenate([product[k * depth : (k + 1) * depth, :] for k in order]).astype(jnp.bfloat16)
    first = 0
    for back in backs:
        first %= product.shape[0]
        back[...] = product[first : first + back.shape[0], :]
        first += back.shape[0]


def middle(n_row, row, weight, cotangent, pieces, order, depths):
    sizes = [piece[0].shape[0] for piece in pieces]
    nodes = cotangent.shape[0]
    features = weight.shape[0]
    shape = jax.ShapeDtypeStruct
    outs = [
        shape((nodes, features), jnp.bfloat16),
        shape((nodes, features), jnp.bfloat16),
        shape((features, nodes), jnp.bfloat16),
    ] + [shape((depth, nodes), jnp.bfloat16) for depth in depths]
    flat = [term for piece in pieces for term in piece]
    return pl.pallas_call(
        functools.partial(middle_kernel, sizes, order, len(pieces[0]), n_row),
        out_shape=outs,
        in_specs=[SMEM] + [VMEM] * (2 + len(flat)),
        out_specs=[VMEM] * len(outs),
        scratch_shapes=[pltpu.VMEM(weight.shape, jnp.bfloat16)],
        compiler_params=params(10),
        cost_estimate=COST,
        name="layer",
    )(row, weight, cotangent, *flat)


def gradient_kernel(scale, order, aggregated, deltas, *outs):
    product = jnp.dot(aggregated[...], deltas[...], preferred_element_type=jnp.float32) * scale
    for out, chunks in zip(outs, order):
        depth = out.shape[1]
        for n, k in enumerate(chunks):
            out[n] = product[k * depth : (k + 1) * depth, :]


def gradient(scale, order, aggregated, deltas):
    depth = aggregated.shape[0] // sum(len(chunks) for chunks in order)
    outs = [jax.ShapeDtypeStruct((len(chunks), depth, deltas.shape[1]), jnp.float32) for chunks in order]
    return pl.pallas_call(
        functools.partial(gradient_kernel, scale, order),
        out_shape=outs,
        in_specs=[VMEM] * 2,
        out_specs=[VMEM] * len(outs),
        compiler_params=params(6),
        cost_estimate=COST,
        name="weight_gradient",
    )(aggregated, deltas)


def swap(value, axis, k):
    size = lax.axis_size(axis)
    return lax.ppermute(value, axis, [(i, i ^ k) for i in range(size)])


def wide_sum(*values):
    total = values[0].astype(jnp.float32)
    for value in values[1:]:
        total = total + value.astype(jnp.float32)
    return (total.astype(values[0].dtype),)


def after(value, *earlier):
    return lax.optimization_barrier((value, *earlier))[0]


def with_chunk(rows, *parts):
    total = functools.reduce(jnp.add, parts)
    high = total.astype(jnp.bfloat16)
    low = (total - high.astype(jnp.float32)).astype(jnp.bfloat16)
    return (jnp.concatenate([rows, jnp.concatenate([high, low], axis=1)]),)


def chunk_sum(depth, *values):
    total = None
    for value in values:
        halves = value[-depth:].astype(jnp.float32)
        wide = halves.shape[1] // 2
        chunk = halves[:, :wide] + halves[:, wide:]
        total = chunk if total is None else total + chunk
    return (total,)


def halves_sum(mine, *received):
    total = mine + jnp.concatenate(received)
    half = total.shape[0] // 2
    return total[:half], total[half:]


def far_sums(depth, mine, *received):
    total = mine.astype(jnp.float32) + jnp.concatenate(received).astype(jnp.float32)
    total = total.astype(mine.dtype)
    own, far = total[:depth], total[depth:]
    return own, jnp.concatenate([far, far[:, :128]], axis=1)


def near_kernel(row, chunk, sibling, half_way, mine, *refs):
    received, (chunks, *sums) = refs[: -1 - 2], refs[-1 - 2 :]
    depth = half_way.shape[0]
    nodes = mine.shape[1]
    for k, ref in enumerate((chunk, sibling)):
        wide = ref.shape[1]
        chunks[:, k * wide : (k + 1) * wide] = ref[...].astype(chunks.dtype)
    passed = half_way[:, :nodes].astype(jnp.float32)
    odd = row[0] % 2
    for n, out in enumerate(sums):
        total = mine[n * depth : (n + 1) * depth, :].astype(jnp.float32) + received[n][...].astype(jnp.float32)
        total += jnp.where(odd == 1 - n, passed, 0.0)
        out[:, :nodes] = total.astype(out.dtype)
        out[:, nodes:] = chunks[...]


def near_payloads(row, chunk, sibling, half_way, mine, received):
    depth, nodes = received[0].shape
    wide = 2 * chunk.shape[1]
    shape = jax.ShapeDtypeStruct
    return pl.pallas_call(
        near_kernel,
        out_shape=[shape((depth, wide), mine.dtype)]
        + [shape((depth, nodes + wide), mine.dtype)] * len(received),
        in_specs=[SMEM] + [VMEM] * (4 + len(received)),
        out_specs=[VMEM] * (1 + len(received)),
        compiler_params=params(8),
        cost_estimate=COST,
        name="near_payloads",
    )(row, chunk, sibling, half_way, mine, *received)


def finish_kernel(keys, row, *refs):
    grad_features, grad_weight = refs[-2:]
    depth, nodes = grad_features.shape
    wide = grad_weight.shape[1]
    parts = [ref for ref in refs[:-2] if ref.shape[1] >= nodes]
    values = [ref[...] for ref in refs[:-2] if ref.shape[1] < nodes] + [part[:, nodes:] for part in parts[1:]]
    total = parts[0][...].astype(jnp.float32)
    for part in parts[1:]:
        total += part[:, :nodes].astype(jnp.float32)
    grad_features[...] = total.astype(grad_features.dtype)
    for key, value in zip(keys, values):
        for k in range(2):
            first = pl.multiple_of((row[0] ^ (key + k)) * depth, depth)
            grad_weight[pl.ds(first, depth), :] = value[:, k * wide : (k + 1) * wide].astype(jnp.float32)


def finish(row, keys, parts, chunks):
    depth, nodes = parts[0].shape
    return pl.pallas_call(
        functools.partial(finish_kernel, keys),
        out_shape=[
            jax.ShapeDtypeStruct((depth, nodes), jnp.bfloat16),
            jax.ShapeDtypeStruct((2 * len(keys) * depth, chunks[0].shape[1] // 2), jnp.float32),
        ],
        in_specs=[SMEM] + [VMEM] * (len(parts) + len(chunks)),
        out_specs=[VMEM] * 2,
        compiler_params=params(8),
        cost_estimate=COST,
        name="finish",
    )(row, *parts, *chunks)


def shards_exchanged(features, weight, adj_values, block_rows, block_cols, block_counts, cotangent):
    n_row = lax.axis_size("row")
    n_col = lax.axis_size("col")
    adj = adj_values[0, 0]
    rows = block_rows[0, 0]
    cols = block_cols[0, 0]
    count = block_counts
    size = adj.shape[1]
    nodes = cotangent.shape[0] * n_row * n_col
    row_blocks = cotangent.shape[0] * n_col // size
    col_blocks = features.shape[0] // size
    row = lax.axis_index("row").reshape(1)
    col = lax.axis_index("col").reshape(1)
    own = after(features.T, row, col)

    depth = features.shape[1]
    near = [k for k in range(2, n_row, 2) if k & (k - 1) == 0]
    far = [k for k in range(2, n_row, 2) if k & (k - 1) != 0]
    sibling = swap(own, "row", 1)
    from_near = [swap(own, "row", k) for k in near]
    rows, cols, *halves, tile = fetch(count, rows, cols, own, adj)
    from_near = [after(part, tile) for part in from_near]
    from_far = [swap(half, "row", k) for k in far for half in halves]

    def pass_on(beyond, received):
        return wide_sum(beyond, received[beyond.shape[0] :])

    layout = [(0,), (2,), (1, 3)]

    def fold(kept, beyond, received):
        (passed,) = fuse("pass_on", pass_on, beyond, received)
        return [kept, received, swap(passed, "col", 2)]

    n_near = 2 * depth * (1 + len(near))
    cut = n_near * 5 // 6
    parts = [own, sibling] + [piece for part in from_near for piece in (part, swap(part, "row", 1))]
    kept, beyond, sent, *carried = forward(
        col, count, rows, cols, tile, parts, row_blocks, [cut, n_near - cut], layout
    )
    received = swap(sent, "col", 1)
    from_far = [after(part, kept) for part in from_far]
    parts = []
    for n in range(0, len(from_far), 2):
        halves = from_far[n : n + 2]
        parts += halves + [swap(half, "row", 1) for half in halves]
    far_piece = forward(
        col, count, rows, cols, tile, parts, row_blocks, [2 * depth * len(far)], layout, carried
    )
    far_received = swap(far_piece[2], "col", 1)
    first = fold(kept, beyond, after(received, far_piece[0]))
    second = fold(*far_piece[:2], after(far_received, first[1]))
    sums = [first, second]

    groups = [[0] + far, near]
    order = [k + side for group in groups for side in range(2) for k in group]
    cuts = [2 * depth * len(group) for group in groups]
    ahead = depth // 2
    output, deltas, aggregated, back, *backs = middle(
        n_row, row, weight, cotangent, sums, order, [sum(cuts), cuts[0] + ahead, cuts[1] - ahead]
    )
    beside = swap(back, "col", 1)
    beyond = [swap(part, "col", 2) for part in backs]

    even, *odd = gradient(1.0 / math.sqrt(nodes), [(0, 4, 2, 6), (1, 5), (3, 7)], aggregated, deltas)
    even, sent = fuse("gradient_sum", halves_sum, even, *[swap(part, "row", 1) for part in odd])
    even, sent = fuse("gradient_sum", halves_sum, even, swap(sent, "row", 2))
    beyond[0] = after(beyond[0], sent)
    even = after(even, beyond[1])
    (chunk,) = fuse("gradient_sum", lambda a, b: ((a + b)[0],), even, swap(sent, "row", 4))
    chunks = [chunk, swap(chunk, "col", 2)]

    (second,) = fuse("with_chunk", with_chunk, beyond[1], *chunks)
    received = [swap(beyond[0], "col", 1), swap(second, "col", 1)]

    def columns(n, *earlier):
        parts = [back, beside, after(beyond[0], *earlier), received[0], beyond[1], received[1]]
        if n == 0:
            depths = cuts[:1]
            parts = parts[:4]
            spots = [[(part, 0)] for part in range(4)]
        else:
            depths = [ahead, cuts[1] - ahead]
            spots = [[(part, cuts[0]), (part, cuts[0] + ahead)] for part in range(2)]
            spots += [[(part, cuts[0]), (part + 2, 0)] for part in (2, 3)]
        out_depths = [cuts[n] // 2] + [cuts[n] // (8 - 4 * n)] * (4 - 2 * n)
        mine, *sent = backward(
            col, count, rows, cols, tile, parts, spots, depths, out_depths, col_blocks
        )
        return [mine] + [swap(part, "row", 1) for part in sent]

    own_sum, far_sum = fuse("far_sums", functools.partial(far_sums, depth), *columns(0, second))
    half_way = lax.ppermute(far_sum, "row", [(i, i ^ (4 if i % 2 else 2)) for i in range(n_row)])
    received[1] = after(received[1], far_sum)
    (chunk,) = fuse("chunk_sum", functools.partial(chunk_sum, depth), second, received[1])
    mine, *from_sibling = columns(1, chunk)
    chunks, *near_sums = near_payloads(row, chunk, swap(chunk, "row", 1), half_way, mine, from_sibling)
    near_sums = [swap(part, "row", k) for part, k in zip(near_sums, near)]
    far_chunks = [swap(chunks, "row", k) for k in far]
    grad_features, grad_weight = finish(row, [0] + far + near, [own_sum] + near_sums, [chunks] + far_chunks)
    return output, grad_weight, grad_features.T


def shards_gathered(features, weight, adj_values, block_rows, block_cols, block_counts, cotangent):
    n_row = lax.axis_size("row")
    n_col = lax.axis_size("col")
    adj = adj_values[0, 0]
    rows = block_rows[0, 0]
    cols = block_cols[0, 0]
    count = block_counts
    size = adj.shape[1]
    nodes = cotangent.shape[0] * n_row * n_col
    row_blocks = cotangent.shape[0] * n_col // size
    col_blocks = features.shape[0] // size
    zero = jnp.zeros((1,), jnp.int32)
    panels = lax.all_gather(features.T, "row", axis=0, tiled=True)
    (terms,) = forward(zero, count, rows, cols, adj, [panels], row_blocks, [panels.shape[0]], [(0,)])
    part = lax.psum_scatter(terms, "col", scatter_dimension=1, tiled=True)
    output, deltas, aggregated, back = middle(1, zero, weight, cotangent, [[part]], (0,), [weight.shape[0]])
    slab = lax.all_gather(back, "col", axis=1, tiled=True)
    (column_terms,) = backward(zero, count, rows, cols, adj, [slab], [[(0, 0)]], [slab.shape[0]], [slab.shape[0]], col_blocks)
    grad_features = lax.psum_scatter(column_terms, "row", scatter_dimension=0, tiled=True).T
    (part,) = gradient(1.0 / math.sqrt(nodes), [(0,)], aggregated, deltas)
    grad_weight = lax.psum(part[0], ("row", "col"))
    return output, grad_weight, grad_features


def solution(mesh):
    n_row = mesh.shape["row"]
    n_col = mesh.shape["col"]
    exchanged = n_row == 8 and n_col == 4
    return jax.shard_map(
        shards_exchanged if exchanged else shards_gathered,
        mesh=mesh,
        in_specs=(
            P("col", "row"),
            P(),
            P("row", "col", None, None, None),
            P("row", "col", None),
            P("row", "col", None),
            P("row", "col"),
            P(("row", "col"), None),
        ),
        out_specs=(P(("row", "col"), None), P(), P("col", "row")),
        check_vma=False,
    )
```

```python
import functools
import math

import jax
import jax.numpy as jnp
from jax import lax
from jax.experimental import pallas as pl
from jax.experimental.pallas import tpu as pltpu
from jax.sharding import PartitionSpec as P

VMEM = pl.BlockSpec(memory_space=pltpu.VMEM)
SMEM = pl.BlockSpec(memory_space=pltpu.SMEM)
HBM = pl.BlockSpec(memory_space=pltpu.HBM)
MIB = 1024 * 1024
NT = (((1,), (1,)), ((), ()))
NN = (((1,), (0,)), ((), ()))


COST = pl.CostEstimate(flops=1, bytes_accessed=1, transcendentals=0)


def params(mib):
    return pltpu.CompilerParams(vmem_limit_bytes=mib * MIB)


def fuse(name, function, *values):
    shapes = jax.eval_shape(function, *values)

    def kernel(*refs):
        results = function(*[ref[...] for ref in refs[: len(values)]])
        for ref, result in zip(refs[len(values) :], results):
            ref[...] = result

    return pl.pallas_call(
        kernel,
        out_shape=shapes,
        in_specs=[VMEM] * len(values),
        out_specs=[VMEM] * len(shapes),
        compiler_params=params(4),
        cost_estimate=COST,
        name=name,
    )(*values)


def turn_of(slots):
    return math.gcd(slots, 8)


def product_loop(count, source_ids, target_ids, adj, source, total, dims):
    turn = math.gcd(adj.shape[0], 48)
    spare = total.shape[0] - 1
    total[...] = jnp.zeros_like(total)

    def step(index, carry):
        first = index * turn
        for k in range(turn):
            slot = first + k
            product = lax.dot_general(
                source[source_ids[slot]], adj[slot], dims, preferred_element_type=jnp.float32
            )
            target = jnp.where(slot < count, target_ids[slot], spare)
            total[target] += product
        return carry

    lax.fori_loop(0, (count + turn - 1) // turn, step, 0)


def fetch_kernel(count, rows, cols, features, tile, *refs):
    outs, (sem, small_sem) = refs[:5], refs[5:]
    half = features.shape[0] // 2
    sources = (rows, cols, features.at[pl.ds(0, half)], features.at[pl.ds(half, half)])
    small = [
        pltpu.make_async_copy(source, target, small_sem.at[n])
        for n, (source, target) in enumerate(zip(sources, outs))
    ]
    for copy in small:
        copy.start()
    turn = turn_of(tile.shape[0])

    def copy_turn(index):
        blocks = pl.ds(index * turn, turn)
        return pltpu.make_async_copy(tile.at[blocks], outs[4].at[blocks], sem.at[index])

    def begin(index, carry):
        copy_turn(index).start()
        return carry

    def wait(index, carry):
        copy_turn(index).wait()
        return carry

    turns = (count[0, 0] + turn - 1) // turn
    lax.fori_loop(0, turns, begin, 0)
    lax.fori_loop(0, turns, wait, 0)
    for copy in small:
        copy.wait()


def fetch(count, rows, cols, features, tile):
    arrays = (rows, cols, features, tile)
    half = jax.ShapeDtypeStruct((features.shape[0] // 2, features.shape[1]), features.dtype)
    outs = [jax.ShapeDtypeStruct(array.shape, array.dtype) for array in (rows, cols)] + [half] * 2
    return pl.pallas_call(
        fetch_kernel,
        out_shape=outs + [jax.ShapeDtypeStruct(tile.shape, tile.dtype)],
        in_specs=[SMEM] + [HBM] * 4,
        out_specs=[VMEM] * 5,
        scratch_shapes=[
            pltpu.SemaphoreType.DMA((tile.shape[0] // turn_of(tile.shape[0]),)),
            pltpu.SemaphoreType.DMA((4,)),
        ],
        compiler_params=params(4),
        cost_estimate=COST,
        name="fetch",
    )(count, *[pltpu.with_memory_space_constraint(array, pltpu.HBM) for array in arrays])


def forward_kernel(n_parts, depths, layout, place, count, rows, cols, adj, *refs):
    parts, refs = refs[:n_parts], refs[n_parts:]
    source, total = refs[-2:]
    outs = refs[-2 - len(depths) * len(layout) : -2]
    carried = refs[: len(refs) - 2 - len(outs)]
    size = adj.shape[1]
    row = 0
    for part in parts:
        depth = part.shape[0]
        for c in range(source.shape[0]):
            source[c, row : row + depth, :] = part[:, c * size : (c + 1) * size]
        row += depth
    product_loop(count[0, 0], cols, rows, adj, source, total, NT)
    blocks = outs[0].shape[1] // size
    ahead = carried[0].shape[0] // len(layout[0]) if carried else 0
    outs = iter(outs)
    row = 0
    for depth in depths:
        for m, chunks in enumerate(layout):
            out = next(outs)
            for n, k in enumerate(chunks):
                begin = n * (ahead + depth)
                if ahead:
                    out[begin : begin + ahead, :] = carried[m][n * ahead : (n + 1) * ahead, :]
                first = (place[0] ^ k) * blocks
                for i in range(blocks):
                    out[begin + ahead : begin + ahead + depth, i * size : (i + 1) * size] = total[
                        first + i, row : row + depth, :
                    ].astype(out.dtype)
        row += depth


def forward(place, count, rows, cols, adj, parts, row_blocks, depths, layout, carried=()):
    size = adj.shape[1]
    col_blocks = parts[0].shape[1] // size
    wide = row_blocks * size // sum(len(chunks) for chunks in layout)
    ahead = carried[0].shape[0] // len(layout[0]) if carried else 0
    outs = [
        jax.ShapeDtypeStruct((len(chunks) * (ahead + depth), wide), jnp.bfloat16)
        for depth in depths
        for chunks in layout
    ]
    return pl.pallas_call(
        functools.partial(forward_kernel, len(parts), depths, layout),
        out_shape=outs,
        in_specs=[SMEM] * 4 + [VMEM] * (1 + len(parts) + len(carried)),
        out_specs=[VMEM] * len(outs),
        scratch_shapes=[
            pltpu.VMEM((col_blocks, sum(depths), size), jnp.bfloat16),
            pltpu.VMEM((row_blocks + 1, sum(depths), size), jnp.float32),
        ],
        compiler_params=params(14),
        cost_estimate=COST,
        name="forward_products",
    )(place, count, rows, cols, adj, *parts, *carried)


def backward_kernel(spots, depths, place, count, rows, cols, adj, *refs):
    n_parts = 1 + max(part for places in spots for part, _ in places)
    parts = refs[:n_parts]
    outs = refs[n_parts:-2]
    source, total = refs[-2:]
    size = adj.shape[1]
    blocks = parts[0].shape[1] // size
    for k, places in enumerate(spots):
        first = (place[0] ^ k) * blocks
        row = 0
        for (part, offset), depth in zip(places, depths):
            for i in range(blocks):
                source[first + i, row : row + depth, :] = parts[part][
                    offset : offset + depth, i * size : (i + 1) * size
                ]
            row += depth
    product_loop(count[0, 0], rows, cols, adj, source, total, NN)
    row = 0
    for out in outs:
        depth = out.shape[0]
        for c in range(total.shape[0] - 1):
            out[:, c * size : (c + 1) * size] = total[c, row : row + depth, :].astype(out.dtype)
        row += depth


def backward(place, count, rows, cols, adj, parts, spots, depths, out_depths, col_blocks):
    size = adj.shape[1]
    row_blocks = len(spots) * parts[0].shape[1] // size
    return pl.pallas_call(
        functools.partial(backward_kernel, spots, depths),
        out_shape=[jax.ShapeDtypeStruct((depth, col_blocks * size), jnp.bfloat16) for depth in out_depths],
        in_specs=[SMEM] * 4 + [VMEM] * (1 + len(parts)),
        out_specs=[VMEM] * len(out_depths),
        scratch_shapes=[
            pltpu.VMEM((row_blocks, sum(out_depths), size), jnp.bfloat16),
            pltpu.VMEM((col_blocks + 1, sum(out_depths), size), jnp.float32),
        ],
        compiler_params=params(14),
        cost_estimate=COST,
        name="backward_products",
    )(place, count, rows, cols, adj, *parts)


def middle_kernel(sizes, order, n_sum, n_row, row, weight, cotangent, *refs):
    terms = refs[: n_sum * len(sizes)]
    outs = refs[n_sum * len(sizes) : -1]
    output, deltas, aggregated, *backs = outs
    ordered = refs[-1]
    depth = weight.shape[0] // n_row
    for j in range(n_row):
        first = pl.multiple_of((row[0] ^ j) * depth, depth)
        ordered[j * depth : (j + 1) * depth, :] = weight[pl.ds(first, depth), :]
    first = 0
    for p, size in enumerate(sizes):
        summed = terms[p * n_sum][:size, :].astype(jnp.float32)
        for k in range(1, n_sum):
            summed += terms[p * n_sum + k][:size, :].astype(jnp.float32)
        aggregated[first : first + size, :] = summed.astype(jnp.bfloat16)
        first += size
    nodes_first = aggregated[...].T
    preact = jnp.dot(nodes_first, ordered[...], preferred_element_type=jnp.float32)
    gate = jax.nn.sigmoid(preact)
    output[...] = (preact * gate).astype(jnp.bfloat16)
    slopes = gate * (1.0 + preact * (1.0 - gate))
    delta = (cotangent[...].astype(jnp.float32) * slopes).astype(jnp.bfloat16)
    deltas[...] = delta
    product = lax.dot_general(ordered[...], delta, NT, preferred_element_type=jnp.float32)
    product = jnp.concatenate([product[k * depth : (k + 1) * depth, :] for k in order]).astype(jnp.bfloat16)
    first = 0
    for back in backs:
        first %= product.shape[0]
        back[...] = product[first : first + back.shape[0], :]
        first += back.shape[0]


def middle(n_row, row, weight, cotangent, pieces, order, depths):
    sizes = [piece[0].shape[0] for piece in pieces]
    nodes = cotangent.shape[0]
    features = weight.shape[0]
    shape = jax.ShapeDtypeStruct
    outs = [
        shape((nodes, features), jnp.bfloat16),
        shape((nodes, features), jnp.bfloat16),
        shape((features, nodes), jnp.bfloat16),
    ] + [shape((depth, nodes), jnp.bfloat16) for depth in depths]
    flat = [term for piece in pieces for term in piece]
    return pl.pallas_call(
        functools.partial(middle_kernel, sizes, order, len(pieces[0]), n_row),
        out_shape=outs,
        in_specs=[SMEM] + [VMEM] * (2 + len(flat)),
        out_specs=[VMEM] * len(outs),
        scratch_shapes=[pltpu.VMEM(weight.shape, jnp.bfloat16)],
        compiler_params=params(10),
        cost_estimate=COST,
        name="layer",
    )(row, weight, cotangent, *flat)


def gradient_kernel(scale, order, aggregated, deltas, *outs):
    product = jnp.dot(aggregated[...], deltas[...], preferred_element_type=jnp.float32) * scale
    for out, chunks in zip(outs, order):
        depth = out.shape[1]
        for n, k in enumerate(chunks):
            out[n] = product[k * depth : (k + 1) * depth, :]


def gradient(scale, order, aggregated, deltas):
    depth = aggregated.shape[0] // sum(len(chunks) for chunks in order)
    outs = [jax.ShapeDtypeStruct((len(chunks), depth, deltas.shape[1]), jnp.float32) for chunks in order]
    return pl.pallas_call(
        functools.partial(gradient_kernel, scale, order),
        out_shape=outs,
        in_specs=[VMEM] * 2,
        out_specs=[VMEM] * len(outs),
        compiler_params=params(6),
        cost_estimate=COST,
        name="weight_gradient",
    )(aggregated, deltas)


def swap(value, axis, k):
    size = lax.axis_size(axis)
    return lax.ppermute(value, axis, [(i, i ^ k) for i in range(size)])


def wide_sum(*values):
    total = values[0].astype(jnp.float32)
    for value in values[1:]:
        total = total + value.astype(jnp.float32)
    return (total.astype(values[0].dtype),)


def after(value, *earlier):
    return lax.optimization_barrier((value, *earlier))[0]


def with_chunk(rows, *parts):
    total = functools.reduce(jnp.add, parts)
    high = total.astype(jnp.bfloat16)
    low = (total - high.astype(jnp.float32)).astype(jnp.bfloat16)
    return (jnp.concatenate([rows, jnp.concatenate([high, low], axis=1)]),)


def chunk_sum(depth, *values):
    total = None
    for value in values:
        halves = value[-depth:].astype(jnp.float32)
        wide = halves.shape[1] // 2
        chunk = halves[:, :wide] + halves[:, wide:]
        total = chunk if total is None else total + chunk
    return (total,)


def halves_sum(mine, *received):
    total = mine + jnp.concatenate(received)
    half = total.shape[0] // 2
    return total[:half], total[half:]


def far_sums(depth, mine, *received):
    total = mine.astype(jnp.float32) + jnp.concatenate(received).astype(jnp.float32)
    total = total.astype(mine.dtype)
    own, far = total[:depth], total[depth:]
    return own, jnp.concatenate([far, far[:, :128]], axis=1)


def near_kernel(row, chunk, sibling, half_way, mine, *refs):
    received, (chunks, *sums) = refs[: -1 - 2], refs[-1 - 2 :]
    depth = half_way.shape[0]
    nodes = mine.shape[1]
    for k, ref in enumerate((chunk, sibling)):
        wide = ref.shape[1]
        chunks[:, k * wide : (k + 1) * wide] = ref[...].astype(chunks.dtype)
    passed = half_way[:, :nodes].astype(jnp.float32)
    odd = row[0] % 2
    for n, out in enumerate(sums):
        total = mine[n * depth : (n + 1) * depth, :].astype(jnp.float32) + received[n][...].astype(jnp.float32)
        total += jnp.where(odd == 1 - n, passed, 0.0)
        out[:, :nodes] = total.astype(out.dtype)
        out[:, nodes:] = chunks[...]


def near_payloads(row, chunk, sibling, half_way, mine, received):
    depth, nodes = received[0].shape
    wide = 2 * chunk.shape[1]
    shape = jax.ShapeDtypeStruct
    return pl.pallas_call(
        near_kernel,
        out_shape=[shape((depth, wide), mine.dtype)]
        + [shape((depth, nodes + wide), mine.dtype)] * len(received),
        in_specs=[SMEM] + [VMEM] * (4 + len(received)),
        out_specs=[VMEM] * (1 + len(received)),
        compiler_params=params(8),
        cost_estimate=COST,
        name="near_payloads",
    )(row, chunk, sibling, half_way, mine, *received)


def finish_kernel(keys, row, *refs):
    grad_features, grad_weight = refs[-2:]
    depth, nodes = grad_features.shape
    wide = grad_weight.shape[1]
    parts = [ref for ref in refs[:-2] if ref.shape[1] >= nodes]
    values = [ref[...] for ref in refs[:-2] if ref.shape[1] < nodes] + [part[:, nodes:] for part in parts[1:]]
    total = parts[0][...].astype(jnp.float32)
    for part in parts[1:]:
        total += part[:, :nodes].astype(jnp.float32)
    grad_features[...] = total.astype(grad_features.dtype)
    for key, value in zip(keys, values):
        for k in range(2):
            first = pl.multiple_of((row[0] ^ (key + k)) * depth, depth)
            grad_weight[pl.ds(first, depth), :] = value[:, k * wide : (k + 1) * wide].astype(jnp.float32)


def finish(row, keys, parts, chunks):
    depth, nodes = parts[0].shape
    return pl.pallas_call(
        functools.partial(finish_kernel, keys),
        out_shape=[
            jax.ShapeDtypeStruct((depth, nodes), jnp.bfloat16),
            jax.ShapeDtypeStruct((2 * len(keys) * depth, chunks[0].shape[1] // 2), jnp.float32),
        ],
        in_specs=[SMEM] + [VMEM] * (len(parts) + len(chunks)),
        out_specs=[VMEM] * 2,
        compiler_params=params(8),
        cost_estimate=COST,
        name="finish",
    )(row, *parts, *chunks)


def shards_exchanged(features, weight, adj_values, block_rows, block_cols, block_counts, cotangent):
    n_row = lax.axis_size("row")
    n_col = lax.axis_size("col")
    adj = adj_values[0, 0]
    rows = block_rows[0, 0]
    cols = block_cols[0, 0]
    count = block_counts
    size = adj.shape[1]
    nodes = cotangent.shape[0] * n_row * n_col
    row_blocks = cotangent.shape[0] * n_col // size
    col_blocks = features.shape[0] // size
    row = lax.axis_index("row").reshape(1)
    col = lax.axis_index("col").reshape(1)
    own = after(features.T, row, col)

    depth = features.shape[1]
    near = [k for k in range(2, n_row, 2) if k & (k - 1) == 0]
    far = [k for k in range(2, n_row, 2) if k & (k - 1) != 0]
    sibling = swap(own, "row", 1)
    from_near = [swap(own, "row", k) for k in near]
    rows, cols, *halves, tile = fetch(count, rows, cols, own, adj)
    from_near = [after(part, tile) for part in from_near]
    from_far = [swap(half, "row", k) for k in far for half in halves]

    def pass_on(beyond, received):
        return wide_sum(beyond, received[beyond.shape[0] :])

    layout = [(0,), (2,), (1, 3)]

    def fold(kept, beyond, received):
        (passed,) = fuse("pass_on", pass_on, beyond, received)
        return [kept, received, swap(passed, "col", 2)]

    n_near = 2 * depth * (1 + len(near))
    cut = n_near * 5 // 6
    parts = [own, sibling] + [piece for part in from_near for piece in (part, swap(part, "row", 1))]
    kept, beyond, sent, *carried = forward(
        col, count, rows, cols, tile, parts, row_blocks, [cut, n_near - cut], layout
    )
    received = swap(sent, "col", 1)
    from_far = [after(part, kept) for part in from_far]
    parts = []
    for n in range(0, len(from_far), 2):
        halves = from_far[n : n + 2]
        parts += halves + [swap(half, "row", 1) for half in halves]
    far_piece = forward(
        col, count, rows, cols, tile, parts, row_blocks, [2 * depth * len(far)], layout, carried
    )
    far_received = swap(far_piece[2], "col", 1)
    first = fold(kept, beyond, after(received, far_piece[0]))
    second = fold(*far_piece[:2], after(far_received, first[1]))
    sums = [first, second]

    groups = [[0] + far, near]
    order = [k + side for group in groups for side in range(2) for k in group]
    cuts = [2 * depth * len(group) for group in groups]
    ahead = depth // 2
    output, deltas, aggregated, back, *backs = middle(
        n_row, row, weight, cotangent, sums, order, [sum(cuts), cuts[0] + ahead, cuts[1] - ahead]
    )
    beside = swap(back, "col", 1)
    beyond = [swap(part, "col", 2) for part in backs]

    even, *odd = gradient(1.0 / math.sqrt(nodes), [(0, 4, 2, 6), (1, 5), (3, 7)], aggregated, deltas)
    even, sent = fuse("gradient_sum", halves_sum, even, *[swap(part, "row", 1) for part in odd])
    even, sent = fuse("gradient_sum", halves_sum, even, swap(sent, "row", 2))
    beyond[0] = after(beyond[0], sent)
    even = after(even, beyond[1])
    (chunk,) = fuse("gradient_sum", lambda a, b: ((a + b)[0],), even, swap(sent, "row", 4))
    chunks = [chunk, swap(chunk, "col", 2)]

    (second,) = fuse("with_chunk", with_chunk, beyond[1], *chunks)
    received = [swap(beyond[0], "col", 1), swap(second, "col", 1)]

    def columns(n, *earlier):
        parts = [back, beside, after(beyond[0], *earlier), received[0], beyond[1], received[1]]
        if n == 0:
            depths = cuts[:1]
            parts = parts[:4]
            spots = [[(part, 0)] for part in range(4)]
        else:
            depths = [ahead, cuts[1] - ahead]
            spots = [[(part, cuts[0]), (part, cuts[0] + ahead)] for part in range(2)]
            spots += [[(part, cuts[0]), (part + 2, 0)] for part in (2, 3)]
        out_depths = [cuts[n] // 2] + [cuts[n] // (8 - 4 * n)] * (4 - 2 * n)
        mine, *sent = backward(
            col, count, rows, cols, tile, parts, spots, depths, out_depths, col_blocks
        )
        return [mine] + [swap(part, "row", 1) for part in sent]

    own_sum, far_sum = fuse("far_sums", functools.partial(far_sums, depth), *columns(0, second))
    half_way = lax.ppermute(far_sum, "row", [(i, i ^ (4 if i % 2 else 2)) for i in range(n_row)])
    received[1] = after(received[1], far_sum)
    (chunk,) = fuse("chunk_sum", functools.partial(chunk_sum, depth), second, received[1])
    mine, *from_sibling = columns(1, chunk)
    chunks, *near_sums = near_payloads(row, chunk, swap(chunk, "row", 1), half_way, mine, from_sibling)
    near_sums = [swap(part, "row", k) for part, k in zip(near_sums, near)]
    far_chunks = [swap(chunks, "row", k) for k in far]
    grad_features, grad_weight = finish(row, [0] + far + near, [own_sum] + near_sums, [chunks] + far_chunks)
    return output, grad_weight, grad_features.T


def shards_gathered(features, weight, adj_values, block_rows, block_cols, block_counts, cotangent):
    n_row = lax.axis_size("row")
    n_col = lax.axis_size("col")
    adj = adj_values[0, 0]
    rows = block_rows[0, 0]
    cols = block_cols[0, 0]
    count = block_counts
    size = adj.shape[1]
    nodes = cotangent.shape[0] * n_row * n_col
    row_blocks = cotangent.shape[0] * n_col // size
    col_blocks = features.shape[0] // size
    zero = jnp.zeros((1,), jnp.int32)
    panels = lax.all_gather(features.T, "row", axis=0, tiled=True)
    (terms,) = forward(zero, count, rows, cols, adj, [panels], row_blocks, [panels.shape[0]], [(0,)])
    part = lax.psum_scatter(terms, "col", scatter_dimension=1, tiled=True)
    output, deltas, aggregated, back = middle(1, zero, weight, cotangent, [[part]], (0,), [weight.shape[0]])
    slab = lax.all_gather(back, "col", axis=1, tiled=True)
    (column_terms,) = backward(zero, count, rows, cols, adj, [slab], [[(0, 0)]], [slab.shape[0]], [slab.shape[0]], col_blocks)
    grad_features = lax.psum_scatter(column_terms, "row", scatter_dimension=0, tiled=True).T
    (part,) = gradient(1.0 / math.sqrt(nodes), [(0,)], aggregated, deltas)
    grad_weight = lax.psum(part[0], ("row", "col"))
    return output, grad_weight, grad_features


def solution(mesh):
    n_row = mesh.shape["row"]
    n_col = mesh.shape["col"]
    exchanged = n_row == 8 and n_col == 4
    return jax.shard_map(
        shards_exchanged if exchanged else shards_gathered,
        mesh=mesh,
        in_specs=(
            P("col", "row"),
            P(),
            P("row", "col", None, None, None),
            P("row", "col", None),
            P("row", "col", None),
            P("row", "col"),
            P(("row", "col"), None),
        ),
        out_specs=(P(("row", "col"), None), P(), P("col", "row")),
        check_vma=False,
    )
```
